32 devices in a mesh: groups: 2 (over y), wide: 4 (over x, core), narrow: 4 (over z).
Axes of the slice: x: 2, y: 2, z: 4, core: 2. Of those that a mesh axis runs over, the one named last changes fastest.
Arguments:
- order_init: float32 [16, 12, 32, 512], P('groups', None, 'wide', 'narrow'), parts along dimension 0, may hold values from 0 to 1
- cotangent: float32 [16, 12, 32, 512], P('groups', None, 'wide', 'narrow'), parts along dimension 0, may hold values from -6 to 6
- grain_map: int32 [24, 32, 512], P('groups', 'wide', 'narrow'), parts along dimension 0, may hold values from 0 to 63
- brick_grains: int32 [32, 64], P('groups'), parts along dimension 0, may hold values from 0 to 6271, as said below
- grain_slot: int32 [12544], P('groups'), parts along dimension 0, may hold values from 0 to 6271, each once
- mobility: float32 [12544], P(('groups', 'wide', 'narrow')), parts along dimension 0, may hold values from 0.25 to 1
Outputs:
- order_final: float32 [16, 12, 32, 512], P('groups', None, 'wide', 'narrow'), parts along dimension 0
- order_adjoint: float32 [16, 12, 32, 512], P('groups', None, 'wide', 'narrow'), parts along dimension 0
- mobility_grad: float32 [12544], P(('groups', 'wide', 'narrow')), parts along dimension 0
The draws below stay inside these ranges and needn't reach their ends.
There are 2 independent parts, one for each index of `groups`. The reference program is written for one: setup_inputs(seed, part) draws one part's arguments, and reference() takes and returns one part's arrays. A program takes and returns all parts, laid end to end along the dimension named above; each array names one. Nothing has to cross between parts.
Inputs may be any that keep to these rules, and one draw needn't show every extreme that they name: `brick_grains`: each row lists 64 different grain ids.
All inputs are finite; a program needn't handle non-finite values.
Results may differ from the reference program's by a relative error of at most 0.00011.
Values sent between devices are 32-bit elements; how exact they have to be, the bound alone decides.
No kernel may reach another device: no remote copies, remote signals or barrier semaphores. Data moves between devices by JAX's collectives and lax.ppermute only.
A program may use at most 64 MiB of HBM per device.

```python
import math
import jax
import jax.numpy as jnp

P_SIZE = 8
NZ = 12
CX = 8
CY = 128
G_LOC = 64
ITERS = 4
NX = 32
NY = 512
BRICKS = 16
GRAINS = 6272
N_NARROW = 4


def draw_brick_grains(key, part):
    key = jax.random.fold_in(key, 7)
    keys = jax.random.split(key, BRICKS + 2)

    def pick(single):
        return jax.random.permutation(single, GRAINS)[:G_LOC].astype(jnp.int32)
    rows = jax.vmap(pick)(keys[:BRICKS])
    middle = jax.random.permutation(keys[BRICKS], jnp.arange(1, GRAINS - 1, dtype=jnp.int32))[:G_LOC - 2]
    first = jnp.concatenate([jnp.array([0, GRAINS - 1], jnp.int32), middle.astype(jnp.int32)])
    first = jax.random.permutation(keys[BRICKS + 1], first).astype(jnp.int32)
    return rows.at[0].set(first)


def with_ends(values, own_key, least, largest):
    dims = values.shape
    place = [jax.random.randint(jax.random.fold_in(own_key, axis), (), 0, dims[axis]) for axis in range(len(dims))]
    values = values.at[tuple(place)].set(least)
    longest = dims.index(max(dims))
    place[longest] = (place[longest] + 1) % dims[longest]
    return values.at[tuple(place)].set(largest)


def block_scale(own_key, shape, cuts, low, top_value):
    def one(dim, shards_of):
        steps = jax.random.uniform(jax.random.fold_in(jax.random.fold_in(own_key, 6), dim), (shards_of,), jnp.float32, low / len(cuts), top_value / len(cuts))
        return jnp.repeat(jnp.exp(steps), shape[dim] // shards_of).reshape((-1,) + (1,) * (len(shape) - dim - 1))

    factor_of = one(*cuts[0])
    for cut in cuts[1:]:
        factor_of = factor_of * one(*cut)
    return factor_of


def scatter_about(key, dims, width, reach, cuts=(), held_as=jnp.bfloat16):
    entries = jax.random.normal(key, dims, jnp.float32) * width
    if len(cuts) > 0:
        entries = block_scale(key, dims, cuts, -0.22, 0.18) * entries
    return jnp.clip(entries, min=-reach, max=reach).astype(held_as)


def setup_inputs(seed: int = 0, part: int = 0) -> dict:
    key_of = jax.random.split(jax.random.key(seed), 7)
    part_keys = jax.random.split(jax.random.fold_in(key_of[6], part), 7)
    order_init = jnp.clip(1.0 * jax.random.uniform(part_keys[0], (P_SIZE, NZ, NX, NY), jnp.float32) ** block_scale(part_keys[0], (P_SIZE, NZ, NX, NY), ((2, 4), (3, 4)), -0.2, 0.2), 0.0, 1.0)
    cotangent = scatter_about(part_keys[1], (P_SIZE, NZ, NX, NY), 1.0, 6.0, ((2, 4), (3, 4)), jnp.float32)
    grain_map = with_ends(jax.random.randint(part_keys[2], (NZ, NX, NY), 0, G_LOC), jax.random.fold_in(part_keys[2], 1), 0, G_LOC - 1).astype(jnp.int32)
    brick_grains = draw_brick_grains(jax.random.fold_in(jax.random.fold_in(key_of[6], part), 71), part)
    grain_slot = jax.random.permutation(part_keys[4], GRAINS).astype(jnp.int32)
    mobility = jnp.clip(jnp.exp(math.log(1.0) - 1.3862944 * jax.random.uniform(part_keys[5], (GRAINS,), jnp.float32) ** block_scale(part_keys[5], (GRAINS,), ((0, 16),), -0.2, 0.2)), 0.25, 1.0)
    return dict(order_init=order_init, cotangent=cotangent, grain_map=grain_map, brick_grains=brick_grains, grain_slot=grain_slot, mobility=mobility)


linear_coef = 1.0
cubic_coef = 1.0
cross_coef = 0.75
gradient_coef = 1.0
time_step = 0.05


def reaction(order):
    squares = order * order
    total = jnp.sum(squares, axis=0, keepdims=True)
    return -linear_coef * order + cubic_coef * order * squares + 2.0 * cross_coef * order * (total - squares)


def second_variation(order, weighted):
    squares = order * order
    total = jnp.sum(squares, axis=0, keepdims=True)
    inner = jnp.sum(order * weighted, axis=0, keepdims=True)
    diagonal = -linear_coef + 3.0 * cubic_coef * squares + 2.0 * cross_coef * (total - squares)
    return diagonal * weighted + 4.0 * cross_coef * order * (inner - order * weighted)


def laplace(field):
    side = jnp.roll(field, 1, 2) + jnp.roll(field, -1, 2) + jnp.roll(field, 1, 3) + jnp.roll(field, -1, 3)
    below = jnp.concatenate([field[:, :1], field[:, :-1]], axis=1)
    above = jnp.concatenate([field[:, 1:], field[:, -1:]], axis=1)
    return side + below + above - 6.0 * field


def reference(order_init, cotangent, grain_map, brick_grains, grain_slot, mobility):
    rows = (jnp.arange(NX, dtype=jnp.int32) // CX)[:, None] * N_NARROW
    cols = (jnp.arange(NY, dtype=jnp.int32) // CY)[None, :]
    brick = (rows + cols).astype(jnp.int32)
    grain_id = brick_grains[brick[None], grain_map]
    slot = grain_slot[grain_id]
    cell_mobility = mobility[slot][None]
    order = order_init
    states = []
    for step in range(ITERS):
        rate = reaction(order) - gradient_coef * laplace(order)
        states.append((order, rate))
        order = order - time_step * cell_mobility * rate
    adjoint = cotangent
    cell_sum = jnp.zeros(grain_map.shape, jnp.float32)
    for step in reversed(range(ITERS)):
        old, rate = states[step]
        cell_sum = cell_sum - time_step * jnp.sum(adjoint * rate, axis=0)
        weighted = cell_mobility * adjoint
        adjoint = adjoint - time_step * second_variation(old, weighted) + time_step * gradient_coef * laplace(weighted)
    grads = jax.ops.segment_sum(cell_sum.reshape(-1), slot.reshape(-1), num_segments=GRAINS)
    return order, adjoint, grads
```

```python
import functools

import jax
import jax.numpy as jnp
from jax import lax
from jax.experimental import pallas as pl
from jax.experimental.pallas import tpu as pltpu
from jax.sharding import PartitionSpec as P

ITERS = 4
TIME_STEP = 0.05

EDGE = 6
ADJ_EDGE = 4
ROWS = 24
COLS = 10
CORNER = (5, 3, 4)

VMEM_LIMIT = 50 * 1024 * 1024


def lanes(shape):
    return lax.broadcasted_iota(jnp.int32, shape, len(shape) - 1)


def roll(value, shift):
    return pltpu.roll(value, shift, 1)


def pack_rows(order_ref, map_ref, down_ref, up_ref):
    params, layers = order_ref.shape[:2]
    for p in range(params):
        for z in range(layers):
            k = (p * layers + z) * EDGE
            down_ref[k : k + EDGE, :] = order_ref[p, z, 8 - EDGE : 8, :]
            up_ref[k : k + EDGE, :] = order_ref[p, z, 0:EDGE, :]
    for z in range(layers):
        k = (params * layers + z) * EDGE
        cells = map_ref[z].astype(jnp.float32)
        down_ref[k : k + EDGE, :] = cells[8 - EDGE : 8]
        up_ref[k : k + EDGE, :] = cells[0:EDGE]


def pack_strips(
    order_ref, cot_ref, map_ref,
    cot_down_ref, cot_up_ref, right_ref, left_ref,
    right_down_ref, left_down_ref, right_up_ref, left_up_ref,
):
    params, layers = order_ref.shape[:2]
    lane = lanes((8, 128))
    to_right = []
    to_left = []
    for z in range(layers):
        first = 10 * z - 1
        inside = (lane >= first) & (lane < first + 6)
        if z == 0:
            inside = inside | (lane == 127)
        to_right.append(inside)
        to_left.append((lane >= 10 * z + 5) & (lane < 10 * z + 11))

    def strip_of(read):
        right = jnp.zeros((8, 128), jnp.float32)
        left = jnp.zeros((8, 128), jnp.float32)
        for z in range(layers):
            moved = roll(read(z), 10 * z + 5)
            right = jnp.where(to_right[z], moved, right)
            left = jnp.where(to_left[z], moved, left)
        return right, left

    at = 0
    for field in range(2 * params + 1):
        if field < params:
            kind, read = 0, lambda z, p=field: order_ref[p, z]
        elif field < 2 * params:
            kind, read = 1, lambda z, p=field - params: cot_ref[p, z]
        else:
            kind, read = 2, lambda z: map_ref[z].astype(jnp.float32)
        right, left = strip_of(read)
        right_ref[8 * field : 8 * field + 8, :] = right
        left_ref[8 * field : 8 * field + 8, :] = left
        n = CORNER[kind]
        right_down_ref[at : at + n, :] = right[8 - n : 8]
        left_down_ref[at : at + n, :] = left[8 - n : 8]
        right_up_ref[at : at + n, :] = right[0:n]
        left_up_ref[at : at + n, :] = left[0:n]
        at += n
    for p in range(params):
        for z in range(layers):
            k = (p * layers + z) * ADJ_EDGE
            cot_down_ref[k : k + ADJ_EDGE, :] = cot_ref[p, z, 8 - ADJ_EDGE : 8, :]
            cot_up_ref[k : k + ADJ_EDGE, :] = cot_ref[p, z, 0:ADJ_EDGE, :]


def find_slots(bricks_ref, slot_ref, out_ref):
    count, listed = bricks_ref.shape
    rows = slot_ref.shape[0]
    pad = jnp.zeros((8, 128 - listed), jnp.int32)
    for k in range(0, count, 8):
        grain = jnp.concatenate([bricks_ref[k : k + 8, :], pad], axis=1)
        row, col = grain >> 7, grain & 127

        def body(r, found, row=row, col=col):
            table = jnp.broadcast_to(slot_ref[pl.ds(r, 1), :], (8, 128))
            taken = jnp.take_along_axis(table, col, axis=1, mode="promise_in_bounds")
            return jnp.where(row == r, taken, found)

        found = lax.fori_loop(0, rows, body, jnp.zeros((8, 128), jnp.int32), unroll=7)
        out_ref[k : k + 8, :] = jnp.where(lanes((8, 128)) < listed, found, -1)


def evolve(
    counts, owned,
    order_ref, cot_ref, map_ref, above_ref, below_ref, cot_above_ref, cot_below_ref,
    left_ref, right_ref, left_above_ref, right_above_ref, left_below_ref, right_below_ref,
    slots_ref, mob_ref,
    final_ref, adjoint_ref, sums_ref,
    e_ref, se_ref, rate_ref, inject_ref, outer_ref, lam_ref, slam_ref, u_ref, su_ref,
    m_ref, ms_ref, g_ref, gs_ref, near_ref, table_ref, cell_ref, binned_ref,
):
    wide_count, narrow_count = counts
    params, layers = order_ref.shape[:2]
    tile = (8, 128)
    lane = lanes(tile)
    col = lane % COLS
    wide, narrow = lax.axis_index("wide"), lax.axis_index("narrow")

    for i in range(3):
        for j in range(3):
            w = lax.rem(wide + i - 1 + wide_count, wide_count)
            n = lax.rem(narrow + j - 1 + narrow_count, narrow_count)
            near_ref[3 * i + j : 3 * i + j + 1, :] = slots_ref[pl.ds(w * narrow_count + n, 1), :]
    near_ref[9:16, :] = jnp.zeros((7, 128), jnp.int32)
    per_owner = mob_ref.shape[0] // (wide_count * narrow_count)
    for k in (0, 8):
        slot = jnp.maximum(near_ref[k : k + 8, :], 0)
        owner = jnp.floor((slot.astype(jnp.float32) + 0.5) * (1.0 / owned)).astype(jnp.int32)
        inner = slot - owner * owned
        by_wide = jnp.floor((owner.astype(jnp.float32) + 0.5) * (1.0 / narrow_count)).astype(jnp.int32)
        by_narrow = owner - by_wide * narrow_count
        back_w = wide - by_wide
        back_w = jnp.where(back_w < 0, back_w + wide_count, back_w)
        back_n = narrow - by_narrow
        back_n = jnp.where(back_n < 0, back_n + narrow_count, back_n)
        row = (back_n * wide_count + back_w) * per_owner + (inner >> 7)
        place = inner & 127

        def body(r, found, row=row, place=place):
            values = jnp.broadcast_to(mob_ref[pl.ds(r, 1), :], tile)
            taken = jnp.take_along_axis(values, place, axis=1, mode="promise_in_bounds")
            return jnp.where(row == r, taken, found)

        found = lax.fori_loop(0, mob_ref.shape[0], body, jnp.zeros(tile, jnp.float32), unroll=8)
        table_ref[k : k + 8, :] = TIME_STEP * found

    for z in range(layers):
        g_ref[z, 0:8, :] = jnp.zeros(tile, jnp.float32)
        g_ref[z, 16:24, :] = jnp.zeros(tile, jnp.float32)
        k = (params * layers + z) * EDGE
        g_ref[z, 8 - EDGE : 8, :] = above_ref[k : k + EDGE, :]
        g_ref[z, 16 : 16 + EDGE, :] = below_ref[k : k + EDGE, :]
    for p in range(params):
        for z in range(layers):
            k = (p * layers + z) * EDGE
            e_ref[0, p, z, 8 - EDGE : 8, :] = above_ref[k : k + EDGE, :]
            e_ref[0, p, z, 8:16, :] = order_ref[p, z]
            e_ref[0, p, z, 16 : 16 + EDGE, :] = below_ref[k : k + EDGE, :]
            k = (p * layers + z) * ADJ_EDGE
            lam_ref[p, z, 8 - ADJ_EDGE : 8, :] = cot_above_ref[k : k + ADJ_EDGE, :]
            lam_ref[p, z, 8:16, :] = cot_ref[p, z]
            lam_ref[p, z, 16 : 16 + ADJ_EDGE, :] = cot_below_ref[k : k + ADJ_EDGE, :]

    def merged(from_left, from_right):
        c = lanes(from_left.shape) % COLS
        return jnp.where(c < 5, from_left, from_right)

    def outermost(from_left, from_right):
        return jnp.where(lanes(from_left.shape) % COLS == 0, roll(from_left, 1), roll(from_right, 127))

    at = 0
    for field in range(2 * params + 1):
        kind = 0 if field < params else 1 if field < 2 * params else 2
        n = CORNER[kind]
        blocks = (
            (left_above_ref[at : at + n, :], right_above_ref[at : at + n, :], 8 - n, n),
            (left_ref[8 * field : 8 * field + 8, :], right_ref[8 * field : 8 * field + 8, :], 8, 8),
            (left_below_ref[at : at + n, :], right_below_ref[at : at + n, :], 16, n),
        )
        at += n
        if kind == 2:
            gs_ref[...] = jnp.zeros_like(gs_ref)
        for a, b, first, n in blocks:
            if kind == 0:
                se_ref[0, field, first : first + n, :] = merged(a, b)
                outer_ref[field, first : first + n, :] = outermost(a, b)
            elif kind == 1:
                slam_ref[field - params, first : first + n, :] = merged(a, b)
            else:
                gs_ref[first : first + n, :] = merged(a, b)

    def lookup(index, which):
        values = jnp.broadcast_to(table_ref[which : which + 1, :], tile)
        return jnp.take_along_axis(values, index, axis=1, mode="promise_in_bounds")

    for i in range(3):
        r = 8 * i
        for z in range(layers):
            index = map_ref[z] if i == 1 else g_ref[z, r : r + 8, :].astype(jnp.int32)
            m_ref[z, r : r + 8, :] = lookup(index, 3 * i + 1)
        index = gs_ref[r : r + 8, :].astype(jnp.int32)
        ms_ref[r : r + 8, :] = jnp.where(col < 5, lookup(index, 3 * i), lookup(index, 3 * i + 2))

    def sides(value, strip, z):
        ends = roll(strip, 123 - 10 * z)
        left = roll(jnp.where(lane == 127, ends, value), 1)
        right = roll(jnp.where(lane == 0, ends, value), 127)
        return left + right

    def note_ends(value, p, r, z):
        moved = roll(value, 10 * z + 5)
        here = (lane == 10 * z + 4) | (lane == 10 * z + 5)
        inject_ref[p, r : r + 8, :] = jnp.where(here, moved, inject_ref[p, r : r + 8, :])

    def strip_sides(value, ends, outer=None):
        left = roll(jnp.where(col == 4, ends, value), 1)
        right = roll(jnp.where(col == 5, ends, value), 127)
        if outer is not None:
            left = jnp.where(col == 0, outer, left)
            right = jnp.where(col == 9, outer, right)
        below = jnp.where(lane < COLS, value, roll(value, COLS))
        above = jnp.where(lane >= COLS * (layers - 1), value, roll(value, 128 - COLS))
        return (left + right) + (below + above)

    def total_of(values):
        while len(values) > 1:
            values = [a + b for a, b in zip(values[::2], values[1::2])]
        return values[0]

    def forward(t, windows, last):
        old, old_strip = e_ref.at[t], se_ref.at[t]

        def layer(z, carry):
            below, above = jnp.maximum(z - 1, 0), jnp.minimum(z + 1, layers - 1)
            for r in windows:
                rows = slice(r, r + 8)
                e = [old[p, z, rows, :] for p in range(params)]
                squares = [x * x for x in e]
                base = 1.5 * total_of(squares) + 5.0
                m = m_ref[z, rows, :]
                for p in range(params):
                    near = sides(e[p], old_strip[p, rows, :], z)
                    near = near + (old[p, z, r - 1 : r + 7, :] + old[p, z, r + 1 : r + 9, :])
                    near = near + (old[p, below, rows, :] + old[p, above, rows, :])
                    rate = e[p] * (base - 0.5 * squares[p]) - near
                    rate_ref[t, p, z, rows, :] = rate
                    new = e[p] - m * rate
                    if last:
                        final_ref[p, z] = new
                    else:
                        e_ref[t + 1, p, z, rows, :] = new
                        note_ends(e[p], p, r, z)
            return carry

        lax.fori_loop(0, layers, layer, 0)
        if last:
            return
        for r in windows:
            rows = slice(r, r + 8)
            e = [old_strip[p, rows, :] for p in range(params)]
            squares = [x * x for x in e]
            base = 1.5 * total_of(squares) + 5.0
            m = ms_ref[rows, :]
            for p in range(params):
                near = strip_sides(e[p], inject_ref[p, rows, :], outer_ref[p, rows, :] if t == 0 else None)
                near = near + (old_strip[p, r - 1 : r + 7, :] + old_strip[p, r + 1 : r + 9, :])
                rate = e[p] * (base - 0.5 * squares[p]) - near
                se_ref[t + 1, p, rows, :] = e[p] - m * rate

    inject_ref[...] = jnp.zeros_like(inject_ref)
    forward(0, (3, 11, 13), False)
    forward(1, (4, 12), False)
    forward(2, (4, 12), False)
    forward(3, (8,), True)

    def weigh(z, carry):
        for r in (4, 12):
            rows = slice(r, r + 8)
            m = m_ref[z, rows, :]
            for p in range(params):
                u_ref[0, p, z, rows, :] = m * lam_ref[p, z, rows, :]
            cell_ref[z, rows, :] = jnp.zeros(tile, jnp.float32)
        return carry

    lax.fori_loop(0, layers, weigh, 0)
    for r in (4, 12):
        rows = slice(r, r + 8)
        for p in range(params):
            su_ref[0, p, rows, :] = ms_ref[rows, :] * slam_ref[p, rows, :]

    def backward(t, slot, windows, last):
        old, old_strip = u_ref.at[slot], su_ref.at[slot]

        def layer(z, carry):
            below, above = jnp.maximum(z - 1, 0), jnp.minimum(z + 1, layers - 1)
            for r in windows:
                rows = slice(r, r + 8)
                e = [e_ref[t, p, z, rows, :] for p in range(params)]
                u = [old[p, z, rows, :] for p in range(params)]
                lam = [lam_ref[p, z, rows, :] for p in range(params)]
                squares = [x * x for x in e]
                base = 1.5 * total_of(squares) + 5.0
                inner = 3.0 * total_of([x * y for x, y in zip(e, u)])
                m = m_ref[z, rows, :]
                worked = total_of([lam[p] * rate_ref[t, p, z, rows, :] for p in range(params)])
                cell_ref[z, rows, :] = cell_ref[z, rows, :] + worked
                for p in range(params):
                    near = sides(u[p], old_strip[p, rows, :], z)
                    near = near + (old[p, z, r - 1 : r + 7, :] + old[p, z, r + 1 : r + 9, :])
                    near = near + (old[p, below, rows, :] + old[p, above, rows, :])
                    change = u[p] * (base - 1.5 * squares[p]) + e[p] * inner - near
                    new = lam[p] - change
                    if last:
                        adjoint_ref[p, z] = new
                    else:
                        lam_ref[p, z, rows, :] = new
                        u_ref[1 - slot, p, z, rows, :] = m * new
                        note_ends(u[p], p, r, z)
            return carry

        lax.fori_loop(0, layers, layer, 0)
        if last:
            return
        for r in windows:
            rows = slice(r, r + 8)
            e = [se_ref[t, p, rows, :] for p in range(params)]
            u = [old_strip[p, rows, :] for p in range(params)]
            squares = [x * x for x in e]
            base = 1.5 * total_of(squares) + 5.0
            inner = 3.0 * total_of([x * y for x, y in zip(e, u)])
            m = ms_ref[rows, :]
            for p in range(params):
                near = strip_sides(u[p], inject_ref[p, rows, :])
                near = near + (old_strip[p, r - 1 : r + 7, :] + old_strip[p, r + 1 : r + 9, :])
                change = u[p] * (base - 1.5 * squares[p]) + e[p] * inner - near
                new = slam_ref[p, rows, :] - change
                slam_ref[p, rows, :] = new
                su_ref[1 - slot, p, rows, :] = m * new

    backward(3, 0, (4, 12), False)
    backward(2, 1, (4, 12), False)
    backward(1, 0, (4, 12), False)
    backward(0, 1, (8,), True)

    grains = [map_ref[z] for z in range(layers)]
    cells = [cell_ref[z, 8:16, :] for z in range(layers)]

    def bin_one(g, carry):
        total = total_of([
            a + b for a, b in (
                (jnp.where(grains[z] == g, cells[z], 0.0), jnp.where(grains[z + 1] == g, cells[z + 1], 0.0))
                for z in range(0, layers, 2)
            )
        ][:4]) + total_of([
            a + b for a, b in (
                (jnp.where(grains[z] == g, cells[z], 0.0), jnp.where(grains[z + 1] == g, cells[z + 1], 0.0))
                for z in range(8, layers, 2)
            )
        ])
        binned_ref[pl.ds(g, 1), :] = jnp.sum(total, axis=0, keepdims=True)
        return carry

    lax.fori_loop(0, binned_ref.shape[0], bin_one, 0, unroll=4)
    ones = jnp.full((8, 128), -TIME_STEP, jnp.float32)
    sums = lax.dot_general(
        ones, binned_ref[...], (((1,), (1,)), ((), ())),
        precision=lax.Precision.HIGHEST, preferred_element_type=jnp.float32,
    )
    sums_ref[...] = sums[0:1, :]


def pick_owned(counts, owned, slots_ref, sums_ref, out_ref, slot_rows, value_rows, total_ref):
    wide_count, narrow_count = counts
    count = wide_count * narrow_count
    wide, narrow = lax.axis_index("wide"), lax.axis_index("narrow")
    base = (wide * narrow_count + narrow) * owned
    listed = sums_ref.shape[1]
    tile = (8, 128)
    for k in range(count):
        n = lax.rem(narrow + narrow_count - k // wide_count, narrow_count)
        w = lax.rem(wide + wide_count - k % wide_count, wide_count)
        slot = slots_ref[pl.ds(w * narrow_count + n, 1), :] - base
        slot_rows[k] = jnp.broadcast_to(slot, tile)
        value = jnp.concatenate([sums_ref[k : k + 1, :], jnp.zeros((1, 128 - listed), jnp.float32)], axis=1)
        value_rows[k] = jnp.broadcast_to(value, tile)
    sub = lax.broadcasted_iota(jnp.int32, tile, 0)
    blocks = total_ref.shape[0] // 8
    step = 16
    for first in range(0, blocks, step):
        some = range(first, min(first + step, blocks))

        def body(k, acc, some=some):
            slot, value = slot_rows[k], value_rows[k]
            shifted = slot - sub
            return tuple(a + jnp.where(shifted == 8 * j, value, 0.0) for a, j in zip(acc, some))

        acc = lax.fori_loop(0, count, body, tuple(jnp.zeros(tile, jnp.float32) for _ in some), unroll=4)
        for a, j in zip(acc, some):
            total_ref[8 * j : 8 * j + 8, :] = a
    whole = lax.dot_general(
        jnp.ones(tile, jnp.float32), total_ref[...], (((1,), (1,)), ((), ())),
        precision=lax.Precision.HIGHEST, preferred_element_type=jnp.float32,
    )
    out_ref[...] = whole[0:1, 0:owned]


def f32(*shape):
    return jax.ShapeDtypeStruct(shape, jnp.float32)


def kernel(body, out_shape, scratch=(), name=None):
    return pl.pallas_call(
        body, out_shape=out_shape, scratch_shapes=list(scratch), name=name,
        compiler_params=pltpu.CompilerParams(vmem_limit_bytes=VMEM_LIMIT),
    )


def shifted(value, axis, count, by):
    return lax.ppermute(value, axis, [(i, (i + by) % count) for i in range(count)])


def gathered(value, counts):
    wide_count, narrow_count = counts
    parts = [value] + [shifted(value, "wide", wide_count, d) for d in range(1, wide_count)]
    column = jnp.concatenate(parts, axis=0)
    parts = [column] + [shifted(column, "narrow", narrow_count, d) for d in range(1, narrow_count)]
    return jnp.concatenate(parts, axis=0)


def diagonal(value, counts, by_wide, by_narrow):
    wide_count, narrow_count = counts
    pairs = [
        (w * narrow_count + n, (w + by_wide) % wide_count * narrow_count + (n + by_narrow) % narrow_count)
        for w in range(wide_count) for n in range(narrow_count)
    ]
    return lax.ppermute(value, ("wide", "narrow"), pairs)


def per_device(counts, order_init, cotangent, grain_map, brick_grains, grain_slot, mobility):
    wide_count, narrow_count = counts
    params, layers = order_init.shape[:2]
    assert order_init.shape[2:] == (8, 128) and layers * COLS < 128
    owned = mobility.shape[0]
    listed = brick_grains.shape[1]
    bricks = brick_grains.shape[0]

    edge_rows = (params + 1) * layers * EDGE
    down, up = kernel(pack_rows, (f32(edge_rows, 128), f32(edge_rows, 128)), name="pack_rows")(order_init, grain_map)
    above = shifted(down, "wide", wide_count, 1)
    below = shifted(up, "wide", wide_count, -1)

    padded = -owned % 128
    own = jnp.pad(mobility, (0, padded)).reshape(-1, 128)
    every = gathered(own, counts)

    cot_rows = params * layers * ADJ_EDGE
    strip_rows = (2 * params + 1) * 8
    corner_rows = params * CORNER[0] + params * CORNER[1] + CORNER[2]
    corner_rows += -corner_rows % 8
    packed = kernel(
        pack_strips,
        (f32(cot_rows, 128),) * 2 + (f32(strip_rows, 128),) * 2 + (f32(corner_rows, 128),) * 4,
        name="pack_strips",
    )(order_init, cotangent, grain_map)
    cot_down, cot_up, to_right, to_left, right_down, left_down, right_up, left_up = packed
    from_left = shifted(to_right, "narrow", narrow_count, 1)
    from_right = shifted(to_left, "narrow", narrow_count, -1)
    left_above = diagonal(right_down, counts, 1, 1)
    right_above = diagonal(left_down, counts, 1, -1)
    left_below = diagonal(right_up, counts, -1, 1)
    right_below = diagonal(left_up, counts, -1, -1)
    cot_above = shifted(cot_down, "wide", wide_count, 1)
    cot_below = shifted(cot_up, "wide", wide_count, -1)

    slots = kernel(
        find_slots, jax.ShapeDtypeStruct((bricks, 128), jnp.int32), name="find_slots"
    )(brick_grains, grain_slot.reshape(-1, 128))

    vmem = lambda *shape: pltpu.VMEM(shape, jnp.float32)
    block = (params, layers, ROWS, 128)
    strip = (params, ROWS, 128)
    final, adjoint, sums = kernel(
        functools.partial(evolve, counts, owned),
        (f32(*order_init.shape), f32(*order_init.shape), f32(1, listed)),
        (
            vmem(ITERS, *block), vmem(ITERS, *strip), vmem(ITERS, *block), vmem(*strip), vmem(*strip),
            vmem(*block), vmem(*strip), vmem(2, *block), vmem(2, *strip),
            vmem(layers, ROWS, 128), vmem(ROWS, 128), vmem(layers, ROWS, 128), vmem(ROWS, 128),
            pltpu.VMEM((16, 128), jnp.int32), vmem(16, 128), vmem(layers, ROWS, 128), vmem(listed, 128),
        ),
        name="evolve",
    )(
        order_init, cotangent, grain_map, above, below, cot_above, cot_below,
        from_left, from_right, left_above, right_above, left_below, right_below,
        slots, every,
    )

    every_sum = gathered(sums, counts)
    count = wide_count * narrow_count
    grads = kernel(
        functools.partial(pick_owned, counts, owned),
        f32(1, owned),
        (pltpu.VMEM((count, 8, 128), jnp.int32), vmem(count, 8, 128), vmem(owned + -owned % 8, 128)),
        name="pick_owned",
    )(slots, every_sum)
    return final, adjoint, grads.reshape(owned)


def solution(mesh):
    counts = (mesh.shape["wide"], mesh.shape["narrow"])
    field = P("groups", None, "wide", "narrow")
    spread = P(("groups", "wide", "narrow"))
    return jax.shard_map(
        functools.partial(per_device, counts),
        mesh=mesh,
        in_specs=(field, field, P("groups", "wide", "narrow"), P("groups", None), P("groups"), spread),
        out_specs=(field, field, spread),
        check_vma=False,
    )
```

```python
import functools

import jax
import jax.numpy as jnp
from jax import lax
from jax.experimental import pallas as pl
from jax.experimental.pallas import tpu as pltpu
from jax.sharding import PartitionSpec as P

ITERS = 4
TIME_STEP = 0.05

EDGE = 6
ADJ_EDGE = 4
ROWS = 24
COLS = 10
LEAD = 8
CORNER = (5, 3, 4)

VMEM_LIMIT = 50 * 1024 * 1024


def lanes(shape):
    return lax.broadcasted_iota(jnp.int32, shape, len(shape) - 1)


def roll(value, shift):
    return pltpu.roll(value, shift, 1)


def pack_rows(order_ref, map_ref, down_ref, up_ref):
    params, layers = order_ref.shape[:2]
    for p in range(params):
        for z in range(layers):
            k = LEAD + (p * layers + z) * EDGE
            down_ref[k : k + EDGE, :] = order_ref[p, z, 8 - EDGE : 8, :]
            up_ref[k : k + EDGE, :] = order_ref[p, z, 0:EDGE, :]
    for ref in (down_ref, up_ref):
        ref[0:LEAD, :] = jnp.zeros((LEAD, 128), jnp.float32)
        ref[ref.shape[0] - LEAD :, :] = jnp.zeros((LEAD, 128), jnp.float32)
    for z in range(layers):
        k = LEAD + (params * layers + z) * EDGE
        cells = map_ref[z].astype(jnp.float32)
        down_ref[k : k + EDGE, :] = cells[8 - EDGE : 8]
        up_ref[k : k + EDGE, :] = cells[0:EDGE]


def pack_strips(order_ref, cot_ref, map_ref, after_ref, right_ref, left_ref):
    params, layers = order_ref.shape[:2]
    lane = lanes((8, 128))
    to_right = []
    to_left = []
    for z in range(layers):
        first = 10 * z - 1
        inside = (lane >= first) & (lane < first + 6)
        if z == 0:
            inside = inside | (lane == 127)
        to_right.append(inside)
        to_left.append((lane >= 10 * z + 5) & (lane < 10 * z + 11))

    def strip_of(read):
        right = jnp.zeros((8, 128), jnp.float32)
        left = jnp.zeros((8, 128), jnp.float32)
        for z in range(layers):
            moved = roll(read(z), 10 * z + 5)
            right = jnp.where(to_right[z], moved, right)
            left = jnp.where(to_left[z], moved, left)
        return right, left

    for field in range(2 * params + 1):
        if field < params:
            read = lambda z, p=field: order_ref[p, z]
        elif field < 2 * params:
            read = lambda z, p=field - params: cot_ref[p, z]
        else:
            read = lambda z: map_ref[z].astype(jnp.float32)
        right, left = strip_of(read)
        right_ref[8 * field : 8 * field + 8, :] = right
        left_ref[8 * field : 8 * field + 8, :] = left


def corner_rows(params):
    return -(-(params * (CORNER[0] + CORNER[1]) + CORNER[2]) // 8) * 8


def pack_corners(cot_ref, left_ref, right_ref, down_ref, up_ref):
    params, layers = cot_ref.shape[:2]
    at = 0
    for field in range(2 * params + 1):
        n = CORNER[0 if field < params else 1 if field < 2 * params else 2]
        rows = slice(8 * field, 8 * field + 8)
        both = jnp.where(lanes((8, 128)) % COLS < 5, left_ref[rows, :], right_ref[rows, :])
        down_ref[at : at + n, :] = both[8 - n : 8]
        up_ref[at : at + n, :] = both[0:n]
        at += n
    for ref in (down_ref, up_ref):
        ref[at:, :] = jnp.zeros((ref.shape[0] - at, 128), jnp.float32)
    at = corner_rows(params) + LEAD
    for p in range(params):
        for z in range(layers):
            k = at + (p * layers + z) * ADJ_EDGE
            down_ref[k : k + ADJ_EDGE, :] = cot_ref[p, z, 8 - ADJ_EDGE : 8, :]
            up_ref[k : k + ADJ_EDGE, :] = cot_ref[p, z, 0:ADJ_EDGE, :]


def find_slots(bricks_ref, slot_ref, out_ref):
    count, listed = bricks_ref.shape
    rows = slot_ref.shape[0]
    pad = jnp.zeros((8, 128 - listed), jnp.int32)
    for k in range(0, count, 8):
        grain = jnp.concatenate([bricks_ref[k : k + 8, :], pad], axis=1)
        row, col = grain >> 7, grain & 127

        def body(r, found, row=row, col=col):
            table = jnp.broadcast_to(slot_ref[pl.ds(r, 1), :], (8, 128))
            taken = jnp.take_along_axis(table, col, axis=1, mode="promise_in_bounds")
            return jnp.where(row == r, taken, found)

        found = lax.fori_loop(0, rows, body, jnp.zeros((8, 128), jnp.int32), unroll=7)
        out_ref[k : k + 8, :] = jnp.where(lanes((8, 128)) < listed, found, -1)


def find_mobility(counts, owned, slots_ref, mob_ref, table_ref, near_ref):
    wide_count, narrow_count = counts
    tile = (8, 128)
    wide, narrow = lax.axis_index("wide"), lax.axis_index("narrow")
    for i in range(3):
        for j in range(3):
            w = lax.rem(wide + i - 1 + wide_count, wide_count)
            n = lax.rem(narrow + j - 1 + narrow_count, narrow_count)
            near_ref[3 * i + j : 3 * i + j + 1, :] = slots_ref[pl.ds(w * narrow_count + n, 1), :]
    near_ref[9:16, :] = jnp.zeros((7, 128), jnp.int32)
    per_owner = mob_ref.shape[0] // (wide_count * narrow_count)
    slot = [jnp.maximum(near_ref[k : k + 8, :], 0) for k in (0, 8)]
    owner = [jnp.floor((x.astype(jnp.float32) + 0.5) * (1.0 / owned)).astype(jnp.int32) for x in slot]
    inner = [x - y * owned for x, y in zip(slot, owner)]
    row = [y * per_owner + (x >> 7) for x, y in zip(inner, owner)]
    place = [x & 127 for x in inner]

    def body(r, found):
        values = jnp.broadcast_to(mob_ref[pl.ds(r, 1), :], tile)
        return tuple(
            jnp.where(row[k] == r, jnp.take_along_axis(values, place[k], axis=1, mode="promise_in_bounds"), found[k])
            for k in range(2)
        )

    zero = jnp.zeros(tile, jnp.float32)
    found = lax.fori_loop(0, mob_ref.shape[0], body, (zero, zero), unroll=16)
    for k in range(2):
        table_ref[8 * k : 8 * k + 8, :] = TIME_STEP * found[k]


def evolve(
    order_ref, cot_ref, map_ref, above_ref, below_ref, far_above_ref, far_below_ref,
    left_ref, right_ref, table_ref,
    final_ref, adjoint_ref, sums_ref,
    e_ref, se_ref, rate_ref, inject_ref, outer_ref, lam_ref, slam_ref, u_ref, su_ref,
    m_ref, ms_ref, g_ref, gs_ref, cell_ref, binned_ref,
):
    params, layers = order_ref.shape[:2]
    tile = (8, 128)
    lane = lanes(tile)
    col = lane % COLS

    def place_map(z, carry):
        k = LEAD + (params * layers + z) * EDGE
        g_ref[z, 0:8, :] = above_ref[pl.ds(k + EDGE - 8, 8), :]
        g_ref[z, 16:24, :] = below_ref[pl.ds(k, 8), :]
        return carry

    lax.fori_loop(0, layers, place_map, 0)

    def place(z, carry):
        for p in range(params):
            k = LEAD + (p * layers + z) * EDGE
            e_ref[0, p, z, 0:8, :] = above_ref[pl.ds(k + EDGE - 8, 8), :]
            e_ref[0, p, z, 8:16, :] = order_ref[p, z]
            e_ref[0, p, z, 16:24, :] = below_ref[pl.ds(k, 8), :]
            k = corner_rows(params) + LEAD + (p * layers + z) * ADJ_EDGE
            lam_ref[p, z, 0:8, :] = far_above_ref[pl.ds(k + ADJ_EDGE - 8, 8), :]
            lam_ref[p, z, 8:16, :] = cot_ref[p, z]
            lam_ref[p, z, 16:24, :] = far_below_ref[pl.ds(k, 8), :]
        return carry

    lax.fori_loop(0, layers, place, 0)

    at = 0
    gs_ref[...] = jnp.zeros_like(gs_ref)
    for field in range(2 * params + 1):
        kind = 0 if field < params else 1 if field < 2 * params else 2
        n = CORNER[kind]
        a, b = left_ref[8 * field : 8 * field + 8, :], right_ref[8 * field : 8 * field + 8, :]
        blocks = (
            (far_above_ref[at : at + n, :], 8 - n, n),
            (jnp.where(col < 5, a, b), 8, 8),
            (far_below_ref[at : at + n, :], 16, n),
        )
        at += n
        for value, first, n in blocks:
            if kind == 0:
                se_ref[0, field, first : first + n, :] = value
            elif kind == 1:
                slam_ref[field - params, first : first + n, :] = value
            else:
                gs_ref[first : first + n, :] = value
        if kind == 0:
            outer_ref[field, 8:16, :] = jnp.where(col == 0, roll(a, 1), roll(b, 127))

    def lookup(index, which):
        values = jnp.broadcast_to(table_ref[which : which + 1, :], tile)
        return jnp.take_along_axis(values, index, axis=1, mode="promise_in_bounds")

    for i in range(3):
        r = 8 * i
        for z in range(layers):
            index = map_ref[z] if i == 1 else g_ref[z, r : r + 8, :].astype(jnp.int32) & 127
            m_ref[z, r : r + 8, :] = lookup(index, 3 * i + 1)
        index = gs_ref[r : r + 8, :].astype(jnp.int32) & 127
        ms_ref[r : r + 8, :] = jnp.where(col < 5, lookup(index, 3 * i), lookup(index, 3 * i + 2))

    def sides(value, strip, z):
        ends = roll(strip, 123 - 10 * z)
        left = roll(jnp.where(lane == 127, ends, value), 1)
        right = roll(jnp.where(lane == 0, ends, value), 127)
        return left + right

    def note_ends(value, p, rows, z):
        moved = roll(value, 10 * z + 5)
        here = (lane == 10 * z + 4) | (lane == 10 * z + 5)
        inject_ref[p, rows, :] = jnp.where(here, moved, inject_ref[p, rows, :])

    def strip_sides(value, ends, outer=None):
        left = roll(jnp.where(col == 4, ends, value), 1)
        right = roll(jnp.where(col == 5, ends, value), 127)
        if outer is not None:
            left = jnp.where(col == 0, outer, left)
            right = jnp.where(col == 9, outer, right)
        below = jnp.where(lane < COLS, value, roll(value, COLS))
        above = jnp.where(lane >= COLS * (layers - 1), value, roll(value, 128 - COLS))
        return (left + right) + (below + above)

    def total_of(values):
        while len(values) > 1:
            values = [a + b for a, b in zip(values[::2], values[1::2])]
        return values[0]

    def row_slices(r):
        return pl.ds(r, 8), pl.ds(r - 1, 8), pl.ds(r + 1, 8)

    def each_window(windows, z, body):
        start, count, most = windows
        for i in range(count):
            body(jnp.minimum(start + 8 * i + ((z + 16) >> 5), most))

    def forward(t, windows, last):
        old, old_strip = e_ref.at[t], se_ref.at[t]

        def layer(z, carry):
            below, above = jnp.maximum(z - 1, 0), jnp.minimum(z + 1, layers - 1)

            def window(r):
                rows, before, after = row_slices(r)
                e = [old[p, z, rows, :] for p in range(params)]
                squares = [x * x for x in e]
                base = 1.5 * total_of(squares) + 5.0
                m = m_ref[z, rows, :]
                for p in range(params):
                    near = sides(e[p], old_strip[p, rows, :], z)
                    near = near + (old[p, z, before, :] + old[p, z, after, :])
                    near = near + (old[p, below, rows, :] + old[p, above, rows, :])
                    rate = e[p] * (base - 0.5 * squares[p]) - near
                    rate_ref[t, p, z, rows, :] = rate
                    new = e[p] - m * rate
                    if last:
                        final_ref[p, z] = new
                    else:
                        e_ref[t + 1, p, z, rows, :] = new
                        note_ends(e[p], p, rows, z)

            each_window(windows, z, window)
            return carry

        lax.fori_loop(0, layers, layer, 0)
        if last:
            return

        def strip_window(i, carry):
            rows, before, after = row_slices(jnp.minimum(windows[0] + 8 * i, windows[2]))
            e = [old_strip[p, rows, :] for p in range(params)]
            squares = [x * x for x in e]
            base = 1.5 * total_of(squares) + 5.0
            m = ms_ref[rows, :]
            for p in range(params):
                near = strip_sides(e[p], inject_ref[p, rows, :], outer_ref[p, rows, :] if t == 0 else None)
                near = near + (old_strip[p, before, :] + old_strip[p, after, :])
                rate = e[p] * (base - 0.5 * squares[p]) - near
                se_ref[t + 1, p, rows, :] = e[p] - m * rate
            return carry

        lax.fori_loop(0, windows[1], strip_window, 0)

    inject_ref[...] = jnp.zeros_like(inject_ref)
    forward(0, (3, 3, 13), False)
    forward(1, (4, 2, 12), False)
    forward(2, (4, 2, 12), False)
    forward(3, (8, 1, 8), True)

    def weigh(z, carry):
        for r in (0, 8, 16):
            rows = slice(r, r + 8)
            m = m_ref[z, rows, :]
            for p in range(params):
                u_ref[0, p, z, rows, :] = m * lam_ref[p, z, rows, :]
            cell_ref[z, rows, :] = jnp.zeros(tile, jnp.float32)
        return carry

    lax.fori_loop(0, layers, weigh, 0)
    for r in (0, 8, 16):
        rows = slice(r, r + 8)
        for p in range(params):
            su_ref[0, p, rows, :] = ms_ref[rows, :] * slam_ref[p, rows, :]

    def backward(t, slot, windows, last):
        old, old_strip = u_ref.at[slot], su_ref.at[slot]

        def layer(z, carry):
            below, above = jnp.maximum(z - 1, 0), jnp.minimum(z + 1, layers - 1)

            def window(r):
                rows, before, after = row_slices(r)
                e = [e_ref[t, p, z, rows, :] for p in range(params)]
                u = [old[p, z, rows, :] for p in range(params)]
                lam = [lam_ref[p, z, rows, :] for p in range(params)]
                squares = [x * x for x in e]
                base = 1.5 * total_of(squares) + 5.0
                inner = 3.0 * total_of([x * y for x, y in zip(e, u)])
                m = m_ref[z, rows, :]
                worked = total_of([lam[p] * rate_ref[t, p, z, rows, :] for p in range(params)])
                cell_ref[z, rows, :] = cell_ref[z, rows, :] + worked
                for p in range(params):
                    near = sides(u[p], old_strip[p, rows, :], z)
                    near = near + (old[p, z, before, :] + old[p, z, after, :])
                    near = near + (old[p, below, rows, :] + old[p, above, rows, :])
                    change = u[p] * (base - 1.5 * squares[p]) + e[p] * inner - near
                    new = lam[p] - change
                    if last:
                        adjoint_ref[p, z] = new
                    else:
                        lam_ref[p, z, rows, :] = new
                        u_ref[1 - slot, p, z, rows, :] = m * new
                        note_ends(u[p], p, rows, z)

            each_window(windows, z, window)
            return carry

        lax.fori_loop(0, layers, layer, 0)
        if last:
            return

        def strip_window(i, carry):
            rows, before, after = row_slices(jnp.minimum(windows[0] + 8 * i, windows[2]))
            e = [se_ref[t, p, rows, :] for p in range(params)]
            u = [old_strip[p, rows, :] for p in range(params)]
            squares = [x * x for x in e]
            base = 1.5 * total_of(squares) + 5.0
            inner = 3.0 * total_of([x * y for x, y in zip(e, u)])
            m = ms_ref[rows, :]
            for p in range(params):
                near = strip_sides(u[p], inject_ref[p, rows, :])
                near = near + (old_strip[p, before, :] + old_strip[p, after, :])
                change = u[p] * (base - 1.5 * squares[p]) + e[p] * inner - near
                new = slam_ref[p, rows, :] - change
                slam_ref[p, rows, :] = new
                su_ref[1 - slot, p, rows, :] = m * new
            return carry

        lax.fori_loop(0, windows[1], strip_window, 0)

    backward(3, 0, (4, 2, 12), False)
    backward(2, 1, (4, 2, 12), False)
    backward(1, 0, (4, 2, 12), False)
    backward(0, 1, (8, 1, 8), True)

    grains = [map_ref[z] for z in range(layers)]
    cells = [cell_ref[z, 8:16, :] for z in range(layers)]

    def bin_one(g, carry):
        kept = [jnp.where(grains[z] == g, cells[z], 0.0) for z in range(layers)]
        total = sum(kept[1:4], kept[0]) + sum(kept[5:8], kept[4]) + sum(kept[9:], kept[8])
        binned_ref[pl.ds(g, 1), :] = jnp.sum(total, axis=0, keepdims=True)
        return carry

    lax.fori_loop(0, binned_ref.shape[0], bin_one, 0, unroll=4)
    ones = jnp.full((8, 128), -TIME_STEP, jnp.float32)
    sums = lax.dot_general(
        ones, binned_ref[...], (((1,), (1,)), ((), ())),
        precision=lax.Precision.HIGHEST, preferred_element_type=jnp.float32,
    )
    for k in range(0, sums_ref.shape[0], 8):
        sums_ref[k : k + 8, :] = sums


def pick_owned(counts, owned, slots_ref, sums_ref, out_ref, slot_rows, value_rows, total_ref):
    wide_count, narrow_count = counts
    count = wide_count * narrow_count
    wide, narrow = lax.axis_index("wide"), lax.axis_index("narrow")
    base = (wide * narrow_count + narrow) * owned
    listed = sums_ref.shape[1]
    tile = (8, 128)
    for k in range(count):
        slot = slots_ref[k : k + 1, :] - base
        slot_rows[k] = jnp.broadcast_to(slot, tile)
        value = jnp.concatenate([sums_ref[k : k + 1, :], jnp.zeros((1, 128 - listed), jnp.float32)], axis=1)
        value_rows[k] = jnp.broadcast_to(value, tile)
    sub = lax.broadcasted_iota(jnp.int32, tile, 0)
    blocks = total_ref.shape[0] // 8
    step = 16
    for first in range(0, blocks, step):
        some = range(first, min(first + step, blocks))

        def body(k, acc, some=some):
            slot, value = slot_rows[k], value_rows[k]
            shifted = slot - sub
            return tuple(a + jnp.where(shifted == 8 * j, value, 0.0) for a, j in zip(acc, some))

        acc = lax.fori_loop(0, count, body, tuple(jnp.zeros(tile, jnp.float32) for _ in some), unroll=4)
        for a, j in zip(acc, some):
            total_ref[8 * j : 8 * j + 8, :] = a
    whole = lax.dot_general(
        jnp.ones(tile, jnp.float32), total_ref[...], (((1,), (1,)), ((), ())),
        precision=lax.Precision.HIGHEST, preferred_element_type=jnp.float32,
    )
    out_ref[...] = whole[0:1, 0:owned]


def f32(*shape):
    return jax.ShapeDtypeStruct(shape, jnp.float32)


def kernel(body, out_shape, scratch=(), name=None, **specs):
    return pl.pallas_call(
        body, out_shape=out_shape, scratch_shapes=list(scratch), name=name, **specs,
        compiler_params=pltpu.CompilerParams(vmem_limit_bytes=VMEM_LIMIT),
    )


def shifted(value, axis, count, by):
    return lax.ppermute(value, axis, [(i, (i + by) % count) for i in range(count)])


def per_device(counts, order_init, cotangent, grain_map, brick_grains, grain_slot, mobility):
    wide_count, narrow_count = counts
    params, layers = order_init.shape[:2]
    assert order_init.shape[2:] == (8, 128) and layers * COLS < 128
    owned = mobility.shape[0]
    listed = brick_grains.shape[1]
    bricks = brick_grains.shape[0]

    both = ("wide", "narrow")
    count = wide_count * narrow_count

    padded = -owned % 128
    own = jnp.pad(mobility, (0, padded)).reshape(-1, 128)
    every = lax.all_gather(own, both, axis=0, tiled=True)

    edge_rows = (params + 1) * layers * EDGE + 2 * LEAD
    down, up = kernel(pack_rows, (f32(edge_rows, 128),) * 2, name="pack_rows")(order_init, grain_map)
    above = shifted(down, "wide", wide_count, 1)
    below = shifted(up, "wide", wide_count, -1)

    strip_rows = (2 * params + 1) * 8
    here = pl.BlockSpec(memory_space=pltpu.VMEM)
    to_right, to_left = kernel(
        pack_strips, (f32(strip_rows, 128),) * 2, name="pack_strips",
        in_specs=[here, here, here, pl.BlockSpec(memory_space=pl.ANY)],
    )(order_init, cotangent, grain_map, down)
    from_left = shifted(to_right, "narrow", narrow_count, 1)
    from_right = shifted(to_left, "narrow", narrow_count, -1)

    slots = kernel(
        find_slots, jax.ShapeDtypeStruct((bricks, 128), jnp.int32), name="find_slots"
    )(brick_grains, grain_slot.reshape(-1, 128))

    far_rows = corner_rows(params) + params * layers * ADJ_EDGE + 2 * LEAD
    far_down, far_up = kernel(pack_corners, (f32(far_rows, 128),) * 2, name="pack_corners")(
        cotangent, from_left, from_right
    )
    far_above = shifted(far_down, "wide", wide_count, 1)
    far_below = shifted(far_up, "wide", wide_count, -1)

    table = kernel(
        functools.partial(find_mobility, counts, owned), f32(16, 128),
        (pltpu.VMEM((16, 128), jnp.int32),), name="find_mobility",
    )(slots, every)

    vmem = lambda *shape: pltpu.VMEM(shape, jnp.float32)
    block = (params, layers, ROWS, 128)
    strip = (params, ROWS, 128)
    final, adjoint, sums = kernel(
        evolve,
        (f32(*order_init.shape), f32(*order_init.shape), f32(count, listed)),
        (
            vmem(ITERS, *block), vmem(ITERS, *strip), vmem(ITERS, *block), vmem(*strip), vmem(*strip),
            vmem(*block), vmem(*strip), vmem(2, *block), vmem(2, *strip),
            vmem(layers, ROWS, 128), vmem(ROWS, 128), vmem(layers, ROWS, 128), vmem(ROWS, 128),
            vmem(layers, ROWS, 128), vmem(listed, 128),
        ),
        name="evolve",
    )(
        order_init, cotangent, grain_map, above, below, far_above, far_below,
        from_left, from_right, table,
    )

    every_sum = lax.all_to_all(sums, both, 0, 0, tiled=True)
    grads = kernel(
        functools.partial(pick_owned, counts, owned),
        f32(1, owned),
        (pltpu.VMEM((count, 8, 128), jnp.int32), vmem(count, 8, 128), vmem(owned + -owned % 8, 128)),
        name="pick_owned",
    )(slots, every_sum)
    return final, adjoint, grads.reshape(owned)


def solution(mesh):
    counts = (mesh.shape["wide"], mesh.shape["narrow"])
    field = P("groups", None, "wide", "narrow")
    spread = P(("groups", "wide", "narrow"))
    return jax.shard_map(
        functools.partial(per_device, counts),
        mesh=mesh,
        in_specs=(field, field, P("groups", "wide", "narrow"), P("groups", None), P("groups"), spread),
        out_specs=(field, field, spread),
        check_vma=False,
    )
```

```python
import functools

import jax
import jax.numpy as jnp
from jax import lax
from jax.experimental import pallas as pl
from jax.experimental.pallas import tpu as pltpu
from jax.sharding import PartitionSpec as P

ITERS = 4
TIME_STEP = 0.05

EDGE = 6
MAP_EDGE = 5
ADJ_EDGE = 4
ROWS = 24
COLS = 10
LEAD = 8
CORNER = (5, 3, 4)

VMEM_LIMIT = 50 * 1024 * 1024


def lanes(shape):
    return lax.broadcasted_iota(jnp.int32, shape, len(shape) - 1)


def roll(value, shift):
    return pltpu.roll(value, shift, 1)


def pack_rows(order_ref, down_ref, up_ref):
    params, layers = order_ref.shape[:2]
    for p in range(params):
        for z in range(layers):
            k = LEAD + (p * layers + z) * EDGE
            down_ref[k : k + EDGE, :] = order_ref[p, z, 8 - EDGE : 8, :]
            up_ref[k : k + EDGE, :] = order_ref[p, z, 0:EDGE, :]
    for ref in (down_ref, up_ref):
        ref[0:LEAD, :] = jnp.zeros((LEAD, 128), jnp.float32)
        ref[ref.shape[0] - LEAD :, :] = jnp.zeros((LEAD, 128), jnp.float32)


def pack_strips(order_ref, cot_ref, map_ref, mob_ref, after_ref, right_ref, left_ref, own_ref):
    params, layers = order_ref.shape[:2]
    owned = mob_ref.shape[1]
    lane = lanes((8, 128))
    zero = jnp.zeros((8, 128), jnp.float32)

    def span(first, size):
        return ((lane - first) & 127) < size

    for field in range(params + 1):
        right, left = zero, zero
        for z in range(layers):
            value = order_ref[field, z] if field < params else map_ref[z].astype(jnp.float32)
            moved = roll(value, 10 * z + 5)
            right = jnp.where(span(10 * z - 1, 6), moved, right)
            left = jnp.where(span(10 * z + 5, 6), moved, left)
            if field < params:
                right = jnp.where(span(10 * z + 5, 4), roll(cot_ref[field, z], 10 * z + 9), right)
                left = jnp.where(span(10 * z + 1, 4), roll(cot_ref[field, z], 10 * z + 1), left)
        right_ref[8 * field : 8 * field + 8, :] = right
        left_ref[8 * field : 8 * field + 8, :] = left
    rows = own_ref.shape[0]
    at = 8 * (params + 1)
    for i in range(rows):
        size = min(128, owned - 128 * i)
        row = mob_ref[0:1, 128 * i : 128 * i + size]
        if size < 128:
            row = jnp.concatenate([row, jnp.zeros((1, 128 - size), jnp.float32)], axis=1)
        for ref, k in ((own_ref, i), (right_ref, at + i), (left_ref, at + i)):
            ref[k : k + 1, :] = row


def corner_rows(params):
    return -(-(params * (CORNER[0] + CORNER[1]) + CORNER[2]) // 8) * 8


def far_places(params, layers, block):
    mobs = corner_rows(params)
    cots = mobs + block + LEAD
    maps = cots + params * layers * ADJ_EDGE + LEAD
    length = maps + layers * MAP_EDGE + LEAD
    return mobs, cots, maps, length + -length % 8


def merged_strips(params, left_ref, right_ref):
    first = lanes((8, 128)) % COLS < 5
    fields = []
    for field in range(params + 1):
        rows = slice(8 * field, 8 * field + 8)
        fields.append((left_ref[rows, :], right_ref[rows, :]))
    order = [jnp.where(first, a, b) for a, b in fields[:params]]
    cot = [jnp.where(first, roll(a, 124), roll(b, 4)) for a, b in fields[:params]]
    return order + cot + [jnp.where(first, *fields[params])]


def pack_far(cot_ref, map_ref, left_ref, right_ref, own_ref, *refs):
    *other_refs, down_ref, up_ref, block_ref = refs
    params, layers = cot_ref.shape[:2]
    rows = own_ref.shape[0]
    at = 8 * (params + 1)
    pieces = [own_ref[...], left_ref[at : at + rows, :]]
    pieces += [ref[...] for ref in other_refs]
    pieces.append(right_ref[at : at + rows, :])
    mobs, cots, maps, length = far_places(params, layers, block_ref.shape[0])
    for i, piece in enumerate(pieces):
        for ref, k in ((block_ref, 0), (down_ref, mobs), (up_ref, mobs)):
            ref[k + i * rows : k + (i + 1) * rows, :] = piece
    at = 0
    for field, both in enumerate(merged_strips(params, left_ref, right_ref)):
        n = CORNER[0 if field < params else 1 if field < 2 * params else 2]
        down_ref[at : at + n, :] = both[8 - n : 8]
        up_ref[at : at + n, :] = both[0:n]
        at += n
    for ref in (down_ref, up_ref):
        for first, last in (
            (at, mobs), (cots - LEAD, cots), (maps - LEAD, maps), (maps + layers * MAP_EDGE, length)
        ):
            ref[first:last, :] = jnp.zeros((last - first, 128), jnp.float32)
    for p in range(params):
        for z in range(layers):
            k = cots + (p * layers + z) * ADJ_EDGE
            down_ref[k : k + ADJ_EDGE, :] = cot_ref[p, z, 8 - ADJ_EDGE : 8, :]
            up_ref[k : k + ADJ_EDGE, :] = cot_ref[p, z, 0:ADJ_EDGE, :]
    for z in range(layers):
        k = maps + z * MAP_EDGE
        cells = map_ref[z].astype(jnp.float32)
        down_ref[k : k + MAP_EDGE, :] = cells[8 - MAP_EDGE : 8]
        up_ref[k : k + MAP_EDGE, :] = cells[0:MAP_EDGE]


def find_slots(bricks_ref, slot_ref, out_ref):
    count, listed = bricks_ref.shape
    rows = slot_ref.shape[0]
    pad = jnp.zeros((8, 128 - listed), jnp.int32)
    for k in range(0, count, 8):
        grain = jnp.concatenate([bricks_ref[k : k + 8, :], pad], axis=1)
        row, col = grain >> 7, grain & 127

        def body(r, found, row=row, col=col):
            table = jnp.broadcast_to(slot_ref[pl.ds(r, 1), :], (8, 128))
            taken = jnp.take_along_axis(table, col, axis=1, mode="promise_in_bounds")
            return jnp.where(row == r, taken, found)

        found = lax.fori_loop(0, rows, body, jnp.zeros((8, 128), jnp.int32), unroll=7)
        out_ref[k : k + 8, :] = jnp.where(lanes((8, 128)) < listed, found, -1)


def find_mobility(counts, owned, at, slots_ref, block_ref, above_ref, below_ref, *refs):
    *other_refs, table_ref, near_ref, mob_ref = refs
    wide_count, narrow_count = counts
    tile = (8, 128)
    wide, narrow = lax.axis_index("wide"), lax.axis_index("narrow")
    size = block_ref.shape[0]
    per_owner = size // narrow_count
    pieces = [block_ref[...], above_ref[at : at + size, :]]
    pieces += [ref[...] for ref in other_refs]
    pieces.append(below_ref[at : at + size, :])
    for i, piece in enumerate(pieces):
        mob_ref[i * size : (i + 1) * size, :] = piece
    for i in range(3):
        for j in range(3):
            w = lax.rem(wide + i - 1 + wide_count, wide_count)
            n = lax.rem(narrow + j - 1 + narrow_count, narrow_count)
            near_ref[3 * i + j : 3 * i + j + 1, :] = slots_ref[pl.ds(w * narrow_count + n, 1), :]
    near_ref[9:16, :] = jnp.zeros((7, 128), jnp.int32)
    slot = [jnp.maximum(near_ref[k : k + 8, :], 0) for k in (0, 8)]
    owner = [jnp.floor((x.astype(jnp.float32) + 0.5) * (1.0 / owned)).astype(jnp.int32) for x in slot]
    inner = [x - y * owned for x, y in zip(slot, owner)]
    by_wide = [jnp.floor((y.astype(jnp.float32) + 0.5) * (1.0 / narrow_count)).astype(jnp.int32) for y in owner]
    back_w = [wide - y for y in by_wide]
    back_n = [narrow - (x - y * narrow_count) for x, y in zip(owner, by_wide)]
    back_w = [jnp.where(x < 0, x + wide_count, x) for x in back_w]
    back_n = [jnp.where(x < 0, x + narrow_count, x) for x in back_n]
    row = [(a * narrow_count + b) * per_owner + (x >> 7) for a, b, x in zip(back_w, back_n, inner)]
    place = [x & 127 for x in inner]

    def body(r, found):
        values = jnp.broadcast_to(mob_ref[pl.ds(r, 1), :], tile)
        return tuple(
            jnp.where(row[k] == r, jnp.take_along_axis(values, place[k], axis=1, mode="promise_in_bounds"), found[k])
            for k in range(2)
        )

    zero = jnp.zeros(tile, jnp.float32)
    found = lax.fori_loop(0, mob_ref.shape[0], body, (zero, zero), unroll=16)
    for k in range(2):
        table_ref[8 * k : 8 * k + 8, :] = TIME_STEP * found[k]


def evolve(
    block,
    order_ref, cot_ref, map_ref, above_ref, below_ref, far_above_ref, far_below_ref,
    left_ref, right_ref, table_ref,
    final_ref, adjoint_ref, sums_ref,
    e_refs, se_refs, rate_refs, lam_refs, slam_refs, u_refs, su_refs,
    inject_ref, outer_ref, m_ref, ms_ref, g_ref, gs_ref, work_ref, binned_ref,
):
    params, layers = order_ref.shape[:2]
    tile = (8, 128)
    lane = lanes(tile)
    col = lane % COLS
    _, cots, maps, _ = far_places(params, layers, block)

    def place(z, carry):
        k = maps + z * MAP_EDGE
        g_ref[z, 0:8, :] = far_above_ref[pl.ds(k + MAP_EDGE - 8, 8), :]
        g_ref[z, 16:24, :] = far_below_ref[pl.ds(k, 8), :]
        for p in range(params):
            k = LEAD + (p * layers + z) * EDGE
            e_refs[0][p, z, 0:8, :] = above_ref[pl.ds(k + EDGE - 8, 8), :]
            e_refs[0][p, z, 8:16, :] = order_ref[p, z]
            e_refs[0][p, z, 16:24, :] = below_ref[pl.ds(k, 8), :]
            k = cots + (p * layers + z) * ADJ_EDGE
            lam_refs[0][p, z, 0:8, :] = far_above_ref[pl.ds(k + ADJ_EDGE - 8, 8), :]
            lam_refs[0][p, z, 8:16, :] = cot_ref[p, z]
            lam_refs[0][p, z, 16:24, :] = far_below_ref[pl.ds(k, 8), :]
        return carry

    lax.fori_loop(0, layers, place, 0)

    at = 0
    gs_ref[...] = jnp.zeros_like(gs_ref)
    for field, both in enumerate(merged_strips(params, left_ref, right_ref)):
        kind = 0 if field < params else 1 if field < 2 * params else 2
        n = CORNER[kind]
        ref = se_refs[0].at[field] if kind == 0 else slam_refs[0].at[field - params] if kind == 1 else gs_ref
        ref[8 - n : 8, :] = far_above_ref[at : at + n, :]
        ref[8:16, :] = both
        ref[16 : 16 + n, :] = far_below_ref[at : at + n, :]
        at += n
    for p in range(params):
        a, b = left_ref[8 * p : 8 * p + 8, :], right_ref[8 * p : 8 * p + 8, :]
        outer_ref[p, 8:16, :] = jnp.where(col == 0, roll(a, 1), roll(b, 127))

    def lookup(index, which):
        values = jnp.broadcast_to(table_ref[which : which + 1, :], tile)
        return jnp.take_along_axis(values, index, axis=1, mode="promise_in_bounds")

    for i in range(3):
        r = 8 * i
        for z in range(layers):
            index = map_ref[z] if i == 1 else g_ref[z, r : r + 8, :].astype(jnp.int32) & 127
            m_ref[z, r : r + 8, :] = lookup(index, 3 * i + 1)
        index = gs_ref[r : r + 8, :].astype(jnp.int32) & 127
        ms_ref[r : r + 8, :] = jnp.where(col < 5, lookup(index, 3 * i), lookup(index, 3 * i + 2))

    def sides(value, strip, z):
        ends = roll(strip, 123 - 10 * z)
        left = roll(jnp.where(lane == 127, ends, value), 1)
        right = roll(jnp.where(lane == 0, ends, value), 127)
        return left + right

    def note_ends(values, i, z):
        here = (lane == 10 * z + 4) | (lane == 10 * z + 5)
        kept = [inject_ref[p, i] for p in range(params)]
        moved = [roll(x, 10 * z + 5) for x in values]
        for p in range(params):
            inject_ref[p, i] = jnp.where(here, moved[p], kept[p])

    def strip_sides(value, ends, outer=None):
        left = roll(jnp.where(col == 4, ends, value), 1)
        right = roll(jnp.where(col == 5, ends, value), 127)
        if outer is not None:
            left = jnp.where(col == 0, outer, left)
            right = jnp.where(col == 9, outer, right)
        below = jnp.where(lane < COLS, value, roll(value, COLS))
        above = jnp.where(lane >= COLS * (layers - 1), value, roll(value, 128 - COLS))
        return (left + right) + (below + above)

    def total_of(values):
        while len(values) > 1:
            values = [a + b for a, b in zip(values[::2], values[1::2])]
        return values[0]

    def row_slices(r):
        return pl.ds(r, 8), pl.ds(r - 1, 8), pl.ds(r + 1, 8)

    def each_window(windows, z, body):
        start, count, most = windows
        for i in range(count):
            body(i, jnp.minimum(start + 8 * i + ((z + 16) >> 5), most))

    def neighbours(ref, strip_ref, values, z, r):
        rows, before, after = row_slices(r)
        below, above = jnp.maximum(z - 1, 0), jnp.minimum(z + 1, layers - 1)
        near = []
        for p in range(params):
            total = sides(values[p], strip_ref[p, rows, :], z)
            total = total + (ref[p, z, before, :] + ref[p, z, after, :])
            near.append(total + (ref[p, below, rows, :] + ref[p, above, rows, :]))
        return near

    def strip_neighbours(ref, values, i, r, outer=False):
        rows, before, after = row_slices(r)
        near = []
        for p in range(params):
            total = strip_sides(values[p], inject_ref[p, i], outer_ref[p, rows, :] if outer else None)
            near.append(total + (ref[p, before, :] + ref[p, after, :]))
        return near

    def rates(e, near):
        squares = [x * x for x in e]
        base = 1.5 * total_of(squares) + 5.0
        return [x * (base - 0.5 * y) - n for x, y, n in zip(e, squares, near)]

    def changes(e, u, near):
        squares = [x * x for x in e]
        base = 1.5 * total_of(squares) + 5.0
        inner = 3.0 * total_of([x * y for x, y in zip(e, u)])
        return [y * (base - 1.5 * s) + x * inner - n for x, y, s, n in zip(e, u, squares, near)]

    def forward(t, windows, last):
        old, old_strip = e_refs[t], se_refs[t]

        def layer(z, carry):
            def window(i, r):
                rows = pl.ds(r, 8)
                e = [old[p, z, rows, :] for p in range(params)]
                m = m_ref[z, rows, :]
                rate = rates(e, neighbours(old, old_strip, e, z, r))
                new = [x - m * y for x, y in zip(e, rate)]
                for p in range(params):
                    rate_refs[t][p, z, rows, :] = rate[p]
                    if last:
                        final_ref[p, z] = new[p]
                    else:
                        e_refs[t + 1][p, z, rows, :] = new[p]
                if not last:
                    note_ends(e, i, z)

            each_window(windows, z, window)
            return carry

        lax.fori_loop(0, layers, layer, 0)
        if last:
            return

        def strip_window(i, carry):
            r = jnp.minimum(windows[0] + 8 * i, windows[2])
            rows = pl.ds(r, 8)
            e = [old_strip[p, rows, :] for p in range(params)]
            m = ms_ref[rows, :]
            rate = rates(e, strip_neighbours(old_strip, e, i, r, t == 0))
            for p in range(params):
                se_refs[t + 1][p, rows, :] = e[p] - m * rate[p]
            return carry

        lax.fori_loop(0, windows[1], strip_window, 0)

    inject_ref[...] = jnp.zeros_like(inject_ref)
    forward(0, (3, 3, 13), False)
    forward(1, (4, 2, 12), False)
    forward(2, (4, 2, 12), False)
    forward(3, (8, 1, 8), True)

    def weigh(z, carry):
        for r in (0, 8, 16):
            rows = slice(r, r + 8)
            m = m_ref[z, rows, :]
            for p in range(params):
                u_refs[0][p, z, rows, :] = m * lam_refs[0][p, z, rows, :]
        return carry

    lax.fori_loop(0, layers, weigh, 0)
    for r in (0, 8, 16):
        rows = slice(r, r + 8)
        for p in range(params):
            su_refs[0][p, rows, :] = ms_ref[rows, :] * slam_refs[0][p, rows, :]

    def backward(t, slot, windows, last):
        old, old_strip = u_refs[slot], su_refs[slot]

        def layer(z, carry):
            def window(i, r):
                rows = pl.ds(r, 8)
                e = [e_refs[t][p, z, rows, :] for p in range(params)]
                u = [old[p, z, rows, :] for p in range(params)]
                m = m_ref[z, rows, :]
                change = changes(e, u, neighbours(old, old_strip, u, z, r))
                lam = [lam_refs[slot][p, z, rows, :] for p in range(params)]
                work_ref[t, z, i] = total_of([lam[p] * rate_refs[t][p, z, rows, :] for p in range(params)])
                new = [x - y for x, y in zip(lam, change)]
                for p in range(params):
                    if last:
                        adjoint_ref[p, z] = new[p]
                    else:
                        lam_refs[1 - slot][p, z, rows, :] = new[p]
                        u_refs[1 - slot][p, z, rows, :] = m * new[p]
                if not last:
                    note_ends(u, i, z)

            each_window(windows, z, window)
            return carry

        lax.fori_loop(0, layers, layer, 0)
        if last:
            return

        def strip_window(i, carry):
            r = windows[0] + 8 * i
            rows = pl.ds(r, 8)
            e = [se_refs[t][p, rows, :] for p in range(params)]
            u = [old_strip[p, rows, :] for p in range(params)]
            m = ms_ref[rows, :]
            change = changes(e, u, strip_neighbours(old_strip, u, i, r))
            for p in range(params):
                new = slam_refs[slot][p, rows, :] - change[p]
                slam_refs[1 - slot][p, rows, :] = new
                su_refs[1 - slot][p, rows, :] = m * new
            return carry

        lax.fori_loop(0, windows[1], strip_window, 0)

    backward(3, 0, (4, 2, 12), False)
    backward(2, 1, (4, 2, 12), False)
    backward(1, 0, (4, 2, 12), False)
    backward(0, 1, (8, 1, 8), True)

    grains = [map_ref[z] for z in range(layers)]
    cells = []
    for z in range(layers):
        upper = work_ref[1, z, 0] + work_ref[2, z, 0] + work_ref[3, z, 0]
        lower = work_ref[1, z, 1] + work_ref[2, z, 1] + work_ref[3, z, 1]
        cells.append(jnp.concatenate([upper[4:8], lower[0:4]], axis=0) + work_ref[0, z, 0])

    def bin_one(g, carry):
        kept = [jnp.where(grains[z] == g, cells[z], 0.0) for z in range(layers)]
        total = sum(kept[1:4], kept[0]) + sum(kept[5:8], kept[4]) + sum(kept[9:], kept[8])
        binned_ref[pl.ds(g, 1), :] = jnp.sum(total, axis=0, keepdims=True)
        return carry

    lax.fori_loop(0, binned_ref.shape[0], bin_one, 0, unroll=4)
    ones = jnp.full((8, 128), -TIME_STEP, jnp.float32)
    sums = lax.dot_general(
        ones, binned_ref[...], (((1,), (1,)), ((), ())),
        precision=lax.Precision.HIGHEST, preferred_element_type=jnp.float32,
    )
    for k in range(0, sums_ref.shape[0], 8):
        sums_ref[k : k + 8, :] = sums


def pick_owned(counts, owned, slots_ref, sums_ref, out_ref, slot_rows, value_rows, total_ref):
    wide_count, narrow_count = counts
    count = wide_count * narrow_count
    wide, narrow = lax.axis_index("wide"), lax.axis_index("narrow")
    base = (wide * narrow_count + narrow) * owned
    listed = sums_ref.shape[1]
    tile = (8, 128)
    for k in range(count):
        slot = slots_ref[k : k + 1, :] - base
        slot_rows[k] = jnp.broadcast_to(slot, tile)
        value = jnp.concatenate([sums_ref[k : k + 1, :], jnp.zeros((1, 128 - listed), jnp.float32)], axis=1)
        value_rows[k] = jnp.broadcast_to(value, tile)
    sub = lax.broadcasted_iota(jnp.int32, tile, 0)
    blocks = total_ref.shape[0] // 8
    step = 16
    for first in range(0, blocks, step):
        some = range(first, min(first + step, blocks))

        def body(k, acc, some=some):
            slot, value = slot_rows[k], value_rows[k]
            shifted = slot - sub
            return tuple(a + jnp.where(shifted == 8 * j, value, 0.0) for a, j in zip(acc, some))

        acc = lax.fori_loop(0, count, body, tuple(jnp.zeros(tile, jnp.float32) for _ in some), unroll=4)
        for a, j in zip(acc, some):
            total_ref[8 * j : 8 * j + 8, :] = a
    whole = lax.dot_general(
        jnp.ones(tile, jnp.float32), total_ref[...], (((1,), (1,)), ((), ())),
        precision=lax.Precision.HIGHEST, preferred_element_type=jnp.float32,
    )
    out_ref[...] = whole[0:1, 0:owned]


def f32(*shape):
    return jax.ShapeDtypeStruct(shape, jnp.float32)


def kernel(body, out_shape, scratch=(), name=None, **specs):
    return pl.pallas_call(
        body, out_shape=out_shape, scratch_shapes=list(scratch), name=name, **specs,
        compiler_params=pltpu.CompilerParams(vmem_limit_bytes=VMEM_LIMIT),
    )


def shifted(value, axis, count, by):
    return lax.ppermute(value, axis, [(i, (i + by) % count) for i in range(count)])


def per_device(counts, order_init, cotangent, grain_map, brick_grains, grain_slot, mobility):
    wide_count, narrow_count = counts
    params, layers = order_init.shape[:2]
    assert order_init.shape[2:] == (8, 128) and layers * COLS < 128
    owned = mobility.shape[0]
    listed = brick_grains.shape[1]
    bricks = brick_grains.shape[0]

    both = ("wide", "narrow")
    count = wide_count * narrow_count

    edge_rows = params * layers * EDGE + 2 * LEAD
    down, up = kernel(pack_rows, (f32(edge_rows, 128),) * 2, name="pack_rows")(order_init)
    above = shifted(down, "wide", wide_count, 1)
    below = shifted(up, "wide", wide_count, -1)

    owned_rows = -(-owned // 128)
    strip_rows = (params + 1) * 8 + owned_rows
    here = pl.BlockSpec(memory_space=pltpu.VMEM)
    to_right, to_left, own = kernel(
        pack_strips, (f32(strip_rows, 128),) * 2 + (f32(owned_rows, 128),), name="pack_strips",
        in_specs=[here] * 4 + [pl.BlockSpec(memory_space=pl.ANY)],
    )(order_init, cotangent, grain_map, mobility.reshape(1, owned), down)
    from_left = shifted(to_right, "narrow", narrow_count, 1)
    from_right = shifted(to_left, "narrow", narrow_count, -1)
    others = [shifted(own, "narrow", narrow_count, d) for d in range(2, narrow_count - 1)]

    block_rows = narrow_count * owned_rows
    far_rows = far_places(params, layers, block_rows)[3]
    far_down, far_up, block = kernel(
        pack_far, (f32(far_rows, 128),) * 2 + (f32(block_rows, 128),), name="pack_far"
    )(cotangent, grain_map, from_left, from_right, own, *others)
    far_above = shifted(far_down, "wide", wide_count, 1)
    far_below = shifted(far_up, "wide", wide_count, -1)
    others = [shifted(block, "wide", wide_count, d) for d in range(2, wide_count - 1)]

    slots = kernel(
        find_slots, jax.ShapeDtypeStruct((bricks, 128), jnp.int32), name="find_slots"
    )(brick_grains, grain_slot.reshape(-1, 128))
    table = kernel(
        functools.partial(find_mobility, counts, owned, far_places(params, layers, block_rows)[0]),
        f32(16, 128),
        (pltpu.VMEM((16, 128), jnp.int32), pltpu.VMEM((wide_count * block_rows, 128), jnp.float32)),
        name="find_mobility",
    )(slots, block, far_above, far_below, *others)

    vmem = lambda *shape: pltpu.VMEM(shape, jnp.float32)
    padded = (params, layers, ROWS, 128)
    strip = (params, ROWS, 128)
    final, adjoint, sums = kernel(
        functools.partial(evolve, block_rows),
        (f32(*order_init.shape), f32(*order_init.shape), f32(count, listed)),
        (
            [vmem(*padded)] * ITERS, [vmem(*strip)] * ITERS, [vmem(*padded)] * ITERS,
            [vmem(*padded)] * 2, [vmem(*strip)] * 2, [vmem(*padded)] * 2, [vmem(*strip)] * 2,
            vmem(params, 3, 8, 128), vmem(*strip),
            vmem(layers, ROWS, 128), vmem(ROWS, 128), vmem(layers, ROWS, 128), vmem(ROWS, 128),
            vmem(ITERS, layers, 2, 8, 128), vmem(listed, 128),
        ),
        name="evolve",
    )(
        order_init, cotangent, grain_map, above, below, far_above, far_below,
        from_left, from_right, table,
    )

    every_sum = lax.all_to_all(sums, both, 0, 0, tiled=True)
    grads = kernel(
        functools.partial(pick_owned, counts, owned),
        f32(1, owned),
        (pltpu.VMEM((count, 8, 128), jnp.int32), vmem(count, 8, 128), vmem(owned + -owned % 8, 128)),
        name="pick_owned",
    )(slots, every_sum)
    return final, adjoint, grads.reshape(owned)


def solution(mesh):
    counts = (mesh.shape["wide"], mesh.shape["narrow"])
    field = P("groups", None, "wide", "narrow")
    spread = P(("groups", "wide", "narrow"))
    return jax.shard_map(
        functools.partial(per_device, counts),
        mesh=mesh,
        in_specs=(field, field, P("groups", "wide", "narrow"), P("groups", None), P("groups"), spread),
        out_specs=(field, field, spread),
        check_vma=False,
    )
```

```python
import functools

import jax
import jax.numpy as jnp
from jax import lax
from jax.experimental import pallas as pl
from jax.experimental.pallas import tpu as pltpu
from jax.sharding import PartitionSpec as P

ITERS = 4
TIME_STEP = 0.05

EDGE = 6
MAP_EDGE = 5
ADJ_EDGE = 4
ROWS = 24
COLS = 10
LEAD = 8
CORNER = (5, 3, 4)

VMEM_LIMIT = 24 * 1024 * 1024


def lanes(shape):
    return lax.broadcasted_iota(jnp.int32, shape, len(shape) - 1)


def roll(value, shift):
    return pltpu.roll(value, shift, 1)


def pack(
    order_hbm, cot_hbm, map_hbm, mob_ref,
    down_ref, up_ref, right_ref, left_ref, own_ref, cot_down_ref, cot_up_ref,
    order_ref, cot_ref, map_ref, sems,
):
    copies = [
        pltpu.make_async_copy(source, target, sems.at[i])
        for i, (source, target) in enumerate(
            ((order_hbm, order_ref), (cot_hbm, cot_ref), (map_hbm, map_ref))
        )
    ]
    for copy in copies:
        copy.start()
    params, layers = order_ref.shape[:2]
    maps = row_places(params, layers)[0]
    gap = jnp.zeros((LEAD, 128), jnp.float32)
    for ref in (down_ref, up_ref):
        ref[0:LEAD, :] = gap
        ref[maps - LEAD : maps, :] = gap
        ref[ref.shape[0] - LEAD :, :] = gap
    for ref in (cot_down_ref, cot_up_ref):
        ref[0:LEAD, :] = gap
        ref[ref.shape[0] - LEAD :, :] = gap
    owned = mob_ref.shape[1]
    at = 8 * (params + 1)
    for i in range(own_ref.shape[0]):
        size = min(128, owned - 128 * i)
        row = mob_ref[0:1, 128 * i : 128 * i + size]
        if size < 128:
            row = jnp.concatenate([row, jnp.zeros((1, 128 - size), jnp.float32)], axis=1)
        for ref, k in ((own_ref, i), (right_ref, at + i), (left_ref, at + i)):
            ref[k : k + 1, :] = row

    copies[0].wait()
    for p in range(params):
        for z in range(layers):
            k = LEAD + (p * layers + z) * EDGE
            down_ref[k : k + EDGE, :] = order_ref[p, z, 8 - EDGE : 8, :]
            up_ref[k : k + EDGE, :] = order_ref[p, z, 0:EDGE, :]
    copies[2].wait()
    for z in range(layers):
        k = maps + z * MAP_EDGE
        cells = map_ref[z].astype(jnp.float32)
        down_ref[k : k + MAP_EDGE, :] = cells[8 - MAP_EDGE : 8]
        up_ref[k : k + MAP_EDGE, :] = cells[0:MAP_EDGE]
    copies[1].wait()
    for p in range(params):
        for z in range(layers):
            k = LEAD + (p * layers + z) * ADJ_EDGE
            cot_down_ref[k : k + ADJ_EDGE, :] = cot_ref[p, z, 8 - ADJ_EDGE : 8, :]
            cot_up_ref[k : k + ADJ_EDGE, :] = cot_ref[p, z, 0:ADJ_EDGE, :]

    lane = lanes((8, 128))
    zero = jnp.zeros((8, 128), jnp.float32)

    def span(first, size):
        return ((lane - first) & 127) < size

    for field in range(params + 1):
        right, left = zero, zero
        for z in range(layers):
            value = order_ref[field, z] if field < params else map_ref[z].astype(jnp.float32)
            moved = roll(value, 10 * z + 5)
            right = jnp.where(span(10 * z - 1, 6), moved, right)
            left = jnp.where(span(10 * z + 5, 6), moved, left)
            if field < params:
                right = jnp.where(span(10 * z + 5, 4), roll(cot_ref[field, z], 10 * z + 9), right)
                left = jnp.where(span(10 * z + 1, 4), roll(cot_ref[field, z], 10 * z + 1), left)
        right_ref[8 * field : 8 * field + 8, :] = right
        left_ref[8 * field : 8 * field + 8, :] = left


def row_places(params, layers):
    maps = LEAD + params * layers * EDGE + LEAD
    length = maps + layers * MAP_EDGE
    return maps, length + -length % 8 + LEAD


def corner_rows(params):
    return -(-(params * (CORNER[0] + CORNER[1]) + CORNER[2]) // 8) * 8


def merged_strips(params, left_ref, right_ref):
    first = lanes((8, 128)) % COLS < 5
    fields = []
    for field in range(params + 1):
        rows = slice(8 * field, 8 * field + 8)
        fields.append((left_ref[rows, :], right_ref[rows, :]))
    order = [jnp.where(first, a, b) for a, b in fields[:params]]
    cot = [jnp.where(first, roll(a, 124), roll(b, 4)) for a, b in fields[:params]]
    return order, cot, jnp.where(first, *fields[params])


def pack_far(params, left_ref, right_ref, own_ref, *refs):
    *other_refs, down_ref, up_ref, block_ref = refs
    rows = own_ref.shape[0]
    at = 8 * (params + 1)
    pieces = [own_ref[...], left_ref[at : at + rows, :]]
    pieces += [ref[...] for ref in other_refs]
    pieces.append(right_ref[at : at + rows, :])
    mobs = corner_rows(params)
    for i, piece in enumerate(pieces):
        for ref, k in ((block_ref, 0), (down_ref, mobs), (up_ref, mobs)):
            ref[k + i * rows : k + (i + 1) * rows, :] = piece
    at = 0
    order, cot, cells = merged_strips(params, left_ref, right_ref)
    for n, fields in zip(CORNER, (order, cot, [cells])):
        for both in fields:
            down_ref[at : at + n, :] = both[8 - n : 8]
            up_ref[at : at + n, :] = both[0:n]
            at += n
    for ref in (down_ref, up_ref):
        ref[at:mobs, :] = jnp.zeros((mobs - at, 128), jnp.float32)


def find_slots(bricks_ref, slot_ref, out_ref):
    count, listed = bricks_ref.shape
    rows = slot_ref.shape[0]
    pad = jnp.zeros((8, 128 - listed), jnp.int32)
    for k in range(0, count, 8):
        grain = jnp.concatenate([bricks_ref[k : k + 8, :], pad], axis=1)
        row, col = grain >> 7, grain & 127

        def body(r, found, row=row, col=col):
            table = jnp.broadcast_to(slot_ref[pl.ds(r, 1), :], (8, 128))
            taken = jnp.take_along_axis(table, col, axis=1, mode="promise_in_bounds")
            return jnp.where(row == r, taken, found)

        found = lax.fori_loop(0, rows, body, jnp.zeros((8, 128), jnp.int32), unroll=7)
        out_ref[k : k + 8, :] = jnp.where(lanes((8, 128)) < listed, found, -1)


def find_mobility(counts, owned, at, slots_ref, block_ref, above_ref, below_ref, *refs):
    *other_refs, table_ref, near_ref, mob_ref = refs
    wide_count, narrow_count = counts
    tile = (8, 128)
    wide, narrow = lax.axis_index("wide"), lax.axis_index("narrow")
    size = block_ref.shape[0]
    per_owner = size // narrow_count
    pieces = [block_ref[...], above_ref[at : at + size, :]]
    pieces += [ref[...] for ref in other_refs]
    pieces.append(below_ref[at : at + size, :])
    for i, piece in enumerate(pieces):
        mob_ref[i * size : (i + 1) * size, :] = piece
    for i in range(3):
        for j in range(3):
            w = lax.rem(wide + i - 1 + wide_count, wide_count)
            n = lax.rem(narrow + j - 1 + narrow_count, narrow_count)
            near_ref[3 * i + j : 3 * i + j + 1, :] = slots_ref[pl.ds(w * narrow_count + n, 1), :]
    near_ref[9:16, :] = jnp.zeros((7, 128), jnp.int32)
    slot = [jnp.maximum(near_ref[k : k + 8, :], 0) for k in (0, 8)]
    owner = [jnp.floor((x.astype(jnp.float32) + 0.5) * (1.0 / owned)).astype(jnp.int32) for x in slot]
    inner = [x - y * owned for x, y in zip(slot, owner)]
    by_wide = [jnp.floor((y.astype(jnp.float32) + 0.5) * (1.0 / narrow_count)).astype(jnp.int32) for y in owner]
    back_w = [wide - y for y in by_wide]
    back_n = [narrow - (x - y * narrow_count) for x, y in zip(owner, by_wide)]
    back_w = [jnp.where(x < 0, x + wide_count, x) for x in back_w]
    back_n = [jnp.where(x < 0, x + narrow_count, x) for x in back_n]
    row = [(a * narrow_count + b) * per_owner + (x >> 7) for a, b, x in zip(back_w, back_n, inner)]
    place = [x & 127 for x in inner]

    def body(r, found):
        values = jnp.broadcast_to(mob_ref[pl.ds(r, 1), :], tile)
        return tuple(
            jnp.where(row[k] == r, jnp.take_along_axis(values, place[k], axis=1, mode="promise_in_bounds"), found[k])
            for k in range(2)
        )

    zero = jnp.zeros(tile, jnp.float32)
    found = lax.fori_loop(0, mob_ref.shape[0], body, (zero, zero), unroll=16)
    for k in range(2):
        table_ref[8 * k : 8 * k + 8, :] = TIME_STEP * found[k]


def total_of(values):
    while len(values) > 1:
        values = [a + b for a, b in zip(values[::2], values[1::2])]
    return values[0]


def each_tile(layers, windows, body):
    start, count, most = windows
    group = 2 if count == 1 else 1

    def some(step, carry):
        stores = []
        for j in range(group):
            z = step * group + j
            for i in range(count):
                stores += body(z, i, jnp.minimum(start + 8 * i + ((z + 16) >> 5), most))
        for store in stores:
            store()
        return carry

    lax.fori_loop(0, layers // group, some, 0)


def each_window(windows, body):
    def one(i, carry):
        body(windows[0] + 8 * i)
        return carry

    lax.fori_loop(0, windows[1], one, 0)


def put(ref, index, value):
    def store():
        ref[index] = value

    return store


def neighbours(ref, ends_ref, values, z, r):
    params, layers = ref.shape[:2]
    lane = lanes((8, 128))
    rows, before, after = pl.ds(r, 8), pl.ds(r - 1, 8), pl.ds(r + 1, 8)
    below, above = jnp.maximum(z - 1, 0), jnp.minimum(z + 1, layers - 1)
    near = []
    for p in range(params):
        ends = ends_ref[p, z, rows, :]
        left = roll(jnp.where(lane == 127, ends, values[p]), 1)
        right = roll(jnp.where(lane == 0, ends, values[p]), 127)
        total = (left + right) + (ref[p, z, before, :] + ref[p, z, after, :])
        near.append(total + (ref[p, below, rows, :] + ref[p, above, rows, :]))
    return near


def strip_neighbours(ref, core_ref, values, r, outer_ref=None):
    params, layers = core_ref.shape[:2]
    lane = lanes((8, 128))
    col = lane % COLS
    rows, before, after = pl.ds(r, 8), pl.ds(r - 1, 8), pl.ds(r + 1, 8)
    near = []
    for p in range(params):
        value = values[p]
        ends = jnp.zeros((8, 128), jnp.float32)
        for z in range(layers):
            here = (lane == 10 * z + 4) | (lane == 10 * z + 5)
            ends = jnp.where(here, roll(core_ref[p, z, rows, :], 10 * z + 5), ends)
        left = roll(jnp.where(col == 4, ends, value), 1)
        right = roll(jnp.where(col == 5, ends, value), 127)
        if outer_ref is not None:
            outer = outer_ref[p, rows, :]
            left = jnp.where(col == 0, outer, left)
            right = jnp.where(col == 9, outer, right)
        below = jnp.where(lane < COLS, value, roll(value, COLS))
        above = jnp.where(lane >= COLS * (layers - 1), value, roll(value, 128 - COLS))
        total = (left + right) + (below + above)
        near.append(total + (ref[p, before, :] + ref[p, after, :]))
    return near


def spread_ends(ends_ref, values, rows):
    params, layers = ends_ref.shape[:2]
    for p in range(params):
        for z in range(layers):
            ends_ref[p, z, rows, :] = roll(values[p], 123 - 10 * z)


def rates(e, near):
    squares = [x * x for x in e]
    base = 1.5 * total_of(squares) + 5.0
    return [x * (base - 0.5 * y) - n for x, y, n in zip(e, squares, near)]


def changes(e, u, near):
    squares = [x * x for x in e]
    base = 1.5 * total_of(squares) + 5.0
    inner = 3.0 * total_of([x * y for x, y in zip(e, u)])
    return [y * (base - 1.5 * s) + x * inner - n for x, y, s, n in zip(e, u, squares, near)]


def forward(
    order_ref, map_ref, above_ref, below_ref, far_above_ref, far_below_ref, left_ref, right_ref, table_ref,
    final_ref, e_refs, rate_refs, se_refs, m_ref, ms_ref,
    first_strip_ref, outer_ref, ends_ref, g_ref, gs_ref,
):
    params, layers = order_ref.shape[:2]
    tile = (8, 128)
    col = lanes(tile) % COLS
    maps = row_places(params, layers)[0]
    strip_refs = [first_strip_ref, *se_refs]
    every = range(params)

    def place(z, carry):
        k = maps + z * MAP_EDGE
        g_ref[z, 0:8, :] = above_ref[pl.ds(k + MAP_EDGE - 8, 8), :]
        g_ref[z, 16:24, :] = below_ref[pl.ds(k, 8), :]
        for p in every:
            k = LEAD + (p * layers + z) * EDGE
            e_refs[0][p, z, 0:8, :] = above_ref[pl.ds(k + EDGE - 8, 8), :]
            e_refs[0][p, z, 8:16, :] = order_ref[p, z]
            e_refs[0][p, z, 16:24, :] = below_ref[pl.ds(k, 8), :]
        return carry

    lax.fori_loop(0, layers, place, 0)

    order, _, cells = merged_strips(params, left_ref, right_ref)
    n = CORNER[0]
    for p in every:
        ref = first_strip_ref.at[p]
        ref[0:8, :] = jnp.zeros(tile, jnp.float32)
        ref[16:24, :] = jnp.zeros(tile, jnp.float32)
        ref[8 - n : 8, :] = far_above_ref[n * p : n * p + n, :]
        ref[8:16, :] = order[p]
        ref[16 : 16 + n, :] = far_below_ref[n * p : n * p + n, :]
        a, b = left_ref[8 * p : 8 * p + 8, :], right_ref[8 * p : 8 * p + 8, :]
        outer_ref[p, 8:16, :] = jnp.where(col == 0, roll(a, 1), roll(b, 127))
    at, n = params * (CORNER[0] + CORNER[1]), CORNER[2]
    gs_ref[...] = jnp.zeros_like(gs_ref)
    gs_ref[8 - n : 8, :] = far_above_ref[at : at + n, :]
    gs_ref[8:16, :] = cells
    gs_ref[16 : 16 + n, :] = far_below_ref[at : at + n, :]
    for r in (0, 8, 16):
        rows = slice(r, r + 8)
        spread_ends(ends_ref, [first_strip_ref[p, rows, :] for p in every], rows)

    def lookup(index, which):
        values = jnp.broadcast_to(table_ref[which : which + 1, :], tile)
        return jnp.take_along_axis(values, index, axis=1, mode="promise_in_bounds")

    for i in range(3):
        r = 8 * i
        for z in range(layers):
            index = map_ref[z] if i == 1 else g_ref[z, r : r + 8, :].astype(jnp.int32) & 127
            m_ref[z, r : r + 8, :] = lookup(index, 3 * i + 1)
        index = gs_ref[r : r + 8, :].astype(jnp.int32) & 127
        ms_ref[r : r + 8, :] = jnp.where(col < 5, lookup(index, 3 * i), lookup(index, 3 * i + 2))

    def step(t, windows, strip_windows, end_windows):
        old, old_strip = e_refs[t], strip_refs[t]
        last = t == ITERS - 1

        def core(z, i, r):
            rows = pl.ds(r, 8)
            e = [old[p, z, rows, :] for p in every]
            m = m_ref[z, rows, :]
            rate = rates(e, neighbours(old, ends_ref, e, z, r))
            stores = []
            for p in every:
                new = e[p] - m * rate[p]
                stores.append(put(rate_refs[t], (p, z, rows, slice(None)), rate[p]))
                if last:
                    stores.append(put(final_ref, (p, z), new))
                else:
                    stores.append(put(e_refs[t + 1], (p, z, rows, slice(None)), new))
            return stores

        each_tile(layers, windows, core)
        if last:
            return

        def strip(r):
            rows = pl.ds(r, 8)
            e = [old_strip[p, rows, :] for p in every]
            m = ms_ref[rows, :]
            rate = rates(e, strip_neighbours(old_strip, old, e, r, outer_ref if t == 0 else None))
            for p in every:
                strip_refs[t + 1][p, rows, :] = e[p] - m * rate[p]

        each_window(strip_windows, strip)

        def ends(r):
            rows = pl.ds(r, 8)
            spread_ends(ends_ref, [strip_refs[t + 1][p, rows, :] for p in every], rows)

        each_window(end_windows, ends)

    step(0, (3, 3, 13), (4, 2), (4, 2))
    step(1, (4, 2, 12), (4, 2), (4, 2))
    step(2, (4, 2, 12), (4, 2), (8, 1))
    step(3, (8, 1, 8), None, None)


def backward(
    cot_ref, map_ref, above_ref, below_ref, far_above_ref, far_below_ref, left_ref, right_ref,
    e_refs, rate_refs, se_refs, m_ref, ms_ref,
    adjoint_ref, sums_ref,
    lam_refs, slam_refs, u_refs, su_refs, ends_ref, work_ref, binned_ref,
):
    params, layers = cot_ref.shape[:2]
    tile = (8, 128)
    every = range(params)

    def place(z, carry):
        m = [m_ref[z, 8 * i : 8 * i + 8, :] for i in range(3)]
        for p in every:
            k = LEAD + (p * layers + z) * ADJ_EDGE
            blocks = (above_ref[pl.ds(k + ADJ_EDGE - 8, 8), :], cot_ref[p, z], below_ref[pl.ds(k, 8), :])
            for i in range(3):
                lam_refs[0][p, z, 8 * i : 8 * i + 8, :] = blocks[i]
                u_refs[0][p, z, 8 * i : 8 * i + 8, :] = m[i] * blocks[i]
        return carry

    lax.fori_loop(0, layers, place, 0)
    _, cot, _ = merged_strips(params, left_ref, right_ref)
    n = CORNER[1]
    for p in every:
        at = params * CORNER[0] + n * p
        ref = slam_refs[0].at[p]
        ref[0:8, :] = jnp.zeros(tile, jnp.float32)
        ref[16:24, :] = jnp.zeros(tile, jnp.float32)
        ref[8 - n : 8, :] = far_above_ref[at : at + n, :]
        ref[8:16, :] = cot[p]
        ref[16 : 16 + n, :] = far_below_ref[at : at + n, :]
        for r in (0, 8, 16):
            su_refs[0][p, r : r + 8, :] = ms_ref[r : r + 8, :] * ref[r : r + 8, :]

    def spread(slot, windows):
        def ends(r):
            rows = pl.ds(r, 8)
            spread_ends(ends_ref, [su_refs[slot][p, rows, :] for p in every], rows)

        each_window(windows, ends)

    def step(t, slot, windows, strip_windows, end_windows):
        old, old_strip = u_refs[slot], su_refs[slot]
        last = t == 0

        def core(z, i, r):
            rows = pl.ds(r, 8)
            e = [e_refs[t][p, z, rows, :] for p in every]
            u = [old[p, z, rows, :] for p in every]
            m = m_ref[z, rows, :]
            change = changes(e, u, neighbours(old, ends_ref, u, z, r))
            lam = [lam_refs[slot][p, z, rows, :] for p in every]
            work = total_of([lam[p] * rate_refs[t][p, z, rows, :] for p in every])
            stores = [put(work_ref, (t, z, i), work)]
            for p in every:
                new = lam[p] - change[p]
                if last:
                    stores.append(put(adjoint_ref, (p, z), new))
                else:
                    stores.append(put(lam_refs[1 - slot], (p, z, rows, slice(None)), new))
                    stores.append(put(u_refs[1 - slot], (p, z, rows, slice(None)), m * new))
            return stores

        each_tile(layers, windows, core)
        if last:
            return

        def strip(r):
            rows = pl.ds(r, 8)
            e = [se_refs[t - 1][p, rows, :] for p in every]
            u = [old_strip[p, rows, :] for p in every]
            m = ms_ref[rows, :]
            change = changes(e, u, strip_neighbours(old_strip, old, u, r))
            for p in every:
                new = slam_refs[slot][p, rows, :] - change[p]
                slam_refs[1 - slot][p, rows, :] = new
                su_refs[1 - slot][p, rows, :] = m * new

        each_window(strip_windows, strip)
        spread(1 - slot, end_windows)

    spread(0, (4, 2))
    step(3, 0, (4, 2, 12), (4, 2), (4, 2))
    step(2, 1, (4, 2, 12), (4, 2), (4, 2))
    step(1, 0, (4, 2, 12), (8, 1), (8, 1))
    step(0, 1, (8, 1, 8), None, None)

    grains = [map_ref[z] for z in range(layers)]
    cells = []
    for z in range(layers):
        upper = work_ref[1, z, 0] + work_ref[2, z, 0] + work_ref[3, z, 0]
        lower = work_ref[1, z, 1] + work_ref[2, z, 1] + work_ref[3, z, 1]
        cells.append(jnp.concatenate([upper[4:8], lower[0:4]], axis=0) + work_ref[0, z, 0])

    def bin_one(g, carry):
        kept = [jnp.where(grains[z] == g, cells[z], 0.0) for z in range(layers)]
        total = sum(kept[1:4], kept[0]) + sum(kept[5:8], kept[4]) + sum(kept[9:], kept[8])
        binned_ref[pl.ds(g, 1), :] = jnp.sum(total, axis=0, keepdims=True)
        return carry

    lax.fori_loop(0, binned_ref.shape[0], bin_one, 0, unroll=4)
    ones = jnp.full((8, 128), -TIME_STEP, jnp.float32)
    sums = lax.dot_general(
        ones, binned_ref[...], (((1,), (1,)), ((), ())),
        precision=lax.Precision.HIGHEST, preferred_element_type=jnp.float32,
    )
    for k in range(0, sums_ref.shape[0], 8):
        sums_ref[k : k + 8, :] = sums


def pick_owned(counts, owned, slots_ref, sums_ref, out_ref, slot_rows, value_rows, total_ref):
    wide_count, narrow_count = counts
    count = wide_count * narrow_count
    wide, narrow = lax.axis_index("wide"), lax.axis_index("narrow")
    base = (wide * narrow_count + narrow) * owned
    listed = sums_ref.shape[1]
    tile = (8, 128)
    for k in range(count):
        slot = slots_ref[k : k + 1, :] - base
        slot_rows[k] = jnp.broadcast_to(slot, tile)
        value = jnp.concatenate([sums_ref[k : k + 1, :], jnp.zeros((1, 128 - listed), jnp.float32)], axis=1)
        value_rows[k] = jnp.broadcast_to(value, tile)
    sub = lax.broadcasted_iota(jnp.int32, tile, 0)
    blocks = total_ref.shape[0] // 8
    step = 16
    for first in range(0, blocks, step):
        some = range(first, min(first + step, blocks))

        def body(k, acc, some=some):
            slot, value = slot_rows[k], value_rows[k]
            shifted = slot - sub
            return tuple(a + jnp.where(shifted == 8 * j, value, 0.0) for a, j in zip(acc, some))

        acc = lax.fori_loop(0, count, body, tuple(jnp.zeros(tile, jnp.float32) for _ in some), unroll=4)
        for a, j in zip(acc, some):
            total_ref[8 * j : 8 * j + 8, :] = a
    whole = lax.dot_general(
        jnp.ones(tile, jnp.float32), total_ref[...], (((1,), (1,)), ((), ())),
        precision=lax.Precision.HIGHEST, preferred_element_type=jnp.float32,
    )
    out_ref[...] = whole[0:1, 0:owned]


def f32(*shape):
    return jax.ShapeDtypeStruct(shape, jnp.float32)


def kernel(body, out_shape, scratch=(), name=None, **specs):
    return pl.pallas_call(
        body, out_shape=out_shape, scratch_shapes=list(scratch), name=name, **specs,
        compiler_params=pltpu.CompilerParams(vmem_limit_bytes=VMEM_LIMIT),
    )


def shifted(value, axis, count, by):
    return lax.ppermute(value, axis, [(i, (i + by) % count) for i in range(count)])


def per_device(counts, order_init, cotangent, grain_map, brick_grains, grain_slot, mobility):
    wide_count, narrow_count = counts
    params, layers = order_init.shape[:2]
    assert order_init.shape[2:] == (8, 128) and layers * COLS < 128
    owned = mobility.shape[0]
    listed = brick_grains.shape[1]
    bricks = brick_grains.shape[0]

    both = ("wide", "narrow")
    count = wide_count * narrow_count

    owned_rows = -(-owned // 128)
    strip_rows = (params + 1) * 8 + owned_rows
    edge_rows = row_places(params, layers)[1]
    cot_rows = params * layers * ADJ_EDGE + 2 * LEAD
    away, here = pl.BlockSpec(memory_space=pltpu.HBM), pl.BlockSpec(memory_space=pltpu.VMEM)
    vmem = lambda *shape: pltpu.VMEM(shape, jnp.float32)
    down, up, to_right, to_left, own, cot_down, cot_up = kernel(
        pack,
        (f32(edge_rows, 128),) * 2 + (f32(strip_rows, 128),) * 2 + (f32(owned_rows, 128),)
        + (f32(cot_rows, 128),) * 2,
        (
            vmem(*order_init.shape), vmem(*cotangent.shape), pltpu.VMEM(grain_map.shape, jnp.int32),
            pltpu.SemaphoreType.DMA((3,)),
        ),
        name="pack", in_specs=[away, away, away, here],
    )(order_init, cotangent, grain_map, mobility.reshape(1, owned))
    above = shifted(down, "wide", wide_count, 1)
    below = shifted(up, "wide", wide_count, -1)
    from_left = shifted(to_right, "narrow", narrow_count, 1)
    from_right = shifted(to_left, "narrow", narrow_count, -1)
    others = [shifted(own, "narrow", narrow_count, d) for d in range(2, narrow_count - 1)]

    block_rows = narrow_count * owned_rows
    far_rows = corner_rows(params) + block_rows
    far_down, far_up, block = kernel(
        functools.partial(pack_far, params),
        (f32(far_rows, 128),) * 2 + (f32(block_rows, 128),), name="pack_far",
    )(from_left, from_right, own, *others)
    far_above = shifted(far_down, "wide", wide_count, 1)
    far_below = shifted(far_up, "wide", wide_count, -1)
    others = [shifted(block, "wide", wide_count, d) for d in range(2, wide_count - 1)]
    cot_above = shifted(cot_down, "wide", wide_count, 1)
    cot_below = shifted(cot_up, "wide", wide_count, -1)

    slots = kernel(
        find_slots, jax.ShapeDtypeStruct((bricks, 128), jnp.int32), name="find_slots"
    )(brick_grains, grain_slot.reshape(-1, 128))
    table = kernel(
        functools.partial(find_mobility, counts, owned, corner_rows(params)),
        f32(16, 128),
        (pltpu.VMEM((16, 128), jnp.int32), vmem(wide_count * block_rows, 128)),
        name="find_mobility",
    )(slots, block, far_above, far_below, *others)

    padded, strip = (params, layers, ROWS, 128), (params, ROWS, 128)
    final, states, rate, strips, m, ms = kernel(
        forward,
        (
            f32(*order_init.shape), [f32(*padded)] * ITERS, [f32(*padded)] * ITERS,
            [f32(*strip)] * (ITERS - 1), f32(layers, ROWS, 128), f32(ROWS, 128),
        ),
        (vmem(*strip), vmem(*strip), vmem(*padded), vmem(layers, ROWS, 128), vmem(ROWS, 128)),
        name="forward",
    )(order_init, grain_map, above, below, far_above, far_below, from_left, from_right, table)
    adjoint, sums = kernel(
        backward,
        (f32(*order_init.shape), f32(count, listed)),
        (
            [vmem(*padded)] * 2, [vmem(*strip)] * 2, [vmem(*padded)] * 2, [vmem(*strip)] * 2,
            vmem(*padded), vmem(ITERS, layers, 2, 8, 128), vmem(listed, 128),
        ),
        name="backward",
    )(
        cotangent, grain_map, cot_above, cot_below, far_above, far_below, from_left, from_right,
        states, rate, strips, m, ms,
    )

    every_sum = lax.all_to_all(sums, both, 0, 0, tiled=True)
    grads = kernel(
        functools.partial(pick_owned, counts, owned),
        f32(1, owned),
        (pltpu.VMEM((count, 8, 128), jnp.int32), vmem(count, 8, 128), vmem(owned + -owned % 8, 128)),
        name="pick_owned",
    )(slots, every_sum)
    return final, adjoint, grads.reshape(owned)


def solution(mesh):
    counts = (mesh.shape["wide"], mesh.shape["narrow"])
    field = P("groups", None, "wide", "narrow")
    spread = P(("groups", "wide", "narrow"))
    return jax.shard_map(
        functools.partial(per_device, counts),
        mesh=mesh,
        in_specs=(field, field, P("groups", "wide", "narrow"), P("groups", None), P("groups"), spread),
        out_specs=(field, field, spread),
        check_vma=False,
    )
```

```python
import functools

import jax
import jax.numpy as jnp
from jax import lax
from jax.experimental import pallas as pl
from jax.experimental.pallas import tpu as pltpu
from jax.sharding import PartitionSpec as P

ITERS = 4
TIME_STEP = 0.05

EDGE = 6
MAP_EDGE = 5
ADJ_EDGE = 4
ROWS = 24
COLS = 10
LEAD = 8
CORNER = (5, 3, 4)

VMEM_LIMIT = 24 * 1024 * 1024


def lanes(shape):
    return lax.broadcasted_iota(jnp.int32, shape, len(shape) - 1)


def roll(value, shift):
    return pltpu.roll(value, shift, 1)


def pack_rows(*refs):
    count = (len(refs) - 3) // 2
    sources, targets = refs[:count], refs[count : 2 * count]
    down_ref, up_ref, sems = refs[2 * count :]
    copies = [pltpu.make_async_copy(a, b, sems.at[i]) for i, (a, b) in enumerate(zip(sources, targets))]
    for copy in copies:
        copy.start()
    order_ref, map_ref = targets[:2]
    params, layers = order_ref.shape[:2]
    maps = row_places(params, layers)[0]
    gap = jnp.zeros((LEAD, 128), jnp.float32)
    for ref in (down_ref, up_ref):
        ref[0:LEAD, :] = gap
        ref[maps - LEAD : maps, :] = gap
        ref[ref.shape[0] - 2 * LEAD : ref.shape[0] - LEAD, :] = gap
        ref[ref.shape[0] - LEAD :, :] = gap
    copies[0].wait()
    for p in range(params):
        for z in range(layers):
            k = LEAD + (p * layers + z) * EDGE
            down_ref[k : k + EDGE, :] = order_ref[p, z, 8 - EDGE : 8, :]
            up_ref[k : k + EDGE, :] = order_ref[p, z, 0:EDGE, :]
    copies[1].wait()
    for z in range(layers):
        k = maps + z * MAP_EDGE
        cells = map_ref[z].astype(jnp.float32)
        down_ref[k : k + MAP_EDGE, :] = cells[8 - MAP_EDGE : 8]
        up_ref[k : k + MAP_EDGE, :] = cells[0:MAP_EDGE]
    for copy in copies[2:]:
        copy.wait()


def around(axis, count):
    place = lax.axis_index(axis)
    return lax.rem(place + count - 1, count), lax.rem(place + 1, count)


def pack_strips(order_ref, cot_ref, map_ref, mob_ref, after_ref, out_ref):
    params, layers = order_ref.shape[:2]
    count = out_ref.shape[0]
    before, after = around("narrow", count)
    owned = mob_ref.shape[1]
    at = 8 * (params + 1)
    out_ref[...] = jnp.zeros_like(out_ref)
    for i in range(-(-owned // 128)):
        size = min(128, owned - 128 * i)
        row = mob_ref[0:1, 128 * i : 128 * i + size]
        if size < 128:
            row = jnp.concatenate([row, jnp.zeros((1, 128 - size), jnp.float32)], axis=1)
        for j in range(count):
            out_ref[j, at + i : at + i + 1, :] = row

    lane = lanes((8, 128))
    zero = jnp.zeros((8, 128), jnp.float32)

    def span(first, size):
        return ((lane - first) & 127) < size

    for field in range(params + 1):
        right, left = zero, zero
        for z in range(layers):
            value = order_ref[field, z] if field < params else map_ref[z].astype(jnp.float32)
            moved = roll(value, 10 * z + 5)
            right = jnp.where(span(10 * z - 1, 6), moved, right)
            left = jnp.where(span(10 * z + 5, 6), moved, left)
            if field < params:
                right = jnp.where(span(10 * z + 5, 4), roll(cot_ref[field, z], 10 * z + 9), right)
                left = jnp.where(span(10 * z + 1, 4), roll(cot_ref[field, z], 10 * z + 1), left)
        out_ref[after, 8 * field : 8 * field + 8, :] = right
        out_ref[before, 8 * field : 8 * field + 8, :] = left


def row_places(params, layers):
    maps = LEAD + params * layers * EDGE + LEAD
    length = maps + layers * MAP_EDGE
    return maps, length + -length % 8 + LEAD


def corner_rows(params):
    return -(-(params * (CORNER[0] + CORNER[1]) + CORNER[2]) // 8) * 8


def side_strips(params, strips_ref):
    before, after = around("narrow", strips_ref.shape[0])
    rows = [slice(8 * field, 8 * field + 8) for field in range(params + 1)]
    return [(strips_ref[before, r, :], strips_ref[after, r, :]) for r in rows]


def merged_strips(params, strips_ref):
    first = lanes((8, 128)) % COLS < 5
    fields = side_strips(params, strips_ref)
    order = [jnp.where(first, a, b) for a, b in fields[:params]]
    cot = [jnp.where(first, roll(a, 124), roll(b, 4)) for a, b in fields[:params]]
    return order, cot, jnp.where(first, *fields[params])


def pack_far(params, owned_rows, strips_ref, slots_ref, out_ref):
    count = out_ref.shape[0]
    before, after = around("wide", count)
    mobs = corner_rows(params)
    out_ref[...] = jnp.zeros_like(out_ref)
    at = 8 * (params + 1)
    for i in range(strips_ref.shape[0]):
        piece = strips_ref[i, at : at + owned_rows, :]
        for j in range(count):
            out_ref[j, mobs + i * owned_rows : mobs + (i + 1) * owned_rows, :] = piece
    at = 0
    order, cot, cells = merged_strips(params, strips_ref)
    for n, fields in zip(CORNER, (order, cot, [cells])):
        for both in fields:
            out_ref[after, at : at + n, :] = both[8 - n : 8]
            out_ref[before, at : at + n, :] = both[0:n]
            at += n


def find_slots(bricks_ref, slot_ref, out_ref):
    count, listed = bricks_ref.shape
    rows = slot_ref.shape[0]
    pad = jnp.zeros((8, 128 - listed), jnp.int32)
    for k in range(0, count, 8):
        grain = jnp.concatenate([bricks_ref[k : k + 8, :], pad], axis=1)
        row, col = grain >> 7, grain & 127

        def body(r, found, row=row, col=col):
            table = jnp.broadcast_to(slot_ref[pl.ds(r, 1), :], (8, 128))
            taken = jnp.take_along_axis(table, col, axis=1, mode="promise_in_bounds")
            return jnp.where(row == r, taken, found)

        found = lax.fori_loop(0, rows, body, jnp.zeros((8, 128), jnp.int32), unroll=7)
        out_ref[k : k + 8, :] = jnp.where(lanes((8, 128)) < listed, found, -1)


def find_mobility(
    counts, owned, owned_rows, slots_ref, far_ref, cot_ref, table_ref, cot_down_ref, cot_up_ref, near_ref, mob_ref
):
    params, layers = cot_ref.shape[:2]
    for ref in (cot_down_ref, cot_up_ref):
        ref[0:LEAD, :] = jnp.zeros((LEAD, 128), jnp.float32)
        ref[ref.shape[0] - LEAD :, :] = jnp.zeros((LEAD, 128), jnp.float32)
    for p in range(params):
        for z in range(layers):
            k = LEAD + (p * layers + z) * ADJ_EDGE
            cot_down_ref[k : k + ADJ_EDGE, :] = cot_ref[p, z, 8 - ADJ_EDGE : 8, :]
            cot_up_ref[k : k + ADJ_EDGE, :] = cot_ref[p, z, 0:ADJ_EDGE, :]

    wide_count, narrow_count = counts
    tile = (8, 128)
    wide, narrow = lax.axis_index("wide"), lax.axis_index("narrow")
    size, at = narrow_count * owned_rows, corner_rows(params)
    for i in range(wide_count):
        mob_ref[i * size : (i + 1) * size, :] = far_ref[i, at : at + size, :]
    for i in range(3):
        for j in range(3):
            w = lax.rem(wide + i - 1 + wide_count, wide_count)
            n = lax.rem(narrow + j - 1 + narrow_count, narrow_count)
            near_ref[3 * i + j : 3 * i + j + 1, :] = slots_ref[pl.ds(w * narrow_count + n, 1), :]
    near_ref[9:16, :] = jnp.zeros((7, 128), jnp.int32)
    slot = [jnp.maximum(near_ref[k : k + 8, :], 0) for k in (0, 8)]
    owner = [jnp.floor((x.astype(jnp.float32) + 0.5) * (1.0 / owned)).astype(jnp.int32) for x in slot]
    inner = [x - y * owned for x, y in zip(slot, owner)]
    row = [y * owned_rows + (x >> 7) for x, y in zip(inner, owner)]
    place = [x & 127 for x in inner]

    def body(r, found):
        values = jnp.broadcast_to(mob_ref[pl.ds(r, 1), :], tile)
        return tuple(
            jnp.where(row[k] == r, jnp.take_along_axis(values, place[k], axis=1, mode="promise_in_bounds"), found[k])
            for k in range(2)
        )

    zero = jnp.zeros(tile, jnp.float32)
    found = lax.fori_loop(0, mob_ref.shape[0], body, (zero, zero), unroll=16)
    for k in range(2):
        table_ref[8 * k : 8 * k + 8, :] = TIME_STEP * found[k]


def total_of(values):
    while len(values) > 1:
        values = [a + b for a, b in zip(values[::2], values[1::2])]
    return values[0]


def each_tile(layers, windows, body):
    start, count, most = windows
    group = 4 // count if count < 3 else 1

    def some(step, carry):
        stores = []
        for j in range(group):
            z = step * group + j
            for i in range(count):
                stores += body(z, i, jnp.minimum(start + 8 * i + ((z + 16) >> 5), most))
        for store in stores:
            store()
        return carry

    lax.fori_loop(0, layers // group, some, 0)


def each_window(windows, body):
    def one(i, carry):
        body(windows[0] + 8 * i)
        return carry

    lax.fori_loop(0, windows[1], one, 0)


def put(ref, index, value):
    def store():
        ref[index] = value

    return store


def neighbours(ref, ends_ref, values, z, r):
    params, layers = ref.shape[:2]
    lane = lanes((8, 128))
    rows, before, after = pl.ds(r, 8), pl.ds(r - 1, 8), pl.ds(r + 1, 8)
    below, above = jnp.maximum(z - 1, 0), jnp.minimum(z + 1, layers - 1)
    near = []
    for p in range(params):
        ends = ends_ref[p, z, rows, :]
        left = roll(jnp.where(lane == 127, ends, values[p]), 1)
        right = roll(jnp.where(lane == 0, ends, values[p]), 127)
        total = (left + right) + (ref[p, z, before, :] + ref[p, z, after, :])
        near.append(total + (ref[p, below, rows, :] + ref[p, above, rows, :]))
    return near


def strip_neighbours(ref, core_ref, values, r, outer_ref=None):
    params, layers = core_ref.shape[:2]
    lane = lanes((8, 128))
    col = lane % COLS
    rows, before, after = pl.ds(r, 8), pl.ds(r - 1, 8), pl.ds(r + 1, 8)
    near = []
    for p in range(params):
        value = values[p]
        ends = jnp.zeros((8, 128), jnp.float32)
        for z in range(layers):
            here = (lane == 10 * z + 4) | (lane == 10 * z + 5)
            ends = jnp.where(here, roll(core_ref[p, z, rows, :], 10 * z + 5), ends)
        left = roll(jnp.where(col == 4, ends, value), 1)
        right = roll(jnp.where(col == 5, ends, value), 127)
        if outer_ref is not None:
            outer = outer_ref[p, rows, :]
            left = jnp.where(col == 0, outer, left)
            right = jnp.where(col == 9, outer, right)
        below = jnp.where(lane < COLS, value, roll(value, COLS))
        above = jnp.where(lane >= COLS * (layers - 1), value, roll(value, 128 - COLS))
        total = (left + right) + (below + above)
        near.append(total + (ref[p, before, :] + ref[p, after, :]))
    return near


def spread_ends(ends_ref, values, rows):
    params, layers = ends_ref.shape[:2]
    for p in range(params):
        for z in range(layers):
            ends_ref[p, z, rows, :] = roll(values[p], 123 - 10 * z)


def rates(e, near):
    squares = [x * x for x in e]
    base = 1.5 * total_of(squares) + 5.0
    return [x * (base - 0.5 * y) - n for x, y, n in zip(e, squares, near)]


def changes(e, u, near):
    squares = [x * x for x in e]
    base = 1.5 * total_of(squares) + 5.0
    inner = 3.0 * total_of([x * y for x, y in zip(e, u)])
    return [y * (base - 1.5 * s) + x * inner - n for x, y, s, n in zip(e, u, squares, near)]


def forward(
    order_ref, map_ref, above_ref, below_ref, far_ref, strips_ref, table_ref,
    final_ref, e_refs, rate_refs, se_refs, m_ref, ms_ref,
    first_strip_ref, outer_ref, ends_ref, g_ref, gs_ref,
):
    params, layers = order_ref.shape[:2]
    tile = (8, 128)
    col = lanes(tile) % COLS
    maps = row_places(params, layers)[0]
    strip_refs = [first_strip_ref, *se_refs]
    every = range(params)

    def place(z, carry):
        k = maps + z * MAP_EDGE
        g_ref[z, 0:8, :] = above_ref[pl.ds(k + MAP_EDGE - 8, 8), :]
        g_ref[z, 16:24, :] = below_ref[pl.ds(k, 8), :]
        for p in every:
            k = LEAD + (p * layers + z) * EDGE
            e_refs[0][p, z, 0:8, :] = above_ref[pl.ds(k + EDGE - 8, 8), :]
            e_refs[0][p, z, 8:16, :] = order_ref[p, z]
            e_refs[0][p, z, 16:24, :] = below_ref[pl.ds(k, 8), :]
        return carry

    lax.fori_loop(0, layers, place, 0)

    far_above, far_below = around("wide", far_ref.shape[0])
    sides = side_strips(params, strips_ref)
    order, _, cells = merged_strips(params, strips_ref)
    n = CORNER[0]
    for p in every:
        ref = first_strip_ref.at[p]
        ref[0:8, :] = jnp.zeros(tile, jnp.float32)
        ref[16:24, :] = jnp.zeros(tile, jnp.float32)
        ref[8 - n : 8, :] = far_ref[far_above, n * p : n * p + n, :]
        ref[8:16, :] = order[p]
        ref[16 : 16 + n, :] = far_ref[far_below, n * p : n * p + n, :]
        outer_ref[p, 8:16, :] = jnp.where(col == 0, roll(sides[p][0], 1), roll(sides[p][1], 127))
    at, n = params * (CORNER[0] + CORNER[1]), CORNER[2]
    gs_ref[...] = jnp.zeros_like(gs_ref)
    gs_ref[8 - n : 8, :] = far_ref[far_above, at : at + n, :]
    gs_ref[8:16, :] = cells
    gs_ref[16 : 16 + n, :] = far_ref[far_below, at : at + n, :]
    for r in (0, 8, 16):
        rows = slice(r, r + 8)
        spread_ends(ends_ref, [first_strip_ref[p, rows, :] for p in every], rows)

    def lookup(index, which):
        values = jnp.broadcast_to(table_ref[which : which + 1, :], tile)
        return jnp.take_along_axis(values, index, axis=1, mode="promise_in_bounds")

    for i in range(3):
        r = 8 * i
        for z in range(layers):
            index = map_ref[z] if i == 1 else g_ref[z, r : r + 8, :].astype(jnp.int32) & 127
            m_ref[z, r : r + 8, :] = lookup(index, 3 * i + 1)
        index = gs_ref[r : r + 8, :].astype(jnp.int32) & 127
        ms_ref[r : r + 8, :] = jnp.where(col < 5, lookup(index, 3 * i), lookup(index, 3 * i + 2))

    def step(t, windows, strip_windows, end_windows):
        old, old_strip = e_refs[t], strip_refs[t]
        last = t == ITERS - 1

        def core(z, i, r):
            rows = pl.ds(r, 8)
            e = [old[p, z, rows, :] for p in every]
            m = m_ref[z, rows, :]
            rate = rates(e, neighbours(old, ends_ref, e, z, r))
            stores = []
            for p in every:
                new = e[p] - m * rate[p]
                stores.append(put(rate_refs[t], (p, z, rows, slice(None)), rate[p]))
                if last:
                    stores.append(put(final_ref, (p, z), new))
                else:
                    stores.append(put(e_refs[t + 1], (p, z, rows, slice(None)), new))
            return stores

        each_tile(layers, windows, core)
        if last:
            return

        def strip(r):
            rows = pl.ds(r, 8)
            e = [old_strip[p, rows, :] for p in every]
            m = ms_ref[rows, :]
            rate = rates(e, strip_neighbours(old_strip, old, e, r, outer_ref if t == 0 else None))
            for p in every:
                strip_refs[t + 1][p, rows, :] = e[p] - m * rate[p]

        each_window(strip_windows, strip)

        def ends(r):
            rows = pl.ds(r, 8)
            spread_ends(ends_ref, [strip_refs[t + 1][p, rows, :] for p in every], rows)

        each_window(end_windows, ends)

    step(0, (3, 3, 13), (4, 2), (4, 2))
    step(1, (4, 2, 12), (4, 2), (4, 2))
    step(2, (4, 2, 12), (4, 2), (8, 1))
    step(3, (8, 1, 8), None, None)


def backward(
    cot_ref, map_ref, above_ref, below_ref, far_ref, strips_ref,
    e_refs, rate_refs, se_refs, m_ref, ms_ref,
    adjoint_ref, sums_ref,
    lam_refs, slam_refs, u_refs, su_refs, ends_ref, work_ref, binned_ref,
):
    params, layers = cot_ref.shape[:2]
    tile = (8, 128)
    every = range(params)

    def place(z, carry):
        m = [m_ref[z, 8 * i : 8 * i + 8, :] for i in range(3)]
        for p in every:
            k = LEAD + (p * layers + z) * ADJ_EDGE
            blocks = (above_ref[pl.ds(k + ADJ_EDGE - 8, 8), :], cot_ref[p, z], below_ref[pl.ds(k, 8), :])
            for i in range(3):
                lam_refs[0][p, z, 8 * i : 8 * i + 8, :] = blocks[i]
                u_refs[0][p, z, 8 * i : 8 * i + 8, :] = m[i] * blocks[i]
        return carry

    lax.fori_loop(0, layers, place, 0)
    far_above, far_below = around("wide", far_ref.shape[0])
    _, cot, _ = merged_strips(params, strips_ref)
    n = CORNER[1]
    for p in every:
        at = params * CORNER[0] + n * p
        ref = slam_refs[0].at[p]
        ref[0:8, :] = jnp.zeros(tile, jnp.float32)
        ref[16:24, :] = jnp.zeros(tile, jnp.float32)
        ref[8 - n : 8, :] = far_ref[far_above, at : at + n, :]
        ref[8:16, :] = cot[p]
        ref[16 : 16 + n, :] = far_ref[far_below, at : at + n, :]
        for r in (0, 8, 16):
            su_refs[0][p, r : r + 8, :] = ms_ref[r : r + 8, :] * ref[r : r + 8, :]

    def spread(slot, windows):
        def ends(r):
            rows = pl.ds(r, 8)
            spread_ends(ends_ref, [su_refs[slot][p, rows, :] for p in every], rows)

        each_window(windows, ends)

    def step(t, slot, windows, strip_windows, end_windows):
        old, old_strip = u_refs[slot], su_refs[slot]
        last = t == 0

        def core(z, i, r):
            rows = pl.ds(r, 8)
            e = [e_refs[t][p, z, rows, :] for p in every]
            u = [old[p, z, rows, :] for p in every]
            m = m_ref[z, rows, :]
            change = changes(e, u, neighbours(old, ends_ref, u, z, r))
            lam = [lam_refs[slot][p, z, rows, :] for p in every]
            work = total_of([lam[p] * rate_refs[t][p, z, rows, :] for p in every])
            stores = [put(work_ref, (t, z, i), work)]
            for p in every:
                new = lam[p] - change[p]
                if last:
                    stores.append(put(adjoint_ref, (p, z), new))
                else:
                    stores.append(put(lam_refs[1 - slot], (p, z, rows, slice(None)), new))
                    stores.append(put(u_refs[1 - slot], (p, z, rows, slice(None)), m * new))
            return stores

        each_tile(layers, windows, core)
        if last:
            return

        def strip(r):
            rows = pl.ds(r, 8)
            e = [se_refs[t - 1][p, rows, :] for p in every]
            u = [old_strip[p, rows, :] for p in every]
            m = ms_ref[rows, :]
            change = changes(e, u, strip_neighbours(old_strip, old, u, r))
            for p in every:
                new = slam_refs[slot][p, rows, :] - change[p]
                slam_refs[1 - slot][p, rows, :] = new
                su_refs[1 - slot][p, rows, :] = m * new

        each_window(strip_windows, strip)
        spread(1 - slot, end_windows)

    spread(0, (4, 2))
    step(3, 0, (4, 2, 12), (4, 2), (4, 2))
    step(2, 1, (4, 2, 12), (4, 2), (4, 2))
    step(1, 0, (4, 2, 12), (8, 1), (8, 1))
    step(0, 1, (8, 1, 8), None, None)

    grains = [map_ref[z] for z in range(layers)]
    cells = []
    for z in range(layers):
        upper = work_ref[1, z, 0] + work_ref[2, z, 0] + work_ref[3, z, 0]
        lower = work_ref[1, z, 1] + work_ref[2, z, 1] + work_ref[3, z, 1]
        cells.append(jnp.concatenate([upper[4:8], lower[0:4]], axis=0) + work_ref[0, z, 0])

    def bin_one(g, carry):
        kept = [jnp.where(grains[z] == g, cells[z], 0.0) for z in range(layers)]
        total = sum(kept[1:4], kept[0]) + sum(kept[5:8], kept[4]) + sum(kept[9:], kept[8])
        binned_ref[pl.ds(g, 1), :] = jnp.sum(total, axis=0, keepdims=True)
        return carry

    lax.fori_loop(0, binned_ref.shape[0], bin_one, 0, unroll=4)
    ones = jnp.full((8, 128), -TIME_STEP, jnp.float32)
    sums = lax.dot_general(
        ones, binned_ref[...], (((1,), (1,)), ((), ())),
        precision=lax.Precision.HIGHEST, preferred_element_type=jnp.float32,
    )
    for k in range(0, sums_ref.shape[0], 8):
        sums_ref[k : k + 8, :] = sums


def pick_owned(counts, owned, slots_ref, sums_ref, out_ref, slot_rows, value_rows, total_ref):
    wide_count, narrow_count = counts
    count = wide_count * narrow_count
    wide, narrow = lax.axis_index("wide"), lax.axis_index("narrow")
    base = (wide * narrow_count + narrow) * owned
    listed = sums_ref.shape[1]
    tile = (8, 128)
    for k in range(count):
        slot = slots_ref[k : k + 1, :] - base
        slot_rows[k] = jnp.broadcast_to(slot, tile)
        value = jnp.concatenate([sums_ref[k : k + 1, :], jnp.zeros((1, 128 - listed), jnp.float32)], axis=1)
        value_rows[k] = jnp.broadcast_to(value, tile)
    sub = lax.broadcasted_iota(jnp.int32, tile, 0)
    blocks = total_ref.shape[0] // 8
    step = 16
    for first in range(0, blocks, step):
        some = range(first, min(first + step, blocks))

        def body(k, acc, some=some):
            slot, value = slot_rows[k], value_rows[k]
            shifted = slot - sub
            return tuple(a + jnp.where(shifted == 8 * j, value, 0.0) for a, j in zip(acc, some))

        acc = lax.fori_loop(0, count, body, tuple(jnp.zeros(tile, jnp.float32) for _ in some), unroll=4)
        for a, j in zip(acc, some):
            total_ref[8 * j : 8 * j + 8, :] = a
    whole = lax.dot_general(
        jnp.ones(tile, jnp.float32), total_ref[...], (((1,), (1,)), ((), ())),
        precision=lax.Precision.HIGHEST, preferred_element_type=jnp.float32,
    )
    out_ref[...] = whole[0:1, 0:owned]


def f32(*shape):
    return jax.ShapeDtypeStruct(shape, jnp.float32)


def kernel(body, out_shape, scratch=(), name=None, **specs):
    return pl.pallas_call(
        body, out_shape=out_shape, scratch_shapes=list(scratch), name=name, **specs,
        compiler_params=pltpu.CompilerParams(vmem_limit_bytes=VMEM_LIMIT),
    )


def shifted(value, axis, count, by):
    return lax.ppermute(value, axis, [(i, (i + by) % count) for i in range(count)])


def per_device(counts, order_init, cotangent, grain_map, brick_grains, grain_slot, mobility):
    wide_count, narrow_count = counts
    params, layers = order_init.shape[:2]
    assert order_init.shape[2:] == (8, 128) and layers * COLS < 128
    owned = mobility.shape[0]
    listed = brick_grains.shape[1]
    bricks = brick_grains.shape[0]

    both = ("wide", "narrow")
    count = wide_count * narrow_count

    owned_rows = -(-owned // 128)
    strip_rows = 8 * (params + 1) + owned_rows
    strip_rows += -strip_rows % 8
    edge_rows = row_places(params, layers)[1]
    cot_rows = params * layers * ADJ_EDGE + 2 * LEAD
    anywhere, here = pl.BlockSpec(memory_space=pl.ANY), pl.BlockSpec(memory_space=pltpu.VMEM)
    vmem = lambda *shape: pltpu.VMEM(shape, jnp.float32)

    arguments = (
        order_init, grain_map, cotangent, mobility.reshape(1, owned), brick_grains, grain_slot.reshape(-1, 128)
    )
    *fetched, down, up = kernel(
        pack_rows,
        tuple(jax.ShapeDtypeStruct(x.shape, x.dtype) for x in arguments) + (f32(edge_rows, 128),) * 2,
        (pltpu.SemaphoreType.DMA((len(arguments),)),), name="pack_rows",
        in_specs=[pl.BlockSpec(memory_space=pltpu.HBM)] * len(arguments),
    )(*(pltpu.with_memory_space_constraint(x, pltpu.HBM) for x in arguments))
    order_init, grain_map, cotangent, mobility, brick_grains, grain_slot = fetched
    above = shifted(down, "wide", wide_count, 1)
    below = shifted(up, "wide", wide_count, -1)
    slots = kernel(
        find_slots, jax.ShapeDtypeStruct((bricks, 128), jnp.int32), name="find_slots"
    )(brick_grains, grain_slot)
    strips = kernel(
        pack_strips, f32(narrow_count, strip_rows, 128),
        name="pack_strips", in_specs=[here] * 4 + [anywhere],
    )(order_init, cotangent, grain_map, mobility, down)
    strips = lax.all_to_all(strips, "narrow", 0, 0, tiled=True)

    far_rows = corner_rows(params) + narrow_count * owned_rows
    far_rows += -far_rows % 8
    far = kernel(
        functools.partial(pack_far, params, owned_rows), f32(wide_count, far_rows, 128),
        name="pack_far", in_specs=[here, anywhere],
    )(strips, slots)
    far = lax.all_to_all(far, "wide", 0, 0, tiled=True)

    table, cot_down, cot_up = kernel(
        functools.partial(find_mobility, counts, owned, owned_rows),
        (f32(16, 128),) + (f32(cot_rows, 128),) * 2,
        (pltpu.VMEM((16, 128), jnp.int32), vmem(count * owned_rows, 128)),
        name="find_mobility",
    )(slots, far, cotangent)
    cot_above = shifted(cot_down, "wide", wide_count, 1)
    cot_below = shifted(cot_up, "wide", wide_count, -1)

    padded, strip = (params, layers, ROWS, 128), (params, ROWS, 128)
    final, states, rate, halos, m, ms = kernel(
        forward,
        (
            f32(*order_init.shape), [f32(*padded)] * ITERS, [f32(*padded)] * ITERS,
            [f32(*strip)] * (ITERS - 1), f32(layers, ROWS, 128), f32(ROWS, 128),
        ),
        (vmem(*strip), vmem(*strip), vmem(*padded), vmem(layers, ROWS, 128), vmem(ROWS, 128)),
        name="forward",
    )(order_init, grain_map, above, below, far, strips, table)
    adjoint, sums = kernel(
        backward,
        (f32(*order_init.shape), f32(count, listed)),
        (
            [vmem(*padded)] * 2, [vmem(*strip)] * 2, [vmem(*padded)] * 2, [vmem(*strip)] * 2,
            vmem(*padded), vmem(ITERS, layers, 2, 8, 128), vmem(listed, 128),
        ),
        name="backward",
    )(
        cotangent, grain_map, cot_above, cot_below, far, strips,
        states, rate, halos, m, ms,
    )

    every_sum = lax.all_to_all(sums, both, 0, 0, tiled=True)
    grads = kernel(
        functools.partial(pick_owned, counts, owned),
        f32(1, owned),
        (pltpu.VMEM((count, 8, 128), jnp.int32), vmem(count, 8, 128), vmem(owned + -owned % 8, 128)),
        name="pick_owned",
    )(slots, every_sum)
    return final, adjoint, grads.reshape(owned)


def solution(mesh):
    counts = (mesh.shape["wide"], mesh.shape["narrow"])
    field = P("groups", None, "wide", "narrow")
    spread = P(("groups", "wide", "narrow"))
    return jax.shard_map(
        functools.partial(per_device, counts),
        mesh=mesh,
        in_specs=(field, field, P("groups", "wide", "narrow"), P("groups", None), P("groups"), spread),
        out_specs=(field, field, spread),
        check_vma=False,
    )
```

```python
import functools

import jax
import jax.numpy as jnp
from jax import lax
from jax.experimental import pallas as pl
from jax.experimental.pallas import tpu as pltpu
from jax.sharding import PartitionSpec as P

ITERS = 4
TIME_STEP = 0.05

EDGE = 6
MAP_EDGE = 5
ADJ_EDGE = 4
ROWS = 24
COLS = 10
LEAD = 8
CORNER = (5, 3, 4)

VMEM_LIMIT = 24 * 1024 * 1024


def lanes(shape):
    return lax.broadcasted_iota(jnp.int32, shape, len(shape) - 1)


def roll(value, shift):
    return pltpu.roll(value, shift, 1)


def is_odd(axis):
    return lax.rem(lax.axis_index(axis), 2) == 1


def pack(*refs):
    count = (len(refs) - 6) // 2
    sources, targets = refs[:count], refs[count : 2 * count]
    *row_refs, strip_a_ref, strip_b_ref, own_ref, sems = refs[2 * count :]
    copies = [pltpu.make_async_copy(a, b, sems.at[i]) for i, (a, b) in enumerate(zip(sources, targets))]
    for copy in copies:
        copy.start()
    order_ref, map_ref, cot_ref, mob_ref = targets[:4]
    params, layers = order_ref.shape[:2]
    maps = row_places(params, layers)[0]
    gap = jnp.zeros((LEAD, 128), jnp.float32)
    odd = is_odd("wide")
    odd_y = is_odd("narrow")
    last = (jnp.where(odd, 0, 1), jnp.where(odd, 1, 0))
    for ref in row_refs:
        ref[0:LEAD, :] = gap
        ref[maps - LEAD : maps, :] = gap
        ref[ref.shape[0] - 2 * LEAD : ref.shape[0] - LEAD, :] = gap
        ref[ref.shape[0] - LEAD :, :] = gap
    copies[0].wait()
    for p in range(params):
        for z in range(layers):
            k = LEAD + (p * layers + z) * EDGE
            for ref, is_last in zip(row_refs, last):
                ref[k : k + EDGE, :] = order_ref[p, z, pl.ds((8 - EDGE) * is_last, EDGE), :]
    copies[1].wait()
    for z in range(layers):
        k = maps + z * MAP_EDGE
        for ref, is_last in zip(row_refs, last):
            ref[k : k + MAP_EDGE, :] = map_ref[z, pl.ds((8 - MAP_EDGE) * is_last, MAP_EDGE), :].astype(jnp.float32)
    for copy in copies[2:]:
        copy.wait()

    lane = lanes((8, 128))
    zero = jnp.zeros((8, 128), jnp.float32)

    def span(first, size):
        return ((lane - first) & 127) < size

    for field in range(params + 1):
        right, left = zero, zero
        for z in range(layers):
            value = order_ref[field, z] if field < params else map_ref[z].astype(jnp.float32)
            moved = roll(value, 10 * z + 5)
            right = jnp.where(span(10 * z - 1, 6), moved, right)
            left = jnp.where(span(10 * z + 5, 6), moved, left)
            if field < params:
                right = jnp.where(span(10 * z + 5, 4), roll(cot_ref[field, z], 10 * z + 9), right)
                left = jnp.where(span(10 * z + 1, 4), roll(cot_ref[field, z], 10 * z + 1), left)
        rows = slice(8 * field, 8 * field + 8)
        strip_a_ref[rows, :] = jnp.where(odd_y, left, right)
        strip_b_ref[rows, :] = jnp.where(odd_y, right, left)
    owned = mob_ref.shape[1]
    at = 8 * (params + 1)
    for i in range(own_ref.shape[0]):
        size = min(128, owned - 128 * i)
        row = mob_ref[0:1, 128 * i : 128 * i + size]
        if size < 128:
            row = jnp.concatenate([row, jnp.zeros((1, 128 - size), jnp.float32)], axis=1)
        for ref, k in ((own_ref, i), (strip_a_ref, at + i), (strip_b_ref, at + i)):
            ref[k : k + 1, :] = row


def row_places(params, layers):
    maps = LEAD + params * layers * EDGE + LEAD
    length = maps + layers * MAP_EDGE
    return maps, length + -length % 8 + LEAD


def corner_rows(params):
    return -(-(params * (CORNER[0] + CORNER[1]) + CORNER[2]) // 8) * 8


def side_strips(params, strip_a_ref, strip_b_ref):
    odd = is_odd("narrow")
    fields = []
    for field in range(params + 1):
        rows = slice(8 * field, 8 * field + 8)
        a, b = strip_a_ref[rows, :], strip_b_ref[rows, :]
        fields.append((jnp.where(odd, a, b), jnp.where(odd, b, a)))
    return fields


def merged_strips(params, *strip_refs):
    first = lanes((8, 128)) % COLS < 5
    fields = side_strips(params, *strip_refs)
    order = [jnp.where(first, a, b) for a, b in fields[:params]]
    cot = [jnp.where(first, roll(a, 124), roll(b, 4)) for a, b in fields[:params]]
    return order, cot, jnp.where(first, *fields[params])


def pieces_back(odd, own, a, b, others):
    return [own, jnp.where(odd, a, b), *others, jnp.where(odd, b, a)]


def pack_far(params, strip_a_ref, strip_b_ref, own_ref, slots_ref, *refs):
    *other_refs, far_a_ref, far_b_ref, block_ref = refs
    rows = own_ref.shape[0]
    at = 8 * (params + 1)
    pieces = pieces_back(
        is_odd("narrow"), own_ref[...], strip_a_ref[at : at + rows, :], strip_b_ref[at : at + rows, :],
        [ref[...] for ref in other_refs],
    )
    mobs = corner_rows(params)
    for i, piece in enumerate(pieces):
        for ref, k in ((block_ref, 0), (far_a_ref, mobs), (far_b_ref, mobs)):
            ref[k + i * rows : k + (i + 1) * rows, :] = piece
    at = 0
    odd = is_odd("wide")
    order, cot, cells = merged_strips(params, strip_a_ref, strip_b_ref)
    for n, fields in zip(CORNER, (order, cot, [cells])):
        for both in fields:
            far_a_ref[at : at + n, :] = jnp.where(odd, both[0:n], both[8 - n : 8])
            far_b_ref[at : at + n, :] = jnp.where(odd, both[8 - n : 8], both[0:n])
            at += n
    for ref in (far_a_ref, far_b_ref):
        ref[at:mobs, :] = jnp.zeros((mobs - at, 128), jnp.float32)


def find_slots(bricks_ref, slot_ref, out_ref):
    count, listed = bricks_ref.shape
    rows = slot_ref.shape[0]
    pad = jnp.zeros((8, 128 - listed), jnp.int32)
    for k in range(0, count, 8):
        grain = jnp.concatenate([bricks_ref[k : k + 8, :], pad], axis=1)
        row, col = grain >> 7, grain & 127

        def body(r, found, row=row, col=col):
            table = jnp.broadcast_to(slot_ref[pl.ds(r, 1), :], (8, 128))
            taken = jnp.take_along_axis(table, col, axis=1, mode="promise_in_bounds")
            return jnp.where(row == r, taken, found)

        found = lax.fori_loop(0, rows, body, jnp.zeros((8, 128), jnp.int32), unroll=7)
        out_ref[k : k + 8, :] = jnp.where(lanes((8, 128)) < listed, found, -1)


def find_mobility(counts, owned, slots_ref, block_ref, far_a_ref, far_b_ref, cot_ref, *refs):
    *other_refs, table_ref, cot_a_ref, cot_b_ref, near_ref, mob_ref = refs
    params, layers = cot_ref.shape[:2]
    odd = is_odd("wide")
    last = (jnp.where(odd, 0, 1), jnp.where(odd, 1, 0))
    for ref in (cot_a_ref, cot_b_ref):
        ref[0:LEAD, :] = jnp.zeros((LEAD, 128), jnp.float32)
        ref[ref.shape[0] - LEAD :, :] = jnp.zeros((LEAD, 128), jnp.float32)
    for p in range(params):
        for z in range(layers):
            k = LEAD + (p * layers + z) * ADJ_EDGE
            for ref, is_last in zip((cot_a_ref, cot_b_ref), last):
                ref[k : k + ADJ_EDGE, :] = cot_ref[p, z, pl.ds((8 - ADJ_EDGE) * is_last, ADJ_EDGE), :]

    wide_count, narrow_count = counts
    tile = (8, 128)
    wide, narrow = lax.axis_index("wide"), lax.axis_index("narrow")
    size, at = block_ref.shape[0], corner_rows(params)
    owned_rows = size // narrow_count
    pieces = pieces_back(
        odd, block_ref[...], far_a_ref[at : at + size, :], far_b_ref[at : at + size, :],
        [ref[...] for ref in other_refs],
    )
    for i, piece in enumerate(pieces):
        mob_ref[i * size : (i + 1) * size, :] = piece
    for i in range(3):
        for j in range(3):
            w = lax.rem(wide + i - 1 + wide_count, wide_count)
            n = lax.rem(narrow + j - 1 + narrow_count, narrow_count)
            near_ref[3 * i + j : 3 * i + j + 1, :] = slots_ref[pl.ds(w * narrow_count + n, 1), :]
    near_ref[9:16, :] = jnp.zeros((7, 128), jnp.int32)
    slot = [jnp.maximum(near_ref[k : k + 8, :], 0) for k in (0, 8)]
    owner = [jnp.floor((x.astype(jnp.float32) + 0.5) * (1.0 / owned)).astype(jnp.int32) for x in slot]
    inner = [x - y * owned for x, y in zip(slot, owner)]
    by_wide = [jnp.floor((y.astype(jnp.float32) + 0.5) * (1.0 / narrow_count)).astype(jnp.int32) for y in owner]
    back_w = [wide - y for y in by_wide]
    back_n = [narrow - (x - y * narrow_count) for x, y in zip(owner, by_wide)]
    back_w = [jnp.where(x < 0, x + wide_count, x) for x in back_w]
    back_n = [jnp.where(x < 0, x + narrow_count, x) for x in back_n]
    row = [(a * narrow_count + b) * owned_rows + (x >> 7) for a, b, x in zip(back_w, back_n, inner)]
    place = [x & 127 for x in inner]

    def body(r, found):
        values = jnp.broadcast_to(mob_ref[pl.ds(r, 1), :], tile)
        return tuple(
            jnp.where(row[k] == r, jnp.take_along_axis(values, place[k], axis=1, mode="promise_in_bounds"), found[k])
            for k in range(2)
        )

    zero = jnp.zeros(tile, jnp.float32)
    found = lax.fori_loop(0, mob_ref.shape[0], body, (zero, zero), unroll=16)
    for k in range(2):
        table_ref[8 * k : 8 * k + 8, :] = TIME_STEP * found[k]


def total_of(values):
    while len(values) > 1:
        values = [a + b for a, b in zip(values[::2], values[1::2])]
    return values[0]


def each_tile(layers, windows, body):
    start, count, most = windows
    group = 12 // (2 * count) * 2 if layers % 12 == 0 else 1

    def some(step, carry):
        stores = []
        for j in range(group):
            z = step * group + j
            for i in range(count):
                stores += body(z, i, jnp.minimum(start + 8 * i + ((z + 16) >> 5), most))
            if len(stores) >= 64 or j == group - 1:
                for store in stores:
                    store()
                stores = []
        return carry

    lax.fori_loop(0, layers // group, some, 0)


def each_window(windows, body):
    def one(i, carry):
        body(windows[0] + 8 * i)
        return carry

    lax.fori_loop(0, windows[1], one, 0)


def put(ref, index, value):
    def store():
        ref[index] = value

    return store


def neighbours(ref, ends_ref, values, z, r):
    params, layers = ref.shape[:2]
    lane = lanes((8, 128))
    rows, before, after = pl.ds(r, 8), pl.ds(r - 1, 8), pl.ds(r + 1, 8)
    below, above = jnp.maximum(z - 1, 0), jnp.minimum(z + 1, layers - 1)
    near = []
    for p in range(params):
        ends = ends_ref[p, z, rows, :]
        left = roll(jnp.where(lane == 127, ends, values[p]), 1)
        right = roll(jnp.where(lane == 0, ends, values[p]), 127)
        total = (left + right) + (ref[p, z, before, :] + ref[p, z, after, :])
        near.append(total + (ref[p, below, rows, :] + ref[p, above, rows, :]))
    return near


def strip_neighbours(ref, core_ref, values, r, outer_ref=None):
    params, layers = core_ref.shape[:2]
    lane = lanes((8, 128))
    col = lane % COLS
    rows, before, after = pl.ds(r, 8), pl.ds(r - 1, 8), pl.ds(r + 1, 8)
    near = []
    for p in range(params):
        value = values[p]
        ends = jnp.zeros((8, 128), jnp.float32)
        for z in range(layers):
            here = (lane == 10 * z + 4) | (lane == 10 * z + 5)
            ends = jnp.where(here, roll(core_ref[p, z, rows, :], 10 * z + 5), ends)
        left = roll(jnp.where(col == 4, ends, value), 1)
        right = roll(jnp.where(col == 5, ends, value), 127)
        if outer_ref is not None:
            outer = outer_ref[p, rows, :]
            left = jnp.where(col == 0, outer, left)
            right = jnp.where(col == 9, outer, right)
        below = jnp.where(lane < COLS, value, roll(value, COLS))
        above = jnp.where(lane >= COLS * (layers - 1), value, roll(value, 128 - COLS))
        total = (left + right) + (below + above)
        near.append(total + (ref[p, before, :] + ref[p, after, :]))
    return near


def spread_ends(ends_ref, values, rows):
    params, layers = ends_ref.shape[:2]
    for p in range(params):
        for z in range(layers):
            ends_ref[p, z, rows, :] = roll(values[p], 123 - 10 * z)


def rates(e, near):
    squares = [x * x for x in e]
    base = 1.5 * total_of(squares) + 5.0
    return [x * (base - 0.5 * y) - n for x, y, n in zip(e, squares, near)]


def changes(e, u, near):
    squares = [x * x for x in e]
    base = 1.5 * total_of(squares) + 5.0
    inner = 3.0 * total_of([x * y for x, y in zip(e, u)])
    return [y * (base - 1.5 * s) + x * inner - n for x, y, s, n in zip(e, u, squares, near)]


def forward(
    order_ref, map_ref, row_a_ref, row_b_ref, far_a_ref, far_b_ref, strip_a_ref, strip_b_ref, table_ref,
    final_ref, e_refs, rate_refs, se_refs, m_ref, ms_ref,
    first_strip_ref, outer_ref, ends_ref, g_ref, gs_ref,
):
    params, layers = order_ref.shape[:2]
    tile = (8, 128)
    col = lanes(tile) % COLS
    maps = row_places(params, layers)[0]
    strip_refs = [first_strip_ref, *se_refs]
    every = range(params)

    odd = is_odd("wide")
    from_before = (jnp.where(odd, 1, 0), jnp.where(odd, 0, 1))

    def place(z, carry):
        for ref, before in zip((row_a_ref, row_b_ref), from_before):
            k, target = maps + z * MAP_EDGE + before * (MAP_EDGE - 8), pl.ds(16 - 16 * before, 8)
            g_ref[z, target, :] = ref[pl.ds(k, 8), :]
            for p in every:
                k = LEAD + (p * layers + z) * EDGE + before * (EDGE - 8)
                e_refs[0][p, z, target, :] = ref[pl.ds(k, 8), :]
        for p in every:
            e_refs[0][p, z, 8:16, :] = order_ref[p, z]
        return carry

    lax.fori_loop(0, layers, place, 0)

    sides = side_strips(params, strip_a_ref, strip_b_ref)
    order, _, cells = merged_strips(params, strip_a_ref, strip_b_ref)
    n = CORNER[0]
    for p in every:
        ref = first_strip_ref.at[p]
        ref[0:8, :] = jnp.zeros(tile, jnp.float32)
        ref[16:24, :] = jnp.zeros(tile, jnp.float32)
        a, b = far_a_ref[n * p : n * p + n, :], far_b_ref[n * p : n * p + n, :]
        ref[8 - n : 8, :] = jnp.where(odd, a, b)
        ref[8:16, :] = order[p]
        ref[16 : 16 + n, :] = jnp.where(odd, b, a)
        outer_ref[p, 8:16, :] = jnp.where(col == 0, roll(sides[p][0], 1), roll(sides[p][1], 127))
    at, n = params * (CORNER[0] + CORNER[1]), CORNER[2]
    gs_ref[...] = jnp.zeros_like(gs_ref)
    a, b = far_a_ref[at : at + n, :], far_b_ref[at : at + n, :]
    gs_ref[8 - n : 8, :] = jnp.where(odd, a, b)
    gs_ref[8:16, :] = cells
    gs_ref[16 : 16 + n, :] = jnp.where(odd, b, a)
    for r in (0, 8, 16):
        rows = slice(r, r + 8)
        spread_ends(ends_ref, [first_strip_ref[p, rows, :] for p in every], rows)

    def lookup(index, which):
        values = jnp.broadcast_to(table_ref[which : which + 1, :], tile)
        return jnp.take_along_axis(values, index, axis=1, mode="promise_in_bounds")

    for i in range(3):
        r = 8 * i
        for z in range(layers):
            index = map_ref[z] if i == 1 else g_ref[z, r : r + 8, :].astype(jnp.int32) & 127
            m_ref[z, r : r + 8, :] = lookup(index, 3 * i + 1)
        index = gs_ref[r : r + 8, :].astype(jnp.int32) & 127
        ms_ref[r : r + 8, :] = jnp.where(col < 5, lookup(index, 3 * i), lookup(index, 3 * i + 2))

    def step(t, windows, strip_windows, end_windows):
        old, old_strip = e_refs[t], strip_refs[t]
        last = t == ITERS - 1

        def core(z, i, r):
            rows = pl.ds(r, 8)
            e = [old[p, z, rows, :] for p in every]
            m = m_ref[z, rows, :]
            rate = rates(e, neighbours(old, ends_ref, e, z, r))
            stores = []
            for p in every:
                new = e[p] - m * rate[p]
                stores.append(put(rate_refs[t], (p, z, rows, slice(None)), rate[p]))
                if last:
                    stores.append(put(final_ref, (p, z), new))
                else:
                    stores.append(put(e_refs[t + 1], (p, z, rows, slice(None)), new))
            return stores

        each_tile(layers, windows, core)
        if last:
            return

        def strip(r):
            rows = pl.ds(r, 8)
            e = [old_strip[p, rows, :] for p in every]
            m = ms_ref[rows, :]
            rate = rates(e, strip_neighbours(old_strip, old, e, r, outer_ref if t == 0 else None))
            for p in every:
                strip_refs[t + 1][p, rows, :] = e[p] - m * rate[p]

        each_window(strip_windows, strip)

        def ends(r):
            rows = pl.ds(r, 8)
            spread_ends(ends_ref, [strip_refs[t + 1][p, rows, :] for p in every], rows)

        each_window(end_windows, ends)

    step(0, (3, 3, 13), (4, 2), (4, 2))
    step(1, (4, 2, 12), (4, 2), (4, 2))
    step(2, (4, 2, 12), (4, 2), (8, 1))
    step(3, (8, 1, 8), None, None)


def backward(
    cot_ref, map_ref, row_a_ref, row_b_ref, far_a_ref, far_b_ref, strip_a_ref, strip_b_ref,
    e_refs, rate_refs, se_refs, m_ref, ms_ref,
    adjoint_ref, sums_ref,
    lam_refs, slam_refs, u_refs, su_refs, ends_ref, work_ref, binned_ref,
):
    params, layers = cot_ref.shape[:2]
    tile = (8, 128)
    every = range(params)

    odd = is_odd("wide")
    from_before = (jnp.where(odd, 1, 0), jnp.where(odd, 0, 1))

    def place(z, carry):
        for ref, before in zip((row_a_ref, row_b_ref), from_before):
            rows = pl.ds(16 - 16 * before, 8)
            m = m_ref[z, rows, :]
            for p in every:
                k = LEAD + (p * layers + z) * ADJ_EDGE + before * (ADJ_EDGE - 8)
                value = ref[pl.ds(k, 8), :]
                lam_refs[0][p, z, rows, :] = value
                u_refs[0][p, z, rows, :] = m * value
        m = m_ref[z, 8:16, :]
        for p in every:
            lam_refs[0][p, z, 8:16, :] = cot_ref[p, z]
            u_refs[0][p, z, 8:16, :] = m * cot_ref[p, z]
        return carry

    lax.fori_loop(0, layers, place, 0)
    _, cot, _ = merged_strips(params, strip_a_ref, strip_b_ref)
    n = CORNER[1]
    for p in every:
        at = params * CORNER[0] + n * p
        ref = slam_refs[0].at[p]
        ref[0:8, :] = jnp.zeros(tile, jnp.float32)
        ref[16:24, :] = jnp.zeros(tile, jnp.float32)
        a, b = far_a_ref[at : at + n, :], far_b_ref[at : at + n, :]
        ref[8 - n : 8, :] = jnp.where(odd, a, b)
        ref[8:16, :] = cot[p]
        ref[16 : 16 + n, :] = jnp.where(odd, b, a)
        for r in (0, 8, 16):
            su_refs[0][p, r : r + 8, :] = ms_ref[r : r + 8, :] * ref[r : r + 8, :]

    def spread(slot, windows):
        def ends(r):
            rows = pl.ds(r, 8)
            spread_ends(ends_ref, [su_refs[slot][p, rows, :] for p in every], rows)

        each_window(windows, ends)

    def step(t, slot, windows, strip_windows, end_windows):
        old, old_strip = u_refs[slot], su_refs[slot]
        last = t == 0

        def core(z, i, r):
            rows = pl.ds(r, 8)
            e = [e_refs[t][p, z, rows, :] for p in every]
            u = [old[p, z, rows, :] for p in every]
            m = m_ref[z, rows, :]
            change = changes(e, u, neighbours(old, ends_ref, u, z, r))
            lam = [lam_refs[slot][p, z, rows, :] for p in every]
            work = total_of([lam[p] * rate_refs[t][p, z, rows, :] for p in every])
            stores = [put(work_ref, (t, z, i), work)]
            for p in every:
                new = lam[p] - change[p]
                if last:
                    stores.append(put(adjoint_ref, (p, z), new))
                else:
                    stores.append(put(lam_refs[1 - slot], (p, z, rows, slice(None)), new))
                    stores.append(put(u_refs[1 - slot], (p, z, rows, slice(None)), m * new))
            return stores

        each_tile(layers, windows, core)
        if last:
            return

        def strip(r):
            rows = pl.ds(r, 8)
            e = [se_refs[t - 1][p, rows, :] for p in every]
            u = [old_strip[p, rows, :] for p in every]
            m = ms_ref[rows, :]
            change = changes(e, u, strip_neighbours(old_strip, old, u, r))
            for p in every:
                new = slam_refs[slot][p, rows, :] - change[p]
                slam_refs[1 - slot][p, rows, :] = new
                su_refs[1 - slot][p, rows, :] = m * new

        each_window(strip_windows, strip)
        spread(1 - slot, end_windows)

    spread(0, (4, 2))
    step(3, 0, (4, 2, 12), (4, 2), (4, 2))
    step(2, 1, (4, 2, 12), (4, 2), (4, 2))
    step(1, 0, (4, 2, 12), (8, 1), (8, 1))
    step(0, 1, (8, 1, 8), None, None)

    grains = [map_ref[z] for z in range(layers)]
    cells = []
    for z in range(layers):
        upper = work_ref[1, z, 0] + work_ref[2, z, 0] + work_ref[3, z, 0]
        lower = work_ref[1, z, 1] + work_ref[2, z, 1] + work_ref[3, z, 1]
        cells.append(jnp.concatenate([upper[4:8], lower[0:4]], axis=0) + work_ref[0, z, 0])

    def bin_one(g, carry):
        kept = [jnp.where(grains[z] == g, cells[z], 0.0) for z in range(layers)]
        total = sum(kept[1:4], kept[0]) + sum(kept[5:8], kept[4]) + sum(kept[9:], kept[8])
        binned_ref[pl.ds(g, 1), :] = jnp.sum(total, axis=0, keepdims=True)
        return carry

    lax.fori_loop(0, binned_ref.shape[0], bin_one, 0, unroll=4)
    ones = jnp.full((8, 128), -TIME_STEP, jnp.float32)
    sums = lax.dot_general(
        ones, binned_ref[...], (((1,), (1,)), ((), ())),
        precision=lax.Precision.HIGHEST, preferred_element_type=jnp.float32,
    )
    for k in range(0, sums_ref.shape[0], 8):
        sums_ref[k : k + 8, :] = sums


def pick_owned(counts, owned, slots_ref, sums_ref, out_ref, slot_rows, value_rows, total_ref):
    wide_count, narrow_count = counts
    count = wide_count * narrow_count
    wide, narrow = lax.axis_index("wide"), lax.axis_index("narrow")
    base = (wide * narrow_count + narrow) * owned
    listed = sums_ref.shape[1]
    tile = (8, 128)
    for k in range(count):
        slot = slots_ref[k : k + 1, :] - base
        slot_rows[k] = jnp.broadcast_to(slot, tile)
        value = jnp.concatenate([sums_ref[k : k + 1, :], jnp.zeros((1, 128 - listed), jnp.float32)], axis=1)
        value_rows[k] = jnp.broadcast_to(value, tile)
    sub = lax.broadcasted_iota(jnp.int32, tile, 0)
    blocks = total_ref.shape[0] // 8
    step = 16
    for first in range(0, blocks, step):
        some = range(first, min(first + step, blocks))

        def body(k, acc, some=some):
            slot, value = slot_rows[k], value_rows[k]
            shifted = slot - sub
            return tuple(a + jnp.where(shifted == 8 * j, value, 0.0) for a, j in zip(acc, some))

        acc = lax.fori_loop(0, count, body, tuple(jnp.zeros(tile, jnp.float32) for _ in some), unroll=4)
        for a, j in zip(acc, some):
            total_ref[8 * j : 8 * j + 8, :] = a
    whole = lax.dot_general(
        jnp.ones(tile, jnp.float32), total_ref[...], (((1,), (1,)), ((), ())),
        precision=lax.Precision.HIGHEST, preferred_element_type=jnp.float32,
    )
    out_ref[...] = whole[0:1, 0:owned]


def f32(*shape):
    return jax.ShapeDtypeStruct(shape, jnp.float32)


def kernel(body, out_shape, scratch=(), name=None, **specs):
    return pl.pallas_call(
        body, out_shape=out_shape, scratch_shapes=list(scratch), name=name, **specs,
        compiler_params=pltpu.CompilerParams(vmem_limit_bytes=VMEM_LIMIT),
    )


def shifted(value, axis, count, by):
    return lax.ppermute(value, axis, [(i, (i + by) % count) for i in range(count)])


def swapped(value, axis, count, partner):
    step = [1 if (i + partner) % 2 == 0 else -1 for i in range(count)]
    return lax.ppermute(value, axis, [(i, (i + by) % count) for i, by in enumerate(step)])


def per_device(counts, order_init, cotangent, grain_map, brick_grains, grain_slot, mobility):
    wide_count, narrow_count = counts
    params, layers = order_init.shape[:2]
    assert order_init.shape[2:] == (8, 128) and layers * COLS < 128
    owned = mobility.shape[0]
    listed = brick_grains.shape[1]
    bricks = brick_grains.shape[0]

    both = ("wide", "narrow")
    count = wide_count * narrow_count

    owned_rows = -(-owned // 128)
    strip_rows = 8 * (params + 1) + owned_rows
    edge_rows = row_places(params, layers)[1]
    cot_rows = params * layers * ADJ_EDGE + 2 * LEAD
    anywhere, here = pl.BlockSpec(memory_space=pl.ANY), pl.BlockSpec(memory_space=pltpu.VMEM)
    vmem = lambda *shape: pltpu.VMEM(shape, jnp.float32)

    arguments = (
        order_init, grain_map, cotangent, mobility.reshape(1, owned), brick_grains, grain_slot.reshape(-1, 128)
    )
    *fetched, row_a, row_b, strip_a, strip_b, own = kernel(
        pack,
        tuple(jax.ShapeDtypeStruct(x.shape, x.dtype) for x in arguments)
        + (f32(edge_rows, 128),) * 2 + (f32(strip_rows, 128),) * 2 + (f32(owned_rows, 128),),
        (pltpu.SemaphoreType.DMA((len(arguments),)),), name="pack",
        in_specs=[pl.BlockSpec(memory_space=pltpu.HBM)] * len(arguments),
    )(*(pltpu.with_memory_space_constraint(x, pltpu.HBM) for x in arguments))
    order_init, grain_map, cotangent, _, brick_grains, grain_slot = fetched
    strip_a = swapped(strip_a, "narrow", narrow_count, 0)
    strip_b = swapped(strip_b, "narrow", narrow_count, 1)
    row_a = swapped(row_a, "wide", wide_count, 0)
    row_b = swapped(row_b, "wide", wide_count, 1)
    others = [shifted(own, "narrow", narrow_count, d) for d in range(2, narrow_count - 1)]
    slots = kernel(
        find_slots, jax.ShapeDtypeStruct((bricks, 128), jnp.int32), name="find_slots"
    )(brick_grains, grain_slot)

    block_rows = narrow_count * owned_rows
    far_rows = corner_rows(params) + block_rows
    far_a, far_b, block = kernel(
        functools.partial(pack_far, params),
        (f32(far_rows, 128),) * 2 + (f32(block_rows, 128),),
        name="pack_far", in_specs=[here] * 3 + [anywhere] + [here] * len(others),
    )(strip_a, strip_b, own, slots, *others)
    far_a = swapped(far_a, "wide", wide_count, 0)
    far_b = swapped(far_b, "wide", wide_count, 1)
    others = [shifted(block, "wide", wide_count, d) for d in range(2, wide_count - 1)]

    table, cot_a, cot_b = kernel(
        functools.partial(find_mobility, counts, owned),
        (f32(16, 128),) + (f32(cot_rows, 128),) * 2,
        (pltpu.VMEM((16, 128), jnp.int32), vmem(wide_count * block_rows, 128)),
        name="find_mobility",
    )(slots, block, far_a, far_b, cotangent, *others)
    cot_a = swapped(cot_a, "wide", wide_count, 0)
    cot_b = swapped(cot_b, "wide", wide_count, 1)

    padded, strip = (params, layers, ROWS, 128), (params, ROWS, 128)
    final, states, rate, halos, m, ms = kernel(
        forward,
        (
            f32(*order_init.shape), [f32(*padded)] * ITERS, [f32(*padded)] * ITERS,
            [f32(*strip)] * (ITERS - 1), f32(layers, ROWS, 128), f32(ROWS, 128),
        ),
        (vmem(*strip), vmem(*strip), vmem(*padded), vmem(layers, ROWS, 128), vmem(ROWS, 128)),
        name="forward",
    )(order_init, grain_map, row_a, row_b, far_a, far_b, strip_a, strip_b, table)
    adjoint, sums = kernel(
        backward,
        (f32(*order_init.shape), f32(count, listed)),
        (
            [vmem(*padded)] * 2, [vmem(*strip)] * 2, [vmem(*padded)] * 2, [vmem(*strip)] * 2,
            vmem(*padded), vmem(ITERS, layers, 2, 8, 128), vmem(listed, 128),
        ),
        name="backward",
    )(
        cotangent, grain_map, cot_a, cot_b, far_a, far_b, strip_a, strip_b,
        states, rate, halos, m, ms,
    )

    every_sum = lax.all_to_all(sums, both, 0, 0, tiled=True)
    grads = kernel(
        functools.partial(pick_owned, counts, owned),
        f32(1, owned),
        (pltpu.VMEM((count, 8, 128), jnp.int32), vmem(count, 8, 128), vmem(owned + -owned % 8, 128)),
        name="pick_owned",
    )(slots, every_sum)
    return final, adjoint, grads.reshape(owned)


def solution(mesh):
    counts = (mesh.shape["wide"], mesh.shape["narrow"])
    field = P("groups", None, "wide", "narrow")
    spread = P(("groups", "wide", "narrow"))
    return jax.shard_map(
        functools.partial(per_device, counts),
        mesh=mesh,
        in_specs=(field, field, P("groups", "wide", "narrow"), P("groups", None), P("groups"), spread),
        out_specs=(field, field, spread),
        check_vma=False,
    )
```

```python
import functools

import jax
import jax.numpy as jnp
from jax import lax
from jax.experimental import pallas as pl
from jax.experimental.pallas import tpu as pltpu
from jax.sharding import PartitionSpec as P

ITERS = 4
TIME_STEP = 0.05

EDGE = 6
MAP_EDGE = 5
ADJ_EDGE = 4
ROWS = 24
COLS = 10
LEAD = 8
CORNER = (5, 3, 4)

VMEM_LIMIT = 24 * 1024 * 1024


def lanes(shape):
    return lax.broadcasted_iota(jnp.int32, shape, len(shape) - 1)


def roll(value, shift):
    return pltpu.roll(value, shift, 1)


def is_odd(axis):
    return lax.rem(lax.axis_index(axis), 2) == 1


def pack(*refs):
    count = (len(refs) - 6) // 2
    sources, targets = refs[:count], refs[count : 2 * count]
    *row_refs, strip_a_ref, strip_b_ref, block_ref, sems = refs[2 * count :]
    copies = [pltpu.make_async_copy(a, b, sems.at[i]) for i, (a, b) in enumerate(zip(sources, targets))]
    for copy in copies:
        copy.start()
    order_ref, map_ref, cot_ref, mob_ref = targets[:4]
    params, layers = order_ref.shape[:2]
    maps, cots = row_places(params, layers)
    gap = jnp.zeros((LEAD, 128), jnp.float32)
    odd = is_odd("wide")
    odd_y = is_odd("narrow")
    last = (jnp.where(odd, 0, 1), jnp.where(odd, 1, 0))
    for ref in row_refs:
        ref[0:LEAD, :] = gap
        ref[maps - LEAD : maps, :] = gap
        ref[cots - 2 * LEAD : cots - LEAD, :] = gap
        ref[cots - LEAD : cots, :] = gap
    row_refs[0][cots : cots + LEAD, :] = gap
    row_refs[0][row_refs[0].shape[0] - LEAD :, :] = gap
    copies[0].wait()
    for p in range(params):
        for z in range(layers):
            k = LEAD + (p * layers + z) * EDGE
            for ref, is_last in zip(row_refs, last):
                ref[k : k + EDGE, :] = order_ref[p, z, pl.ds((8 - EDGE) * is_last, EDGE), :]
    copies[1].wait()
    for z in range(layers):
        k = maps + z * MAP_EDGE
        for ref, is_last in zip(row_refs, last):
            ref[k : k + MAP_EDGE, :] = map_ref[z, pl.ds((8 - MAP_EDGE) * is_last, MAP_EDGE), :].astype(jnp.float32)
    for copy in copies[2:]:
        copy.wait()
    rows = pl.ds((8 - ADJ_EDGE) * last[0], ADJ_EDGE)
    for p in range(params):
        for z in range(layers):
            k = cots + LEAD + (p * layers + z) * ADJ_EDGE
            row_refs[0][k : k + ADJ_EDGE, :] = cot_ref[p, z, rows, :]

    lane = lanes((8, 128))
    zero = jnp.zeros((8, 128), jnp.float32)

    def span(first, size):
        return ((lane - first) & 127) < size

    for field in range(params + 1):
        right, left = zero, zero
        for z in range(layers):
            value = order_ref[field, z] if field < params else map_ref[z].astype(jnp.float32)
            moved = roll(value, 10 * z + 5)
            right = jnp.where(span(10 * z - 1, 6), moved, right)
            left = jnp.where(span(10 * z + 5, 6), moved, left)
            if field < params:
                right = jnp.where(span(10 * z + 5, 4), roll(cot_ref[field, z], 10 * z + 9), right)
                left = jnp.where(span(10 * z + 1, 4), roll(cot_ref[field, z], 10 * z + 1), left)
        rows = slice(8 * field, 8 * field + 8)
        strip_a_ref[rows, :] = jnp.where(odd_y, left, right)
        strip_b_ref[rows, :] = jnp.where(odd_y, right, left)
    owned = mob_ref.shape[1]
    owned_rows = -(-owned // 128)
    block_ref[...] = jnp.zeros_like(block_ref)
    first = lax.axis_index("narrow") * owned_rows
    for i in range(owned_rows):
        size = min(128, owned - 128 * i)
        row = mob_ref[0:1, 128 * i : 128 * i + size]
        if size < 128:
            row = jnp.concatenate([row, jnp.zeros((1, 128 - size), jnp.float32)], axis=1)
        block_ref[pl.ds(first + i, 1), :] = row
    strip_a_ref[8 * (params + 1) :, :] = block_ref[...]


def pack_cot(cot_ref, after_ref, out_ref):
    params, layers = cot_ref.shape[:2]
    out_ref[0:LEAD, :] = jnp.zeros((LEAD, 128), jnp.float32)
    out_ref[out_ref.shape[0] - LEAD :, :] = jnp.zeros((LEAD, 128), jnp.float32)
    rows = pl.ds(jnp.where(is_odd("wide"), 8 - ADJ_EDGE, 0), ADJ_EDGE)
    for p in range(params):
        for z in range(layers):
            k = LEAD + (p * layers + z) * ADJ_EDGE
            out_ref[k : k + ADJ_EDGE, :] = cot_ref[p, z, rows, :]


def pack_second(strip_ref, block_ref, strip_a_ref, slots_ref, out_ref):
    at = strip_ref.shape[0]
    out_ref[0:at, :] = strip_ref[...]
    out_ref[at:, :] = block_ref[...] + strip_a_ref[at:, :]


def row_places(params, layers):
    maps = LEAD + params * layers * EDGE + LEAD
    length = maps + layers * MAP_EDGE
    return maps, length + -length % 8 + LEAD


def corner_rows(params):
    return -(-(params * (CORNER[0] + CORNER[1]) + CORNER[2]) // 8) * 8


def side_strips(params, strip_a_ref, strip_b_ref):
    odd = is_odd("narrow")
    fields = []
    for field in range(params + 1):
        rows = slice(8 * field, 8 * field + 8)
        a, b = strip_a_ref[rows, :], strip_b_ref[rows, :]
        fields.append((jnp.where(odd, a, b), jnp.where(odd, b, a)))
    return fields


def merged_strips(params, *strip_refs):
    first = lanes((8, 128)) % COLS < 5
    fields = side_strips(params, *strip_refs)
    order = [jnp.where(first, a, b) for a, b in fields[:params]]
    cot = [jnp.where(first, roll(a, 124), roll(b, 4)) for a, b in fields[:params]]
    return order, cot, jnp.where(first, *fields[params])


def pack_far(params, strip_a_ref, strip_b_ref, block_ref, far_a_ref, far_b_ref):
    at = 8 * (params + 1)
    mobs = corner_rows(params)
    far_a_ref[mobs:, :] = block_ref[...] + strip_a_ref[at:, :] + strip_b_ref[at:, :]
    at = 0
    odd = is_odd("wide")
    order, cot, cells = merged_strips(params, strip_a_ref, strip_b_ref)
    for n, fields in zip(CORNER, (order, cot, [cells])):
        for both in fields:
            far_a_ref[at : at + n, :] = jnp.where(odd, both[0:n], both[8 - n : 8])
            far_b_ref[at : at + n, :] = jnp.where(odd, both[8 - n : 8], both[0:n])
            at += n
    for ref in (far_a_ref, far_b_ref):
        ref[at:mobs, :] = jnp.zeros((mobs - at, 128), jnp.float32)


def pack_far_second(corner_ref, sent_ref, far_a_ref, out_ref):
    at = corner_ref.shape[0]
    size = sent_ref.shape[0] - at
    out_ref[0:at, :] = corner_ref[...]
    odd = is_odd("wide")
    own, other = sent_ref[at:, :], far_a_ref[at:, :]
    out_ref[at : at + size, :] = jnp.where(odd, other, own)
    out_ref[at + size :, :] = jnp.where(odd, own, other)


def find_slots(bricks_ref, slot_ref, out_ref):
    count, listed = bricks_ref.shape
    rows = slot_ref.shape[0]
    for k in range(0, out_ref.shape[0], 8):
        pairs = [
            jnp.concatenate([bricks_ref[2 * j : 2 * j + 1, :], bricks_ref[2 * j + 1 : 2 * j + 2, :]], axis=1)
            for j in range(k, k + 8)
        ]
        grain = jnp.concatenate(pairs, axis=0)
        row, col = grain >> 7, grain & 127

        def body(r, found, row=row, col=col):
            table = jnp.broadcast_to(slot_ref[pl.ds(r, 1), :], (8, 128))
            taken = jnp.take_along_axis(table, col, axis=1, mode="promise_in_bounds")
            return jnp.where(row == r, taken, found)

        out_ref[k : k + 8, :] = lax.fori_loop(0, rows, body, jnp.zeros((8, 128), jnp.int32), unroll=7)


def find_mobility(counts, owned, slots_ref, *refs):
    *mob_refs, table_ref, near_ref, all_ref = refs
    wide_count, narrow_count = counts
    tile = (8, 128)
    wide, narrow = lax.axis_index("wide"), lax.axis_index("narrow")
    if len(mob_refs) == 1:
        mob_ref = mob_refs[0]
    else:
        sent_ref, got_ref = mob_refs
        mob_ref = all_ref
        size = mob_ref.shape[0] // 2
        upper = wide >= 2
        own, other = sent_ref[sent_ref.shape[0] - size :, :], got_ref[got_ref.shape[0] - size :, :]
        mob_ref[0:size, :] = jnp.where(upper, other, own)
        mob_ref[size:, :] = jnp.where(upper, own, other)
    near_ref[...] = jnp.zeros_like(near_ref)
    for k in range(9):
        w = lax.rem(wide + k // 3 - 1 + wide_count, wide_count)
        n = lax.rem(narrow + k % 3 - 1 + narrow_count, narrow_count)
        brick = w * narrow_count + n
        row = slots_ref[pl.ds(brick >> 1, 1), :]
        half = jnp.where((brick & 1) == 0, row[:, 0:64], row[:, 64:128])
        near_ref[k // 2 : k // 2 + 1, 64 * (k % 2) : 64 * (k % 2) + 64] = half
    slot = near_ref[...]
    owned_rows = -(-owned // 128)
    owner = jnp.floor((slot.astype(jnp.float32) + 0.5) * (1.0 / owned)).astype(jnp.int32)
    inner = slot - owner * owned
    row = owner * owned_rows + (inner >> 7)
    place = inner & 127

    def body(r, found):
        values = jnp.broadcast_to(mob_ref[pl.ds(r, 1), :], tile)
        taken = jnp.take_along_axis(values, place, axis=1, mode="promise_in_bounds")
        return jnp.where(row == r, taken, found)

    found = lax.fori_loop(0, mob_ref.shape[0], body, jnp.zeros(tile, jnp.float32), unroll=16)
    table_ref[...] = TIME_STEP * found


def total_of(values):
    while len(values) > 1:
        values = [a + b for a, b in zip(values[::2], values[1::2])]
    return values[0]


def each_tile(layers, windows, body):
    start, count, most = windows
    group = 12 // (2 * count) * 2 if layers % 12 == 0 else 1

    def some(step, carry):
        stores = []
        for j in range(group):
            z = step * group + j
            for i in range(count):
                stores += body(z, i, jnp.minimum(start + 8 * i + ((z + 16) >> 5), most))
            if len(stores) >= 64 or j == group - 1:
                for store in stores:
                    store()
                stores = []
        return carry

    lax.fori_loop(0, layers // group, some, 0)


def each_window(windows, body):
    def one(i, carry):
        body(windows[0] + 8 * i)
        return carry

    lax.fori_loop(0, windows[1], one, 0)


def put(ref, index, value):
    def store():
        ref[index] = value

    return store


def neighbours(ref, ends_ref, values, z, r):
    params, layers = ref.shape[:2]
    lane = lanes((8, 128))
    rows, before, after = pl.ds(r, 8), pl.ds(r - 1, 8), pl.ds(r + 1, 8)
    below, above = jnp.maximum(z - 1, 0), jnp.minimum(z + 1, layers - 1)
    near = []
    for p in range(params):
        ends = ends_ref[p, z, rows, :]
        left = roll(jnp.where(lane == 127, ends, values[p]), 1)
        right = roll(jnp.where(lane == 0, ends, values[p]), 127)
        total = (left + right) + (ref[p, z, before, :] + ref[p, z, after, :])
        near.append(total + (ref[p, below, rows, :] + ref[p, above, rows, :]))
    return near


def strip_neighbours(ref, core_ref, values, r, outer_ref=None):
    params, layers = core_ref.shape[:2]
    lane = lanes((8, 128))
    col = lane % COLS
    rows, before, after = pl.ds(r, 8), pl.ds(r - 1, 8), pl.ds(r + 1, 8)
    near = []
    for p in range(params):
        value = values[p]
        ends = jnp.zeros((8, 128), jnp.float32)
        for z in range(layers):
            here = (lane == 10 * z + 4) | (lane == 10 * z + 5)
            ends = jnp.where(here, roll(core_ref[p, z, rows, :], 10 * z + 5), ends)
        left = roll(jnp.where(col == 4, ends, value), 1)
        right = roll(jnp.where(col == 5, ends, value), 127)
        if outer_ref is not None:
            outer = outer_ref[p, rows, :]
            left = jnp.where(col == 0, outer, left)
            right = jnp.where(col == 9, outer, right)
        below = jnp.where(lane < COLS, value, roll(value, COLS))
        above = jnp.where(lane >= COLS * (layers - 1), value, roll(value, 128 - COLS))
        total = (left + right) + (below + above)
        near.append(total + (ref[p, before, :] + ref[p, after, :]))
    return near


def spread_ends(ends_ref, values, rows):
    params, layers = ends_ref.shape[:2]
    for p in range(params):
        for z in range(layers):
            ends_ref[p, z, rows, :] = roll(values[p], 123 - 10 * z)


def rates(e, near):
    squares = [x * x for x in e]
    base = 1.5 * total_of(squares) + 5.0
    return [x * (base - 0.5 * y) - n for x, y, n in zip(e, squares, near)]


def changes(e, u, near):
    squares = [x * x for x in e]
    base = 1.5 * total_of(squares) + 5.0
    inner = 3.0 * total_of([x * y for x, y in zip(e, u)])
    return [y * (base - 1.5 * s) + x * inner - n for x, y, s, n in zip(e, u, squares, near)]


def forward(
    order_ref, map_ref, row_a_ref, row_b_ref, far_a_ref, far_b_ref, strip_a_ref, strip_b_ref, table_ref,
    final_ref, e_refs, rate_refs, se_refs, m_ref, ms_ref,
    first_strip_ref, outer_ref, ends_ref, g_ref, gs_ref,
):
    params, layers = order_ref.shape[:2]
    tile = (8, 128)
    col = lanes(tile) % COLS
    maps = row_places(params, layers)[0]
    strip_refs = [first_strip_ref, *se_refs]
    every = range(params)

    odd = is_odd("wide")
    from_before = (jnp.where(odd, 1, 0), jnp.where(odd, 0, 1))

    def place(z, carry):
        for ref, before in zip((row_a_ref, row_b_ref), from_before):
            k, target = maps + z * MAP_EDGE + before * (MAP_EDGE - 8), pl.ds(16 - 16 * before, 8)
            g_ref[z, target, :] = ref[pl.ds(k, 8), :]
            for p in every:
                k = LEAD + (p * layers + z) * EDGE + before * (EDGE - 8)
                e_refs[0][p, z, target, :] = ref[pl.ds(k, 8), :]
        for p in every:
            e_refs[0][p, z, 8:16, :] = order_ref[p, z]
        return carry

    lax.fori_loop(0, layers, place, 0)

    sides = side_strips(params, strip_a_ref, strip_b_ref)
    order, _, cells = merged_strips(params, strip_a_ref, strip_b_ref)
    n = CORNER[0]
    for p in every:
        ref = first_strip_ref.at[p]
        ref[0:8, :] = jnp.zeros(tile, jnp.float32)
        ref[16:24, :] = jnp.zeros(tile, jnp.float32)
        a, b = far_a_ref[n * p : n * p + n, :], far_b_ref[n * p : n * p + n, :]
        ref[8 - n : 8, :] = jnp.where(odd, a, b)
        ref[8:16, :] = order[p]
        ref[16 : 16 + n, :] = jnp.where(odd, b, a)
        outer_ref[p, 8:16, :] = jnp.where(col == 0, roll(sides[p][0], 1), roll(sides[p][1], 127))
    at, n = params * (CORNER[0] + CORNER[1]), CORNER[2]
    gs_ref[...] = jnp.zeros_like(gs_ref)
    a, b = far_a_ref[at : at + n, :], far_b_ref[at : at + n, :]
    gs_ref[8 - n : 8, :] = jnp.where(odd, a, b)
    gs_ref[8:16, :] = cells
    gs_ref[16 : 16 + n, :] = jnp.where(odd, b, a)
    for r in (0, 8, 16):
        rows = slice(r, r + 8)
        spread_ends(ends_ref, [first_strip_ref[p, rows, :] for p in every], rows)

    def lookup(index, which):
        values = jnp.broadcast_to(table_ref[which // 2 : which // 2 + 1, :], tile)
        return jnp.take_along_axis(values, index + 64 * (which % 2), axis=1, mode="promise_in_bounds")

    for i in range(3):
        r = 8 * i
        for z in range(layers):
            index = map_ref[z] if i == 1 else g_ref[z, r : r + 8, :].astype(jnp.int32) & 63
            m_ref[z, r : r + 8, :] = lookup(index, 3 * i + 1)
        index = gs_ref[r : r + 8, :].astype(jnp.int32) & 63
        ms_ref[r : r + 8, :] = jnp.where(col < 5, lookup(index, 3 * i), lookup(index, 3 * i + 2))

    def step(t, windows, strip_windows, end_windows):
        old, old_strip = e_refs[t], strip_refs[t]
        last = t == ITERS - 1

        def core(z, i, r):
            rows = pl.ds(r, 8)
            e = [old[p, z, rows, :] for p in every]
            m = m_ref[z, rows, :]
            rate = rates(e, neighbours(old, ends_ref, e, z, r))
            stores = []
            for p in every:
                new = e[p] - m * rate[p]
                stores.append(put(rate_refs[t], (p, z, rows, slice(None)), rate[p]))
                if last:
                    stores.append(put(final_ref, (p, z), new))
                else:
                    stores.append(put(e_refs[t + 1], (p, z, rows, slice(None)), new))
            return stores

        each_tile(layers, windows, core)
        if last:
            return

        def strip(r):
            rows = pl.ds(r, 8)
            e = [old_strip[p, rows, :] for p in every]
            m = ms_ref[rows, :]
            rate = rates(e, strip_neighbours(old_strip, old, e, r, outer_ref if t == 0 else None))
            for p in every:
                strip_refs[t + 1][p, rows, :] = e[p] - m * rate[p]

        each_window(strip_windows, strip)

        def ends(r):
            rows = pl.ds(r, 8)
            spread_ends(ends_ref, [strip_refs[t + 1][p, rows, :] for p in every], rows)

        each_window(end_windows, ends)

    step(0, (3, 3, 13), (4, 2), (4, 2))
    step(1, (4, 2, 12), (4, 2), (4, 2))
    step(2, (4, 2, 12), (4, 2), (8, 1))
    step(3, (8, 1, 8), None, None)


def backward(
    cot_ref, map_ref, row_a_ref, row_b_ref, far_a_ref, far_b_ref, strip_a_ref, strip_b_ref,
    e_refs, rate_refs, se_refs, m_ref, ms_ref,
    lam_out_ref, u_out_ref, ends_ref, sums_ref,
    first_lam_ref, slam_refs, first_u_ref, su_refs, work_ref, binned_ref,
):
    params, layers = cot_ref.shape[:2]
    lam_refs, u_refs = (first_lam_ref, lam_out_ref), (first_u_ref, u_out_ref)
    cots = row_places(params, layers)[1]
    tile = (8, 128)
    every = range(params)

    odd = is_odd("wide")
    from_before = (jnp.where(odd, 1, 0), jnp.where(odd, 0, 1))

    def place(z, carry):
        for ref, base, before in zip((row_a_ref, row_b_ref), (cots, 0), from_before):
            rows = pl.ds(16 - 16 * before, 8)
            m = m_ref[z, rows, :]
            for p in every:
                k = base + LEAD + (p * layers + z) * ADJ_EDGE + before * (ADJ_EDGE - 8)
                value = ref[pl.ds(k, 8), :]
                lam_refs[0][p, z, rows, :] = value
                u_refs[0][p, z, rows, :] = m * value
        m = m_ref[z, 8:16, :]
        for p in every:
            lam_refs[0][p, z, 8:16, :] = cot_ref[p, z]
            u_refs[0][p, z, 8:16, :] = m * cot_ref[p, z]
        return carry

    lax.fori_loop(0, layers, place, 0)
    _, cot, _ = merged_strips(params, strip_a_ref, strip_b_ref)
    n = CORNER[1]
    for p in every:
        at = params * CORNER[0] + n * p
        ref = slam_refs[0].at[p]
        ref[0:8, :] = jnp.zeros(tile, jnp.float32)
        ref[16:24, :] = jnp.zeros(tile, jnp.float32)
        a, b = far_a_ref[at : at + n, :], far_b_ref[at : at + n, :]
        ref[8 - n : 8, :] = jnp.where(odd, a, b)
        ref[8:16, :] = cot[p]
        ref[16 : 16 + n, :] = jnp.where(odd, b, a)
        for r in (0, 8, 16):
            su_refs[0][p, r : r + 8, :] = ms_ref[r : r + 8, :] * ref[r : r + 8, :]

    def spread(slot, windows):
        def ends(r):
            rows = pl.ds(r, 8)
            spread_ends(ends_ref, [su_refs[slot][p, rows, :] for p in every], rows)

        each_window(windows, ends)

    def step(t, slot, windows, strip_windows, end_windows):
        old, old_strip = u_refs[slot], su_refs[slot]

        def core(z, i, r):
            rows = pl.ds(r, 8)
            e = [e_refs[t][p, z, rows, :] for p in every]
            u = [old[p, z, rows, :] for p in every]
            m = m_ref[z, rows, :]
            change = changes(e, u, neighbours(old, ends_ref, u, z, r))
            lam = [lam_refs[slot][p, z, rows, :] for p in every]
            work = total_of([lam[p] * rate_refs[t][p, z, rows, :] for p in every])
            stores = [put(work_ref, (t - 1, z, i), work)]
            for p in every:
                new = lam[p] - change[p]
                stores.append(put(lam_refs[1 - slot], (p, z, rows, slice(None)), new))
                stores.append(put(u_refs[1 - slot], (p, z, rows, slice(None)), m * new))
            return stores

        each_tile(layers, windows, core)

        def strip(r):
            rows = pl.ds(r, 8)
            e = [se_refs[t - 1][p, rows, :] for p in every]
            u = [old_strip[p, rows, :] for p in every]
            m = ms_ref[rows, :]
            change = changes(e, u, strip_neighbours(old_strip, old, u, r))
            for p in every:
                new = slam_refs[slot][p, rows, :] - change[p]
                slam_refs[1 - slot][p, rows, :] = new
                su_refs[1 - slot][p, rows, :] = m * new

        each_window(strip_windows, strip)
        spread(1 - slot, end_windows)

    spread(0, (4, 2))
    step(3, 0, (4, 2, 12), (4, 2), (4, 2))
    step(2, 1, (4, 2, 12), (4, 2), (4, 2))
    step(1, 0, (4, 2, 12), (8, 1), (8, 1))

    grains = [map_ref[z] for z in range(layers)]
    cells = []
    for z in range(layers):
        upper = work_ref[0, z, 0] + work_ref[1, z, 0] + work_ref[2, z, 0]
        lower = work_ref[0, z, 1] + work_ref[1, z, 1] + work_ref[2, z, 1]
        first = total_of([lam_out_ref[p, z, 8:16, :] * rate_refs[0][p, z, 8:16, :] for p in every])
        cells.append(jnp.concatenate([upper[4:8], lower[0:4]], axis=0) + first)

    def bin_one(g, carry):
        kept = [jnp.where(grains[z] == g, cells[z], 0.0) for z in range(layers)]
        total = sum(kept[1:4], kept[0]) + sum(kept[5:8], kept[4]) + sum(kept[9:], kept[8])
        binned_ref[pl.ds(g, 1), :] = jnp.sum(total, axis=0, keepdims=True)
        return carry

    lax.fori_loop(0, binned_ref.shape[0], bin_one, 0, unroll=4)
    ones = jnp.full((8, 128), -TIME_STEP, jnp.float32)
    sums = lax.dot_general(
        ones, binned_ref[...], (((1,), (1,)), ((), ())),
        precision=lax.Precision.HIGHEST, preferred_element_type=jnp.float32,
    )
    brick = lax.axis_index("wide") * lax.axis_size("narrow") + lax.axis_index("narrow")
    sub = lax.broadcasted_iota(jnp.int32, tile, 0)
    here = (sub == ((brick >> 1) & 7)) & ((lanes(tile) >= 64) == ((brick & 1) == 1))
    sums_ref[...] = jnp.zeros_like(sums_ref)
    sums_ref[pl.ds(pl.multiple_of(8 * (brick >> 4), 8), 8), :] = jnp.where(
        here, jnp.concatenate([sums, sums], axis=1), 0.0
    )


def backward_last(first_e_ref, lam_ref, u_ref, ends_ref, adjoint_ref):
    params, layers = adjoint_ref.shape[:2]
    every = range(params)

    def core(z, i, r):
        rows = pl.ds(r, 8)
        e = [first_e_ref[p, z, rows, :] for p in every]
        u = [u_ref[p, z, rows, :] for p in every]
        change = changes(e, u, neighbours(u_ref, ends_ref, u, z, r))
        return [put(adjoint_ref, (p, z), lam_ref[p, z, rows, :] - change[p]) for p in every]

    each_tile(layers, (8, 1, 8), core)


def pick_owned(owned, slots_ref, sums_ref, out_ref, total_ref):
    base = (lax.axis_index("wide") * lax.axis_size("narrow") + lax.axis_index("narrow")) * owned
    tile = (8, 128)
    sub = lax.broadcasted_iota(jnp.int32, tile, 0)
    blocks = total_ref.shape[0] // 8
    step = 25
    for first in range(0, blocks, step):
        some = range(first, min(first + step, blocks))

        def body(k, acc, some=some):
            shifted = jnp.broadcast_to(slots_ref[pl.ds(k, 1), :], tile) - (sub + base)
            value = jnp.broadcast_to(sums_ref[pl.ds(k, 1), :], tile)
            return tuple(a + jnp.where(shifted == 8 * j, value, 0.0) for a, j in zip(acc, some))

        zero = tuple(jnp.zeros(tile, jnp.float32) for _ in some)
        acc = lax.fori_loop(0, slots_ref.shape[0], body, zero, unroll=8)
        for a, j in zip(acc, some):
            total_ref[8 * j : 8 * j + 8, :] = a
    whole = lax.dot_general(
        jnp.ones(tile, jnp.float32), total_ref[...], (((1,), (1,)), ((), ())),
        precision=lax.Precision.HIGHEST, preferred_element_type=jnp.float32,
    )
    out_ref[...] = whole[0:1, 0:owned]


def f32(*shape):
    return jax.ShapeDtypeStruct(shape, jnp.float32)


def kernel(body, out_shape, scratch=(), name=None, **specs):
    return pl.pallas_call(
        body, out_shape=out_shape, scratch_shapes=list(scratch), name=name, **specs,
        compiler_params=pltpu.CompilerParams(vmem_limit_bytes=VMEM_LIMIT),
    )


def swapped(value, axis, count, partner):
    step = [1 if (i + partner) % 2 == 0 else -1 for i in range(count)]
    return lax.ppermute(value, axis, [(i, (i + by) % count) for i, by in enumerate(step)])


def per_device(counts, order_init, cotangent, grain_map, brick_grains, grain_slot, mobility):
    wide_count, narrow_count = counts
    params, layers = order_init.shape[:2]
    assert order_init.shape[2:] == (8, 128) and layers * COLS < 128
    owned = mobility.shape[0]
    listed = brick_grains.shape[1]
    bricks = brick_grains.shape[0]

    both = ("wide", "narrow")
    count = wide_count * narrow_count
    small = counts == (4, 4)
    assert listed == 64 and bricks == count and count % 16 == 0

    owned_rows = -(-owned // 128)
    block_rows = narrow_count * owned_rows
    strip_rows = 8 * (params + 1)
    edge_rows = row_places(params, layers)[1]
    cot_rows = params * layers * ADJ_EDGE + 2 * LEAD
    vmem = lambda *shape: pltpu.VMEM(shape, jnp.float32)

    arguments = (
        order_init, grain_map, cotangent, mobility.reshape(1, owned), brick_grains, grain_slot.reshape(-1, 128)
    )
    *fetched, near_a, row_b, strip_a, strip_b, block = kernel(
        pack,
        tuple(jax.ShapeDtypeStruct(x.shape, x.dtype) for x in arguments)
        + (
            f32(edge_rows + cot_rows, 128), f32(edge_rows, 128),
            f32(strip_rows + block_rows, 128), f32(strip_rows, 128), f32(block_rows, 128),
        ),
        (pltpu.SemaphoreType.DMA((len(arguments),)),), name="pack",
        in_specs=[pl.BlockSpec(memory_space=pltpu.HBM)] * len(arguments),
    )(*(pltpu.with_memory_space_constraint(x, pltpu.HBM) for x in arguments))
    order_init, grain_map, cotangent, _, brick_grains, grain_slot = fetched
    strip_a = swapped(strip_a, "narrow", narrow_count, 0)
    near_a = swapped(near_a, "wide", wide_count, 0)
    row_b = swapped(row_b, "wide", wide_count, 1)
    slots = kernel(
        find_slots, jax.ShapeDtypeStruct((bricks // 2, 128), jnp.int32), name="find_slots"
    )(brick_grains, grain_slot)

    here, anywhere = pl.BlockSpec(memory_space=pltpu.VMEM), pl.BlockSpec(memory_space=pl.ANY)
    strip_b = kernel(
        pack_second, f32(strip_rows + block_rows, 128), name="pack_second",
        in_specs=[here, here, here, anywhere],
    )(strip_b, block, strip_a, slots)
    strip_b = swapped(strip_b, "narrow", narrow_count, 1)
    corners = corner_rows(params)
    sent, corner_b = kernel(
        functools.partial(pack_far, params),
        (f32(corners + block_rows, 128), f32(corners, 128)), name="pack_far",
    )(strip_a, strip_b, block)
    far_a = swapped(sent, "wide", wide_count, 0)
    sent = kernel(pack_far_second, f32(corners + 2 * block_rows, 128), name="pack_far_second")(corner_b, sent, far_a)
    far_b = swapped(sent, "wide", wide_count, 1)
    cot_b = kernel(pack_cot, f32(cot_rows, 128), name="pack_cot", in_specs=[here, anywhere])(cotangent, sent)
    cot_b = swapped(cot_b, "wide", wide_count, 1)

    if small:
        mobs = (sent, far_b)
    else:
        own = jnp.pad(mobility, (0, -owned % 128)).reshape(owned_rows, 128)
        mobs = (lax.all_gather(own, both, axis=0, tiled=True),)
    table = kernel(
        functools.partial(find_mobility, counts, owned), f32(8, 128),
        (pltpu.VMEM((8, 128), jnp.int32), vmem(wide_count * block_rows, 128)),
        name="find_mobility",
    )(slots, *mobs)

    padded, strip = (params, layers, ROWS, 128), (params, ROWS, 128)
    final, states, rate, halos, m, ms = kernel(
        forward,
        (
            f32(*order_init.shape), [f32(*padded)] * ITERS, [f32(*padded)] * ITERS,
            [f32(*strip)] * (ITERS - 1), f32(layers, ROWS, 128), f32(ROWS, 128),
        ),
        (vmem(*strip), vmem(*strip), vmem(*padded), vmem(layers, ROWS, 128), vmem(ROWS, 128)),
        name="forward",
    )(order_init, grain_map, near_a, row_b, far_a, far_b, strip_a, strip_b, table)
    lam, u, ends, sums = kernel(
        backward,
        (f32(*padded), f32(*padded), f32(*padded), f32(bricks // 2, 128)),
        (
            vmem(*padded), [vmem(*strip)] * 2, vmem(*padded), [vmem(*strip)] * 2,
            vmem(ITERS - 1, layers, 2, 8, 128), vmem(listed, 128),
        ),
        name="backward",
    )(
        cotangent, grain_map, near_a, cot_b, far_a, far_b, strip_a, strip_b,
        states, rate, halos, m, ms,
    )
    adjoint = kernel(backward_last, f32(*order_init.shape), name="backward_last")(states[0], lam, u, ends)

    if small:
        for axis in both:
            for partner in range(2):
                sums = sums + swapped(sums, axis, 4, partner)
    else:
        sums = lax.psum(sums, both)
    grads = kernel(
        functools.partial(pick_owned, owned), f32(1, owned),
        (vmem(owned + -owned % 8, 128),), name="pick_owned",
    )(slots, sums)
    return final, adjoint, grads.reshape(owned)


def solution(mesh):
    counts = (mesh.shape["wide"], mesh.shape["narrow"])
    field = P("groups", None, "wide", "narrow")
    spread = P(("groups", "wide", "narrow"))
    return jax.shard_map(
        functools.partial(per_device, counts),
        mesh=mesh,
        in_specs=(field, field, P("groups", "wide", "narrow"), P("groups", None), P("groups"), spread),
        out_specs=(field, field, spread),
        check_vma=False,
    )
```

```python
import functools

import jax
import jax.numpy as jnp
from jax import lax
from jax.experimental import pallas as pl
from jax.experimental.pallas import tpu as pltpu
from jax.sharding import PartitionSpec as P

ITERS = 4
TIME_STEP = 0.05

EDGE = 6
MAP_EDGE = 5
ADJ_EDGE = 4
ROWS = 24
COLS = 10
LEAD = 8
CORNER = (5, 3, 4)

VMEM_LIMIT = 24 * 1024 * 1024


def lanes(shape):
    return lax.broadcasted_iota(jnp.int32, shape, len(shape) - 1)


def roll(value, shift):
    return pltpu.roll(value, shift, 1)


def is_odd(axis):
    return lax.rem(lax.axis_index(axis), 2) == 1


def pack_strips(*refs):
    count = (len(refs) - 4) // 2
    sources, targets = refs[:count], refs[count : 2 * count]
    strip_a_ref, strip_b_ref, block_ref, sems = refs[2 * count :]
    copies = [pltpu.make_async_copy(a, b, sems.at[i]) for i, (a, b) in enumerate(zip(sources, targets))]
    for copy in copies:
        copy.start()
    order_ref, map_ref, cot_ref, mob_ref = targets[:4]
    params, layers = order_ref.shape[:2]
    odd = is_odd("narrow")
    for copy in copies:
        copy.wait()

    lane = lanes((8, 128))
    zero = jnp.zeros((8, 128), jnp.float32)

    def span(first, size):
        return ((lane - first) & 127) < size

    for field in range(params + 1):
        right, left = zero, zero
        for z in range(layers):
            value = order_ref[field, z] if field < params else map_ref[z].astype(jnp.float32)
            moved = roll(value, 10 * z + 5)
            right = jnp.where(span(10 * z - 1, 6), moved, right)
            left = jnp.where(span(10 * z + 5, 6), moved, left)
            if field < params:
                right = jnp.where(span(10 * z + 5, 4), roll(cot_ref[field, z], 10 * z + 9), right)
                left = jnp.where(span(10 * z + 1, 4), roll(cot_ref[field, z], 10 * z + 1), left)
        rows = slice(8 * field, 8 * field + 8)
        strip_a_ref[rows, :] = jnp.where(odd, left, right)
        strip_b_ref[rows, :] = jnp.where(odd, right, left)
    owned = mob_ref.shape[1]
    owned_rows = -(-owned // 128)
    block_ref[...] = jnp.zeros_like(block_ref)
    first = lax.axis_index("narrow") * owned_rows
    for i in range(owned_rows):
        size = min(128, owned - 128 * i)
        row = mob_ref[0:1, 128 * i : 128 * i + size]
        if size < 128:
            row = jnp.concatenate([row, jnp.zeros((1, 128 - size), jnp.float32)], axis=1)
        block_ref[pl.ds(first + i, 1), :] = row
    for ref in (strip_a_ref, strip_b_ref):
        ref[8 * (params + 1) :, :] = block_ref[...]


def pack_rows(order_ref, map_ref, cot_ref, after_ref, near_a_ref, row_b_ref):
    params, layers = order_ref.shape[:2]
    maps, cots = row_places(params, layers)
    gap = jnp.zeros((LEAD, 128), jnp.float32)
    odd = is_odd("wide")
    last = (jnp.where(odd, 0, 1), jnp.where(odd, 1, 0))
    row_refs = (near_a_ref, row_b_ref)
    for ref in row_refs:
        ref[0:LEAD, :] = gap
        ref[maps - LEAD : maps, :] = gap
        ref[cots - 2 * LEAD : cots - LEAD, :] = gap
        ref[cots - LEAD : cots, :] = gap
    near_a_ref[cots : cots + LEAD, :] = gap
    near_a_ref[near_a_ref.shape[0] - LEAD :, :] = gap
    for p in range(params):
        for z in range(layers):
            k = LEAD + (p * layers + z) * EDGE
            for ref, is_last in zip(row_refs, last):
                ref[k : k + EDGE, :] = order_ref[p, z, pl.ds((8 - EDGE) * is_last, EDGE), :]
    for z in range(layers):
        k = maps + z * MAP_EDGE
        for ref, is_last in zip(row_refs, last):
            ref[k : k + MAP_EDGE, :] = map_ref[z, pl.ds((8 - MAP_EDGE) * is_last, MAP_EDGE), :].astype(jnp.float32)
    rows = pl.ds((8 - ADJ_EDGE) * last[0], ADJ_EDGE)
    for p in range(params):
        for z in range(layers):
            k = cots + LEAD + (p * layers + z) * ADJ_EDGE
            near_a_ref[k : k + ADJ_EDGE, :] = cot_ref[p, z, rows, :]


def pack_cot(cot_ref, after_ref, out_ref):
    params, layers = cot_ref.shape[:2]
    out_ref[0:LEAD, :] = jnp.zeros((LEAD, 128), jnp.float32)
    out_ref[out_ref.shape[0] - LEAD :, :] = jnp.zeros((LEAD, 128), jnp.float32)
    rows = pl.ds(jnp.where(is_odd("wide"), 8 - ADJ_EDGE, 0), ADJ_EDGE)
    for p in range(params):
        for z in range(layers):
            k = LEAD + (p * layers + z) * ADJ_EDGE
            out_ref[k : k + ADJ_EDGE, :] = cot_ref[p, z, rows, :]


def row_places(params, layers):
    maps = LEAD + params * layers * EDGE + LEAD
    length = maps + layers * MAP_EDGE
    return maps, length + -length % 8 + LEAD


def corner_rows(params):
    return -(-(params * (CORNER[0] + CORNER[1]) + CORNER[2]) // 8) * 8


def side_strips(params, strip_a_ref, strip_b_ref):
    odd = is_odd("narrow")
    fields = []
    for field in range(params + 1):
        rows = slice(8 * field, 8 * field + 8)
        a, b = strip_a_ref[rows, :], strip_b_ref[rows, :]
        fields.append((jnp.where(odd, a, b), jnp.where(odd, b, a)))
    return fields


def merged_strips(params, *strip_refs):
    first = lanes((8, 128)) % COLS < 5
    fields = side_strips(params, *strip_refs)
    order = [jnp.where(first, a, b) for a, b in fields[:params]]
    cot = [jnp.where(first, roll(a, 124), roll(b, 4)) for a, b in fields[:params]]
    return order, cot, jnp.where(first, *fields[params])


def pack_far(params, strip_a_ref, strip_b_ref, block_ref, *refs):
    *other_refs, far_a_ref, far_b_ref, out_block_ref = refs
    at = 8 * (params + 1)
    mobs = corner_rows(params)
    block = block_ref[...] + strip_a_ref[at:, :] + strip_b_ref[at:, :]
    for ref in other_refs:
        block = block + ref[...]
    out_block_ref[...] = block
    at = 0
    odd = is_odd("wide")
    order, cot, cells = merged_strips(params, strip_a_ref, strip_b_ref)
    for n, fields in zip(CORNER, (order, cot, [cells])):
        for both in fields:
            far_a_ref[at : at + n, :] = jnp.where(odd, both[0:n], both[8 - n : 8])
            far_b_ref[at : at + n, :] = jnp.where(odd, both[8 - n : 8], both[0:n])
            at += n
    for ref in (far_a_ref, far_b_ref):
        ref[at:mobs, :] = jnp.zeros((mobs - at, 128), jnp.float32)
        ref[mobs:, :] = block


def find_slots(bricks_ref, slot_ref, after_ref, out_ref):
    count, listed = bricks_ref.shape
    rows = slot_ref.shape[0]
    for k in range(0, out_ref.shape[0], 8):
        pairs = [
            jnp.concatenate([bricks_ref[2 * j : 2 * j + 1, :], bricks_ref[2 * j + 1 : 2 * j + 2, :]], axis=1)
            for j in range(k, k + 8)
        ]
        grain = jnp.concatenate(pairs, axis=0)
        row, col = grain >> 7, grain & 127

        def body(r, found, row=row, col=col):
            table = jnp.broadcast_to(slot_ref[pl.ds(r, 1), :], (8, 128))
            taken = jnp.take_along_axis(table, col, axis=1, mode="promise_in_bounds")
            return jnp.where(row == r, taken, found)

        out_ref[k : k + 8, :] = lax.fori_loop(0, rows, body, jnp.zeros((8, 128), jnp.int32), unroll=7)


def find_mobility(counts, owned, slots_ref, *refs):
    *mob_refs, table_ref, near_ref, all_ref = refs
    wide_count, narrow_count = counts
    tile = (8, 128)
    wide, narrow = lax.axis_index("wide"), lax.axis_index("narrow")
    if len(mob_refs) == 1:
        mob_ref = mob_refs[0]
    else:
        block_ref, far_a_ref, far_b_ref, other_ref = mob_refs
        mob_ref = all_ref
        size = block_ref.shape[0]
        odd = is_odd("wide")
        step = jnp.where(odd, 1, 3)
        for place, ref in (
            (wide, block_ref), (wide + 4 - step, far_a_ref), (wide + step, far_b_ref), (wide + 2, other_ref)
        ):
            at = pl.multiple_of(size * (place & 3), size)
            mob_ref[pl.ds(at, size), :] = ref[ref.shape[0] - size :, :]
    near_ref[...] = jnp.zeros_like(near_ref)
    for k in range(9):
        w = lax.rem(wide + k // 3 - 1 + wide_count, wide_count)
        n = lax.rem(narrow + k % 3 - 1 + narrow_count, narrow_count)
        brick = w * narrow_count + n
        row = slots_ref[pl.ds(brick >> 1, 1), :]
        half = jnp.where((brick & 1) == 0, row[:, 0:64], row[:, 64:128])
        near_ref[k // 2 : k // 2 + 1, 64 * (k % 2) : 64 * (k % 2) + 64] = half
    slot = near_ref[...]
    owned_rows = -(-owned // 128)
    owner = jnp.floor((slot.astype(jnp.float32) + 0.5) * (1.0 / owned)).astype(jnp.int32)
    inner = slot - owner * owned
    row = owner * owned_rows + (inner >> 7)
    place = inner & 127

    def body(r, found):
        values = jnp.broadcast_to(mob_ref[pl.ds(r, 1), :], tile)
        taken = jnp.take_along_axis(values, place, axis=1, mode="promise_in_bounds")
        return jnp.where(row == r, taken, found)

    found = lax.fori_loop(0, mob_ref.shape[0], body, jnp.zeros(tile, jnp.float32), unroll=16)
    table_ref[...] = TIME_STEP * found


def total_of(values):
    while len(values) > 1:
        values = [a + b for a, b in zip(values[::2], values[1::2])]
    return values[0]


def each_tile(layers, windows, body):
    start, count, most = windows
    group = 12 // (2 * count) * 2 if layers % 12 == 0 else 1

    def some(step, carry):
        stores = []
        for j in range(group):
            z = step * group + j
            for i in range(count):
                stores += body(z, i, jnp.minimum(start + 8 * i + ((z + 16) >> 5), most))
            if len(stores) >= 64 or j == group - 1:
                for store in stores:
                    store()
                stores = []
        return carry

    lax.fori_loop(0, layers // group, some, 0)


def each_window(windows, body):
    def one(i, carry):
        body(windows[0] + 8 * i)
        return carry

    lax.fori_loop(0, windows[1], one, 0)


def put(ref, index, value):
    def store():
        ref[index] = value

    return store


def neighbours(ref, ends_ref, values, z, r):
    params, layers = ref.shape[:2]
    lane = lanes((8, 128))
    rows, before, after = pl.ds(r, 8), pl.ds(r - 1, 8), pl.ds(r + 1, 8)
    below, above = jnp.maximum(z - 1, 0), jnp.minimum(z + 1, layers - 1)
    near = []
    for p in range(params):
        ends = ends_ref[p, z, rows, :]
        left = roll(jnp.where(lane == 127, ends, values[p]), 1)
        right = roll(jnp.where(lane == 0, ends, values[p]), 127)
        total = (left + right) + (ref[p, z, before, :] + ref[p, z, after, :])
        near.append(total + (ref[p, below, rows, :] + ref[p, above, rows, :]))
    return near


def strip_neighbours(ref, core_ref, values, r, outer_ref=None):
    params, layers = core_ref.shape[:2]
    lane = lanes((8, 128))
    col = lane % COLS
    rows, before, after = pl.ds(r, 8), pl.ds(r - 1, 8), pl.ds(r + 1, 8)
    near = []
    for p in range(params):
        value = values[p]
        ends = jnp.zeros((8, 128), jnp.float32)
        for z in range(layers):
            here = (lane == 10 * z + 4) | (lane == 10 * z + 5)
            ends = jnp.where(here, roll(core_ref[p, z, rows, :], 10 * z + 5), ends)
        left = roll(jnp.where(col == 4, ends, value), 1)
        right = roll(jnp.where(col == 5, ends, value), 127)
        if outer_ref is not None:
            outer = outer_ref[p, rows, :]
            left = jnp.where(col == 0, outer, left)
            right = jnp.where(col == 9, outer, right)
        below = jnp.where(lane < COLS, value, roll(value, COLS))
        above = jnp.where(lane >= COLS * (layers - 1), value, roll(value, 128 - COLS))
        total = (left + right) + (below + above)
        near.append(total + (ref[p, before, :] + ref[p, after, :]))
    return near


def spread_ends(ends_ref, values, rows):
    params, layers = ends_ref.shape[:2]
    for p in range(params):
        for z in range(layers):
            ends_ref[p, z, rows, :] = roll(values[p], 123 - 10 * z)


def rates(e, near):
    squares = [x * x for x in e]
    base = 1.5 * total_of(squares) + 5.0
    return [x * (base - 0.5 * y) - n for x, y, n in zip(e, squares, near)]


def changes(e, u, near):
    squares = [x * x for x in e]
    base = 1.5 * total_of(squares) + 5.0
    inner = 3.0 * total_of([x * y for x, y in zip(e, u)])
    return [y * (base - 1.5 * s) + x * inner - n for x, y, s, n in zip(e, u, squares, near)]


def forward(
    order_ref, map_ref, row_a_ref, row_b_ref, far_a_ref, far_b_ref, strip_a_ref, strip_b_ref, table_ref,
    final_ref, e_refs, rate_refs, se_refs, m_ref, ms_ref,
    first_strip_ref, outer_ref, ends_ref, g_ref, gs_ref,
):
    params, layers = order_ref.shape[:2]
    tile = (8, 128)
    col = lanes(tile) % COLS
    maps = row_places(params, layers)[0]
    strip_refs = [first_strip_ref, *se_refs]
    every = range(params)

    odd = is_odd("wide")
    from_before = (jnp.where(odd, 1, 0), jnp.where(odd, 0, 1))

    def place(z, carry):
        for ref, before in zip((row_a_ref, row_b_ref), from_before):
            k, target = maps + z * MAP_EDGE + before * (MAP_EDGE - 8), pl.ds(16 - 16 * before, 8)
            g_ref[z, target, :] = ref[pl.ds(k, 8), :]
            for p in every:
                k = LEAD + (p * layers + z) * EDGE + before * (EDGE - 8)
                e_refs[0][p, z, target, :] = ref[pl.ds(k, 8), :]
        for p in every:
            e_refs[0][p, z, 8:16, :] = order_ref[p, z]
        return carry

    lax.fori_loop(0, layers, place, 0)

    sides = side_strips(params, strip_a_ref, strip_b_ref)
    order, _, cells = merged_strips(params, strip_a_ref, strip_b_ref)
    n = CORNER[0]
    for p in every:
        ref = first_strip_ref.at[p]
        ref[0:8, :] = jnp.zeros(tile, jnp.float32)
        ref[16:24, :] = jnp.zeros(tile, jnp.float32)
        a, b = far_a_ref[n * p : n * p + n, :], far_b_ref[n * p : n * p + n, :]
        ref[8 - n : 8, :] = jnp.where(odd, a, b)
        ref[8:16, :] = order[p]
        ref[16 : 16 + n, :] = jnp.where(odd, b, a)
        outer_ref[p, 8:16, :] = jnp.where(col == 0, roll(sides[p][0], 1), roll(sides[p][1], 127))
    at, n = params * (CORNER[0] + CORNER[1]), CORNER[2]
    gs_ref[...] = jnp.zeros_like(gs_ref)
    a, b = far_a_ref[at : at + n, :], far_b_ref[at : at + n, :]
    gs_ref[8 - n : 8, :] = jnp.where(odd, a, b)
    gs_ref[8:16, :] = cells
    gs_ref[16 : 16 + n, :] = jnp.where(odd, b, a)
    for r in (0, 8, 16):
        rows = slice(r, r + 8)
        spread_ends(ends_ref, [first_strip_ref[p, rows, :] for p in every], rows)

    def lookup(index, which):
        values = jnp.broadcast_to(table_ref[which // 2 : which // 2 + 1, :], tile)
        return jnp.take_along_axis(values, index + 64 * (which % 2), axis=1, mode="promise_in_bounds")

    for i in range(3):
        r = 8 * i
        for z in range(layers):
            index = map_ref[z] if i == 1 else g_ref[z, r : r + 8, :].astype(jnp.int32) & 63
            m_ref[z, r : r + 8, :] = lookup(index, 3 * i + 1)
        index = gs_ref[r : r + 8, :].astype(jnp.int32) & 63
        ms_ref[r : r + 8, :] = jnp.where(col < 5, lookup(index, 3 * i), lookup(index, 3 * i + 2))

    def step(t, windows, strip_windows, end_windows):
        old, old_strip = e_refs[t], strip_refs[t]
        last = t == ITERS - 1

        def core(z, i, r):
            rows = pl.ds(r, 8)
            e = [old[p, z, rows, :] for p in every]
            m = m_ref[z, rows, :]
            rate = rates(e, neighbours(old, ends_ref, e, z, r))
            stores = []
            for p in every:
                new = e[p] - m * rate[p]
                stores.append(put(rate_refs[t], (p, z, rows, slice(None)), rate[p]))
                if last:
                    stores.append(put(final_ref, (p, z), new))
                else:
                    stores.append(put(e_refs[t + 1], (p, z, rows, slice(None)), new))
            return stores

        each_tile(layers, windows, core)
        if last:
            return

        def strip(r):
            rows = pl.ds(r, 8)
            e = [old_strip[p, rows, :] for p in every]
            m = ms_ref[rows, :]
            rate = rates(e, strip_neighbours(old_strip, old, e, r, outer_ref if t == 0 else None))
            for p in every:
                strip_refs[t + 1][p, rows, :] = e[p] - m * rate[p]

        each_window(strip_windows, strip)

        def ends(r):
            rows = pl.ds(r, 8)
            spread_ends(ends_ref, [strip_refs[t + 1][p, rows, :] for p in every], rows)

        each_window(end_windows, ends)

    step(0, (3, 3, 13), (4, 2), (4, 2))
    step(1, (4, 2, 12), (4, 2), (4, 2))
    step(2, (4, 2, 12), (4, 2), (8, 1))
    step(3, (8, 1, 8), None, None)


def backward(
    cot_ref, map_ref, row_a_ref, row_b_ref, far_a_ref, far_b_ref, strip_a_ref, strip_b_ref,
    e_refs, rate_refs, se_refs, m_ref, ms_ref,
    lam_out_ref, u_out_ref, ends_ref, sums_ref,
    first_lam_ref, slam_refs, first_u_ref, su_refs, work_ref, binned_ref,
):
    params, layers = cot_ref.shape[:2]
    lam_refs, u_refs = (first_lam_ref, lam_out_ref), (first_u_ref, u_out_ref)
    cots = row_places(params, layers)[1]
    tile = (8, 128)
    every = range(params)

    odd = is_odd("wide")
    from_before = (jnp.where(odd, 1, 0), jnp.where(odd, 0, 1))

    def place(z, carry):
        for ref, base, before in zip((row_a_ref, row_b_ref), (cots, 0), from_before):
            rows = pl.ds(16 - 16 * before, 8)
            m = m_ref[z, rows, :]
            for p in every:
                k = base + LEAD + (p * layers + z) * ADJ_EDGE + before * (ADJ_EDGE - 8)
                value = ref[pl.ds(k, 8), :]
                lam_refs[0][p, z, rows, :] = value
                u_refs[0][p, z, rows, :] = m * value
        m = m_ref[z, 8:16, :]
        for p in every:
            lam_refs[0][p, z, 8:16, :] = cot_ref[p, z]
            u_refs[0][p, z, 8:16, :] = m * cot_ref[p, z]
        return carry

    lax.fori_loop(0, layers, place, 0)
    _, cot, _ = merged_strips(params, strip_a_ref, strip_b_ref)
    n = CORNER[1]
    for p in every:
        at = params * CORNER[0] + n * p
        ref = slam_refs[0].at[p]
        ref[0:8, :] = jnp.zeros(tile, jnp.float32)
        ref[16:24, :] = jnp.zeros(tile, jnp.float32)
        a, b = far_a_ref[at : at + n, :], far_b_ref[at : at + n, :]
        ref[8 - n : 8, :] = jnp.where(odd, a, b)
        ref[8:16, :] = cot[p]
        ref[16 : 16 + n, :] = jnp.where(odd, b, a)
        for r in (0, 8, 16):
            su_refs[0][p, r : r + 8, :] = ms_ref[r : r + 8, :] * ref[r : r + 8, :]

    def spread(slot, windows):
        def ends(r):
            rows = pl.ds(r, 8)
            spread_ends(ends_ref, [su_refs[slot][p, rows, :] for p in every], rows)

        each_window(windows, ends)

    def step(t, slot, windows, strip_windows, end_windows):
        old, old_strip = u_refs[slot], su_refs[slot]

        def core(z, i, r):
            rows = pl.ds(r, 8)
            e = [e_refs[t][p, z, rows, :] for p in every]
            u = [old[p, z, rows, :] for p in every]
            m = m_ref[z, rows, :]
            change = changes(e, u, neighbours(old, ends_ref, u, z, r))
            lam = [lam_refs[slot][p, z, rows, :] for p in every]
            work = total_of([lam[p] * rate_refs[t][p, z, rows, :] for p in every])
            stores = [put(work_ref, (t - 1, z, i), work)]
            for p in every:
                new = lam[p] - change[p]
                stores.append(put(lam_refs[1 - slot], (p, z, rows, slice(None)), new))
                stores.append(put(u_refs[1 - slot], (p, z, rows, slice(None)), m * new))
            return stores

        each_tile(layers, windows, core)

        def strip(r):
            rows = pl.ds(r, 8)
            e = [se_refs[t - 1][p, rows, :] for p in every]
            u = [old_strip[p, rows, :] for p in every]
            m = ms_ref[rows, :]
            change = changes(e, u, strip_neighbours(old_strip, old, u, r))
            for p in every:
                new = slam_refs[slot][p, rows, :] - change[p]
                slam_refs[1 - slot][p, rows, :] = new
                su_refs[1 - slot][p, rows, :] = m * new

        each_window(strip_windows, strip)
        spread(1 - slot, end_windows)

    spread(0, (4, 2))
    step(3, 0, (4, 2, 12), (4, 2), (4, 2))
    step(2, 1, (4, 2, 12), (4, 2), (4, 2))
    step(1, 0, (4, 2, 12), (8, 1), (8, 1))

    grains = [map_ref[z] for z in range(layers)]
    cells = []
    for z in range(layers):
        upper = work_ref[0, z, 0] + work_ref[1, z, 0] + work_ref[2, z, 0]
        lower = work_ref[0, z, 1] + work_ref[1, z, 1] + work_ref[2, z, 1]
        first = total_of([lam_out_ref[p, z, 8:16, :] * rate_refs[0][p, z, 8:16, :] for p in every])
        cells.append(jnp.concatenate([upper[4:8], lower[0:4]], axis=0) + first)

    def bin_one(g, carry):
        kept = [jnp.where(grains[z] == g, cells[z], 0.0) for z in range(layers)]
        total = sum(kept[1:4], kept[0]) + sum(kept[5:8], kept[4]) + sum(kept[9:], kept[8])
        binned_ref[pl.ds(g, 1), :] = jnp.sum(total, axis=0, keepdims=True)
        return carry

    lax.fori_loop(0, binned_ref.shape[0], bin_one, 0, unroll=4)
    ones = jnp.full((8, 128), -TIME_STEP, jnp.float32)
    sums = lax.dot_general(
        ones, binned_ref[...], (((1,), (1,)), ((), ())),
        precision=lax.Precision.HIGHEST, preferred_element_type=jnp.float32,
    )
    for k in range(0, sums_ref.shape[0], 8):
        sums_ref[k : k + 8, :] = sums


def backward_last(first_e_ref, lam_ref, u_ref, ends_ref, adjoint_ref):
    params, layers = adjoint_ref.shape[:2]
    every = range(params)

    def core(z, i, r):
        rows = pl.ds(r, 8)
        e = [first_e_ref[p, z, rows, :] for p in every]
        u = [u_ref[p, z, rows, :] for p in every]
        change = changes(e, u, neighbours(u_ref, ends_ref, u, z, r))
        return [put(adjoint_ref, (p, z), lam_ref[p, z, rows, :] - change[p]) for p in every]

    each_tile(layers, (8, 1, 8), core)


def pick_owned(owned, slots_ref, sums_ref, out_ref, total_ref, dense_ref):
    base = (lax.axis_index("wide") * lax.axis_size("narrow") + lax.axis_index("narrow")) * owned
    tile = (8, 128)
    for k in range(dense_ref.shape[0]):
        dense_ref[k : k + 1, 0:64] = sums_ref[2 * k : 2 * k + 1, :]
        dense_ref[k : k + 1, 64:128] = sums_ref[2 * k + 1 : 2 * k + 2, :]
    sub = lax.broadcasted_iota(jnp.int32, tile, 0)
    blocks = total_ref.shape[0] // 8
    step = 25
    for first in range(0, blocks, step):
        some = range(first, min(first + step, blocks))

        def body(k, acc, some=some):
            shifted = jnp.broadcast_to(slots_ref[pl.ds(k, 1), :], tile) - (sub + base)
            value = jnp.broadcast_to(dense_ref[pl.ds(k, 1), :], tile)
            return tuple(a + jnp.where(shifted == 8 * j, value, 0.0) for a, j in zip(acc, some))

        zero = tuple(jnp.zeros(tile, jnp.float32) for _ in some)
        acc = lax.fori_loop(0, slots_ref.shape[0], body, zero, unroll=8)
        for a, j in zip(acc, some):
            total_ref[8 * j : 8 * j + 8, :] = a
    whole = lax.dot_general(
        jnp.ones(tile, jnp.float32), total_ref[...], (((1,), (1,)), ((), ())),
        precision=lax.Precision.HIGHEST, preferred_element_type=jnp.float32,
    )
    out_ref[...] = whole[0:1, 0:owned]


def f32(*shape):
    return jax.ShapeDtypeStruct(shape, jnp.float32)


def kernel(body, out_shape, scratch=(), name=None, cost=0, **specs):
    if cost:
        specs["cost_estimate"] = pl.CostEstimate(flops=cost, bytes_accessed=cost // 1000, transcendentals=0)
    return pl.pallas_call(
        body, out_shape=out_shape, scratch_shapes=list(scratch), name=name, **specs,
        compiler_params=pltpu.CompilerParams(vmem_limit_bytes=VMEM_LIMIT),
    )


def opposite(value, axis):
    return lax.ppermute(value, axis, [(i, (i + 2) % 4) for i in range(4)])


def swapped(value, axis, count, partner):
    step = [1 if (i + partner) % 2 == 0 else -1 for i in range(count)]
    return lax.ppermute(value, axis, [(i, (i + by) % count) for i, by in enumerate(step)])


def per_device(counts, order_init, cotangent, grain_map, brick_grains, grain_slot, mobility):
    wide_count, narrow_count = counts
    params, layers = order_init.shape[:2]
    assert order_init.shape[2:] == (8, 128) and layers * COLS < 128
    owned = mobility.shape[0]
    listed = brick_grains.shape[1]
    bricks = brick_grains.shape[0]

    both = ("wide", "narrow")
    count = wide_count * narrow_count
    small = counts == (4, 4)
    assert listed == 64 and bricks == count and count % 16 == 0

    owned_rows = -(-owned // 128)
    block_rows = narrow_count * owned_rows
    strip_rows = 8 * (params + 1)
    edge_rows = row_places(params, layers)[1]
    cot_rows = params * layers * ADJ_EDGE + 2 * LEAD
    vmem = lambda *shape: pltpu.VMEM(shape, jnp.float32)

    arguments = (
        order_init, grain_map, cotangent, mobility.reshape(1, owned), brick_grains, grain_slot.reshape(-1, 128)
    )
    here, anywhere = pl.BlockSpec(memory_space=pltpu.VMEM), pl.BlockSpec(memory_space=pl.ANY)
    *fetched, strip_a, strip_b, block = kernel(
        pack_strips,
        tuple(jax.ShapeDtypeStruct(x.shape, x.dtype) for x in arguments)
        + (f32(strip_rows + block_rows, 128),) * 2 + (f32(block_rows, 128),),
        (pltpu.SemaphoreType.DMA((len(arguments),)),), name="pack_strips",
        in_specs=[pl.BlockSpec(memory_space=pltpu.HBM)] * len(arguments),
    )(*(pltpu.with_memory_space_constraint(x, pltpu.HBM) for x in arguments))
    order_init, grain_map, cotangent, _, brick_grains, grain_slot = fetched
    near_a, row_b = kernel(
        pack_rows, (f32(edge_rows + cot_rows, 128), f32(edge_rows, 128)), name="pack_rows",
        in_specs=[here] * 3 + [anywhere],
    )(order_init, grain_map, cotangent, strip_b)
    strip_b = swapped(strip_b, "narrow", narrow_count, 1)
    strip_a = swapped(strip_a, "narrow", narrow_count, 0)
    others = [opposite(block, "narrow")] if small else []
    near_a = swapped(near_a, "wide", wide_count, 0)
    row_b = swapped(row_b, "wide", wide_count, 1)

    corners = corner_rows(params)
    far_a, far_b, block = kernel(
        functools.partial(pack_far, params),
        (f32(corners + block_rows, 128),) * 2 + (f32(block_rows, 128),), name="pack_far", cost=100_000_000_000,
    )(strip_a, strip_b, block, *others)
    far_b = swapped(far_b, "wide", wide_count, 1)
    far_a = swapped(far_a, "wide", wide_count, 0)
    slots = kernel(
        find_slots, jax.ShapeDtypeStruct((bricks // 2, 128), jnp.int32), name="find_slots",
        in_specs=[here, here, anywhere],
    )(brick_grains, grain_slot, block)
    cot_b = kernel(pack_cot, f32(cot_rows, 128), name="pack_cot", in_specs=[here, anywhere])(cotangent, far_a)
    cot_b = swapped(cot_b, "wide", wide_count, 1)

    if small:
        mobs = (block, far_a, far_b, opposite(block, "wide"))
    else:
        own = jnp.pad(mobility, (0, -owned % 128)).reshape(owned_rows, 128)
        mobs = (lax.all_gather(own, both, axis=0, tiled=True),)
    table = kernel(
        functools.partial(find_mobility, counts, owned), f32(8, 128),
        (pltpu.VMEM((8, 128), jnp.int32), vmem(wide_count * block_rows, 128)),
        name="find_mobility", cost=3_000_000_000,
    )(slots, *mobs)

    padded, strip = (params, layers, ROWS, 128), (params, ROWS, 128)
    final, states, rate, halos, m, ms = kernel(
        forward,
        (
            f32(*order_init.shape), [f32(*padded)] * ITERS, [f32(*padded)] * ITERS,
            [f32(*strip)] * (ITERS - 1), f32(layers, ROWS, 128), f32(ROWS, 128),
        ),
        (vmem(*strip), vmem(*strip), vmem(*padded), vmem(layers, ROWS, 128), vmem(ROWS, 128)),
        name="forward", cost=0,
    )(order_init, grain_map, near_a, row_b, far_a, far_b, strip_a, strip_b, table)
    lam, u, ends, sums = kernel(
        backward,
        (f32(*padded), f32(*padded), f32(*padded), f32(bricks, listed)),
        (
            vmem(*padded), [vmem(*strip)] * 2, vmem(*padded), [vmem(*strip)] * 2,
            vmem(ITERS - 1, layers, 2, 8, 128), vmem(listed, 128),
        ),
        name="backward",
    )(
        cotangent, grain_map, near_a, cot_b, far_a, far_b, strip_a, strip_b,
        states, rate, halos, m, ms,
    )
    adjoint = kernel(backward_last, f32(*order_init.shape), name="backward_last")(states[0], lam, u, ends)

    sums = lax.all_to_all(sums, both, 0, 0, tiled=True)
    grads = kernel(
        functools.partial(pick_owned, owned), f32(1, owned),
        (vmem(owned + -owned % 8, 128), vmem(bricks // 2, 128)), name="pick_owned",
    )(slots, sums)
    return final, adjoint, grads.reshape(owned)


def solution(mesh):
    counts = (mesh.shape["wide"], mesh.shape["narrow"])
    field = P("groups", None, "wide", "narrow")
    spread = P(("groups", "wide", "narrow"))
    return jax.shard_map(
        functools.partial(per_device, counts),
        mesh=mesh,
        in_specs=(field, field, P("groups", "wide", "narrow"), P("groups", None), P("groups"), spread),
        out_specs=(field, field, spread),
        check_vma=False,
    )
```

```python
import functools

import jax
import jax.numpy as jnp
from jax import lax
from jax.experimental import pallas as pl
from jax.experimental.pallas import tpu as pltpu
from jax.sharding import PartitionSpec as P

ITERS = 4
TIME_STEP = 0.05

EDGE = 6
MAP_EDGE = 5
ADJ_EDGE = 4
ROWS = 24
COLS = 10
LEAD = 8
CORNER = (5, 3, 4)

VMEM_LIMIT = 24 * 1024 * 1024


def lanes(shape):
    return lax.broadcasted_iota(jnp.int32, shape, len(shape) - 1)


def roll(value, shift):
    return pltpu.roll(value, shift, 1)


def is_odd(axis):
    return lax.rem(lax.axis_index(axis), 2) == 1


def pack_strips(*refs):
    count = (len(refs) - 4) // 2
    sources, targets = refs[:count], refs[count : 2 * count]
    strip_a_ref, strip_b_ref, block_ref, sems = refs[2 * count :]
    copies = [pltpu.make_async_copy(a, b, sems.at[i]) for i, (a, b) in enumerate(zip(sources, targets))]
    for copy in copies:
        copy.start()
    order_ref, map_ref, cot_ref, mob_ref = targets[:4]
    params, layers = order_ref.shape[:2]
    odd = is_odd("narrow")
    for copy in copies:
        copy.wait()

    lane = lanes((8, 128))
    zero = jnp.zeros((8, 128), jnp.float32)

    def span(first, size):
        return ((lane - first) & 127) < size

    for field in range(params + 1):
        right, left = zero, zero
        for z in range(layers):
            value = order_ref[field, z] if field < params else map_ref[z].astype(jnp.float32)
            moved = roll(value, 10 * z + 5)
            right = jnp.where(span(10 * z - 1, 6), moved, right)
            left = jnp.where(span(10 * z + 5, 6), moved, left)
            if field < params:
                right = jnp.where(span(10 * z + 5, 4), roll(cot_ref[field, z], 10 * z + 9), right)
                left = jnp.where(span(10 * z + 1, 4), roll(cot_ref[field, z], 10 * z + 1), left)
        rows = slice(8 * field, 8 * field + 8)
        strip_a_ref[rows, :] = jnp.where(odd, left, right)
        strip_b_ref[rows, :] = jnp.where(odd, right, left)
    owned = mob_ref.shape[1]
    owned_rows = -(-owned // 128)
    block_ref[...] = jnp.zeros_like(block_ref)
    first = lax.axis_index("narrow") * owned_rows
    for i in range(owned_rows):
        size = min(128, owned - 128 * i)
        row = mob_ref[0:1, 128 * i : 128 * i + size]
        if size < 128:
            row = jnp.concatenate([row, jnp.zeros((1, 128 - size), jnp.float32)], axis=1)
        block_ref[pl.ds(first + i, 1), :] = row
    strip_b_ref[8 * (params + 1) :, :] = block_ref[...]


def pack_rows(order_ref, map_ref, cot_ref, after_ref, near_a_ref, row_b_ref):
    params, layers = order_ref.shape[:2]
    maps, cots = row_places(params, layers)
    gap = jnp.zeros((LEAD, 128), jnp.float32)
    odd = is_odd("wide")
    last = (jnp.where(odd, 0, 1), jnp.where(odd, 1, 0))
    row_refs = (near_a_ref, row_b_ref)
    for ref in row_refs:
        ref[0:LEAD, :] = gap
        ref[maps - LEAD : maps, :] = gap
        ref[cots - 2 * LEAD : cots - LEAD, :] = gap
        ref[cots - LEAD : cots, :] = gap
    near_a_ref[cots : cots + LEAD, :] = gap
    near_a_ref[near_a_ref.shape[0] - LEAD :, :] = gap
    for p in range(params):
        for z in range(layers):
            k = LEAD + (p * layers + z) * EDGE
            for ref, is_last in zip(row_refs, last):
                ref[k : k + EDGE, :] = order_ref[p, z, pl.ds((8 - EDGE) * is_last, EDGE), :]
    for z in range(layers):
        k = maps + z * MAP_EDGE
        for ref, is_last in zip(row_refs, last):
            ref[k : k + MAP_EDGE, :] = map_ref[z, pl.ds((8 - MAP_EDGE) * is_last, MAP_EDGE), :].astype(jnp.float32)
    rows = pl.ds((8 - ADJ_EDGE) * last[0], ADJ_EDGE)
    for p in range(params):
        for z in range(layers):
            k = cots + LEAD + (p * layers + z) * ADJ_EDGE
            near_a_ref[k : k + ADJ_EDGE, :] = cot_ref[p, z, rows, :]


def pack_second(strip_ref, block_ref, strip_b_ref, out_ref):
    at = strip_ref.shape[0]
    out_ref[0:at, :] = strip_ref[...]
    out_ref[at:, :] = block_ref[...] + strip_b_ref[at:, :]


def pack_cot(cot_ref, after_ref, out_ref):
    params, layers = cot_ref.shape[:2]
    out_ref[0:LEAD, :] = jnp.zeros((LEAD, 128), jnp.float32)
    out_ref[out_ref.shape[0] - LEAD :, :] = jnp.zeros((LEAD, 128), jnp.float32)
    rows = pl.ds(jnp.where(is_odd("wide"), 8 - ADJ_EDGE, 0), ADJ_EDGE)
    for p in range(params):
        for z in range(layers):
            k = LEAD + (p * layers + z) * ADJ_EDGE
            out_ref[k : k + ADJ_EDGE, :] = cot_ref[p, z, rows, :]


def row_places(params, layers):
    maps = LEAD + params * layers * EDGE + LEAD
    length = maps + layers * MAP_EDGE
    return maps, length + -length % 8 + LEAD


def corner_rows(params):
    return -(-(params * (CORNER[0] + CORNER[1]) + CORNER[2]) // 8) * 8


def side_strips(params, strip_a_ref, strip_b_ref):
    odd = is_odd("narrow")
    fields = []
    for field in range(params + 1):
        rows = slice(8 * field, 8 * field + 8)
        a, b = strip_a_ref[rows, :], strip_b_ref[rows, :]
        fields.append((jnp.where(odd, a, b), jnp.where(odd, b, a)))
    return fields


def merged_strips(params, *strip_refs):
    first = lanes((8, 128)) % COLS < 5
    fields = side_strips(params, *strip_refs)
    order = [jnp.where(first, a, b) for a, b in fields[:params]]
    cot = [jnp.where(first, roll(a, 124), roll(b, 4)) for a, b in fields[:params]]
    return order, cot, jnp.where(first, *fields[params])


def pack_far(params, strip_a_ref, strip_b_ref, block_ref, *refs):
    far_a_ref, far_b_ref, out_block_ref = refs
    at = 8 * (params + 1)
    mobs = corner_rows(params)
    block = block_ref[...] + strip_a_ref[at:, :] + strip_b_ref[at:, :]
    out_block_ref[...] = block
    at = 0
    odd = is_odd("wide")
    order, cot, cells = merged_strips(params, strip_a_ref, strip_b_ref)
    for n, fields in zip(CORNER, (order, cot, [cells])):
        for both in fields:
            far_a_ref[at : at + n, :] = jnp.where(odd, both[0:n], both[8 - n : 8])
            far_b_ref[at : at + n, :] = jnp.where(odd, both[8 - n : 8], both[0:n])
            at += n
    for ref in (far_a_ref, far_b_ref):
        ref[at:mobs, :] = jnp.zeros((mobs - at, 128), jnp.float32)
        ref[mobs:, :] = block


def find_slots(bricks_ref, slot_ref, after_ref, out_ref):
    count, listed = bricks_ref.shape
    rows = slot_ref.shape[0]
    for k in range(0, out_ref.shape[0], 8):
        pairs = [
            jnp.concatenate([bricks_ref[2 * j : 2 * j + 1, :], bricks_ref[2 * j + 1 : 2 * j + 2, :]], axis=1)
            for j in range(k, k + 8)
        ]
        grain = jnp.concatenate(pairs, axis=0)
        row, col = grain >> 7, grain & 127

        def body(r, found, row=row, col=col):
            table = jnp.broadcast_to(slot_ref[pl.ds(r, 1), :], (8, 128))
            taken = jnp.take_along_axis(table, col, axis=1, mode="promise_in_bounds")
            return jnp.where(row == r, taken, found)

        out_ref[k : k + 8, :] = lax.fori_loop(0, rows, body, jnp.zeros((8, 128), jnp.int32), unroll=7)


def find_mobility(counts, owned, slots_ref, *refs):
    *mob_refs, table_ref, near_ref, all_ref = refs
    wide_count, narrow_count = counts
    tile = (8, 128)
    wide, narrow = lax.axis_index("wide"), lax.axis_index("narrow")
    if len(mob_refs) == 1:
        mob_ref = mob_refs[0]
    else:
        block_ref, far_a_ref, far_b_ref, other_ref = mob_refs
        mob_ref = all_ref
        size = block_ref.shape[0]
        odd = is_odd("wide")
        step = jnp.where(odd, 1, 3)
        for place, ref in (
            (wide, block_ref), (wide + 4 - step, far_a_ref), (wide + step, far_b_ref), (wide + 2, other_ref)
        ):
            at = pl.multiple_of(size * (place & 3), size)
            mob_ref[pl.ds(at, size), :] = ref[ref.shape[0] - size :, :]
    near_ref[...] = jnp.zeros_like(near_ref)
    for k in range(9):
        w = lax.rem(wide + k // 3 - 1 + wide_count, wide_count)
        n = lax.rem(narrow + k % 3 - 1 + narrow_count, narrow_count)
        brick = w * narrow_count + n
        row = slots_ref[pl.ds(brick >> 1, 1), :]
        half = jnp.where((brick & 1) == 0, row[:, 0:64], row[:, 64:128])
        near_ref[k // 2 : k // 2 + 1, 64 * (k % 2) : 64 * (k % 2) + 64] = half
    slot = near_ref[...]
    owned_rows = -(-owned // 128)
    owner = jnp.floor((slot.astype(jnp.float32) + 0.5) * (1.0 / owned)).astype(jnp.int32)
    inner = slot - owner * owned
    row = owner * owned_rows + (inner >> 7)
    place = inner & 127

    def body(r, found):
        values = jnp.broadcast_to(mob_ref[pl.ds(r, 1), :], tile)
        taken = jnp.take_along_axis(values, place, axis=1, mode="promise_in_bounds")
        return jnp.where(row == r, taken, found)

    found = lax.fori_loop(0, mob_ref.shape[0], body, jnp.zeros(tile, jnp.float32), unroll=16)
    table_ref[...] = TIME_STEP * found


def total_of(values):
    while len(values) > 1:
        values = [a + b for a, b in zip(values[::2], values[1::2])]
    return values[0]


def each_tile(layers, windows, body):
    start, count, most = windows
    group = 12 // (2 * count) * 2 if layers % 12 == 0 else 1

    def some(step, carry):
        stores = []
        for j in range(group):
            z = step * group + j
            for i in range(count):
                stores += body(z, i, jnp.minimum(start + 8 * i + ((z + 16) >> 5), most))
            if len(stores) >= 64 or j == group - 1:
                for store in stores:
                    store()
                stores = []
        return carry

    lax.fori_loop(0, layers // group, some, 0)


def each_window(windows, body):
    def one(i, carry):
        body(windows[0] + 8 * i)
        return carry

    lax.fori_loop(0, windows[1], one, 0)


def put(ref, index, value):
    def store():
        ref[index] = value

    return store


def neighbours(ref, ends_ref, values, z, r):
    params, layers = ref.shape[:2]
    lane = lanes((8, 128))
    rows, before, after = pl.ds(r, 8), pl.ds(r - 1, 8), pl.ds(r + 1, 8)
    below, above = jnp.maximum(z - 1, 0), jnp.minimum(z + 1, layers - 1)
    near = []
    for p in range(params):
        ends = ends_ref[p, z, rows, :]
        left = roll(jnp.where(lane == 127, ends, values[p]), 1)
        right = roll(jnp.where(lane == 0, ends, values[p]), 127)
        total = (left + right) + (ref[p, z, before, :] + ref[p, z, after, :])
        near.append(total + (ref[p, below, rows, :] + ref[p, above, rows, :]))
    return near


def strip_neighbours(ref, core_ref, values, r, outer_ref=None):
    params, layers = core_ref.shape[:2]
    lane = lanes((8, 128))
    col = lane % COLS
    rows, before, after = pl.ds(r, 8), pl.ds(r - 1, 8), pl.ds(r + 1, 8)
    near = []
    for p in range(params):
        value = values[p]
        ends = jnp.zeros((8, 128), jnp.float32)
        for z in range(layers):
            here = (lane == 10 * z + 4) | (lane == 10 * z + 5)
            ends = jnp.where(here, roll(core_ref[p, z, rows, :], 10 * z + 5), ends)
        left = roll(jnp.where(col == 4, ends, value), 1)
        right = roll(jnp.where(col == 5, ends, value), 127)
        if outer_ref is not None:
            outer = outer_ref[p, rows, :]
            left = jnp.where(col == 0, outer, left)
            right = jnp.where(col == 9, outer, right)
        below = jnp.where(lane < COLS, value, roll(value, COLS))
        above = jnp.where(lane >= COLS * (layers - 1), value, roll(value, 128 - COLS))
        total = (left + right) + (below + above)
        near.append(total + (ref[p, before, :] + ref[p, after, :]))
    return near


def spread_ends(ends_ref, values, rows):
    params, layers = ends_ref.shape[:2]
    for p in range(params):
        for z in range(layers):
            ends_ref[p, z, rows, :] = roll(values[p], 123 - 10 * z)


def rates(e, near):
    squares = [x * x for x in e]
    base = 1.5 * total_of(squares) + 5.0
    return [x * (base - 0.5 * y) - n for x, y, n in zip(e, squares, near)]


def changes(e, u, near):
    squares = [x * x for x in e]
    base = 1.5 * total_of(squares) + 5.0
    inner = 3.0 * total_of([x * y for x, y in zip(e, u)])
    return [y * (base - 1.5 * s) + x * inner - n for x, y, s, n in zip(e, u, squares, near)]


def forward(
    order_ref, map_ref, row_a_ref, row_b_ref, far_a_ref, far_b_ref, strip_a_ref, strip_b_ref, table_ref,
    final_ref, e_refs, rate_refs, se_refs, m_ref, ms_ref,
    first_strip_ref, outer_ref, ends_ref, g_ref, gs_ref,
):
    params, layers = order_ref.shape[:2]
    tile = (8, 128)
    col = lanes(tile) % COLS
    maps = row_places(params, layers)[0]
    strip_refs = [first_strip_ref, *se_refs]
    every = range(params)

    odd = is_odd("wide")
    from_before = (jnp.where(odd, 1, 0), jnp.where(odd, 0, 1))

    def place(z, carry):
        for ref, before in zip((row_a_ref, row_b_ref), from_before):
            k, target = maps + z * MAP_EDGE + before * (MAP_EDGE - 8), pl.ds(16 - 16 * before, 8)
            g_ref[z, target, :] = ref[pl.ds(k, 8), :]
            for p in every:
                k = LEAD + (p * layers + z) * EDGE + before * (EDGE - 8)
                e_refs[0][p, z, target, :] = ref[pl.ds(k, 8), :]
        for p in every:
            e_refs[0][p, z, 8:16, :] = order_ref[p, z]
        return carry

    lax.fori_loop(0, layers, place, 0)

    sides = side_strips(params, strip_a_ref, strip_b_ref)
    order, _, cells = merged_strips(params, strip_a_ref, strip_b_ref)
    n = CORNER[0]
    for p in every:
        ref = first_strip_ref.at[p]
        ref[0:8, :] = jnp.zeros(tile, jnp.float32)
        ref[16:24, :] = jnp.zeros(tile, jnp.float32)
        a, b = far_a_ref[n * p : n * p + n, :], far_b_ref[n * p : n * p + n, :]
        ref[8 - n : 8, :] = jnp.where(odd, a, b)
        ref[8:16, :] = order[p]
        ref[16 : 16 + n, :] = jnp.where(odd, b, a)
        outer_ref[p, 8:16, :] = jnp.where(col == 0, roll(sides[p][0], 1), roll(sides[p][1], 127))
    at, n = params * (CORNER[0] + CORNER[1]), CORNER[2]
    gs_ref[...] = jnp.zeros_like(gs_ref)
    a, b = far_a_ref[at : at + n, :], far_b_ref[at : at + n, :]
    gs_ref[8 - n : 8, :] = jnp.where(odd, a, b)
    gs_ref[8:16, :] = cells
    gs_ref[16 : 16 + n, :] = jnp.where(odd, b, a)
    for r in (0, 8, 16):
        rows = slice(r, r + 8)
        spread_ends(ends_ref, [first_strip_ref[p, rows, :] for p in every], rows)

    def lookup(index, which):
        values = jnp.broadcast_to(table_ref[which // 2 : which // 2 + 1, :], tile)
        return jnp.take_along_axis(values, index + 64 * (which % 2), axis=1, mode="promise_in_bounds")

    for i in range(3):
        r = 8 * i
        for z in range(layers):
            index = map_ref[z] if i == 1 else g_ref[z, r : r + 8, :].astype(jnp.int32) & 63
            m_ref[z, r : r + 8, :] = lookup(index, 3 * i + 1)
        index = gs_ref[r : r + 8, :].astype(jnp.int32) & 63
        ms_ref[r : r + 8, :] = jnp.where(col < 5, lookup(index, 3 * i), lookup(index, 3 * i + 2))

    def step(t, windows, strip_windows, end_windows):
        old, old_strip = e_refs[t], strip_refs[t]
        last = t == ITERS - 1

        def core(z, i, r):
            rows = pl.ds(r, 8)
            e = [old[p, z, rows, :] for p in every]
            m = m_ref[z, rows, :]
            rate = rates(e, neighbours(old, ends_ref, e, z, r))
            stores = []
            for p in every:
                new = e[p] - m * rate[p]
                stores.append(put(rate_refs[t], (p, z, rows, slice(None)), rate[p]))
                if last:
                    stores.append(put(final_ref, (p, z), new))
                else:
                    stores.append(put(e_refs[t + 1], (p, z, rows, slice(None)), new))
            return stores

        each_tile(layers, windows, core)
        if last:
            return

        def strip(r):
            rows = pl.ds(r, 8)
            e = [old_strip[p, rows, :] for p in every]
            m = ms_ref[rows, :]
            rate = rates(e, strip_neighbours(old_strip, old, e, r, outer_ref if t == 0 else None))
            for p in every:
                strip_refs[t + 1][p, rows, :] = e[p] - m * rate[p]

        each_window(strip_windows, strip)

        def ends(r):
            rows = pl.ds(r, 8)
            spread_ends(ends_ref, [strip_refs[t + 1][p, rows, :] for p in every], rows)

        each_window(end_windows, ends)

    step(0, (3, 3, 13), (4, 2), (4, 2))
    step(1, (4, 2, 12), (4, 2), (4, 2))
    step(2, (4, 2, 12), (4, 2), (8, 1))
    step(3, (8, 1, 8), None, None)


def backward(
    cot_ref, map_ref, row_a_ref, row_b_ref, far_a_ref, far_b_ref, strip_a_ref, strip_b_ref,
    e_refs, rate_refs, se_refs, m_ref, ms_ref,
    adjoint_ref, sums_ref,
    lam_refs, slam_refs, u_refs, su_refs, ends_ref, work_ref, binned_ref,
):
    params, layers = cot_ref.shape[:2]
    cots = row_places(params, layers)[1]
    tile = (8, 128)
    every = range(params)

    odd = is_odd("wide")
    from_before = (jnp.where(odd, 1, 0), jnp.where(odd, 0, 1))

    def place(z, carry):
        for ref, base, before in zip((row_a_ref, row_b_ref), (cots, 0), from_before):
            rows = pl.ds(16 - 16 * before, 8)
            m = m_ref[z, rows, :]
            for p in every:
                k = base + LEAD + (p * layers + z) * ADJ_EDGE + before * (ADJ_EDGE - 8)
                value = ref[pl.ds(k, 8), :]
                lam_refs[0][p, z, rows, :] = value
                u_refs[0][p, z, rows, :] = m * value
        m = m_ref[z, 8:16, :]
        for p in every:
            lam_refs[0][p, z, 8:16, :] = cot_ref[p, z]
            u_refs[0][p, z, 8:16, :] = m * cot_ref[p, z]
        return carry

    lax.fori_loop(0, layers, place, 0)
    _, cot, _ = merged_strips(params, strip_a_ref, strip_b_ref)
    n = CORNER[1]
    for p in every:
        at = params * CORNER[0] + n * p
        ref = slam_refs[0].at[p]
        ref[0:8, :] = jnp.zeros(tile, jnp.float32)
        ref[16:24, :] = jnp.zeros(tile, jnp.float32)
        a, b = far_a_ref[at : at + n, :], far_b_ref[at : at + n, :]
        ref[8 - n : 8, :] = jnp.where(odd, a, b)
        ref[8:16, :] = cot[p]
        ref[16 : 16 + n, :] = jnp.where(odd, b, a)
        for r in (0, 8, 16):
            su_refs[0][p, r : r + 8, :] = ms_ref[r : r + 8, :] * ref[r : r + 8, :]

    def spread(slot, windows):
        def ends(r):
            rows = pl.ds(r, 8)
            spread_ends(ends_ref, [su_refs[slot][p, rows, :] for p in every], rows)

        each_window(windows, ends)

    def step(t, slot, windows, strip_windows, end_windows):
        old, old_strip = u_refs[slot], su_refs[slot]

        def core(z, i, r):
            rows = pl.ds(r, 8)
            e = [e_refs[t][p, z, rows, :] for p in every]
            u = [old[p, z, rows, :] for p in every]
            m = m_ref[z, rows, :]
            change = changes(e, u, neighbours(old, ends_ref, u, z, r))
            lam = [lam_refs[slot][p, z, rows, :] for p in every]
            work = total_of([lam[p] * rate_refs[t][p, z, rows, :] for p in every])
            stores = [put(work_ref, (t - 1, z, i), work)]
            for p in every:
                new = lam[p] - change[p]
                stores.append(put(lam_refs[1 - slot], (p, z, rows, slice(None)), new))
                stores.append(put(u_refs[1 - slot], (p, z, rows, slice(None)), m * new))
            return stores

        each_tile(layers, windows, core)

        def strip(r):
            rows = pl.ds(r, 8)
            e = [se_refs[t - 1][p, rows, :] for p in every]
            u = [old_strip[p, rows, :] for p in every]
            m = ms_ref[rows, :]
            change = changes(e, u, strip_neighbours(old_strip, old, u, r))
            for p in every:
                new = slam_refs[slot][p, rows, :] - change[p]
                slam_refs[1 - slot][p, rows, :] = new
                su_refs[1 - slot][p, rows, :] = m * new

        each_window(strip_windows, strip)
        spread(1 - slot, end_windows)

    spread(0, (4, 2))
    step(3, 0, (4, 2, 12), (4, 2), (4, 2))
    step(2, 1, (4, 2, 12), (4, 2), (4, 2))
    step(1, 0, (4, 2, 12), (8, 1), (8, 1))

    def last(z, i, r):
        rows = pl.ds(r, 8)
        e = [e_refs[0][p, z, rows, :] for p in every]
        u = [u_refs[1][p, z, rows, :] for p in every]
        change = changes(e, u, neighbours(u_refs[1], ends_ref, u, z, r))
        return [put(adjoint_ref, (p, z), lam_refs[1][p, z, rows, :] - change[p]) for p in every]

    each_tile(layers, (8, 1, 8), last)

    grains = [map_ref[z] for z in range(layers)]
    cells = []
    for z in range(layers):
        upper = work_ref[0, z, 0] + work_ref[1, z, 0] + work_ref[2, z, 0]
        lower = work_ref[0, z, 1] + work_ref[1, z, 1] + work_ref[2, z, 1]
        first = total_of([lam_refs[1][p, z, 8:16, :] * rate_refs[0][p, z, 8:16, :] for p in every])
        cells.append(jnp.concatenate([upper[4:8], lower[0:4]], axis=0) + first)

    def bin_one(g, carry):
        kept = [jnp.where(grains[z] == g, cells[z], 0.0) for z in range(layers)]
        total = sum(kept[1:4], kept[0]) + sum(kept[5:8], kept[4]) + sum(kept[9:], kept[8])
        binned_ref[pl.ds(g, 1), :] = jnp.sum(total, axis=0, keepdims=True)
        return carry

    lax.fori_loop(0, binned_ref.shape[0], bin_one, 0, unroll=4)
    ones = jnp.full((8, 128), -TIME_STEP, jnp.float32)
    sums = lax.dot_general(
        ones, binned_ref[...], (((1,), (1,)), ((), ())),
        precision=lax.Precision.HIGHEST, preferred_element_type=jnp.float32,
    )
    for k in range(0, sums_ref.shape[0], 8):
        sums_ref[k : k + 8, :] = sums


def pick_owned(owned, slots_ref, sums_ref, out_ref, total_ref, dense_ref):
    base = (lax.axis_index("wide") * lax.axis_size("narrow") + lax.axis_index("narrow")) * owned
    tile = (8, 128)
    for k in range(dense_ref.shape[0]):
        dense_ref[k : k + 1, 0:64] = sums_ref[2 * k : 2 * k + 1, :]
        dense_ref[k : k + 1, 64:128] = sums_ref[2 * k + 1 : 2 * k + 2, :]
    sub = lax.broadcasted_iota(jnp.int32, tile, 0)
    blocks = total_ref.shape[0] // 8
    step = 25
    for first in range(0, blocks, step):
        some = range(first, min(first + step, blocks))

        def body(k, acc, some=some):
            shifted = jnp.broadcast_to(slots_ref[pl.ds(k, 1), :], tile) - (sub + base)
            value = jnp.broadcast_to(dense_ref[pl.ds(k, 1), :], tile)
            return tuple(a + jnp.where(shifted == 8 * j, value, 0.0) for a, j in zip(acc, some))

        zero = tuple(jnp.zeros(tile, jnp.float32) for _ in some)
        acc = lax.fori_loop(0, slots_ref.shape[0], body, zero, unroll=8)
        for a, j in zip(acc, some):
            total_ref[8 * j : 8 * j + 8, :] = a
    whole = lax.dot_general(
        jnp.ones(tile, jnp.float32), total_ref[...], (((1,), (1,)), ((), ())),
        precision=lax.Precision.HIGHEST, preferred_element_type=jnp.float32,
    )
    out_ref[...] = whole[0:1, 0:owned]


def f32(*shape):
    return jax.ShapeDtypeStruct(shape, jnp.float32)


def kernel(body, out_shape, scratch=(), name=None, cost=0, **specs):
    if cost:
        specs["cost_estimate"] = pl.CostEstimate(flops=cost, bytes_accessed=cost // 1000, transcendentals=0)
    return pl.pallas_call(
        body, out_shape=out_shape, scratch_shapes=list(scratch), name=name, **specs,
        compiler_params=pltpu.CompilerParams(vmem_limit_bytes=VMEM_LIMIT),
    )


def opposite(value, axis):
    return lax.ppermute(value, axis, [(i, (i + 2) % 4) for i in range(4)])


def swapped(value, axis, count, partner):
    step = [1 if (i + partner) % 2 == 0 else -1 for i in range(count)]
    return lax.ppermute(value, axis, [(i, (i + by) % count) for i, by in enumerate(step)])


def per_device(counts, order_init, cotangent, grain_map, brick_grains, grain_slot, mobility):
    wide_count, narrow_count = counts
    params, layers = order_init.shape[:2]
    assert order_init.shape[2:] == (8, 128) and layers * COLS < 128
    owned = mobility.shape[0]
    listed = brick_grains.shape[1]
    bricks = brick_grains.shape[0]

    both = ("wide", "narrow")
    count = wide_count * narrow_count
    small = counts == (4, 4)
    assert listed == 64 and bricks == count and count % 16 == 0

    owned_rows = -(-owned // 128)
    block_rows = narrow_count * owned_rows
    strip_rows = 8 * (params + 1)
    edge_rows = row_places(params, layers)[1]
    cot_rows = params * layers * ADJ_EDGE + 2 * LEAD
    vmem = lambda *shape: pltpu.VMEM(shape, jnp.float32)

    arguments = (
        order_init, grain_map, cotangent, mobility.reshape(1, owned), brick_grains, grain_slot.reshape(-1, 128)
    )
    here, anywhere = pl.BlockSpec(memory_space=pltpu.VMEM), pl.BlockSpec(memory_space=pl.ANY)
    *fetched, strip_a, strip_b, block = kernel(
        pack_strips,
        tuple(jax.ShapeDtypeStruct(x.shape, x.dtype) for x in arguments)
        + (f32(strip_rows, 128), f32(strip_rows + block_rows, 128), f32(block_rows, 128)),
        (pltpu.SemaphoreType.DMA((len(arguments),)),), name="pack_strips",
        in_specs=[pl.BlockSpec(memory_space=pltpu.HBM)] * len(arguments),
    )(*(pltpu.with_memory_space_constraint(x, pltpu.HBM) for x in arguments))
    order_init, grain_map, cotangent, _, brick_grains, grain_slot = fetched
    near_a, row_b = kernel(
        pack_rows, (f32(edge_rows + cot_rows, 128), f32(edge_rows, 128)), name="pack_rows",
        in_specs=[here] * 3 + [anywhere],
    )(order_init, grain_map, cotangent, strip_b)
    strip_b = swapped(strip_b, "narrow", narrow_count, 1)
    near_a = swapped(near_a, "wide", wide_count, 0)
    row_b = swapped(row_b, "wide", wide_count, 1)
    strip_a = kernel(pack_second, f32(strip_rows + block_rows, 128), name="pack_second", cost=100_000_000_000)(
        strip_a, block, strip_b
    )
    strip_a = swapped(strip_a, "narrow", narrow_count, 0)

    corners = corner_rows(params)
    far_a, far_b, block = kernel(
        functools.partial(pack_far, params),
        (f32(corners + block_rows, 128),) * 2 + (f32(block_rows, 128),), name="pack_far", cost=0,
    )(strip_a, strip_b, block)
    far_b = swapped(far_b, "wide", wide_count, 1)
    far_a = swapped(far_a, "wide", wide_count, 0)
    slots = kernel(
        find_slots, jax.ShapeDtypeStruct((bricks // 2, 128), jnp.int32), name="find_slots",
        in_specs=[here, here, anywhere],
    )(brick_grains, grain_slot, block)
    cot_b = kernel(pack_cot, f32(cot_rows, 128), name="pack_cot", in_specs=[here, anywhere])(cotangent, far_a)
    cot_b = swapped(cot_b, "wide", wide_count, 1)

    if small:
        mobs = (block, far_a, far_b, opposite(block, "wide"))
    else:
        own = jnp.pad(mobility, (0, -owned % 128)).reshape(owned_rows, 128)
        mobs = (lax.all_gather(own, both, axis=0, tiled=True),)
    table = kernel(
        functools.partial(find_mobility, counts, owned), f32(8, 128),
        (pltpu.VMEM((8, 128), jnp.int32), vmem(wide_count * block_rows, 128)),
        name="find_mobility", cost=2_500_000_000,
    )(slots, *mobs)

    padded, strip = (params, layers, ROWS, 128), (params, ROWS, 128)
    final, states, rate, halos, m, ms = kernel(
        forward,
        (
            f32(*order_init.shape), [f32(*padded)] * ITERS, [f32(*padded)] * ITERS,
            [f32(*strip)] * (ITERS - 1), f32(layers, ROWS, 128), f32(ROWS, 128),
        ),
        (vmem(*strip), vmem(*strip), vmem(*padded), vmem(layers, ROWS, 128), vmem(ROWS, 128)),
        name="forward", cost=0,
    )(order_init, grain_map, near_a, row_b, far_a, far_b, strip_a, strip_b, table)
    adjoint, sums = kernel(
        backward,
        (f32(*order_init.shape), f32(bricks, listed)),
        (
            [vmem(*padded)] * 2, [vmem(*strip)] * 2, [vmem(*padded)] * 2, [vmem(*strip)] * 2, vmem(*padded),
            vmem(ITERS - 1, layers, 2, 8, 128), vmem(listed, 128),
        ),
        name="backward",
    )(
        cotangent, grain_map, near_a, cot_b, far_a, far_b, strip_a, strip_b,
        states, rate, halos, m, ms,
    )

    sums = lax.all_to_all(sums, both, 0, 0, tiled=True)
    grads = kernel(
        functools.partial(pick_owned, owned), f32(1, owned),
        (vmem(owned + -owned % 8, 128), vmem(bricks // 2, 128)), name="pick_owned",
    )(slots, sums)
    return final, adjoint, grads.reshape(owned)


def solution(mesh):
    counts = (mesh.shape["wide"], mesh.shape["narrow"])
    field = P("groups", None, "wide", "narrow")
    spread = P(("groups", "wide", "narrow"))
    return jax.shard_map(
        functools.partial(per_device, counts),
        mesh=mesh,
        in_specs=(field, field, P("groups", "wide", "narrow"), P("groups", None), P("groups"), spread),
        out_specs=(field, field, spread),
        check_vma=False,
    )
```

```python
import functools

import jax
import jax.numpy as jnp
from jax import lax
from jax.experimental import pallas as pl
from jax.experimental.pallas import tpu as pltpu
from jax.sharding import PartitionSpec as P

ITERS = 4
TIME_STEP = 0.05

EDGE = 6
MAP_EDGE = 5
ADJ_EDGE = 4
ROWS = 24
COLS = 10
LEAD = 8
CORNER = (5, 3, 4)

VMEM_LIMIT = 24 * 1024 * 1024


def lanes(shape):
    return lax.broadcasted_iota(jnp.int32, shape, len(shape) - 1)


def roll(value, shift):
    return pltpu.roll(value, shift, 1)


def is_odd(axis):
    return lax.rem(lax.axis_index(axis), 2) == 1


def pack_strips(order_ref, map_ref, cot_ref, mob_ref, after_ref, strip_a_ref, strip_b_ref, block_ref):
    params, layers = order_ref.shape[:2]
    odd = is_odd("narrow")
    lane = lanes((8, 128))
    zero = jnp.zeros((8, 128), jnp.float32)

    def span(first, size):
        return ((lane - first) & 127) < size

    for field in range(params + 1):
        right, left = zero, zero
        for z in range(layers):
            value = order_ref[field, z] if field < params else map_ref[z].astype(jnp.float32)
            moved = roll(value, 10 * z + 5)
            right = jnp.where(span(10 * z - 1, 6), moved, right)
            left = jnp.where(span(10 * z + 5, 6), moved, left)
            if field < params:
                right = jnp.where(span(10 * z + 5, 4), roll(cot_ref[field, z], 10 * z + 9), right)
                left = jnp.where(span(10 * z + 1, 4), roll(cot_ref[field, z], 10 * z + 1), left)
        rows = slice(8 * field, 8 * field + 8)
        strip_a_ref[rows, :] = jnp.where(odd, left, right)
        strip_b_ref[rows, :] = jnp.where(odd, right, left)
    owned = mob_ref.shape[1]
    owned_rows = -(-owned // 128)
    block_ref[...] = jnp.zeros_like(block_ref)
    first = lax.axis_index("narrow") * owned_rows
    for i in range(owned_rows):
        size = min(128, owned - 128 * i)
        row = mob_ref[0:1, 128 * i : 128 * i + size]
        if size < 128:
            row = jnp.concatenate([row, jnp.zeros((1, 128 - size), jnp.float32)], axis=1)
        block_ref[pl.ds(first + i, 1), :] = row
    for ref in (strip_a_ref, strip_b_ref):
        ref[8 * (params + 1) :, :] = block_ref[...]


def pack_rows(*refs):
    count = (len(refs) - 3) // 2
    sources, targets = refs[:count], refs[count : 2 * count]
    near_a_ref, row_b_ref, sems = refs[2 * count :]
    copies = [pltpu.make_async_copy(a, b, sems.at[i]) for i, (a, b) in enumerate(zip(sources, targets))]
    for copy in copies:
        copy.start()
    order_ref, map_ref, cot_ref = targets[:3]
    params, layers = order_ref.shape[:2]
    maps, cots = row_places(params, layers)
    gap = jnp.zeros((LEAD, 128), jnp.float32)
    odd = is_odd("wide")
    last = (jnp.where(odd, 0, 1), jnp.where(odd, 1, 0))
    row_refs = (near_a_ref, row_b_ref)
    for ref in row_refs:
        ref[0:LEAD, :] = gap
        ref[maps - LEAD : maps, :] = gap
        ref[cots - 2 * LEAD : cots - LEAD, :] = gap
        ref[cots - LEAD : cots, :] = gap
    near_a_ref[cots : cots + LEAD, :] = gap
    near_a_ref[near_a_ref.shape[0] - LEAD :, :] = gap
    copies[0].wait()
    for p in range(params):
        for z in range(layers):
            k = LEAD + (p * layers + z) * EDGE
            for ref, is_last in zip(row_refs, last):
                ref[k : k + EDGE, :] = order_ref[p, z, pl.ds((8 - EDGE) * is_last, EDGE), :]
    for copy in copies[1:]:
        copy.wait()
    for z in range(layers):
        k = maps + z * MAP_EDGE
        for ref, is_last in zip(row_refs, last):
            ref[k : k + MAP_EDGE, :] = map_ref[z, pl.ds((8 - MAP_EDGE) * is_last, MAP_EDGE), :].astype(jnp.float32)
    rows = pl.ds((8 - ADJ_EDGE) * last[0], ADJ_EDGE)
    for p in range(params):
        for z in range(layers):
            k = cots + LEAD + (p * layers + z) * ADJ_EDGE
            near_a_ref[k : k + ADJ_EDGE, :] = cot_ref[p, z, rows, :]


def pack_cot(cot_ref, after_ref, out_ref):
    params, layers = cot_ref.shape[:2]
    out_ref[0:LEAD, :] = jnp.zeros((LEAD, 128), jnp.float32)
    out_ref[out_ref.shape[0] - LEAD :, :] = jnp.zeros((LEAD, 128), jnp.float32)
    rows = pl.ds(jnp.where(is_odd("wide"), 8 - ADJ_EDGE, 0), ADJ_EDGE)
    for p in range(params):
        for z in range(layers):
            k = LEAD + (p * layers + z) * ADJ_EDGE
            out_ref[k : k + ADJ_EDGE, :] = cot_ref[p, z, rows, :]


def row_places(params, layers):
    maps = LEAD + params * layers * EDGE + LEAD
    length = maps + layers * MAP_EDGE
    return maps, length + -length % 8 + LEAD


def corner_rows(params):
    return -(-(params * (CORNER[0] + CORNER[1]) + CORNER[2]) // 8) * 8


def side_strips(params, strip_a_ref, strip_b_ref):
    odd = is_odd("narrow")
    fields = []
    for field in range(params + 1):
        rows = slice(8 * field, 8 * field + 8)
        a, b = strip_a_ref[rows, :], strip_b_ref[rows, :]
        fields.append((jnp.where(odd, a, b), jnp.where(odd, b, a)))
    return fields


def merged_strips(params, *strip_refs):
    first = lanes((8, 128)) % COLS < 5
    fields = side_strips(params, *strip_refs)
    order = [jnp.where(first, a, b) for a, b in fields[:params]]
    cot = [jnp.where(first, roll(a, 124), roll(b, 4)) for a, b in fields[:params]]
    return order, cot, jnp.where(first, *fields[params])


def pack_far(params, strip_a_ref, strip_b_ref, block_ref, *refs):
    *other_refs, far_a_ref, far_b_ref, out_block_ref = refs
    at = 8 * (params + 1)
    mobs = corner_rows(params)
    block = block_ref[...] + strip_a_ref[at:, :] + strip_b_ref[at:, :]
    for ref in other_refs:
        block = block + ref[...]
    out_block_ref[...] = block
    at = 0
    odd = is_odd("wide")
    order, cot, cells = merged_strips(params, strip_a_ref, strip_b_ref)
    for n, fields in zip(CORNER, (order, cot, [cells])):
        for both in fields:
            far_a_ref[at : at + n, :] = jnp.where(odd, both[0:n], both[8 - n : 8])
            far_b_ref[at : at + n, :] = jnp.where(odd, both[8 - n : 8], both[0:n])
            at += n
    for ref in (far_a_ref, far_b_ref):
        ref[at:mobs, :] = jnp.zeros((mobs - at, 128), jnp.float32)
        ref[mobs:, :] = block


def find_slots(bricks_ref, slot_ref, after_ref, out_ref):
    count, listed = bricks_ref.shape
    rows = slot_ref.shape[0]
    for k in range(0, out_ref.shape[0], 8):
        pairs = [
            jnp.concatenate([bricks_ref[2 * j : 2 * j + 1, :], bricks_ref[2 * j + 1 : 2 * j + 2, :]], axis=1)
            for j in range(k, k + 8)
        ]
        grain = jnp.concatenate(pairs, axis=0)
        row, col = grain >> 7, grain & 127

        def body(r, found, row=row, col=col):
            table = jnp.broadcast_to(slot_ref[pl.ds(r, 1), :], (8, 128))
            taken = jnp.take_along_axis(table, col, axis=1, mode="promise_in_bounds")
            return jnp.where(row == r, taken, found)

        out_ref[k : k + 8, :] = lax.fori_loop(0, rows, body, jnp.zeros((8, 128), jnp.int32), unroll=7)


def find_mobility(counts, owned, slots_ref, *refs):
    *mob_refs, table_ref, near_ref, all_ref = refs
    wide_count, narrow_count = counts
    tile = (8, 128)
    wide, narrow = lax.axis_index("wide"), lax.axis_index("narrow")
    if len(mob_refs) == 1:
        mob_ref = mob_refs[0]
    else:
        block_ref, far_a_ref, far_b_ref, other_ref = mob_refs
        mob_ref = all_ref
        size = block_ref.shape[0]
        odd = is_odd("wide")
        step = jnp.where(odd, 1, 3)
        for place, ref in (
            (wide, block_ref), (wide + 4 - step, far_a_ref), (wide + step, far_b_ref), (wide + 2, other_ref)
        ):
            at = pl.multiple_of(size * (place & 3), size)
            mob_ref[pl.ds(at, size), :] = ref[ref.shape[0] - size :, :]
    near_ref[...] = jnp.zeros_like(near_ref)
    for k in range(9):
        w = lax.rem(wide + k // 3 - 1 + wide_count, wide_count)
        n = lax.rem(narrow + k % 3 - 1 + narrow_count, narrow_count)
        brick = w * narrow_count + n
        row = slots_ref[pl.ds(brick >> 1, 1), :]
        half = jnp.where((brick & 1) == 0, row[:, 0:64], row[:, 64:128])
        near_ref[k // 2 : k // 2 + 1, 64 * (k % 2) : 64 * (k % 2) + 64] = half
    slot = near_ref[...]
    owned_rows = -(-owned // 128)
    owner = jnp.floor((slot.astype(jnp.float32) + 0.5) * (1.0 / owned)).astype(jnp.int32)
    inner = slot - owner * owned
    row = owner * owned_rows + (inner >> 7)
    place = inner & 127

    def body(r, found):
        values = jnp.broadcast_to(mob_ref[pl.ds(r, 1), :], tile)
        taken = jnp.take_along_axis(values, place, axis=1, mode="promise_in_bounds")
        return jnp.where(row == r, taken, found)

    found = lax.fori_loop(0, mob_ref.shape[0], body, jnp.zeros(tile, jnp.float32), unroll=16)
    table_ref[...] = TIME_STEP * found


def total_of(values):
    while len(values) > 1:
        values = [a + b for a, b in zip(values[::2], values[1::2])]
    return values[0]


def each_tile(layers, windows, body):
    start, count, most = windows
    group = 12 // (2 * count) * 2 if layers % 12 == 0 else 1

    def some(step, carry):
        stores = []
        for j in range(group):
            z = step * group + j
            for i in range(count):
                stores += body(z, i, jnp.minimum(start + 8 * i + ((z + 16) >> 5), most))
            if len(stores) >= 64 or j == group - 1:
                for store in stores:
                    store()
                stores = []
        return carry

    lax.fori_loop(0, layers // group, some, 0)


def each_window(windows, body):
    def one(i, carry):
        body(windows[0] + 8 * i)
        return carry

    lax.fori_loop(0, windows[1], one, 0)


def put(ref, index, value):
    def store():
        ref[index] = value

    return store


def neighbours(ref, ends_ref, value, p, z, r):
    layers = ref.shape[1]
    lane = lanes((8, 128))
    rows, before, after = pl.ds(r, 8), pl.ds(r - 1, 8), pl.ds(r + 1, 8)
    below, above = jnp.maximum(z - 1, 0), jnp.minimum(z + 1, layers - 1)
    ends = ends_ref[p, z, rows, :]
    left = roll(jnp.where(lane == 127, ends, value), 1)
    right = roll(jnp.where(lane == 0, ends, value), 127)
    total = (left + right) + (ref[p, z, before, :] + ref[p, z, after, :])
    return total + (ref[p, below, rows, :] + ref[p, above, rows, :])


def strip_neighbours(ref, core_ref, values, r, outer_ref=None):
    params, layers = core_ref.shape[:2]
    lane = lanes((8, 128))
    col = lane % COLS
    rows, before, after = pl.ds(r, 8), pl.ds(r - 1, 8), pl.ds(r + 1, 8)
    near = []
    for p in range(params):
        value = values[p]
        ends = jnp.zeros((8, 128), jnp.float32)
        for z in range(layers):
            here = (lane == 10 * z + 4) | (lane == 10 * z + 5)
            ends = jnp.where(here, roll(core_ref[p, z, rows, :], 10 * z + 5), ends)
        left = roll(jnp.where(col == 4, ends, value), 1)
        right = roll(jnp.where(col == 5, ends, value), 127)
        if outer_ref is not None:
            outer = outer_ref[p, rows, :]
            left = jnp.where(col == 0, outer, left)
            right = jnp.where(col == 9, outer, right)
        below = jnp.where(lane < COLS, value, roll(value, COLS))
        above = jnp.where(lane >= COLS * (layers - 1), value, roll(value, 128 - COLS))
        total = (left + right) + (below + above)
        near.append(total + (ref[p, before, :] + ref[p, after, :]))
    return near


def spread_ends(ends_ref, values, rows):
    params, layers = ends_ref.shape[:2]
    for p in range(params):
        for z in range(layers):
            ends_ref[p, z, rows, :] = roll(values[p], 123 - 10 * z)


def base_of(e):
    return 1.5 * total_of([x * x for x in e]) + 5.0


def inner_of(e, u):
    return 3.0 * total_of([x * y for x, y in zip(e, u)])


def forward(
    order_ref, map_ref, row_a_ref, row_b_ref, far_a_ref, far_b_ref, strip_a_ref, strip_b_ref, table_ref,
    final_ref, e_refs, rate_refs, se_refs, m_ref, ms_ref,
    first_strip_ref, outer_ref, ends_ref, g_ref, gs_ref,
):
    params, layers = order_ref.shape[:2]
    tile = (8, 128)
    col = lanes(tile) % COLS
    maps = row_places(params, layers)[0]
    strip_refs = [first_strip_ref, *se_refs]
    every = range(params)

    odd = is_odd("wide")
    from_before = (jnp.where(odd, 1, 0), jnp.where(odd, 0, 1))

    def place(z, carry):
        for ref, before in zip((row_a_ref, row_b_ref), from_before):
            k, target = maps + z * MAP_EDGE + before * (MAP_EDGE - 8), pl.ds(16 - 16 * before, 8)
            g_ref[z, target, :] = ref[pl.ds(k, 8), :]
            for p in every:
                k = LEAD + (p * layers + z) * EDGE + before * (EDGE - 8)
                e_refs[0][p, z, target, :] = ref[pl.ds(k, 8), :]
        for p in every:
            e_refs[0][p, z, 8:16, :] = order_ref[p, z]
        return carry

    lax.fori_loop(0, layers, place, 0)

    sides = side_strips(params, strip_a_ref, strip_b_ref)
    order, _, cells = merged_strips(params, strip_a_ref, strip_b_ref)
    n = CORNER[0]
    for p in every:
        ref = first_strip_ref.at[p]
        ref[0:8, :] = jnp.zeros(tile, jnp.float32)
        ref[16:24, :] = jnp.zeros(tile, jnp.float32)
        a, b = far_a_ref[n * p : n * p + n, :], far_b_ref[n * p : n * p + n, :]
        ref[8 - n : 8, :] = jnp.where(odd, a, b)
        ref[8:16, :] = order[p]
        ref[16 : 16 + n, :] = jnp.where(odd, b, a)
        outer_ref[p, 8:16, :] = jnp.where(col == 0, roll(sides[p][0], 1), roll(sides[p][1], 127))
    at, n = params * (CORNER[0] + CORNER[1]), CORNER[2]
    gs_ref[...] = jnp.zeros_like(gs_ref)
    a, b = far_a_ref[at : at + n, :], far_b_ref[at : at + n, :]
    gs_ref[8 - n : 8, :] = jnp.where(odd, a, b)
    gs_ref[8:16, :] = cells
    gs_ref[16 : 16 + n, :] = jnp.where(odd, b, a)
    for r in (0, 8, 16):
        rows = slice(r, r + 8)
        spread_ends(ends_ref, [first_strip_ref[p, rows, :] for p in every], rows)

    def lookup(index, which):
        values = jnp.broadcast_to(table_ref[which // 2 : which // 2 + 1, :], tile)
        return jnp.take_along_axis(values, index + 64 * (which % 2), axis=1, mode="promise_in_bounds")

    for i in range(3):
        r = 8 * i
        for z in range(layers):
            index = map_ref[z] if i == 1 else g_ref[z, r : r + 8, :].astype(jnp.int32) & 63
            m_ref[z, r : r + 8, :] = lookup(index, 3 * i + 1)
        index = gs_ref[r : r + 8, :].astype(jnp.int32) & 63
        ms_ref[r : r + 8, :] = jnp.where(col < 5, lookup(index, 3 * i), lookup(index, 3 * i + 2))

    def step(t, windows, strip_windows, end_windows):
        old, old_strip = e_refs[t], strip_refs[t]
        last = t == ITERS - 1

        def core(z, i, r):
            rows = pl.ds(r, 8)
            base = base_of([old[p, z, rows, :] for p in every])
            m = m_ref[z, rows, :]
            stores = []
            for p in every:
                e = old[p, z, rows, :]
                rate = e * (base - 0.5 * (e * e)) - neighbours(old, ends_ref, e, p, z, r)
                new = e - m * rate
                stores.append(put(rate_refs[t], (p, z, rows, slice(None)), rate))
                if last:
                    stores.append(put(final_ref, (p, z), new))
                else:
                    stores.append(put(e_refs[t + 1], (p, z, rows, slice(None)), new))
            return stores

        each_tile(layers, windows, core)
        if last:
            return

        def strip(r):
            rows = pl.ds(r, 8)
            e = [old_strip[p, rows, :] for p in every]
            m = ms_ref[rows, :]
            base = base_of(e)
            near = strip_neighbours(old_strip, old, e, r, outer_ref if t == 0 else None)
            for p in every:
                rate = e[p] * (base - 0.5 * (e[p] * e[p])) - near[p]
                strip_refs[t + 1][p, rows, :] = e[p] - m * rate

        each_window(strip_windows, strip)

        def ends(r):
            rows = pl.ds(r, 8)
            spread_ends(ends_ref, [strip_refs[t + 1][p, rows, :] for p in every], rows)

        each_window(end_windows, ends)

    step(0, (3, 3, 13), (4, 2), (4, 2))
    step(1, (4, 2, 12), (4, 2), (4, 2))
    step(2, (4, 2, 12), (4, 2), (8, 1))
    step(3, (8, 1, 8), None, None)


def backward(
    cot_ref, map_ref, row_a_ref, row_b_ref, far_a_ref, far_b_ref, strip_a_ref, strip_b_ref,
    e_refs, rate_refs, se_refs, m_ref, ms_ref,
    adjoint_ref, sums_ref,
    lam_refs, slam_refs, u_refs, su_refs, ends_ref, work_ref, binned_ref,
):
    params, layers = cot_ref.shape[:2]
    cots = row_places(params, layers)[1]
    tile = (8, 128)
    every = range(params)

    odd = is_odd("wide")
    from_before = (jnp.where(odd, 1, 0), jnp.where(odd, 0, 1))

    def place(z, carry):
        for ref, base, before in zip((row_a_ref, row_b_ref), (cots, 0), from_before):
            rows = pl.ds(16 - 16 * before, 8)
            m = m_ref[z, rows, :]
            for p in every:
                k = base + LEAD + (p * layers + z) * ADJ_EDGE + before * (ADJ_EDGE - 8)
                value = ref[pl.ds(k, 8), :]
                lam_refs[0][p, z, rows, :] = value
                u_refs[0][p, z, rows, :] = m * value
        m = m_ref[z, 8:16, :]
        for p in every:
            lam_refs[0][p, z, 8:16, :] = cot_ref[p, z]
            u_refs[0][p, z, 8:16, :] = m * cot_ref[p, z]
        return carry

    lax.fori_loop(0, layers, place, 0)
    _, cot, _ = merged_strips(params, strip_a_ref, strip_b_ref)
    n = CORNER[1]
    for p in every:
        at = params * CORNER[0] + n * p
        ref = slam_refs[0].at[p]
        ref[0:8, :] = jnp.zeros(tile, jnp.float32)
        ref[16:24, :] = jnp.zeros(tile, jnp.float32)
        a, b = far_a_ref[at : at + n, :], far_b_ref[at : at + n, :]
        ref[8 - n : 8, :] = jnp.where(odd, a, b)
        ref[8:16, :] = cot[p]
        ref[16 : 16 + n, :] = jnp.where(odd, b, a)
        for r in (0, 8, 16):
            su_refs[0][p, r : r + 8, :] = ms_ref[r : r + 8, :] * ref[r : r + 8, :]

    def spread(slot, windows):
        def ends(r):
            rows = pl.ds(r, 8)
            spread_ends(ends_ref, [su_refs[slot][p, rows, :] for p in every], rows)

        each_window(windows, ends)

    def step(t, slot, windows, strip_windows, end_windows):
        old, old_strip = u_refs[slot], su_refs[slot]

        def core(z, i, r):
            rows = pl.ds(r, 8)
            e = [e_refs[t][p, z, rows, :] for p in every]
            u = [old[p, z, rows, :] for p in every]
            base, inner = base_of(e), inner_of(e, u)
            m = m_ref[z, rows, :]
            work = total_of([lam_refs[slot][p, z, rows, :] * rate_refs[t][p, z, rows, :] for p in every])
            stores = [put(work_ref, (t - 1, z, i), work)]
            for p in every:
                e, u = e_refs[t][p, z, rows, :], old[p, z, rows, :]
                change = u * (base - 1.5 * (e * e)) + e * inner - neighbours(old, ends_ref, u, p, z, r)
                new = lam_refs[slot][p, z, rows, :] - change
                stores.append(put(lam_refs[1 - slot], (p, z, rows, slice(None)), new))
                stores.append(put(u_refs[1 - slot], (p, z, rows, slice(None)), m * new))
            return stores

        each_tile(layers, windows, core)

        def strip(r):
            rows = pl.ds(r, 8)
            e = [se_refs[t - 1][p, rows, :] for p in every]
            u = [old_strip[p, rows, :] for p in every]
            m = ms_ref[rows, :]
            base, inner = base_of(e), inner_of(e, u)
            near = strip_neighbours(old_strip, old, u, r)
            for p in every:
                change = u[p] * (base - 1.5 * (e[p] * e[p])) + e[p] * inner - near[p]
                new = slam_refs[slot][p, rows, :] - change
                slam_refs[1 - slot][p, rows, :] = new
                su_refs[1 - slot][p, rows, :] = m * new

        each_window(strip_windows, strip)
        spread(1 - slot, end_windows)

    spread(0, (4, 2))
    step(3, 0, (4, 2, 12), (4, 2), (4, 2))
    step(2, 1, (4, 2, 12), (4, 2), (4, 2))
    step(1, 0, (4, 2, 12), (8, 1), (8, 1))

    def last(z, i, r):
        rows = pl.ds(r, 8)
        e = [e_refs[0][p, z, rows, :] for p in every]
        u = [u_refs[1][p, z, rows, :] for p in every]
        base, inner = base_of(e), inner_of(e, u)
        stores = []
        for p in every:
            e, u = e_refs[0][p, z, rows, :], u_refs[1][p, z, rows, :]
            change = u * (base - 1.5 * (e * e)) + e * inner - neighbours(u_refs[1], ends_ref, u, p, z, r)
            stores.append(put(adjoint_ref, (p, z), lam_refs[1][p, z, rows, :] - change))
        return stores

    each_tile(layers, (8, 1, 8), last)

    grains = [map_ref[z] for z in range(layers)]
    cells = []
    for z in range(layers):
        upper = work_ref[0, z, 0] + work_ref[1, z, 0] + work_ref[2, z, 0]
        lower = work_ref[0, z, 1] + work_ref[1, z, 1] + work_ref[2, z, 1]
        first = total_of([lam_refs[1][p, z, 8:16, :] * rate_refs[0][p, z, 8:16, :] for p in every])
        cells.append(jnp.concatenate([upper[4:8], lower[0:4]], axis=0) + first)

    def bin_one(g, carry):
        kept = [jnp.where(grains[z] == g, cells[z], 0.0) for z in range(layers)]
        total = sum(kept[1:4], kept[0]) + sum(kept[5:8], kept[4]) + sum(kept[9:], kept[8])
        binned_ref[pl.ds(g, 1), :] = jnp.sum(total, axis=0, keepdims=True)
        return carry

    lax.fori_loop(0, binned_ref.shape[0], bin_one, 0, unroll=4)
    ones = jnp.full((8, 128), -TIME_STEP, jnp.float32)
    sums = lax.dot_general(
        ones, binned_ref[...], (((1,), (1,)), ((), ())),
        precision=lax.Precision.HIGHEST, preferred_element_type=jnp.float32,
    )
    for k in range(0, sums_ref.shape[0], 8):
        sums_ref[k : k + 8, :] = sums


def pick_owned(owned, slots_ref, sums_ref, out_ref, total_ref, dense_ref):
    base = (lax.axis_index("wide") * lax.axis_size("narrow") + lax.axis_index("narrow")) * owned
    tile = (8, 128)
    for k in range(dense_ref.shape[0]):
        dense_ref[k : k + 1, 0:64] = sums_ref[2 * k : 2 * k + 1, :]
        dense_ref[k : k + 1, 64:128] = sums_ref[2 * k + 1 : 2 * k + 2, :]
    sub = lax.broadcasted_iota(jnp.int32, tile, 0)
    blocks = total_ref.shape[0] // 8
    step = 25
    for first in range(0, blocks, step):
        some = range(first, min(first + step, blocks))

        def body(k, acc, some=some):
            shifted = jnp.broadcast_to(slots_ref[pl.ds(k, 1), :], tile) - (sub + base)
            value = jnp.broadcast_to(dense_ref[pl.ds(k, 1), :], tile)
            return tuple(a + jnp.where(shifted == 8 * j, value, 0.0) for a, j in zip(acc, some))

        zero = tuple(jnp.zeros(tile, jnp.float32) for _ in some)
        acc = lax.fori_loop(0, slots_ref.shape[0], body, zero, unroll=8)
        for a, j in zip(acc, some):
            total_ref[8 * j : 8 * j + 8, :] = a
    whole = lax.dot_general(
        jnp.ones(tile, jnp.float32), total_ref[...], (((1,), (1,)), ((), ())),
        precision=lax.Precision.HIGHEST, preferred_element_type=jnp.float32,
    )
    out_ref[...] = whole[0:1, 0:owned]


def f32(*shape):
    return jax.ShapeDtypeStruct(shape, jnp.float32)


def kernel(body, out_shape, scratch=(), name=None, cost=0, **specs):
    if cost:
        specs["cost_estimate"] = pl.CostEstimate(flops=cost, bytes_accessed=cost // 1000, transcendentals=0)
    return pl.pallas_call(
        body, out_shape=out_shape, scratch_shapes=list(scratch), name=name, **specs,
        compiler_params=pltpu.CompilerParams(vmem_limit_bytes=VMEM_LIMIT),
    )


def opposite(value, axis):
    return lax.ppermute(value, axis, [(i, (i + 2) % 4) for i in range(4)])


def swapped(value, axis, count, partner):
    step = [1 if (i + partner) % 2 == 0 else -1 for i in range(count)]
    return lax.ppermute(value, axis, [(i, (i + by) % count) for i, by in enumerate(step)])


def per_device(counts, order_init, cotangent, grain_map, brick_grains, grain_slot, mobility):
    wide_count, narrow_count = counts
    params, layers = order_init.shape[:2]
    assert order_init.shape[2:] == (8, 128) and layers * COLS < 128
    owned = mobility.shape[0]
    listed = brick_grains.shape[1]
    bricks = brick_grains.shape[0]

    both = ("wide", "narrow")
    count = wide_count * narrow_count
    small = counts == (4, 4)
    assert listed == 64 and bricks == count and count % 16 == 0

    owned_rows = -(-owned // 128)
    block_rows = narrow_count * owned_rows
    strip_rows = 8 * (params + 1)
    edge_rows = row_places(params, layers)[1]
    cot_rows = params * layers * ADJ_EDGE + 2 * LEAD
    vmem = lambda *shape: pltpu.VMEM(shape, jnp.float32)

    arguments = (
        order_init, grain_map, cotangent, mobility.reshape(1, owned), brick_grains, grain_slot.reshape(-1, 128)
    )
    here, anywhere = pl.BlockSpec(memory_space=pltpu.VMEM), pl.BlockSpec(memory_space=pl.ANY)
    *fetched, near_a, row_b = kernel(
        pack_rows,
        tuple(jax.ShapeDtypeStruct(x.shape, x.dtype) for x in arguments)
        + (f32(edge_rows + cot_rows, 128), f32(edge_rows, 128)),
        (pltpu.SemaphoreType.DMA((len(arguments),)),), name="pack_rows",
        in_specs=[pl.BlockSpec(memory_space=pltpu.HBM)] * len(arguments),
    )(*(pltpu.with_memory_space_constraint(x, pltpu.HBM) for x in arguments))
    order_init, grain_map, cotangent, mobility_row, brick_grains, grain_slot = fetched
    strip_a, strip_b, block = kernel(
        pack_strips, (f32(strip_rows + block_rows, 128),) * 2 + (f32(block_rows, 128),),
        name="pack_strips", in_specs=[here] * 4 + [anywhere],
    )(order_init, grain_map, cotangent, mobility_row, row_b)
    row_b = swapped(row_b, "wide", wide_count, 1)
    near_a = swapped(near_a, "wide", wide_count, 0)
    strip_b = swapped(strip_b, "narrow", narrow_count, 1)
    strip_a = swapped(strip_a, "narrow", narrow_count, 0)
    others = [opposite(block, "narrow")] if small else []

    corners = corner_rows(params)
    far_a, far_b, block = kernel(
        functools.partial(pack_far, params),
        (f32(corners + block_rows, 128),) * 2 + (f32(block_rows, 128),), name="pack_far", cost=0,
    )(strip_a, strip_b, block, *others)
    far_b = swapped(far_b, "wide", wide_count, 1)
    far_a = swapped(far_a, "wide", wide_count, 0)
    slots = kernel(
        find_slots, jax.ShapeDtypeStruct((bricks // 2, 128), jnp.int32), name="find_slots",
        in_specs=[here, here, anywhere],
    )(brick_grains, grain_slot, block)
    cot_b = kernel(pack_cot, f32(cot_rows, 128), name="pack_cot", in_specs=[here, anywhere])(cotangent, far_a)
    cot_b = swapped(cot_b, "wide", wide_count, 1)

    if small:
        mobs = (block, far_a, far_b, opposite(block, "wide"))
    else:
        own = jnp.pad(mobility, (0, -owned % 128)).reshape(owned_rows, 128)
        mobs = (lax.all_gather(own, both, axis=0, tiled=True),)
    table = kernel(
        functools.partial(find_mobility, counts, owned), f32(8, 128),
        (pltpu.VMEM((8, 128), jnp.int32), vmem(wide_count * block_rows, 128)),
        name="find_mobility", cost=2_500_000_000,
    )(slots, *mobs)

    padded, strip = (params, layers, ROWS, 128), (params, ROWS, 128)
    final, states, rate, halos, m, ms = kernel(
        forward,
        (
            f32(*order_init.shape), [f32(*padded)] * ITERS, [f32(*padded)] * ITERS,
            [f32(*strip)] * (ITERS - 1), f32(layers, ROWS, 128), f32(ROWS, 128),
        ),
        (vmem(*strip), vmem(*strip), vmem(*padded), vmem(layers, ROWS, 128), vmem(ROWS, 128)),
        name="forward", cost=0,
    )(order_init, grain_map, near_a, row_b, far_a, far_b, strip_a, strip_b, table)
    adjoint, sums = kernel(
        backward,
        (f32(*order_init.shape), f32(bricks, listed)),
        (
            [vmem(*padded)] * 2, [vmem(*strip)] * 2, [vmem(*padded)] * 2, [vmem(*strip)] * 2, vmem(*padded),
            vmem(ITERS - 1, layers, 2, 8, 128), vmem(listed, 128),
        ),
        name="backward",
    )(
        cotangent, grain_map, near_a, cot_b, far_a, far_b, strip_a, strip_b,
        states, rate, halos, m, ms,
    )

    sums = lax.all_to_all(sums, both, 0, 0, tiled=True)
    grads = kernel(
        functools.partial(pick_owned, owned), f32(1, owned),
        (vmem(owned + -owned % 8, 128), vmem(bricks // 2, 128)), name="pick_owned",
    )(slots, sums)
    return final, adjoint, grads.reshape(owned)


def solution(mesh):
    counts = (mesh.shape["wide"], mesh.shape["narrow"])
    field = P("groups", None, "wide", "narrow")
    spread = P(("groups", "wide", "narrow"))
    return jax.shard_map(
        functools.partial(per_device, counts),
        mesh=mesh,
        in_specs=(field, field, P("groups", "wide", "narrow"), P("groups", None), P("groups"), spread),
        out_specs=(field, field, spread),
        check_vma=False,
    )
```

```python
import functools

import jax
import jax.numpy as jnp
from jax import lax
from jax.experimental import pallas as pl
from jax.experimental.pallas import tpu as pltpu
from jax.sharding import PartitionSpec as P

ITERS = 4
TIME_STEP = 0.05

EDGE = 6
MAP_EDGE = 5
ADJ_EDGE = 4
ROWS = 24
COLS = 10
LEAD = 8
CORNER = (5, 3, 4)

VMEM_LIMIT = 24 * 1024 * 1024


def lanes(shape):
    return lax.broadcasted_iota(jnp.int32, shape, len(shape) - 1)


def roll(value, shift):
    return pltpu.roll(value, shift, 1)


def is_odd(axis):
    return lax.rem(lax.axis_index(axis), 2) == 1


def pack_strips(*refs):
    count = (len(refs) - 4) // 2
    sources, targets = refs[:count], refs[count : 2 * count]
    strip_a_ref, strip_b_ref, block_ref, sems = refs[2 * count :]
    copies = [pltpu.make_async_copy(a, b, sems.at[i]) for i, (a, b) in enumerate(zip(sources, targets))]
    for copy in copies:
        copy.start()
    order_ref, map_ref, cot_ref, mob_ref = targets[:4]
    params, layers = order_ref.shape[:2]
    odd = is_odd("narrow")
    for copy in copies:
        copy.wait()

    lane = lanes((8, 128))
    zero = jnp.zeros((8, 128), jnp.float32)

    def span(first, size):
        return ((lane - first) & 127) < size

    for field in range(params + 1):
        right, left = zero, zero
        for z in range(layers):
            value = order_ref[field, z] if field < params else map_ref[z].astype(jnp.float32)
            moved = roll(value, 10 * z + 5)
            right = jnp.where(span(10 * z - 1, 6), moved, right)
            left = jnp.where(span(10 * z + 5, 6), moved, left)
            if field < params:
                right = jnp.where(span(10 * z + 5, 4), roll(cot_ref[field, z], 10 * z + 9), right)
                left = jnp.where(span(10 * z + 1, 4), roll(cot_ref[field, z], 10 * z + 1), left)
        rows = slice(8 * field, 8 * field + 8)
        strip_a_ref[rows, :] = jnp.where(odd, left, right)
        strip_b_ref[rows, :] = jnp.where(odd, right, left)
    owned = mob_ref.shape[1]
    owned_rows = -(-owned // 128)
    block_ref[...] = jnp.zeros_like(block_ref)
    first = lax.axis_index("narrow") * owned_rows
    for i in range(owned_rows):
        size = min(128, owned - 128 * i)
        row = mob_ref[0:1, 128 * i : 128 * i + size]
        if size < 128:
            row = jnp.concatenate([row, jnp.zeros((1, 128 - size), jnp.float32)], axis=1)
        block_ref[pl.ds(first + i, 1), :] = row
    for ref in (strip_a_ref, strip_b_ref):
        ref[8 * (params + 1) :, :] = block_ref[...]


def pack_rows(
    order_ref, map_ref, cot_ref, strip_ref, block_ref, after_ref, near_a_ref, row_b_ref, strip_a_ref, out_block_ref
):
    strip_a_ref[...] = strip_ref[...]
    out_block_ref[...] = block_ref[...]
    params, layers = order_ref.shape[:2]
    maps, cots = row_places(params, layers)
    gap = jnp.zeros((LEAD, 128), jnp.float32)
    odd = is_odd("wide")
    last = (jnp.where(odd, 0, 1), jnp.where(odd, 1, 0))
    row_refs = (near_a_ref, row_b_ref)
    for ref in row_refs:
        ref[0:LEAD, :] = gap
        ref[maps - LEAD : maps, :] = gap
        ref[cots - 2 * LEAD : cots - LEAD, :] = gap
        ref[cots - LEAD : cots, :] = gap
    near_a_ref[cots : cots + LEAD, :] = gap
    near_a_ref[near_a_ref.shape[0] - LEAD :, :] = gap
    for p in range(params):
        for z in range(layers):
            k = LEAD + (p * layers + z) * EDGE
            for ref, is_last in zip(row_refs, last):
                ref[k : k + EDGE, :] = order_ref[p, z, pl.ds((8 - EDGE) * is_last, EDGE), :]
    for z in range(layers):
        k = maps + z * MAP_EDGE
        for ref, is_last in zip(row_refs, last):
            ref[k : k + MAP_EDGE, :] = map_ref[z, pl.ds((8 - MAP_EDGE) * is_last, MAP_EDGE), :].astype(jnp.float32)
    rows = pl.ds((8 - ADJ_EDGE) * last[0], ADJ_EDGE)
    for p in range(params):
        for z in range(layers):
            k = cots + LEAD + (p * layers + z) * ADJ_EDGE
            near_a_ref[k : k + ADJ_EDGE, :] = cot_ref[p, z, rows, :]


def relay(strip_ref, out_ref):
    out_ref[...] = strip_ref[...]


def pack_cot(cot_ref, after_ref, out_ref):
    params, layers = cot_ref.shape[:2]
    out_ref[0:LEAD, :] = jnp.zeros((LEAD, 128), jnp.float32)
    out_ref[out_ref.shape[0] - LEAD :, :] = jnp.zeros((LEAD, 128), jnp.float32)
    rows = pl.ds(jnp.where(is_odd("wide"), 8 - ADJ_EDGE, 0), ADJ_EDGE)
    for p in range(params):
        for z in range(layers):
            k = LEAD + (p * layers + z) * ADJ_EDGE
            out_ref[k : k + ADJ_EDGE, :] = cot_ref[p, z, rows, :]


def row_places(params, layers):
    maps = LEAD + params * layers * EDGE + LEAD
    length = maps + layers * MAP_EDGE
    return maps, length + -length % 8 + LEAD


def corner_rows(params):
    return -(-(params * (CORNER[0] + CORNER[1]) + CORNER[2]) // 8) * 8


def side_strips(params, strip_a_ref, strip_b_ref):
    odd = is_odd("narrow")
    fields = []
    for field in range(params + 1):
        rows = slice(8 * field, 8 * field + 8)
        a, b = strip_a_ref[rows, :], strip_b_ref[rows, :]
        fields.append((jnp.where(odd, a, b), jnp.where(odd, b, a)))
    return fields


def merged_strips(params, *strip_refs):
    first = lanes((8, 128)) % COLS < 5
    fields = side_strips(params, *strip_refs)
    order = [jnp.where(first, a, b) for a, b in fields[:params]]
    cot = [jnp.where(first, roll(a, 124), roll(b, 4)) for a, b in fields[:params]]
    return order, cot, jnp.where(first, *fields[params])


def pack_far(params, strip_a_ref, strip_b_ref, block_ref, *refs):
    *other_refs, far_a_ref, far_b_ref, out_block_ref = refs
    at = 8 * (params + 1)
    mobs = corner_rows(params)
    block = block_ref[...] + strip_a_ref[at:, :] + strip_b_ref[at:, :]
    for ref in other_refs:
        block = block + ref[...]
    out_block_ref[...] = block
    at = 0
    odd = is_odd("wide")
    order, cot, cells = merged_strips(params, strip_a_ref, strip_b_ref)
    for n, fields in zip(CORNER, (order, cot, [cells])):
        for both in fields:
            far_a_ref[at : at + n, :] = jnp.where(odd, both[0:n], both[8 - n : 8])
            far_b_ref[at : at + n, :] = jnp.where(odd, both[8 - n : 8], both[0:n])
            at += n
    for ref in (far_a_ref, far_b_ref):
        ref[at:mobs, :] = jnp.zeros((mobs - at, 128), jnp.float32)
        ref[mobs:, :] = block


def find_slots(bricks_ref, slot_ref, after_ref, out_ref):
    count, listed = bricks_ref.shape
    rows = slot_ref.shape[0]
    for k in range(0, out_ref.shape[0], 8):
        pairs = [
            jnp.concatenate([bricks_ref[2 * j : 2 * j + 1, :], bricks_ref[2 * j + 1 : 2 * j + 2, :]], axis=1)
            for j in range(k, k + 8)
        ]
        grain = jnp.concatenate(pairs, axis=0)
        row, col = grain >> 7, grain & 127

        def body(r, found, row=row, col=col):
            table = jnp.broadcast_to(slot_ref[pl.ds(r, 1), :], (8, 128))
            taken = jnp.take_along_axis(table, col, axis=1, mode="promise_in_bounds")
            return jnp.where(row == r, taken, found)

        out_ref[k : k + 8, :] = lax.fori_loop(0, rows, body, jnp.zeros((8, 128), jnp.int32), unroll=7)


def find_mobility(counts, owned, slots_ref, *refs):
    *mob_refs, table_ref, near_ref, all_ref = refs
    wide_count, narrow_count = counts
    tile = (8, 128)
    wide, narrow = lax.axis_index("wide"), lax.axis_index("narrow")
    if len(mob_refs) == 1:
        mob_ref = mob_refs[0]
    else:
        block_ref, far_a_ref, far_b_ref, other_ref = mob_refs
        mob_ref = all_ref
        size = block_ref.shape[0]
        odd = is_odd("wide")
        step = jnp.where(odd, 1, 3)
        for place, ref in (
            (wide, block_ref), (wide + 4 - step, far_a_ref), (wide + step, far_b_ref), (wide + 2, other_ref)
        ):
            at = pl.multiple_of(size * (place & 3), size)
            mob_ref[pl.ds(at, size), :] = ref[ref.shape[0] - size :, :]
    near_ref[...] = jnp.zeros_like(near_ref)
    for k in range(9):
        w = lax.rem(wide + k // 3 - 1 + wide_count, wide_count)
        n = lax.rem(narrow + k % 3 - 1 + narrow_count, narrow_count)
        brick = w * narrow_count + n
        row = slots_ref[pl.ds(brick >> 1, 1), :]
        half = jnp.where((brick & 1) == 0, row[:, 0:64], row[:, 64:128])
        near_ref[k // 2 : k // 2 + 1, 64 * (k % 2) : 64 * (k % 2) + 64] = half
    slot = near_ref[...]
    owned_rows = -(-owned // 128)
    owner = jnp.floor((slot.astype(jnp.float32) + 0.5) * (1.0 / owned)).astype(jnp.int32)
    inner = slot - owner * owned
    row = owner * owned_rows + (inner >> 7)
    place = inner & 127

    def body(r, found):
        values = jnp.broadcast_to(mob_ref[pl.ds(r, 1), :], tile)
        taken = jnp.take_along_axis(values, place, axis=1, mode="promise_in_bounds")
        return jnp.where(row == r, taken, found)

    found = lax.fori_loop(0, mob_ref.shape[0], body, jnp.zeros(tile, jnp.float32), unroll=16)
    table_ref[...] = TIME_STEP * found


def total_of(values):
    while len(values) > 1:
        values = [a + b for a, b in zip(values[::2], values[1::2])]
    return values[0]


def each_tile(layers, windows, body):
    start, count, most = windows
    group = 12 // (2 * count) * 2 if layers % 12 == 0 else 1

    def some(step, carry):
        stores = []
        for j in range(group):
            z = step * group + j
            for i in range(count):
                stores += body(z, i, jnp.minimum(start + 8 * i + ((z + 16) >> 5), most))
            if len(stores) >= 64 or j == group - 1:
                for store in stores:
                    store()
                stores = []
        return carry

    lax.fori_loop(0, layers // group, some, 0)


def each_window(windows, body):
    def one(i, carry):
        body(windows[0] + 8 * i)
        return carry

    lax.fori_loop(0, windows[1], one, 0)


def put(ref, index, value):
    def store():
        ref[index] = value

    return store


def neighbours(ref, ends_ref, value, p, z, r):
    layers = ref.shape[1]
    lane = lanes((8, 128))
    rows, before, after = pl.ds(r, 8), pl.ds(r - 1, 8), pl.ds(r + 1, 8)
    below, above = jnp.maximum(z - 1, 0), jnp.minimum(z + 1, layers - 1)
    ends = ends_ref[p, z, rows, :]
    left = roll(jnp.where(lane == 127, ends, value), 1)
    right = roll(jnp.where(lane == 0, ends, value), 127)
    total = (left + right) + (ref[p, z, before, :] + ref[p, z, after, :])
    return total + (ref[p, below, rows, :] + ref[p, above, rows, :])


def strip_neighbours(ref, core_ref, values, r, outer_ref=None):
    params, layers = core_ref.shape[:2]
    lane = lanes((8, 128))
    col = lane % COLS
    rows, before, after = pl.ds(r, 8), pl.ds(r - 1, 8), pl.ds(r + 1, 8)
    near = []
    for p in range(params):
        value = values[p]
        ends = jnp.zeros((8, 128), jnp.float32)
        for z in range(layers):
            here = (lane == 10 * z + 4) | (lane == 10 * z + 5)
            ends = jnp.where(here, roll(core_ref[p, z, rows, :], 10 * z + 5), ends)
        left = roll(jnp.where(col == 4, ends, value), 1)
        right = roll(jnp.where(col == 5, ends, value), 127)
        if outer_ref is not None:
            outer = outer_ref[p, rows, :]
            left = jnp.where(col == 0, outer, left)
            right = jnp.where(col == 9, outer, right)
        below = jnp.where(lane < COLS, value, roll(value, COLS))
        above = jnp.where(lane >= COLS * (layers - 1), value, roll(value, 128 - COLS))
        total = (left + right) + (below + above)
        near.append(total + (ref[p, before, :] + ref[p, after, :]))
    return near


def spread_ends(ends_ref, values, rows):
    params, layers = ends_ref.shape[:2]
    for p in range(params):
        for z in range(layers):
            ends_ref[p, z, rows, :] = roll(values[p], 123 - 10 * z)


def base_of(e):
    return 1.5 * total_of([x * x for x in e]) + 5.0


def inner_of(e, u):
    return 3.0 * total_of([x * y for x, y in zip(e, u)])


def forward(
    order_ref, map_ref, row_a_ref, row_b_ref, far_a_ref, far_b_ref, strip_a_ref, strip_b_ref, table_ref,
    final_ref, e_refs, rate_refs, se_refs, m_ref, ms_ref,
    first_strip_ref, outer_ref, ends_ref, g_ref, gs_ref,
):
    params, layers = order_ref.shape[:2]
    tile = (8, 128)
    col = lanes(tile) % COLS
    maps = row_places(params, layers)[0]
    strip_refs = [first_strip_ref, *se_refs]
    every = range(params)

    odd = is_odd("wide")
    from_before = (jnp.where(odd, 1, 0), jnp.where(odd, 0, 1))

    def place(z, carry):
        for ref, before in zip((row_a_ref, row_b_ref), from_before):
            k, target = maps + z * MAP_EDGE + before * (MAP_EDGE - 8), pl.ds(16 - 16 * before, 8)
            g_ref[z, target, :] = ref[pl.ds(k, 8), :]
            for p in every:
                k = LEAD + (p * layers + z) * EDGE + before * (EDGE - 8)
                e_refs[0][p, z, target, :] = ref[pl.ds(k, 8), :]
        for p in every:
            e_refs[0][p, z, 8:16, :] = order_ref[p, z]
        return carry

    lax.fori_loop(0, layers, place, 0)

    sides = side_strips(params, strip_a_ref, strip_b_ref)
    order, _, cells = merged_strips(params, strip_a_ref, strip_b_ref)
    n = CORNER[0]
    for p in every:
        ref = first_strip_ref.at[p]
        ref[0:8, :] = jnp.zeros(tile, jnp.float32)
        ref[16:24, :] = jnp.zeros(tile, jnp.float32)
        a, b = far_a_ref[n * p : n * p + n, :], far_b_ref[n * p : n * p + n, :]
        ref[8 - n : 8, :] = jnp.where(odd, a, b)
        ref[8:16, :] = order[p]
        ref[16 : 16 + n, :] = jnp.where(odd, b, a)
        outer_ref[p, 8:16, :] = jnp.where(col == 0, roll(sides[p][0], 1), roll(sides[p][1], 127))
    at, n = params * (CORNER[0] + CORNER[1]), CORNER[2]
    gs_ref[...] = jnp.zeros_like(gs_ref)
    a, b = far_a_ref[at : at + n, :], far_b_ref[at : at + n, :]
    gs_ref[8 - n : 8, :] = jnp.where(odd, a, b)
    gs_ref[8:16, :] = cells
    gs_ref[16 : 16 + n, :] = jnp.where(odd, b, a)
    for r in (0, 8, 16):
        rows = slice(r, r + 8)
        spread_ends(ends_ref, [first_strip_ref[p, rows, :] for p in every], rows)

    def lookup(index, which):
        values = jnp.broadcast_to(table_ref[which // 2 : which // 2 + 1, :], tile)
        return jnp.take_along_axis(values, index + 64 * (which % 2), axis=1, mode="promise_in_bounds")

    for i in range(3):
        r = 8 * i
        for z in range(layers):
            index = map_ref[z] if i == 1 else g_ref[z, r : r + 8, :].astype(jnp.int32) & 63
            m_ref[z, r : r + 8, :] = lookup(index, 3 * i + 1)
        index = gs_ref[r : r + 8, :].astype(jnp.int32) & 63
        ms_ref[r : r + 8, :] = jnp.where(col < 5, lookup(index, 3 * i), lookup(index, 3 * i + 2))

    def step(t, windows, strip_windows, end_windows):
        old, old_strip = e_refs[t], strip_refs[t]
        last = t == ITERS - 1

        def core(z, i, r):
            rows = pl.ds(r, 8)
            base = base_of([old[p, z, rows, :] for p in every])
            m = m_ref[z, rows, :]
            stores = []
            for p in every:
                e = old[p, z, rows, :]
                rate = e * (base - 0.5 * (e * e)) - neighbours(old, ends_ref, e, p, z, r)
                new = e - m * rate
                stores.append(put(rate_refs[t], (p, z, rows, slice(None)), rate))
                if last:
                    stores.append(put(final_ref, (p, z), new))
                else:
                    stores.append(put(e_refs[t + 1], (p, z, rows, slice(None)), new))
            return stores

        each_tile(layers, windows, core)
        if last:
            return

        def strip(r):
            rows = pl.ds(r, 8)
            e = [old_strip[p, rows, :] for p in every]
            m = ms_ref[rows, :]
            base = base_of(e)
            near = strip_neighbours(old_strip, old, e, r, outer_ref if t == 0 else None)
            for p in every:
                rate = e[p] * (base - 0.5 * (e[p] * e[p])) - near[p]
                strip_refs[t + 1][p, rows, :] = e[p] - m * rate

        each_window(strip_windows, strip)

        def ends(r):
            rows = pl.ds(r, 8)
            spread_ends(ends_ref, [strip_refs[t + 1][p, rows, :] for p in every], rows)

        each_window(end_windows, ends)

    step(0, (3, 3, 13), (4, 2), (4, 2))
    step(1, (4, 2, 12), (4, 2), (4, 2))
    step(2, (4, 2, 12), (4, 2), (8, 1))
    step(3, (8, 1, 8), None, None)


def backward(
    cot_ref, map_ref, row_a_ref, row_b_ref, far_a_ref, far_b_ref, strip_a_ref, strip_b_ref,
    e_refs, rate_refs, se_refs, m_ref, ms_ref,
    adjoint_ref, sums_ref,
    lam_refs, slam_refs, u_refs, su_refs, ends_ref, work_ref, binned_ref,
):
    params, layers = cot_ref.shape[:2]
    cots = row_places(params, layers)[1]
    tile = (8, 128)
    every = range(params)

    odd = is_odd("wide")
    from_before = (jnp.where(odd, 1, 0), jnp.where(odd, 0, 1))

    def place(z, carry):
        for ref, base, before in zip((row_a_ref, row_b_ref), (cots, 0), from_before):
            rows = pl.ds(16 - 16 * before, 8)
            m = m_ref[z, rows, :]
            for p in every:
                k = base + LEAD + (p * layers + z) * ADJ_EDGE + before * (ADJ_EDGE - 8)
                value = ref[pl.ds(k, 8), :]
                lam_refs[0][p, z, rows, :] = value
                u_refs[0][p, z, rows, :] = m * value
        m = m_ref[z, 8:16, :]
        for p in every:
            lam_refs[0][p, z, 8:16, :] = cot_ref[p, z]
            u_refs[0][p, z, 8:16, :] = m * cot_ref[p, z]
        return carry

    lax.fori_loop(0, layers, place, 0)
    _, cot, _ = merged_strips(params, strip_a_ref, strip_b_ref)
    n = CORNER[1]
    for p in every:
        at = params * CORNER[0] + n * p
        ref = slam_refs[0].at[p]
        ref[0:8, :] = jnp.zeros(tile, jnp.float32)
        ref[16:24, :] = jnp.zeros(tile, jnp.float32)
        a, b = far_a_ref[at : at + n, :], far_b_ref[at : at + n, :]
        ref[8 - n : 8, :] = jnp.where(odd, a, b)
        ref[8:16, :] = cot[p]
        ref[16 : 16 + n, :] = jnp.where(odd, b, a)
        for r in (0, 8, 16):
            su_refs[0][p, r : r + 8, :] = ms_ref[r : r + 8, :] * ref[r : r + 8, :]

    def spread(slot, windows):
        def ends(r):
            rows = pl.ds(r, 8)
            spread_ends(ends_ref, [su_refs[slot][p, rows, :] for p in every], rows)

        each_window(windows, ends)

    def step(t, slot, windows, strip_windows, end_windows):
        old, old_strip = u_refs[slot], su_refs[slot]

        def core(z, i, r):
            rows = pl.ds(r, 8)
            e = [e_refs[t][p, z, rows, :] for p in every]
            u = [old[p, z, rows, :] for p in every]
            base, inner = base_of(e), inner_of(e, u)
            m = m_ref[z, rows, :]
            work = total_of([lam_refs[slot][p, z, rows, :] * rate_refs[t][p, z, rows, :] for p in every])
            stores = [put(work_ref, (t - 1, z, i), work)]
            for p in every:
                e, u = e_refs[t][p, z, rows, :], old[p, z, rows, :]
                change = u * (base - 1.5 * (e * e)) + e * inner - neighbours(old, ends_ref, u, p, z, r)
                new = lam_refs[slot][p, z, rows, :] - change
                stores.append(put(lam_refs[1 - slot], (p, z, rows, slice(None)), new))
                stores.append(put(u_refs[1 - slot], (p, z, rows, slice(None)), m * new))
            return stores

        each_tile(layers, windows, core)

        def strip(r):
            rows = pl.ds(r, 8)
            e = [se_refs[t - 1][p, rows, :] for p in every]
            u = [old_strip[p, rows, :] for p in every]
            m = ms_ref[rows, :]
            base, inner = base_of(e), inner_of(e, u)
            near = strip_neighbours(old_strip, old, u, r)
            for p in every:
                change = u[p] * (base - 1.5 * (e[p] * e[p])) + e[p] * inner - near[p]
                new = slam_refs[slot][p, rows, :] - change
                slam_refs[1 - slot][p, rows, :] = new
                su_refs[1 - slot][p, rows, :] = m * new

        each_window(strip_windows, strip)
        spread(1 - slot, end_windows)

    spread(0, (4, 2))
    step(3, 0, (4, 2, 12), (4, 2), (4, 2))
    step(2, 1, (4, 2, 12), (4, 2), (4, 2))
    step(1, 0, (4, 2, 12), (8, 1), (8, 1))

    def last(z, i, r):
        rows = pl.ds(r, 8)
        e = [e_refs[0][p, z, rows, :] for p in every]
        u = [u_refs[1][p, z, rows, :] for p in every]
        base, inner = base_of(e), inner_of(e, u)
        stores = []
        for p in every:
            e, u = e_refs[0][p, z, rows, :], u_refs[1][p, z, rows, :]
            change = u * (base - 1.5 * (e * e)) + e * inner - neighbours(u_refs[1], ends_ref, u, p, z, r)
            stores.append(put(adjoint_ref, (p, z), lam_refs[1][p, z, rows, :] - change))
        return stores

    each_tile(layers, (8, 1, 8), last)

    grains = [map_ref[z] for z in range(layers)]
    cells = []
    for z in range(layers):
        upper = work_ref[0, z, 0] + work_ref[1, z, 0] + work_ref[2, z, 0]
        lower = work_ref[0, z, 1] + work_ref[1, z, 1] + work_ref[2, z, 1]
        first = total_of([lam_refs[1][p, z, 8:16, :] * rate_refs[0][p, z, 8:16, :] for p in every])
        cells.append(jnp.concatenate([upper[4:8], lower[0:4]], axis=0) + first)

    def bin_one(g, carry):
        kept = [jnp.where(grains[z] == g, cells[z], 0.0) for z in range(layers)]
        total = sum(kept[1:4], kept[0]) + sum(kept[5:8], kept[4]) + sum(kept[9:], kept[8])
        binned_ref[pl.ds(g, 1), :] = jnp.sum(total, axis=0, keepdims=True)
        return carry

    lax.fori_loop(0, binned_ref.shape[0], bin_one, 0, unroll=4)
    ones = jnp.full((8, 128), -TIME_STEP, jnp.float32)
    sums = lax.dot_general(
        ones, binned_ref[...], (((1,), (1,)), ((), ())),
        precision=lax.Precision.HIGHEST, preferred_element_type=jnp.float32,
    )
    for k in range(0, sums_ref.shape[0], 8):
        sums_ref[k : k + 8, :] = sums


def pick_owned(owned, slots_ref, sums_ref, out_ref, total_ref, dense_ref):
    base = (lax.axis_index("wide") * lax.axis_size("narrow") + lax.axis_index("narrow")) * owned
    tile = (8, 128)
    for k in range(dense_ref.shape[0]):
        dense_ref[k : k + 1, 0:64] = sums_ref[2 * k : 2 * k + 1, :]
        dense_ref[k : k + 1, 64:128] = sums_ref[2 * k + 1 : 2 * k + 2, :]
    sub = lax.broadcasted_iota(jnp.int32, tile, 0)
    blocks = total_ref.shape[0] // 8
    step = 25
    for first in range(0, blocks, step):
        some = range(first, min(first + step, blocks))

        def body(k, acc, some=some):
            shifted = jnp.broadcast_to(slots_ref[pl.ds(k, 1), :], tile) - (sub + base)
            value = jnp.broadcast_to(dense_ref[pl.ds(k, 1), :], tile)
            return tuple(a + jnp.where(shifted == 8 * j, value, 0.0) for a, j in zip(acc, some))

        zero = tuple(jnp.zeros(tile, jnp.float32) for _ in some)
        acc = lax.fori_loop(0, slots_ref.shape[0], body, zero, unroll=8)
        for a, j in zip(acc, some):
            total_ref[8 * j : 8 * j + 8, :] = a
    whole = lax.dot_general(
        jnp.ones(tile, jnp.float32), total_ref[...], (((1,), (1,)), ((), ())),
        precision=lax.Precision.HIGHEST, preferred_element_type=jnp.float32,
    )
    out_ref[...] = whole[0:1, 0:owned]


def f32(*shape):
    return jax.ShapeDtypeStruct(shape, jnp.float32)


def kernel(body, out_shape, scratch=(), name=None, cost=0, **specs):
    if cost:
        specs["cost_estimate"] = pl.CostEstimate(flops=cost, bytes_accessed=cost // 1000, transcendentals=0)
    return pl.pallas_call(
        body, out_shape=out_shape, scratch_shapes=list(scratch), name=name, **specs,
        compiler_params=pltpu.CompilerParams(vmem_limit_bytes=VMEM_LIMIT),
    )


def opposite(value, axis):
    return lax.ppermute(value, axis, [(i, (i + 2) % 4) for i in range(4)])


def swapped(value, axis, count, partner):
    step = [1 if (i + partner) % 2 == 0 else -1 for i in range(count)]
    return lax.ppermute(value, axis, [(i, (i + by) % count) for i, by in enumerate(step)])


def per_device(counts, order_init, cotangent, grain_map, brick_grains, grain_slot, mobility):
    wide_count, narrow_count = counts
    params, layers = order_init.shape[:2]
    assert order_init.shape[2:] == (8, 128) and layers * COLS < 128
    owned = mobility.shape[0]
    listed = brick_grains.shape[1]
    bricks = brick_grains.shape[0]

    both = ("wide", "narrow")
    count = wide_count * narrow_count
    small = counts == (4, 4)
    assert listed == 64 and bricks == count and count % 16 == 0

    owned_rows = -(-owned // 128)
    block_rows = narrow_count * owned_rows
    strip_rows = 8 * (params + 1)
    edge_rows = row_places(params, layers)[1]
    cot_rows = params * layers * ADJ_EDGE + 2 * LEAD
    vmem = lambda *shape: pltpu.VMEM(shape, jnp.float32)

    arguments = (
        order_init, grain_map, cotangent, mobility.reshape(1, owned), brick_grains, grain_slot.reshape(-1, 128)
    )
    here, anywhere = pl.BlockSpec(memory_space=pltpu.VMEM), pl.BlockSpec(memory_space=pl.ANY)
    *fetched, strip_a, strip_b, block = kernel(
        pack_strips,
        tuple(jax.ShapeDtypeStruct(x.shape, x.dtype) for x in arguments)
        + (f32(strip_rows + block_rows, 128),) * 2 + (f32(block_rows, 128),),
        (pltpu.SemaphoreType.DMA((len(arguments),)),), name="pack_strips",
        in_specs=[pl.BlockSpec(memory_space=pltpu.HBM)] * len(arguments),
    )(*(pltpu.with_memory_space_constraint(x, pltpu.HBM) for x in arguments))
    order_init, grain_map, cotangent, _, brick_grains, grain_slot = fetched
    near_a, row_b, strip_a, block = kernel(
        pack_rows,
        (f32(edge_rows + cot_rows, 128), f32(edge_rows, 128), f32(strip_rows + block_rows, 128), f32(block_rows, 128)),
        name="pack_rows", in_specs=[here] * 5 + [anywhere],
    )(order_init, grain_map, cotangent, strip_a, block, strip_b)
    row_b = swapped(row_b, "wide", wide_count, 1)
    near_a = swapped(near_a, "wide", wide_count, 0)
    strip_b = swapped(strip_b, "narrow", narrow_count, 1)
    strip_b = kernel(relay, f32(*strip_b.shape), name="relay", cost=600_000_000)(strip_b)
    strip_a = swapped(strip_a, "narrow", narrow_count, 0)
    others = [opposite(block, "narrow")] if small else []

    corners = corner_rows(params)
    far_a, far_b, block = kernel(
        functools.partial(pack_far, params),
        (f32(corners + block_rows, 128),) * 2 + (f32(block_rows, 128),), name="pack_far", cost=0,
    )(strip_a, strip_b, block, *others)
    far_b = swapped(far_b, "wide", wide_count, 1)
    far_a = swapped(far_a, "wide", wide_count, 0)
    slots = kernel(
        find_slots, jax.ShapeDtypeStruct((bricks // 2, 128), jnp.int32), name="find_slots",
        in_specs=[here, here, anywhere],
    )(brick_grains, grain_slot, block)
    cot_b = kernel(pack_cot, f32(cot_rows, 128), name="pack_cot", in_specs=[here, anywhere])(cotangent, far_a)
    cot_b = swapped(cot_b, "wide", wide_count, 1)

    if small:
        mobs = (block, far_a, far_b, opposite(block, "wide"))
    else:
        own = jnp.pad(mobility, (0, -owned % 128)).reshape(owned_rows, 128)
        mobs = (lax.all_gather(own, both, axis=0, tiled=True),)
    table = kernel(
        functools.partial(find_mobility, counts, owned), f32(8, 128),
        (pltpu.VMEM((8, 128), jnp.int32), vmem(wide_count * block_rows, 128)),
        name="find_mobility", cost=2_500_000_000,
    )(slots, *mobs)

    padded, strip = (params, layers, ROWS, 128), (params, ROWS, 128)
    final, states, rate, halos, m, ms = kernel(
        forward,
        (
            f32(*order_init.shape), [f32(*padded)] * ITERS, [f32(*padded)] * ITERS,
            [f32(*strip)] * (ITERS - 1), f32(layers, ROWS, 128), f32(ROWS, 128),
        ),
        (vmem(*strip), vmem(*strip), vmem(*padded), vmem(layers, ROWS, 128), vmem(ROWS, 128)),
        name="forward", cost=0,
    )(order_init, grain_map, near_a, row_b, far_a, far_b, strip_a, strip_b, table)
    adjoint, sums = kernel(
        backward,
        (f32(*order_init.shape), f32(bricks, listed)),
        (
            [vmem(*padded)] * 2, [vmem(*strip)] * 2, [vmem(*padded)] * 2, [vmem(*strip)] * 2, vmem(*padded),
            vmem(ITERS - 1, layers, 2, 8, 128), vmem(listed, 128),
        ),
        name="backward",
    )(
        cotangent, grain_map, near_a, cot_b, far_a, far_b, strip_a, strip_b,
        states, rate, halos, m, ms,
    )

    sums = lax.all_to_all(sums, both, 0, 0, tiled=True)
    grads = kernel(
        functools.partial(pick_owned, owned), f32(1, owned),
        (vmem(owned + -owned % 8, 128), vmem(bricks // 2, 128)), name="pick_owned",
    )(slots, sums)
    return final, adjoint, grads.reshape(owned)


def solution(mesh):
    counts = (mesh.shape["wide"], mesh.shape["narrow"])
    field = P("groups", None, "wide", "narrow")
    spread = P(("groups", "wide", "narrow"))
    return jax.shard_map(
        functools.partial(per_device, counts),
        mesh=mesh,
        in_specs=(field, field, P("groups", "wide", "narrow"), P("groups", None), P("groups"), spread),
        out_specs=(field, field, spread),
        check_vma=False,
    )
```

```python
import functools

import jax
import jax.numpy as jnp
from jax import lax
from jax.experimental import pallas as pl
from jax.experimental.pallas import tpu as pltpu
from jax.sharding import PartitionSpec as P

ITERS = 4
TIME_STEP = 0.05

EDGE = 6
MAP_EDGE = 5
ADJ_EDGE = 4
ROWS = 32
COLS = 10
LEAD = 8
CORNER = (5, 3, 4)

VMEM_LIMIT = 24 * 1024 * 1024


def lanes(shape):
    return lax.broadcasted_iota(jnp.int32, shape, len(shape) - 1)


def roll(value, shift):
    return pltpu.roll(value, shift, 1)


def is_odd(axis):
    return lax.rem(lax.axis_index(axis), 2) == 1


def pack_strips(order_ref, map_ref, cot_ref, mob_ref, after_ref, strip_a_ref, strip_b_ref, block_ref):
    params, layers = order_ref.shape[:2]
    odd = is_odd("narrow")
    lane = lanes((8, 128))
    zero = jnp.zeros((8, 128), jnp.float32)

    def span(first, size):
        return ((lane - first) & 127) < size

    for field in range(params + 1):
        right, left = zero, zero
        for z in range(layers):
            value = order_ref[field, z] if field < params else map_ref[z].astype(jnp.float32)
            moved = roll(value, 10 * z + 5)
            right = jnp.where(span(10 * z - 1, 6), moved, right)
            left = jnp.where(span(10 * z + 5, 6), moved, left)
            if field < params:
                right = jnp.where(span(10 * z + 5, 4), roll(cot_ref[field, z], 10 * z + 9), right)
                left = jnp.where(span(10 * z + 1, 4), roll(cot_ref[field, z], 10 * z + 1), left)
        rows = slice(8 * field, 8 * field + 8)
        strip_a_ref[rows, :] = jnp.where(odd, left, right)
        strip_b_ref[rows, :] = jnp.where(odd, right, left)
    owned = mob_ref.shape[1]
    owned_rows = -(-owned // 128)
    block_ref[...] = jnp.zeros_like(block_ref)
    first = lax.axis_index("narrow") * owned_rows
    for i in range(owned_rows):
        size = min(128, owned - 128 * i)
        row = mob_ref[0:1, 128 * i : 128 * i + size]
        if size < 128:
            row = jnp.concatenate([row, jnp.zeros((1, 128 - size), jnp.float32)], axis=1)
        block_ref[pl.ds(first + i, 1), :] = row
    for ref in (strip_a_ref, strip_b_ref):
        ref[8 * (params + 1) :, :] = block_ref[...]


def pack_rows(*refs):
    count = (len(refs) - 3) // 2
    sources, targets = refs[:count], refs[count : 2 * count]
    near_a_ref, row_b_ref, sems = refs[2 * count :]
    copies = [pltpu.make_async_copy(a, b, sems.at[i]) for i, (a, b) in enumerate(zip(sources, targets))]
    for copy in copies:
        copy.start()
    order_ref, map_ref, cot_ref = targets[:3]
    params, layers = order_ref.shape[:2]
    maps, cots = row_places(params, layers)
    gap = jnp.zeros((LEAD, 128), jnp.float32)
    odd = is_odd("wide")
    last = (jnp.where(odd, 0, 1), jnp.where(odd, 1, 0))
    row_refs = (near_a_ref, row_b_ref)
    for ref in row_refs:
        ref[0:LEAD, :] = gap
        ref[maps - LEAD : maps, :] = gap
        ref[cots - 2 * LEAD : cots - LEAD, :] = gap
        ref[cots - LEAD : cots, :] = gap
    near_a_ref[cots : cots + LEAD, :] = gap
    near_a_ref[near_a_ref.shape[0] - LEAD :, :] = gap
    copies[0].wait()
    for p in range(params):
        for z in range(layers):
            k = LEAD + (p * layers + z) * EDGE
            for ref, is_last in zip(row_refs, last):
                ref[k : k + EDGE, :] = order_ref[p, z, pl.ds((8 - EDGE) * is_last, EDGE), :]
    for copy in copies[1:]:
        copy.wait()
    for z in range(layers):
        k = maps + z * MAP_EDGE
        for ref, is_last in zip(row_refs, last):
            ref[k : k + MAP_EDGE, :] = map_ref[z, pl.ds((8 - MAP_EDGE) * is_last, MAP_EDGE), :].astype(jnp.float32)
    rows = pl.ds((8 - ADJ_EDGE) * last[0], ADJ_EDGE)
    for p in range(params):
        for z in range(layers):
            k = cots + LEAD + (p * layers + z) * ADJ_EDGE
            near_a_ref[k : k + ADJ_EDGE, :] = cot_ref[p, z, rows, :]


def pack_cot(cot_ref, after_ref, out_ref):
    params, layers = cot_ref.shape[:2]
    out_ref[0:LEAD, :] = jnp.zeros((LEAD, 128), jnp.float32)
    out_ref[out_ref.shape[0] - LEAD :, :] = jnp.zeros((LEAD, 128), jnp.float32)
    rows = pl.ds(jnp.where(is_odd("wide"), 8 - ADJ_EDGE, 0), ADJ_EDGE)
    for p in range(params):
        for z in range(layers):
            k = LEAD + (p * layers + z) * ADJ_EDGE
            out_ref[k : k + ADJ_EDGE, :] = cot_ref[p, z, rows, :]


def row_places(params, layers):
    maps = LEAD + params * layers * EDGE + LEAD
    length = maps + layers * MAP_EDGE
    return maps, length + -length % 8 + LEAD


def corner_rows(params):
    return -(-(params * (CORNER[0] + CORNER[1]) + CORNER[2]) // 8) * 8


def side_strips(params, strip_a_ref, strip_b_ref):
    odd = is_odd("narrow")
    fields = []
    for field in range(params + 1):
        rows = slice(8 * field, 8 * field + 8)
        a, b = strip_a_ref[rows, :], strip_b_ref[rows, :]
        fields.append((jnp.where(odd, a, b), jnp.where(odd, b, a)))
    return fields


def merged_strips(params, *strip_refs):
    first = lanes((8, 128)) % COLS < 5
    fields = side_strips(params, *strip_refs)
    order = [jnp.where(first, a, b) for a, b in fields[:params]]
    cot = [jnp.where(first, roll(a, 124), roll(b, 4)) for a, b in fields[:params]]
    return order, cot, jnp.where(first, *fields[params])


def pack_far(params, strip_a_ref, strip_b_ref, block_ref, *refs):
    *other_refs, far_a_ref, far_b_ref, out_block_ref = refs
    at = 8 * (params + 1)
    mobs = corner_rows(params)
    block = block_ref[...] + strip_a_ref[at:, :] + strip_b_ref[at:, :]
    for ref in other_refs:
        block = block + ref[...]
    out_block_ref[...] = block
    at = 0
    odd = is_odd("wide")
    order, cot, cells = merged_strips(params, strip_a_ref, strip_b_ref)
    for n, fields in zip(CORNER, (order, cot, [cells])):
        for both in fields:
            far_a_ref[at : at + n, :] = jnp.where(odd, both[0:n], both[8 - n : 8])
            far_b_ref[at : at + n, :] = jnp.where(odd, both[8 - n : 8], both[0:n])
            at += n
    for ref in (far_a_ref, far_b_ref):
        ref[at:mobs, :] = jnp.zeros((mobs - at, 128), jnp.float32)
        ref[mobs:, :] = block


def find_slots(bricks_ref, slot_ref, after_ref, out_ref):
    count, listed = bricks_ref.shape
    rows = slot_ref.shape[0]
    for k in range(0, out_ref.shape[0], 8):
        pairs = [
            jnp.concatenate([bricks_ref[2 * j : 2 * j + 1, :], bricks_ref[2 * j + 1 : 2 * j + 2, :]], axis=1)
            for j in range(k, k + 8)
        ]
        grain = jnp.concatenate(pairs, axis=0)
        row, col = grain >> 7, grain & 127

        def body(r, found, row=row, col=col):
            table = jnp.broadcast_to(slot_ref[pl.ds(r, 1), :], (8, 128))
            taken = jnp.take_along_axis(table, col, axis=1, mode="promise_in_bounds")
            return jnp.where(row == r, taken, found)

        out_ref[k : k + 8, :] = lax.fori_loop(0, rows, body, jnp.zeros((8, 128), jnp.int32), unroll=7)


def find_mobility(counts, owned, slots_ref, *refs):
    *mob_refs, table_ref, near_ref, all_ref = refs
    wide_count, narrow_count = counts
    tile = (8, 128)
    wide, narrow = lax.axis_index("wide"), lax.axis_index("narrow")
    if len(mob_refs) == 1:
        mob_ref = mob_refs[0]
    else:
        block_ref, far_a_ref, far_b_ref, other_ref = mob_refs
        mob_ref = all_ref
        size = block_ref.shape[0]
        odd = is_odd("wide")
        step = jnp.where(odd, 1, 3)
        for place, ref in (
            (wide, block_ref), (wide + 4 - step, far_a_ref), (wide + step, far_b_ref), (wide + 2, other_ref)
        ):
            at = pl.multiple_of(size * (place & 3), size)
            mob_ref[pl.ds(at, size), :] = ref[ref.shape[0] - size :, :]
    near_ref[...] = jnp.zeros_like(near_ref)
    for k in range(9):
        w = lax.rem(wide + k // 3 - 1 + wide_count, wide_count)
        n = lax.rem(narrow + k % 3 - 1 + narrow_count, narrow_count)
        brick = w * narrow_count + n
        row = slots_ref[pl.ds(brick >> 1, 1), :]
        half = jnp.where((brick & 1) == 0, row[:, 0:64], row[:, 64:128])
        near_ref[k // 2 : k // 2 + 1, 64 * (k % 2) : 64 * (k % 2) + 64] = half
    slot = near_ref[...]
    owned_rows = -(-owned // 128)
    owner = jnp.floor((slot.astype(jnp.float32) + 0.5) * (1.0 / owned)).astype(jnp.int32)
    inner = slot - owner * owned
    row = owner * owned_rows + (inner >> 7)
    place = inner & 127

    def body(r, found):
        values = jnp.broadcast_to(mob_ref[pl.ds(r, 1), :], tile)
        taken = jnp.take_along_axis(values, place, axis=1, mode="promise_in_bounds")
        return jnp.where(row == r, taken, found)

    found = lax.fori_loop(0, mob_ref.shape[0], body, jnp.zeros(tile, jnp.float32), unroll=16)
    table_ref[...] = TIME_STEP * found


def total_of(values):
    while len(values) > 1:
        values = [a + b for a, b in zip(values[::2], values[1::2])]
    return values[0]


def each_tile(layers, windows, body):
    start, count, most = windows
    group = 12 // (2 * count) * 2 if layers % 12 == 0 else 1

    def some(step, carry):
        stores = []
        for j in range(group):
            z = step * group + j
            for i in range(count):
                r = jnp.minimum(start + 8 * i + ((z + 16) >> 5), most)
                rows = pl.ds(start + 8 * i, 8) if start % 8 == 0 else pl.ds(r, 8)
                stores += body(z, i, rows, r)
            if len(stores) >= 64 or j == group - 1:
                for store in stores:
                    store()
                stores = []
        return carry

    lax.fori_loop(0, layers // group, some, 0)


def each_window(windows, body):
    start, count, most = windows

    def one(i, carry):
        r = jnp.minimum(start + 8 * i, most)
        body(pl.ds(pl.multiple_of(r, 8) if start % 8 == 0 else r, 8), r)
        return carry

    lax.fori_loop(0, count, one, 0)


def put(ref, index, value):
    def store():
        ref[index] = value

    return store


def neighbours(ref, ends_ref, value, p, z, rows, r):
    layers = ref.shape[1]
    lane = lanes((8, 128))
    before, after = pl.ds(r - 1, 8), pl.ds(r + 1, 8)
    below, above = jnp.maximum(z - 1, 0), jnp.minimum(z + 1, layers - 1)
    ends = ends_ref[p, z, rows, :]
    left = roll(jnp.where(lane == 127, ends, value), 1)
    right = roll(jnp.where(lane == 0, ends, value), 127)
    total = (left + right) + (ref[p, z, before, :] + ref[p, z, after, :])
    return total + (ref[p, below, rows, :] + ref[p, above, rows, :])


def strip_neighbours(ref, core_ref, values, rows, r, outer_ref=None):
    params, layers = core_ref.shape[:2]
    lane = lanes((8, 128))
    col = lane % COLS
    before, after = pl.ds(r - 1, 8), pl.ds(r + 1, 8)
    near = []
    for p in range(params):
        value = values[p]
        ends = jnp.zeros((8, 128), jnp.float32)
        for z in range(layers):
            here = (lane == 10 * z + 4) | (lane == 10 * z + 5)
            ends = jnp.where(here, roll(core_ref[p, z, rows, :], 10 * z + 5), ends)
        left = roll(jnp.where(col == 4, ends, value), 1)
        right = roll(jnp.where(col == 5, ends, value), 127)
        if outer_ref is not None:
            outer = outer_ref[p, rows, :]
            left = jnp.where(col == 0, outer, left)
            right = jnp.where(col == 9, outer, right)
        below = jnp.where(lane < COLS, value, roll(value, COLS))
        above = jnp.where(lane >= COLS * (layers - 1), value, roll(value, 128 - COLS))
        total = (left + right) + (below + above)
        near.append(total + (ref[p, before, :] + ref[p, after, :]))
    return near


def spread_ends(ends_ref, values, rows):
    params, layers = ends_ref.shape[:2]
    for p in range(params):
        for z in range(layers):
            ends_ref[p, z, rows, :] = roll(values[p], 123 - 10 * z)


def base_of(e):
    return 1.5 * total_of([x * x for x in e]) + 5.0


def inner_of(e, u):
    return 3.0 * total_of([x * y for x, y in zip(e, u)])


def forward(
    order_ref, map_ref, row_a_ref, row_b_ref, far_a_ref, far_b_ref, strip_a_ref, strip_b_ref, table_ref,
    final_ref, e_refs, rate_refs, se_refs, m_ref, ms_ref,
    first_strip_ref, outer_ref, ends_ref, g_ref, gs_ref,
):
    params, layers = order_ref.shape[:2]
    tile = (8, 128)
    col = lanes(tile) % COLS
    maps = row_places(params, layers)[0]
    strip_refs = [first_strip_ref, *se_refs]
    every = range(params)

    odd = is_odd("wide")
    from_before = (jnp.where(odd, 1, 0), jnp.where(odd, 0, 1))

    def place(z, carry):
        for ref, before in zip((row_a_ref, row_b_ref), from_before):
            k, target = maps + z * MAP_EDGE + before * (MAP_EDGE - 8), pl.ds(20 - 16 * before, 8)
            g_ref[z, target, :] = ref[pl.ds(k, 8), :]
            for p in every:
                k = LEAD + (p * layers + z) * EDGE + before * (EDGE - 8)
                e_refs[0][p, z, target, :] = ref[pl.ds(k, 8), :]
        for p in every:
            e_refs[0][p, z, 12:20, :] = order_ref[p, z]
        return carry

    lax.fori_loop(0, layers, place, 0)

    sides = side_strips(params, strip_a_ref, strip_b_ref)
    order, _, cells = merged_strips(params, strip_a_ref, strip_b_ref)
    n = CORNER[0]
    for p in every:
        ref = first_strip_ref.at[p]
        ref[4:12, :] = jnp.zeros(tile, jnp.float32)
        ref[20:28, :] = jnp.zeros(tile, jnp.float32)
        a, b = far_a_ref[n * p : n * p + n, :], far_b_ref[n * p : n * p + n, :]
        ref[12 - n : 12, :] = jnp.where(odd, a, b)
        ref[12:20, :] = order[p]
        ref[20 : 20 + n, :] = jnp.where(odd, b, a)
        outer_ref[p, 12:20, :] = jnp.where(col == 0, roll(sides[p][0], 1), roll(sides[p][1], 127))
    at, n = params * (CORNER[0] + CORNER[1]), CORNER[2]
    gs_ref[...] = jnp.zeros_like(gs_ref)
    a, b = far_a_ref[at : at + n, :], far_b_ref[at : at + n, :]
    gs_ref[12 - n : 12, :] = jnp.where(odd, a, b)
    gs_ref[12:20, :] = cells
    gs_ref[20 : 20 + n, :] = jnp.where(odd, b, a)

    def first_ends(rows, r):
        spread_ends(ends_ref, [first_strip_ref[p, rows, :] for p in every], rows)

    each_window((7, 3, 17), first_ends)

    def lookup(index, which):
        values = jnp.broadcast_to(table_ref[which // 2 : which // 2 + 1, :], tile)
        return jnp.take_along_axis(values, index + 64 * (which % 2), axis=1, mode="promise_in_bounds")

    for i in range(3):
        r = 4 + 8 * i
        for z in range(layers):
            index = map_ref[z] if i == 1 else g_ref[z, r : r + 8, :].astype(jnp.int32) & 63
            m_ref[z, r : r + 8, :] = lookup(index, 3 * i + 1)
        index = gs_ref[r : r + 8, :].astype(jnp.int32) & 63
        ms_ref[r : r + 8, :] = jnp.where(col < 5, lookup(index, 3 * i), lookup(index, 3 * i + 2))

    def step(t, windows, strip_windows, end_windows):
        old, old_strip = e_refs[t], strip_refs[t]
        last = t == ITERS - 1

        def core(z, i, rows, r):
            base = base_of([old[p, z, rows, :] for p in every])
            m = m_ref[z, rows, :]
            stores = []
            for p in every:
                e = old[p, z, rows, :]
                rate = e * (base - 0.5 * (e * e)) - neighbours(old, ends_ref, e, p, z, rows, r)
                new = e - m * rate
                stores.append(put(rate_refs[t], (p, z, rows, slice(None)), rate))
                if last:
                    stores.append(put(final_ref, (p, z), new))
                else:
                    stores.append(put(e_refs[t + 1], (p, z, rows, slice(None)), new))
            return stores

        each_tile(layers, windows, core)
        if last:
            return

        def strip(rows, r):
            e = [old_strip[p, rows, :] for p in every]
            m = ms_ref[rows, :]
            base = base_of(e)
            near = strip_neighbours(old_strip, old, e, rows, r, outer_ref if t == 0 else None)
            for p in every:
                rate = e[p] * (base - 0.5 * (e[p] * e[p])) - near[p]
                strip_refs[t + 1][p, rows, :] = e[p] - m * rate

        each_window(strip_windows, strip)

        def ends(rows, r):
            spread_ends(ends_ref, [strip_refs[t + 1][p, rows, :] for p in every], rows)

        each_window(end_windows, ends)

    step(0, (7, 3, 17), (8, 2, 16), (8, 2, 16))
    step(1, (8, 2, 16), (8, 2, 16), (8, 2, 16))
    step(2, (8, 2, 16), (8, 2, 16), (12, 1, 12))
    step(3, (12, 1, 12), None, None)


def backward(
    cot_ref, map_ref, row_a_ref, row_b_ref, far_a_ref, far_b_ref, strip_a_ref, strip_b_ref,
    e_refs, rate_refs, se_refs, m_ref, ms_ref,
    adjoint_ref, sums_ref,
    lam_refs, slam_refs, u_refs, su_refs, ends_ref, work_ref, binned_ref,
):
    params, layers = cot_ref.shape[:2]
    cots = row_places(params, layers)[1]
    tile = (8, 128)
    every = range(params)

    odd = is_odd("wide")
    from_before = (jnp.where(odd, 1, 0), jnp.where(odd, 0, 1))

    def place(z, carry):
        for ref, base, before in zip((row_a_ref, row_b_ref), (cots, 0), from_before):
            rows = pl.ds(20 - 16 * before, 8)
            m = m_ref[z, rows, :]
            for p in every:
                k = base + LEAD + (p * layers + z) * ADJ_EDGE + before * (ADJ_EDGE - 8)
                value = ref[pl.ds(k, 8), :]
                lam_refs[0][p, z, rows, :] = value
                u_refs[0][p, z, rows, :] = m * value
        m = m_ref[z, 12:20, :]
        for p in every:
            lam_refs[0][p, z, 12:20, :] = cot_ref[p, z]
            u_refs[0][p, z, 12:20, :] = m * cot_ref[p, z]
        return carry

    lax.fori_loop(0, layers, place, 0)
    _, cot, _ = merged_strips(params, strip_a_ref, strip_b_ref)
    n = CORNER[1]
    for p in every:
        at = params * CORNER[0] + n * p
        ref = slam_refs[0].at[p]
        ref[4:12, :] = jnp.zeros(tile, jnp.float32)
        ref[20:28, :] = jnp.zeros(tile, jnp.float32)
        a, b = far_a_ref[at : at + n, :], far_b_ref[at : at + n, :]
        ref[12 - n : 12, :] = jnp.where(odd, a, b)
        ref[12:20, :] = cot[p]
        ref[20 : 20 + n, :] = jnp.where(odd, b, a)
        for r in (4, 12, 20):
            su_refs[0][p, r : r + 8, :] = ms_ref[r : r + 8, :] * ref[r : r + 8, :]

    def spread(slot, windows):
        def ends(rows, r):
            spread_ends(ends_ref, [su_refs[slot][p, rows, :] for p in every], rows)

        each_window(windows, ends)

    def step(t, slot, windows, strip_windows, end_windows):
        old, old_strip = u_refs[slot], su_refs[slot]

        def core(z, i, rows, r):
            e = [e_refs[t][p, z, rows, :] for p in every]
            u = [old[p, z, rows, :] for p in every]
            base, inner = base_of(e), inner_of(e, u)
            m = m_ref[z, rows, :]
            work = total_of([lam_refs[slot][p, z, rows, :] * rate_refs[t][p, z, rows, :] for p in every])
            stores = [put(work_ref, (t - 1, z, i), work)]
            for p in every:
                e, u = e_refs[t][p, z, rows, :], old[p, z, rows, :]
                change = u * (base - 1.5 * (e * e)) + e * inner - neighbours(old, ends_ref, u, p, z, rows, r)
                new = lam_refs[slot][p, z, rows, :] - change
                stores.append(put(lam_refs[1 - slot], (p, z, rows, slice(None)), new))
                stores.append(put(u_refs[1 - slot], (p, z, rows, slice(None)), m * new))
            return stores

        each_tile(layers, windows, core)

        def strip(rows, r):
            e = [se_refs[t - 1][p, rows, :] for p in every]
            u = [old_strip[p, rows, :] for p in every]
            m = ms_ref[rows, :]
            base, inner = base_of(e), inner_of(e, u)
            near = strip_neighbours(old_strip, old, u, rows, r)
            for p in every:
                change = u[p] * (base - 1.5 * (e[p] * e[p])) + e[p] * inner - near[p]
                new = slam_refs[slot][p, rows, :] - change
                slam_refs[1 - slot][p, rows, :] = new
                su_refs[1 - slot][p, rows, :] = m * new

        each_window(strip_windows, strip)
        spread(1 - slot, end_windows)

    spread(0, (8, 2, 16))
    step(3, 0, (8, 2, 16), (8, 2, 16), (8, 2, 16))
    step(2, 1, (8, 2, 16), (8, 2, 16), (8, 2, 16))
    step(1, 0, (8, 2, 16), (12, 1, 12), (12, 1, 12))

    def last(z, i, rows, r):
        e = [e_refs[0][p, z, rows, :] for p in every]
        u = [u_refs[1][p, z, rows, :] for p in every]
        base, inner = base_of(e), inner_of(e, u)
        stores = []
        for p in every:
            e, u = e_refs[0][p, z, rows, :], u_refs[1][p, z, rows, :]
            change = u * (base - 1.5 * (e * e)) + e * inner - neighbours(u_refs[1], ends_ref, u, p, z, rows, r)
            stores.append(put(adjoint_ref, (p, z), lam_refs[1][p, z, rows, :] - change))
        return stores

    each_tile(layers, (12, 1, 12), last)

    grains = [map_ref[z] for z in range(layers)]
    cells = []
    for z in range(layers):
        upper = work_ref[0, z, 0] + work_ref[1, z, 0] + work_ref[2, z, 0]
        lower = work_ref[0, z, 1] + work_ref[1, z, 1] + work_ref[2, z, 1]
        first = total_of([lam_refs[1][p, z, 12:20, :] * rate_refs[0][p, z, 12:20, :] for p in every])
        cells.append(jnp.concatenate([upper[4:8], lower[0:4]], axis=0) + first)

    def bin_one(g, carry):
        kept = [jnp.where(grains[z] == g, cells[z], 0.0) for z in range(layers)]
        total = sum(kept[1:4], kept[0]) + sum(kept[5:8], kept[4]) + sum(kept[9:], kept[8])
        binned_ref[pl.ds(g, 1), :] = jnp.sum(total, axis=0, keepdims=True)
        return carry

    lax.fori_loop(0, binned_ref.shape[0], bin_one, 0, unroll=4)
    ones = jnp.full((8, 128), -TIME_STEP, jnp.float32)
    sums = lax.dot_general(
        ones, binned_ref[...], (((1,), (1,)), ((), ())),
        precision=lax.Precision.HIGHEST, preferred_element_type=jnp.float32,
    )
    for k in range(0, sums_ref.shape[0], 8):
        sums_ref[k : k + 8, :] = sums


def pick_owned(owned, slots_ref, sums_ref, out_ref, total_ref, dense_ref):
    base = (lax.axis_index("wide") * lax.axis_size("narrow") + lax.axis_index("narrow")) * owned
    tile = (8, 128)
    for k in range(dense_ref.shape[0]):
        dense_ref[k : k + 1, 0:64] = sums_ref[2 * k : 2 * k + 1, :]
        dense_ref[k : k + 1, 64:128] = sums_ref[2 * k + 1 : 2 * k + 2, :]
    sub = lax.broadcasted_iota(jnp.int32, tile, 0)
    blocks = total_ref.shape[0] // 8
    step = 25
    for first in range(0, blocks, step):
        some = range(first, min(first + step, blocks))

        def body(k, acc, some=some):
            shifted = jnp.broadcast_to(slots_ref[pl.ds(k, 1), :], tile) - (sub + base)
            value = jnp.broadcast_to(dense_ref[pl.ds(k, 1), :], tile)
            return tuple(a + jnp.where(shifted == 8 * j, value, 0.0) for a, j in zip(acc, some))

        zero = tuple(jnp.zeros(tile, jnp.float32) for _ in some)
        acc = lax.fori_loop(0, slots_ref.shape[0], body, zero, unroll=8)
        for a, j in zip(acc, some):
            total_ref[8 * j : 8 * j + 8, :] = a
    whole = lax.dot_general(
        jnp.ones(tile, jnp.float32), total_ref[...], (((1,), (1,)), ((), ())),
        precision=lax.Precision.HIGHEST, preferred_element_type=jnp.float32,
    )
    out_ref[...] = whole[0:1, 0:owned]


def f32(*shape):
    return jax.ShapeDtypeStruct(shape, jnp.float32)


def kernel(body, out_shape, scratch=(), name=None, cost=0, **specs):
    if cost:
        specs["cost_estimate"] = pl.CostEstimate(flops=cost, bytes_accessed=cost // 1000, transcendentals=0)
    return pl.pallas_call(
        body, out_shape=out_shape, scratch_shapes=list(scratch), name=name, **specs,
        compiler_params=pltpu.CompilerParams(vmem_limit_bytes=VMEM_LIMIT),
    )


def opposite(value, axis):
    return lax.ppermute(value, axis, [(i, (i + 2) % 4) for i in range(4)])


def swapped(value, axis, count, partner):
    step = [1 if (i + partner) % 2 == 0 else -1 for i in range(count)]
    return lax.ppermute(value, axis, [(i, (i + by) % count) for i, by in enumerate(step)])


def per_device(counts, order_init, cotangent, grain_map, brick_grains, grain_slot, mobility):
    wide_count, narrow_count = counts
    params, layers = order_init.shape[:2]
    assert order_init.shape[2:] == (8, 128) and layers * COLS < 128
    owned = mobility.shape[0]
    listed = brick_grains.shape[1]
    bricks = brick_grains.shape[0]

    both = ("wide", "narrow")
    count = wide_count * narrow_count
    small = counts == (4, 4)
    assert listed == 64 and bricks == count and count % 16 == 0

    owned_rows = -(-owned // 128)
    block_rows = narrow_count * owned_rows
    strip_rows = 8 * (params + 1)
    edge_rows = row_places(params, layers)[1]
    cot_rows = params * layers * ADJ_EDGE + 2 * LEAD
    vmem = lambda *shape: pltpu.VMEM(shape, jnp.float32)

    arguments = (
        order_init, grain_map, cotangent, mobility.reshape(1, owned), brick_grains, grain_slot.reshape(-1, 128)
    )
    here, anywhere = pl.BlockSpec(memory_space=pltpu.VMEM), pl.BlockSpec(memory_space=pl.ANY)
    *fetched, near_a, row_b = kernel(
        pack_rows,
        tuple(jax.ShapeDtypeStruct(x.shape, x.dtype) for x in arguments)
        + (f32(edge_rows + cot_rows, 128), f32(edge_rows, 128)),
        (pltpu.SemaphoreType.DMA((len(arguments),)),), name="pack_rows",
        in_specs=[pl.BlockSpec(memory_space=pltpu.HBM)] * len(arguments),
    )(*(pltpu.with_memory_space_constraint(x, pltpu.HBM) for x in arguments))
    order_init, grain_map, cotangent, mobility_row, brick_grains, grain_slot = fetched
    strip_a, strip_b, block = kernel(
        pack_strips, (f32(strip_rows + block_rows, 128),) * 2 + (f32(block_rows, 128),),
        name="pack_strips", in_specs=[here] * 4 + [anywhere],
    )(order_init, grain_map, cotangent, mobility_row, row_b)
    row_b = swapped(row_b, "wide", wide_count, 1)
    near_a = swapped(near_a, "wide", wide_count, 0)
    strip_b = swapped(strip_b, "narrow", narrow_count, 1)
    strip_a = swapped(strip_a, "narrow", narrow_count, 0)
    others = [opposite(block, "narrow")] if small else []

    corners = corner_rows(params)
    far_a, far_b, block = kernel(
        functools.partial(pack_far, params),
        (f32(corners + block_rows, 128),) * 2 + (f32(block_rows, 128),), name="pack_far", cost=0,
    )(strip_a, strip_b, block, *others)
    far_b = swapped(far_b, "wide", wide_count, 1)
    far_a = swapped(far_a, "wide", wide_count, 0)
    slots = kernel(
        find_slots, jax.ShapeDtypeStruct((bricks // 2, 128), jnp.int32), name="find_slots",
        in_specs=[here, here, anywhere],
    )(brick_grains, grain_slot, block)
    cot_b = kernel(pack_cot, f32(cot_rows, 128), name="pack_cot", in_specs=[here, anywhere])(cotangent, far_a)
    cot_b = swapped(cot_b, "wide", wide_count, 1)

    if small:
        mobs = (block, far_a, far_b, opposite(block, "wide"))
    else:
        own = jnp.pad(mobility, (0, -owned % 128)).reshape(owned_rows, 128)
        mobs = (lax.all_gather(own, both, axis=0, tiled=True),)
    table = kernel(
        functools.partial(find_mobility, counts, owned), f32(8, 128),
        (pltpu.VMEM((8, 128), jnp.int32), vmem(wide_count * block_rows, 128)),
        name="find_mobility", cost=2_500_000_000,
    )(slots, *mobs)

    padded, strip = (params, layers, ROWS, 128), (params, ROWS, 128)
    final, states, rate, halos, m, ms = kernel(
        forward,
        (
            f32(*order_init.shape), [f32(*padded)] * ITERS, [f32(*padded)] * ITERS,
            [f32(*strip)] * (ITERS - 1), f32(layers, ROWS, 128), f32(ROWS, 128),
        ),
        (vmem(*strip), vmem(*strip), vmem(*padded), vmem(layers, ROWS, 128), vmem(ROWS, 128)),
        name="forward", cost=0,
    )(order_init, grain_map, near_a, row_b, far_a, far_b, strip_a, strip_b, table)
    adjoint, sums = kernel(
        backward,
        (f32(*order_init.shape), f32(bricks, listed)),
        (
            [vmem(*padded)] * 2, [vmem(*strip)] * 2, [vmem(*padded)] * 2, [vmem(*strip)] * 2, vmem(*padded),
            vmem(ITERS - 1, layers, 2, 8, 128), vmem(listed, 128),
        ),
        name="backward",
    )(
        cotangent, grain_map, near_a, cot_b, far_a, far_b, strip_a, strip_b,
        states, rate, halos, m, ms,
    )

    sums = lax.all_to_all(sums, both, 0, 0, tiled=True)
    grads = kernel(
        functools.partial(pick_owned, owned), f32(1, owned),
        (vmem(owned + -owned % 8, 128), vmem(bricks // 2, 128)), name="pick_owned",
    )(slots, sums)
    return final, adjoint, grads.reshape(owned)


def solution(mesh):
    counts = (mesh.shape["wide"], mesh.shape["narrow"])
    field = P("groups", None, "wide", "narrow")
    spread = P(("groups", "wide", "narrow"))
    return jax.shard_map(
        functools.partial(per_device, counts),
        mesh=mesh,
        in_specs=(field, field, P("groups", "wide", "narrow"), P("groups", None), P("groups"), spread),
        out_specs=(field, field, spread),
        check_vma=False,
    )
```

```python
import functools

import jax
import jax.numpy as jnp
from jax import lax
from jax.experimental import pallas as pl
from jax.experimental.pallas import tpu as pltpu
from jax.sharding import PartitionSpec as P

ITERS = 4
TIME_STEP = 0.05

EDGE = 6
MAP_EDGE = 5
ADJ_EDGE = 4
ROWS = 24
COLS = 10
LEAD = 8
CORNER = (5, 3, 4)

VMEM_LIMIT = 24 * 1024 * 1024


def lanes(shape):
    return lax.broadcasted_iota(jnp.int32, shape, len(shape) - 1)


def roll(value, shift):
    return pltpu.roll(value, shift, 1)


def is_odd(axis):
    return lax.rem(lax.axis_index(axis), 2) == 1


def pack_strips(order_ref, map_ref, cot_ref, mob_ref, after_ref, strip_a_ref, strip_b_ref, block_ref):
    params, layers = order_ref.shape[:2]
    odd = is_odd("narrow")
    lane = lanes((8, 128))
    zero = jnp.zeros((8, 128), jnp.float32)

    def span(first, size):
        return ((lane - first) & 127) < size

    for field in range(params + 1):
        right, left = zero, zero
        for z in range(layers):
            value = order_ref[field, z] if field < params else map_ref[z].astype(jnp.float32)
            moved = roll(value, 10 * z + 5)
            right = jnp.where(span(10 * z - 1, 6), moved, right)
            left = jnp.where(span(10 * z + 5, 6), moved, left)
            if field < params:
                right = jnp.where(span(10 * z + 5, 4), roll(cot_ref[field, z], 10 * z + 9), right)
                left = jnp.where(span(10 * z + 1, 4), roll(cot_ref[field, z], 10 * z + 1), left)
        rows = slice(8 * field, 8 * field + 8)
        strip_a_ref[rows, :] = jnp.where(odd, left, right)
        strip_b_ref[rows, :] = jnp.where(odd, right, left)
    owned = mob_ref.shape[1]
    owned_rows = -(-owned // 128)
    block_ref[...] = jnp.zeros_like(block_ref)
    first = lax.axis_index("narrow") * owned_rows
    for i in range(owned_rows):
        size = min(128, owned - 128 * i)
        row = mob_ref[0:1, 128 * i : 128 * i + size]
        if size < 128:
            row = jnp.concatenate([row, jnp.zeros((1, 128 - size), jnp.float32)], axis=1)
        block_ref[pl.ds(first + i, 1), :] = row
    for ref in (strip_a_ref, strip_b_ref):
        ref[8 * (params + 1) :, :] = block_ref[...]


def pack_rows(*refs):
    count = (len(refs) - 3) // 2
    sources, targets = refs[:count], refs[count : 2 * count]
    near_a_ref, row_b_ref, sems = refs[2 * count :]
    copies = [pltpu.make_async_copy(a, b, sems.at[i]) for i, (a, b) in enumerate(zip(sources, targets))]
    for copy in copies:
        copy.start()
    order_ref, map_ref, cot_ref = targets[:3]
    params, layers = order_ref.shape[:2]
    maps, cots = row_places(params, layers)
    gap = jnp.zeros((LEAD, 128), jnp.float32)
    odd = is_odd("wide")
    last = (jnp.where(odd, 0, 1), jnp.where(odd, 1, 0))
    row_refs = (near_a_ref, row_b_ref)
    for ref in row_refs:
        ref[0:LEAD, :] = gap
        ref[maps - LEAD : maps, :] = gap
        ref[cots - 2 * LEAD : cots - LEAD, :] = gap
        ref[cots - LEAD : cots, :] = gap
    near_a_ref[cots : cots + LEAD, :] = gap
    near_a_ref[near_a_ref.shape[0] - LEAD :, :] = gap
    copies[0].wait()
    for p in range(params):
        for z in range(layers):
            k = LEAD + (p * layers + z) * EDGE
            for ref, is_last in zip(row_refs, last):
                ref[k : k + EDGE, :] = order_ref[p, z, pl.ds((8 - EDGE) * is_last, EDGE), :]
    for copy in copies[1:]:
        copy.wait()
    for z in range(layers):
        k = maps + z * MAP_EDGE
        for ref, is_last in zip(row_refs, last):
            ref[k : k + MAP_EDGE, :] = map_ref[z, pl.ds((8 - MAP_EDGE) * is_last, MAP_EDGE), :].astype(jnp.float32)
    rows = pl.ds((8 - ADJ_EDGE) * last[0], ADJ_EDGE)
    for p in range(params):
        for z in range(layers):
            k = cots + LEAD + (p * layers + z) * ADJ_EDGE
            near_a_ref[k : k + ADJ_EDGE, :] = cot_ref[p, z, rows, :]


def pack_cot(cot_ref, after_ref, out_ref):
    params, layers = cot_ref.shape[:2]
    out_ref[0:LEAD, :] = jnp.zeros((LEAD, 128), jnp.float32)
    out_ref[out_ref.shape[0] - LEAD :, :] = jnp.zeros((LEAD, 128), jnp.float32)
    rows = pl.ds(jnp.where(is_odd("wide"), 8 - ADJ_EDGE, 0), ADJ_EDGE)
    for p in range(params):
        for z in range(layers):
            k = LEAD + (p * layers + z) * ADJ_EDGE
            out_ref[k : k + ADJ_EDGE, :] = cot_ref[p, z, rows, :]


def row_places(params, layers):
    maps = LEAD + params * layers * EDGE + LEAD
    length = maps + layers * MAP_EDGE
    return maps, length + -length % 8 + LEAD


def corner_rows(params):
    return -(-(params * (CORNER[0] + CORNER[1]) + CORNER[2]) // 8) * 8


def side_strips(params, strip_a_ref, strip_b_ref):
    odd = is_odd("narrow")
    fields = []
    for field in range(params + 1):
        rows = slice(8 * field, 8 * field + 8)
        a, b = strip_a_ref[rows, :], strip_b_ref[rows, :]
        fields.append((jnp.where(odd, a, b), jnp.where(odd, b, a)))
    return fields


def merged_strips(params, *strip_refs):
    first = lanes((8, 128)) % COLS < 5
    fields = side_strips(params, *strip_refs)
    order = [jnp.where(first, a, b) for a, b in fields[:params]]
    cot = [jnp.where(first, roll(a, 124), roll(b, 4)) for a, b in fields[:params]]
    return order, cot, jnp.where(first, *fields[params])


def pack_far(params, strip_a_ref, strip_b_ref, block_ref, *refs):
    *other_refs, far_a_ref, far_b_ref, out_block_ref = refs
    at = 8 * (params + 1)
    mobs = corner_rows(params)
    block = block_ref[...] + strip_a_ref[at:, :] + strip_b_ref[at:, :]
    for ref in other_refs:
        block = block + ref[...]
    out_block_ref[...] = block
    at = 0
    odd = is_odd("wide")
    order, cot, cells = merged_strips(params, strip_a_ref, strip_b_ref)
    for n, fields in zip(CORNER, (order, cot, [cells])):
        for both in fields:
            far_a_ref[at : at + n, :] = jnp.where(odd, both[0:n], both[8 - n : 8])
            far_b_ref[at : at + n, :] = jnp.where(odd, both[8 - n : 8], both[0:n])
            at += n
    for ref in (far_a_ref, far_b_ref):
        ref[at:mobs, :] = jnp.zeros((mobs - at, 128), jnp.float32)
        ref[mobs:, :] = block


def find_slots(bricks_ref, slot_ref, after_ref, out_ref):
    count, listed = bricks_ref.shape
    rows = slot_ref.shape[0]
    for k in range(0, out_ref.shape[0], 8):
        pairs = [
            jnp.concatenate([bricks_ref[2 * j : 2 * j + 1, :], bricks_ref[2 * j + 1 : 2 * j + 2, :]], axis=1)
            for j in range(k, k + 8)
        ]
        grain = jnp.concatenate(pairs, axis=0)
        row, col = grain >> 7, grain & 127

        def body(r, found, row=row, col=col):
            table = jnp.broadcast_to(slot_ref[pl.ds(r, 1), :], (8, 128))
            taken = jnp.take_along_axis(table, col, axis=1, mode="promise_in_bounds")
            return jnp.where(row == r, taken, found)

        out_ref[k : k + 8, :] = lax.fori_loop(0, rows, body, jnp.zeros((8, 128), jnp.int32), unroll=7)


def find_mobility(counts, owned, slots_ref, *refs):
    *mob_refs, table_ref, near_ref, all_ref = refs
    wide_count, narrow_count = counts
    tile = (8, 128)
    wide, narrow = lax.axis_index("wide"), lax.axis_index("narrow")
    if len(mob_refs) == 1:
        mob_ref = mob_refs[0]
    else:
        block_ref, far_a_ref, far_b_ref, other_ref = mob_refs
        mob_ref = all_ref
        size = block_ref.shape[0]
        odd = is_odd("wide")
        step = jnp.where(odd, 1, 3)
        for place, ref in (
            (wide, block_ref), (wide + 4 - step, far_a_ref), (wide + step, far_b_ref), (wide + 2, other_ref)
        ):
            at = pl.multiple_of(size * (place & 3), size)
            mob_ref[pl.ds(at, size), :] = ref[ref.shape[0] - size :, :]
    near_ref[...] = jnp.zeros_like(near_ref)
    for k in range(9):
        w = lax.rem(wide + k // 3 - 1 + wide_count, wide_count)
        n = lax.rem(narrow + k % 3 - 1 + narrow_count, narrow_count)
        brick = w * narrow_count + n
        row = slots_ref[pl.ds(brick >> 1, 1), :]
        half = jnp.where((brick & 1) == 0, row[:, 0:64], row[:, 64:128])
        near_ref[k // 2 : k // 2 + 1, 64 * (k % 2) : 64 * (k % 2) + 64] = half
    slot = near_ref[...]
    owned_rows = -(-owned // 128)
    owner = jnp.floor((slot.astype(jnp.float32) + 0.5) * (1.0 / owned)).astype(jnp.int32)
    inner = slot - owner * owned
    row = owner * owned_rows + (inner >> 7)
    place = inner & 127

    def body(r, found):
        values = jnp.broadcast_to(mob_ref[pl.ds(r, 1), :], tile)
        taken = jnp.take_along_axis(values, place, axis=1, mode="promise_in_bounds")
        return jnp.where(row == r, taken, found)

    found = lax.fori_loop(0, mob_ref.shape[0], body, jnp.zeros(tile, jnp.float32), unroll=16)
    table_ref[...] = TIME_STEP * found


def total_of(values):
    while len(values) > 1:
        values = [a + b for a, b in zip(values[::2], values[1::2])]
    return values[0]


def each_tile(layers, windows, body):
    start, count, most = windows
    nothing = lax.axis_index("wide") >> 20
    stores = []
    for z in range(layers):
        for i in range(count):
            stores += body(z, i, jnp.minimum(start + 8 * i, most) + nothing)
        if len(stores) >= 32 or z == layers - 1:
            for store in stores:
                store()
            stores = []


def each_window(windows, body):
    def one(i, carry):
        body(windows[0] + 8 * i)
        return carry

    lax.fori_loop(0, windows[1], one, 0)


def put(ref, index, value):
    def store():
        ref[index] = value

    return store


def neighbours(ref, ends_ref, value, p, z, r):
    layers = ref.shape[1]
    lane = lanes((8, 128))
    rows, before, after = pl.ds(r, 8), pl.ds(r - 1, 8), pl.ds(r + 1, 8)
    below, above = max(z - 1, 0), min(z + 1, layers - 1)
    ends = ends_ref[p, z, rows, :]
    left = roll(jnp.where(lane == 127, ends, value), 1)
    right = roll(jnp.where(lane == 0, ends, value), 127)
    total = (left + right) + (ref[p, z, before, :] + ref[p, z, after, :])
    return total + (ref[p, below, rows, :] + ref[p, above, rows, :])


def strip_neighbours(ref, core_ref, values, r, outer_ref=None):
    params, layers = core_ref.shape[:2]
    lane = lanes((8, 128))
    col = lane % COLS
    rows, before, after = pl.ds(r, 8), pl.ds(r - 1, 8), pl.ds(r + 1, 8)
    near = []
    for p in range(params):
        value = values[p]
        ends = jnp.zeros((8, 128), jnp.float32)
        for z in range(layers):
            here = (lane == 10 * z + 4) | (lane == 10 * z + 5)
            ends = jnp.where(here, roll(core_ref[p, z, rows, :], 10 * z + 5), ends)
        left = roll(jnp.where(col == 4, ends, value), 1)
        right = roll(jnp.where(col == 5, ends, value), 127)
        if outer_ref is not None:
            outer = outer_ref[p, rows, :]
            left = jnp.where(col == 0, outer, left)
            right = jnp.where(col == 9, outer, right)
        below = jnp.where(lane < COLS, value, roll(value, COLS))
        above = jnp.where(lane >= COLS * (layers - 1), value, roll(value, 128 - COLS))
        total = (left + right) + (below + above)
        near.append(total + (ref[p, before, :] + ref[p, after, :]))
    return near


def spread_ends(ends_ref, values, rows):
    params, layers = ends_ref.shape[:2]
    for p in range(params):
        for z in range(layers):
            ends_ref[p, z, rows, :] = roll(values[p], 123 - 10 * z)


def base_of(e):
    return 1.5 * total_of([x * x for x in e]) + 5.0


def inner_of(e, u):
    return 3.0 * total_of([x * y for x, y in zip(e, u)])


def forward(
    order_ref, map_ref, row_a_ref, row_b_ref, far_a_ref, far_b_ref, strip_a_ref, strip_b_ref, table_ref,
    final_ref, e_refs, rate_refs, se_refs, m_ref, ms_ref,
    first_strip_ref, outer_ref, ends_ref, g_ref, gs_ref,
):
    params, layers = order_ref.shape[:2]
    tile = (8, 128)
    col = lanes(tile) % COLS
    maps = row_places(params, layers)[0]
    strip_refs = [first_strip_ref, *se_refs]
    every = range(params)

    odd = is_odd("wide")
    from_before = (jnp.where(odd, 1, 0), jnp.where(odd, 0, 1))

    def place(z, carry):
        for ref, before in zip((row_a_ref, row_b_ref), from_before):
            k, target = maps + z * MAP_EDGE + before * (MAP_EDGE - 8), pl.ds(16 - 16 * before, 8)
            g_ref[z, target, :] = ref[pl.ds(k, 8), :]
            for p in every:
                k = LEAD + (p * layers + z) * EDGE + before * (EDGE - 8)
                e_refs[0][p, z, target, :] = ref[pl.ds(k, 8), :]
        for p in every:
            e_refs[0][p, z, 8:16, :] = order_ref[p, z]
        return carry

    lax.fori_loop(0, layers, place, 0)

    sides = side_strips(params, strip_a_ref, strip_b_ref)
    order, _, cells = merged_strips(params, strip_a_ref, strip_b_ref)
    n = CORNER[0]
    for p in every:
        ref = first_strip_ref.at[p]
        ref[0:8, :] = jnp.zeros(tile, jnp.float32)
        ref[16:24, :] = jnp.zeros(tile, jnp.float32)
        a, b = far_a_ref[n * p : n * p + n, :], far_b_ref[n * p : n * p + n, :]
        ref[8 - n : 8, :] = jnp.where(odd, a, b)
        ref[8:16, :] = order[p]
        ref[16 : 16 + n, :] = jnp.where(odd, b, a)
        outer_ref[p, 8:16, :] = jnp.where(col == 0, roll(sides[p][0], 1), roll(sides[p][1], 127))
    at, n = params * (CORNER[0] + CORNER[1]), CORNER[2]
    gs_ref[...] = jnp.zeros_like(gs_ref)
    a, b = far_a_ref[at : at + n, :], far_b_ref[at : at + n, :]
    gs_ref[8 - n : 8, :] = jnp.where(odd, a, b)
    gs_ref[8:16, :] = cells
    gs_ref[16 : 16 + n, :] = jnp.where(odd, b, a)
    for r in (0, 8, 16):
        rows = slice(r, r + 8)
        spread_ends(ends_ref, [first_strip_ref[p, rows, :] for p in every], rows)

    def lookup(index, which):
        values = jnp.broadcast_to(table_ref[which // 2 : which // 2 + 1, :], tile)
        return jnp.take_along_axis(values, index + 64 * (which % 2), axis=1, mode="promise_in_bounds")

    for i in range(3):
        r = 8 * i
        for z in range(layers):
            index = map_ref[z] if i == 1 else g_ref[z, r : r + 8, :].astype(jnp.int32) & 63
            m_ref[z, r : r + 8, :] = lookup(index, 3 * i + 1)
        index = gs_ref[r : r + 8, :].astype(jnp.int32) & 63
        ms_ref[r : r + 8, :] = jnp.where(col < 5, lookup(index, 3 * i), lookup(index, 3 * i + 2))

    def step(t, windows, strip_windows, end_windows):
        old, old_strip = e_refs[t], strip_refs[t]
        last = t == ITERS - 1

        def core(z, i, r):
            rows = pl.ds(r, 8)
            base = base_of([old[p, z, rows, :] for p in every])
            m = m_ref[z, rows, :]
            stores = []
            for p in every:
                e = old[p, z, rows, :]
                rate = e * (base - 0.5 * (e * e)) - neighbours(old, ends_ref, e, p, z, r)
                new = e - m * rate
                stores.append(put(rate_refs[t], (p, z, rows, slice(None)), rate))
                if last:
                    stores.append(put(final_ref, (p, z), new))
                else:
                    stores.append(put(e_refs[t + 1], (p, z, rows, slice(None)), new))
            return stores

        each_tile(layers, windows, core)
        if last:
            return

        def strip(r):
            rows = pl.ds(r, 8)
            e = [old_strip[p, rows, :] for p in every]
            m = ms_ref[rows, :]
            base = base_of(e)
            near = strip_neighbours(old_strip, old, e, r, outer_ref if t == 0 else None)
            for p in every:
                rate = e[p] * (base - 0.5 * (e[p] * e[p])) - near[p]
                strip_refs[t + 1][p, rows, :] = e[p] - m * rate

        each_window(strip_windows, strip)

        def ends(r):
            rows = pl.ds(r, 8)
            spread_ends(ends_ref, [strip_refs[t + 1][p, rows, :] for p in every], rows)

        each_window(end_windows, ends)

    step(0, (3, 3, 13), (4, 2), (4, 2))
    step(1, (4, 2, 12), (4, 2), (4, 2))
    step(2, (4, 2, 12), (4, 2), (8, 1))
    step(3, (8, 1, 8), None, None)


def backward(
    cot_ref, map_ref, row_a_ref, row_b_ref, far_a_ref, far_b_ref, strip_a_ref, strip_b_ref,
    e_refs, rate_refs, se_refs, m_ref, ms_ref,
    adjoint_ref, sums_ref,
    lam_refs, slam_refs, u_refs, su_refs, ends_ref, work_ref, binned_ref,
):
    params, layers = cot_ref.shape[:2]
    cots = row_places(params, layers)[1]
    tile = (8, 128)
    every = range(params)

    odd = is_odd("wide")
    from_before = (jnp.where(odd, 1, 0), jnp.where(odd, 0, 1))

    def place(z, carry):
        for ref, base, before in zip((row_a_ref, row_b_ref), (cots, 0), from_before):
            rows = pl.ds(16 - 16 * before, 8)
            m = m_ref[z, rows, :]
            for p in every:
                k = base + LEAD + (p * layers + z) * ADJ_EDGE + before * (ADJ_EDGE - 8)
                value = ref[pl.ds(k, 8), :]
                lam_refs[0][p, z, rows, :] = value
                u_refs[0][p, z, rows, :] = m * value
        m = m_ref[z, 8:16, :]
        for p in every:
            lam_refs[0][p, z, 8:16, :] = cot_ref[p, z]
            u_refs[0][p, z, 8:16, :] = m * cot_ref[p, z]
        return carry

    lax.fori_loop(0, layers, place, 0)
    _, cot, _ = merged_strips(params, strip_a_ref, strip_b_ref)
    n = CORNER[1]
    for p in every:
        at = params * CORNER[0] + n * p
        ref = slam_refs[0].at[p]
        ref[0:8, :] = jnp.zeros(tile, jnp.float32)
        ref[16:24, :] = jnp.zeros(tile, jnp.float32)
        a, b = far_a_ref[at : at + n, :], far_b_ref[at : at + n, :]
        ref[8 - n : 8, :] = jnp.where(odd, a, b)
        ref[8:16, :] = cot[p]
        ref[16 : 16 + n, :] = jnp.where(odd, b, a)
        for r in (0, 8, 16):
            su_refs[0][p, r : r + 8, :] = ms_ref[r : r + 8, :] * ref[r : r + 8, :]

    def spread(slot, windows):
        def ends(r):
            rows = pl.ds(r, 8)
            spread_ends(ends_ref, [su_refs[slot][p, rows, :] for p in every], rows)

        each_window(windows, ends)

    def step(t, slot, windows, strip_windows, end_windows):
        old, old_strip = u_refs[slot], su_refs[slot]

        def core(z, i, r):
            rows = pl.ds(r, 8)
            e = [e_refs[t][p, z, rows, :] for p in every]
            u = [old[p, z, rows, :] for p in every]
            base, inner = base_of(e), inner_of(e, u)
            m = m_ref[z, rows, :]
            work = total_of([lam_refs[slot][p, z, rows, :] * rate_refs[t][p, z, rows, :] for p in every])
            stores = [put(work_ref, (t - 1, z, i), work)]
            for p in every:
                e, u = e_refs[t][p, z, rows, :], old[p, z, rows, :]
                change = u * (base - 1.5 * (e * e)) + e * inner - neighbours(old, ends_ref, u, p, z, r)
                new = lam_refs[slot][p, z, rows, :] - change
                stores.append(put(lam_refs[1 - slot], (p, z, rows, slice(None)), new))
                stores.append(put(u_refs[1 - slot], (p, z, rows, slice(None)), m * new))
            return stores

        each_tile(layers, windows, core)

        def strip(r):
            rows = pl.ds(r, 8)
            e = [se_refs[t - 1][p, rows, :] for p in every]
            u = [old_strip[p, rows, :] for p in every]
            m = ms_ref[rows, :]
            base, inner = base_of(e), inner_of(e, u)
            near = strip_neighbours(old_strip, old, u, r)
            for p in every:
                change = u[p] * (base - 1.5 * (e[p] * e[p])) + e[p] * inner - near[p]
                new = slam_refs[slot][p, rows, :] - change
                slam_refs[1 - slot][p, rows, :] = new
                su_refs[1 - slot][p, rows, :] = m * new

        each_window(strip_windows, strip)
        spread(1 - slot, end_windows)

    spread(0, (4, 2))
    step(3, 0, (4, 2, 12), (4, 2), (4, 2))
    step(2, 1, (4, 2, 12), (4, 2), (4, 2))
    step(1, 0, (4, 2, 12), (8, 1), (8, 1))

    def last(z, i, r):
        rows = pl.ds(r, 8)
        e = [e_refs[0][p, z, rows, :] for p in every]
        u = [u_refs[1][p, z, rows, :] for p in every]
        base, inner = base_of(e), inner_of(e, u)
        stores = []
        for p in every:
            e, u = e_refs[0][p, z, rows, :], u_refs[1][p, z, rows, :]
            change = u * (base - 1.5 * (e * e)) + e * inner - neighbours(u_refs[1], ends_ref, u, p, z, r)
            stores.append(put(adjoint_ref, (p, z), lam_refs[1][p, z, rows, :] - change))
        return stores

    each_tile(layers, (8, 1, 8), last)

    grains = [map_ref[z] for z in range(layers)]
    cells = []
    for z in range(layers):
        upper = work_ref[0, z, 0] + work_ref[1, z, 0] + work_ref[2, z, 0]
        lower = work_ref[0, z, 1] + work_ref[1, z, 1] + work_ref[2, z, 1]
        first = total_of([lam_refs[1][p, z, 8:16, :] * rate_refs[0][p, z, 8:16, :] for p in every])
        cells.append(jnp.concatenate([upper[4:8], lower[0:4]], axis=0) + first)

    def bin_one(g, carry):
        kept = [jnp.where(grains[z] == g, cells[z], 0.0) for z in range(layers)]
        total = sum(kept[1:4], kept[0]) + sum(kept[5:8], kept[4]) + sum(kept[9:], kept[8])
        binned_ref[pl.ds(g, 1), :] = jnp.sum(total, axis=0, keepdims=True)
        return carry

    lax.fori_loop(0, binned_ref.shape[0], bin_one, 0, unroll=4)
    ones = jnp.full((8, 128), -TIME_STEP, jnp.float32)
    sums = lax.dot_general(
        ones, binned_ref[...], (((1,), (1,)), ((), ())),
        precision=lax.Precision.HIGHEST, preferred_element_type=jnp.float32,
    )
    for k in range(0, sums_ref.shape[0], 8):
        sums_ref[k : k + 8, :] = sums


def pick_owned(owned, slots_ref, sums_ref, out_ref, total_ref, dense_ref):
    base = (lax.axis_index("wide") * lax.axis_size("narrow") + lax.axis_index("narrow")) * owned
    tile = (8, 128)
    for k in range(dense_ref.shape[0]):
        dense_ref[k : k + 1, 0:64] = sums_ref[2 * k : 2 * k + 1, :]
        dense_ref[k : k + 1, 64:128] = sums_ref[2 * k + 1 : 2 * k + 2, :]
    sub = lax.broadcasted_iota(jnp.int32, tile, 0)
    blocks = total_ref.shape[0] // 8
    step = 25
    for first in range(0, blocks, step):
        some = range(first, min(first + step, blocks))

        def body(k, acc, some=some):
            shifted = jnp.broadcast_to(slots_ref[pl.ds(k, 1), :], tile) - (sub + base)
            value = jnp.broadcast_to(dense_ref[pl.ds(k, 1), :], tile)
            return tuple(a + jnp.where(shifted == 8 * j, value, 0.0) for a, j in zip(acc, some))

        zero = tuple(jnp.zeros(tile, jnp.float32) for _ in some)
        acc = lax.fori_loop(0, slots_ref.shape[0], body, zero, unroll=8)
        for a, j in zip(acc, some):
            total_ref[8 * j : 8 * j + 8, :] = a
    whole = lax.dot_general(
        jnp.ones(tile, jnp.float32), total_ref[...], (((1,), (1,)), ((), ())),
        precision=lax.Precision.HIGHEST, preferred_element_type=jnp.float32,
    )
    out_ref[...] = whole[0:1, 0:owned]


def f32(*shape):
    return jax.ShapeDtypeStruct(shape, jnp.float32)


def kernel(body, out_shape, scratch=(), name=None, cost=0, **specs):
    if cost:
        specs["cost_estimate"] = pl.CostEstimate(flops=cost, bytes_accessed=cost // 1000, transcendentals=0)
    return pl.pallas_call(
        body, out_shape=out_shape, scratch_shapes=list(scratch), name=name, **specs,
        compiler_params=pltpu.CompilerParams(vmem_limit_bytes=VMEM_LIMIT),
    )


def opposite(value, axis):
    return lax.ppermute(value, axis, [(i, (i + 2) % 4) for i in range(4)])


def swapped(value, axis, count, partner):
    step = [1 if (i + partner) % 2 == 0 else -1 for i in range(count)]
    return lax.ppermute(value, axis, [(i, (i + by) % count) for i, by in enumerate(step)])


def per_device(counts, order_init, cotangent, grain_map, brick_grains, grain_slot, mobility):
    wide_count, narrow_count = counts
    params, layers = order_init.shape[:2]
    assert order_init.shape[2:] == (8, 128) and layers * COLS < 128
    owned = mobility.shape[0]
    listed = brick_grains.shape[1]
    bricks = brick_grains.shape[0]

    both = ("wide", "narrow")
    count = wide_count * narrow_count
    small = counts == (4, 4)
    assert listed == 64 and bricks == count and count % 16 == 0

    owned_rows = -(-owned // 128)
    block_rows = narrow_count * owned_rows
    strip_rows = 8 * (params + 1)
    edge_rows = row_places(params, layers)[1]
    cot_rows = params * layers * ADJ_EDGE + 2 * LEAD
    vmem = lambda *shape: pltpu.VMEM(shape, jnp.float32)

    arguments = (
        order_init, grain_map, cotangent, mobility.reshape(1, owned), brick_grains, grain_slot.reshape(-1, 128)
    )
    here, anywhere = pl.BlockSpec(memory_space=pltpu.VMEM), pl.BlockSpec(memory_space=pl.ANY)
    *fetched, near_a, row_b = kernel(
        pack_rows,
        tuple(jax.ShapeDtypeStruct(x.shape, x.dtype) for x in arguments)
        + (f32(edge_rows + cot_rows, 128), f32(edge_rows, 128)),
        (pltpu.SemaphoreType.DMA((len(arguments),)),), name="pack_rows",
        in_specs=[pl.BlockSpec(memory_space=pltpu.HBM)] * len(arguments),
    )(*(pltpu.with_memory_space_constraint(x, pltpu.HBM) for x in arguments))
    order_init, grain_map, cotangent, mobility_row, brick_grains, grain_slot = fetched
    strip_a, strip_b, block = kernel(
        pack_strips, (f32(strip_rows + block_rows, 128),) * 2 + (f32(block_rows, 128),),
        name="pack_strips", in_specs=[here] * 4 + [anywhere],
    )(order_init, grain_map, cotangent, mobility_row, row_b)
    row_b = swapped(row_b, "wide", wide_count, 1)
    near_a = swapped(near_a, "wide", wide_count, 0)
    strip_b = swapped(strip_b, "narrow", narrow_count, 1)
    strip_a = swapped(strip_a, "narrow", narrow_count, 0)
    others = [opposite(block, "narrow")] if small else []

    corners = corner_rows(params)
    far_a, far_b, block = kernel(
        functools.partial(pack_far, params),
        (f32(corners + block_rows, 128),) * 2 + (f32(block_rows, 128),), name="pack_far", cost=0,
    )(strip_a, strip_b, block, *others)
    far_b = swapped(far_b, "wide", wide_count, 1)
    far_a = swapped(far_a, "wide", wide_count, 0)
    slots = kernel(
        find_slots, jax.ShapeDtypeStruct((bricks // 2, 128), jnp.int32), name="find_slots",
        in_specs=[here, here, anywhere],
    )(brick_grains, grain_slot, block)
    cot_b = kernel(pack_cot, f32(cot_rows, 128), name="pack_cot", in_specs=[here, anywhere])(cotangent, far_a)
    cot_b = swapped(cot_b, "wide", wide_count, 1)

    if small:
        mobs = (block, far_a, far_b, opposite(block, "wide"))
    else:
        own = jnp.pad(mobility, (0, -owned % 128)).reshape(owned_rows, 128)
        mobs = (lax.all_gather(own, both, axis=0, tiled=True),)
    table = kernel(
        functools.partial(find_mobility, counts, owned), f32(8, 128),
        (pltpu.VMEM((8, 128), jnp.int32), vmem(wide_count * block_rows, 128)),
        name="find_mobility", cost=2_500_000_000,
    )(slots, *mobs)

    padded, strip = (params, layers, ROWS, 128), (params, ROWS, 128)
    final, states, rate, halos, m, ms = kernel(
        forward,
        (
            f32(*order_init.shape), [f32(*padded)] * ITERS, [f32(*padded)] * ITERS,
            [f32(*strip)] * (ITERS - 1), f32(layers, ROWS, 128), f32(ROWS, 128),
        ),
        (vmem(*strip), vmem(*strip), vmem(*padded), vmem(layers, ROWS, 128), vmem(ROWS, 128)),
        name="forward", cost=0,
    )(order_init, grain_map, near_a, row_b, far_a, far_b, strip_a, strip_b, table)
    adjoint, sums = kernel(
        backward,
        (f32(*order_init.shape), f32(bricks, listed)),
        (
            [vmem(*padded)] * 2, [vmem(*strip)] * 2, [vmem(*padded)] * 2, [vmem(*strip)] * 2, vmem(*padded),
            vmem(ITERS - 1, layers, 2, 8, 128), vmem(listed, 128),
        ),
        name="backward",
    )(
        cotangent, grain_map, near_a, cot_b, far_a, far_b, strip_a, strip_b,
        states, rate, halos, m, ms,
    )

    sums = lax.all_to_all(sums, both, 0, 0, tiled=True)
    grads = kernel(
        functools.partial(pick_owned, owned), f32(1, owned),
        (vmem(owned + -owned % 8, 128), vmem(bricks // 2, 128)), name="pick_owned",
    )(slots, sums)
    return final, adjoint, grads.reshape(owned)


def solution(mesh):
    counts = (mesh.shape["wide"], mesh.shape["narrow"])
    field = P("groups", None, "wide", "narrow")
    spread = P(("groups", "wide", "narrow"))
    return jax.shard_map(
        functools.partial(per_device, counts),
        mesh=mesh,
        in_specs=(field, field, P("groups", "wide", "narrow"), P("groups", None), P("groups"), spread),
        out_specs=(field, field, spread),
        check_vma=False,
    )
```

```python
import functools

import jax
import jax.numpy as jnp
from jax import lax
from jax.experimental import pallas as pl
from jax.experimental.pallas import tpu as pltpu
from jax.sharding import PartitionSpec as P

ITERS = 4
TIME_STEP = 0.05

EDGE = 6
MAP_EDGE = 5
ADJ_EDGE = 4
ROWS = 24
COLS = 10
LEAD = 8
CORNER = (5, 3, 4)

VMEM_LIMIT = 24 * 1024 * 1024


def lanes(shape):
    return lax.broadcasted_iota(jnp.int32, shape, len(shape) - 1)


def roll(value, shift):
    return pltpu.roll(value, shift, 1)


def is_odd(axis):
    return lax.rem(lax.axis_index(axis), 2) == 1


def pack_strips(order_ref, map_ref, cot_ref, mob_ref, after_ref, strip_a_ref, strip_b_ref, block_ref):
    params, layers = order_ref.shape[:2]
    odd = is_odd("narrow")
    lane = lanes((8, 128))
    zero = jnp.zeros((8, 128), jnp.float32)

    def span(first, size):
        return ((lane - first) & 127) < size

    for field in range(params + 1):
        right, left = zero, zero
        for z in range(layers):
            value = order_ref[field, z] if field < params else map_ref[z].astype(jnp.float32)
            moved = roll(value, 10 * z + 5)
            right = jnp.where(span(10 * z - 1, 6), moved, right)
            left = jnp.where(span(10 * z + 5, 6), moved, left)
            if field < params:
                right = jnp.where(span(10 * z + 5, 4), roll(cot_ref[field, z], 10 * z + 9), right)
                left = jnp.where(span(10 * z + 1, 4), roll(cot_ref[field, z], 10 * z + 1), left)
        rows = slice(8 * field, 8 * field + 8)
        strip_a_ref[rows, :] = jnp.where(odd, left, right)
        strip_b_ref[rows, :] = jnp.where(odd, right, left)
    owned = mob_ref.shape[1]
    owned_rows = -(-owned // 128)
    block_ref[...] = jnp.zeros_like(block_ref)
    first = lax.axis_index("narrow") * owned_rows
    for i in range(owned_rows):
        size = min(128, owned - 128 * i)
        row = mob_ref[0:1, 128 * i : 128 * i + size]
        if size < 128:
            row = jnp.concatenate([row, jnp.zeros((1, 128 - size), jnp.float32)], axis=1)
        block_ref[pl.ds(first + i, 1), :] = row
    for ref in (strip_a_ref, strip_b_ref):
        ref[8 * (params + 1) :, :] = block_ref[...]


def pack_rows(*refs):
    count = (len(refs) - 3) // 2
    sources, targets = refs[:count], refs[count : 2 * count]
    near_a_ref, row_b_ref, sems = refs[2 * count :]
    copies = [pltpu.make_async_copy(a, b, sems.at[i]) for i, (a, b) in enumerate(zip(sources, targets))]
    for copy in copies:
        copy.start()
    order_ref, map_ref, cot_ref = targets[:3]
    params, layers = order_ref.shape[:2]
    maps, cots = row_places(params, layers)
    gap = jnp.zeros((LEAD, 128), jnp.float32)
    odd = is_odd("wide")
    last = (jnp.where(odd, 0, 1), jnp.where(odd, 1, 0))
    row_refs = (near_a_ref, row_b_ref)
    for ref in row_refs:
        ref[0:LEAD, :] = gap
        ref[maps - LEAD : maps, :] = gap
        ref[cots - 2 * LEAD : cots - LEAD, :] = gap
        ref[cots - LEAD : cots, :] = gap
    near_a_ref[cots : cots + LEAD, :] = gap
    near_a_ref[near_a_ref.shape[0] - LEAD :, :] = gap
    copies[0].wait()
    for p in range(params):
        for z in range(layers):
            k = LEAD + (p * layers + z) * EDGE
            for ref, is_last in zip(row_refs, last):
                ref[k : k + EDGE, :] = order_ref[p, z, pl.ds((8 - EDGE) * is_last, EDGE), :]
    for copy in copies[1:]:
        copy.wait()
    for z in range(layers):
        k = maps + z * MAP_EDGE
        for ref, is_last in zip(row_refs, last):
            ref[k : k + MAP_EDGE, :] = map_ref[z, pl.ds((8 - MAP_EDGE) * is_last, MAP_EDGE), :].astype(jnp.float32)
    rows = pl.ds((8 - ADJ_EDGE) * last[0], ADJ_EDGE)
    for p in range(params):
        for z in range(layers):
            k = cots + LEAD + (p * layers + z) * ADJ_EDGE
            near_a_ref[k : k + ADJ_EDGE, :] = cot_ref[p, z, rows, :]


def pack_cot(cot_ref, after_ref, out_ref):
    params, layers = cot_ref.shape[:2]
    out_ref[0:LEAD, :] = jnp.zeros((LEAD, 128), jnp.float32)
    out_ref[out_ref.shape[0] - LEAD :, :] = jnp.zeros((LEAD, 128), jnp.float32)
    rows = pl.ds(jnp.where(is_odd("wide"), 8 - ADJ_EDGE, 0), ADJ_EDGE)
    for p in range(params):
        for z in range(layers):
            k = LEAD + (p * layers + z) * ADJ_EDGE
            out_ref[k : k + ADJ_EDGE, :] = cot_ref[p, z, rows, :]


def row_places(params, layers):
    maps = LEAD + params * layers * EDGE + LEAD
    length = maps + layers * MAP_EDGE
    return maps, length + -length % 8 + LEAD


def corner_rows(params):
    return -(-(params * (CORNER[0] + CORNER[1]) + CORNER[2]) // 8) * 8


def side_strips(params, strip_a_ref, strip_b_ref):
    odd = is_odd("narrow")
    fields = []
    for field in range(params + 1):
        rows = slice(8 * field, 8 * field + 8)
        a, b = strip_a_ref[rows, :], strip_b_ref[rows, :]
        fields.append((jnp.where(odd, a, b), jnp.where(odd, b, a)))
    return fields


def merged_strips(params, *strip_refs):
    first = lanes((8, 128)) % COLS < 5
    fields = side_strips(params, *strip_refs)
    order = [jnp.where(first, a, b) for a, b in fields[:params]]
    cot = [jnp.where(first, roll(a, 124), roll(b, 4)) for a, b in fields[:params]]
    return order, cot, jnp.where(first, *fields[params])


def pack_far(params, strip_a_ref, strip_b_ref, block_ref, *refs):
    *other_refs, far_a_ref, far_b_ref, out_block_ref = refs
    at = 8 * (params + 1)
    mobs = corner_rows(params)
    block = block_ref[...] + strip_a_ref[at:, :] + strip_b_ref[at:, :]
    for ref in other_refs:
        block = block + ref[...]
    out_block_ref[...] = block
    at = 0
    odd = is_odd("wide")
    order, cot, cells = merged_strips(params, strip_a_ref, strip_b_ref)
    for n, fields in zip(CORNER, (order, cot, [cells])):
        for both in fields:
            far_a_ref[at : at + n, :] = jnp.where(odd, both[0:n], both[8 - n : 8])
            far_b_ref[at : at + n, :] = jnp.where(odd, both[8 - n : 8], both[0:n])
            at += n
    for ref in (far_a_ref, far_b_ref):
        ref[at:mobs, :] = jnp.zeros((mobs - at, 128), jnp.float32)
        ref[mobs:, :] = block


def find_slots(bricks_ref, slot_ref, after_ref, out_ref):
    count, listed = bricks_ref.shape
    rows = slot_ref.shape[0]
    for k in range(0, out_ref.shape[0], 8):
        pairs = [
            jnp.concatenate([bricks_ref[2 * j : 2 * j + 1, :], bricks_ref[2 * j + 1 : 2 * j + 2, :]], axis=1)
            for j in range(k, k + 8)
        ]
        grain = jnp.concatenate(pairs, axis=0)
        row, col = grain >> 7, grain & 127

        def body(r, found, row=row, col=col):
            table = jnp.broadcast_to(slot_ref[pl.ds(r, 1), :], (8, 128))
            taken = jnp.take_along_axis(table, col, axis=1, mode="promise_in_bounds")
            return jnp.where(row == r, taken, found)

        out_ref[k : k + 8, :] = lax.fori_loop(0, rows, body, jnp.zeros((8, 128), jnp.int32), unroll=49)


def find_mobility(counts, owned, slots_ref, *refs):
    *mob_refs, table_ref, near_ref, all_ref = refs
    wide_count, narrow_count = counts
    tile = (8, 128)
    wide, narrow = lax.axis_index("wide"), lax.axis_index("narrow")
    if len(mob_refs) == 1:
        mob_ref = mob_refs[0]
    else:
        block_ref, far_a_ref, far_b_ref, other_ref = mob_refs
        mob_ref = all_ref
        size = block_ref.shape[0]
        odd = is_odd("wide")
        step = jnp.where(odd, 1, 3)
        for place, ref in (
            (wide, block_ref), (wide + 4 - step, far_a_ref), (wide + step, far_b_ref), (wide + 2, other_ref)
        ):
            at = pl.multiple_of(size * (place & 3), size)
            mob_ref[pl.ds(at, size), :] = ref[ref.shape[0] - size :, :]
    near_ref[...] = jnp.zeros_like(near_ref)
    for k in range(9):
        w = lax.rem(wide + k // 3 - 1 + wide_count, wide_count)
        n = lax.rem(narrow + k % 3 - 1 + narrow_count, narrow_count)
        brick = w * narrow_count + n
        row = slots_ref[pl.ds(brick >> 1, 1), :]
        half = jnp.where((brick & 1) == 0, row[:, 0:64], row[:, 64:128])
        near_ref[k // 2 : k // 2 + 1, 64 * (k % 2) : 64 * (k % 2) + 64] = half
    slot = near_ref[...]
    owned_rows = -(-owned // 128)
    owner = jnp.floor((slot.astype(jnp.float32) + 0.5) * (1.0 / owned)).astype(jnp.int32)
    inner = slot - owner * owned
    row = owner * owned_rows + (inner >> 7)
    place = inner & 127

    def body(r, found):
        values = jnp.broadcast_to(mob_ref[pl.ds(r, 1), :], tile)
        taken = jnp.take_along_axis(values, place, axis=1, mode="promise_in_bounds")
        return jnp.where(row == r, taken, found)

    found = lax.fori_loop(0, mob_ref.shape[0], body, jnp.zeros(tile, jnp.float32), unroll=32)
    table_ref[...] = TIME_STEP * found


def total_of(values):
    while len(values) > 1:
        values = [a + b for a, b in zip(values[::2], values[1::2])]
    return values[0]


def each_tile(layers, windows, body):
    start, count, most = windows
    nothing = lax.axis_index("wide") >> 20
    stores = []
    for z in range(layers):
        for i in range(count):
            stores += body(z, i, jnp.minimum(start + 8 * i, most) + nothing)
        if len(stores) >= 32 or z == layers - 1:
            for store in stores:
                store()
            stores = []


def each_window(windows, body):
    nothing = lax.axis_index("wide") >> 20
    for i in range(windows[1]):
        body(windows[0] + 8 * i + nothing)


def put(ref, index, value):
    def store():
        ref[index] = value

    return store


def neighbours(ref, ends_ref, value, p, z, r):
    layers = ref.shape[1]
    lane = lanes((8, 128))
    rows, before, after = pl.ds(r, 8), pl.ds(r - 1, 8), pl.ds(r + 1, 8)
    below, above = max(z - 1, 0), min(z + 1, layers - 1)
    ends = ends_ref[p, z, rows, :]
    left = roll(jnp.where(lane == 127, ends, value), 1)
    right = roll(jnp.where(lane == 0, ends, value), 127)
    total = (left + right) + (ref[p, z, before, :] + ref[p, z, after, :])
    return total + (ref[p, below, rows, :] + ref[p, above, rows, :])


def strip_neighbours(ref, core_ref, values, r, outer_ref=None):
    params, layers = core_ref.shape[:2]
    lane = lanes((8, 128))
    col = lane % COLS
    rows, before, after = pl.ds(r, 8), pl.ds(r - 1, 8), pl.ds(r + 1, 8)
    near = []
    for p in range(params):
        value = values[p]
        ends = jnp.zeros((8, 128), jnp.float32)
        for z in range(layers):
            here = (lane == 10 * z + 4) | (lane == 10 * z + 5)
            ends = jnp.where(here, roll(core_ref[p, z, rows, :], 10 * z + 5), ends)
        left = roll(jnp.where(col == 4, ends, value), 1)
        right = roll(jnp.where(col == 5, ends, value), 127)
        if outer_ref is not None:
            outer = outer_ref[p, rows, :]
            left = jnp.where(col == 0, outer, left)
            right = jnp.where(col == 9, outer, right)
        below = jnp.where(lane < COLS, value, roll(value, COLS))
        above = jnp.where(lane >= COLS * (layers - 1), value, roll(value, 128 - COLS))
        total = (left + right) + (below + above)
        near.append(total + (ref[p, before, :] + ref[p, after, :]))
    return near


def spread_ends(ends_ref, values, rows):
    params, layers = ends_ref.shape[:2]
    for p in range(params):
        for z in range(layers):
            ends_ref[p, z, rows, :] = roll(values[p], 123 - 10 * z)


def base_of(e):
    return 1.5 * total_of([x * x for x in e]) + 5.0


def inner_of(e, u):
    return 3.0 * total_of([x * y for x, y in zip(e, u)])


def forward(
    order_ref, map_ref, row_a_ref, row_b_ref, far_a_ref, far_b_ref, strip_a_ref, strip_b_ref, table_ref,
    final_ref, e_refs, rate_refs, se_refs, m_ref, ms_ref,
    first_strip_ref, outer_ref, ends_ref, g_ref, gs_ref,
):
    params, layers = order_ref.shape[:2]
    tile = (8, 128)
    col = lanes(tile) % COLS
    maps = row_places(params, layers)[0]
    strip_refs = [first_strip_ref, *se_refs]
    every = range(params)

    odd = is_odd("wide")
    from_before = (jnp.where(odd, 1, 0), jnp.where(odd, 0, 1))

    def place(z, carry):
        for ref, before in zip((row_a_ref, row_b_ref), from_before):
            k, target = maps + z * MAP_EDGE + before * (MAP_EDGE - 8), pl.ds(16 - 16 * before, 8)
            g_ref[z, target, :] = ref[pl.ds(k, 8), :]
            for p in every:
                k = LEAD + (p * layers + z) * EDGE + before * (EDGE - 8)
                e_refs[0][p, z, target, :] = ref[pl.ds(k, 8), :]
        for p in every:
            e_refs[0][p, z, 8:16, :] = order_ref[p, z]
        return carry

    for z in range(layers):
        place(z, 0)

    sides = side_strips(params, strip_a_ref, strip_b_ref)
    order, _, cells = merged_strips(params, strip_a_ref, strip_b_ref)
    n = CORNER[0]
    for p in every:
        ref = first_strip_ref.at[p]
        ref[0:8, :] = jnp.zeros(tile, jnp.float32)
        ref[16:24, :] = jnp.zeros(tile, jnp.float32)
        a, b = far_a_ref[n * p : n * p + n, :], far_b_ref[n * p : n * p + n, :]
        ref[8 - n : 8, :] = jnp.where(odd, a, b)
        ref[8:16, :] = order[p]
        ref[16 : 16 + n, :] = jnp.where(odd, b, a)
        outer_ref[p, 8:16, :] = jnp.where(col == 0, roll(sides[p][0], 1), roll(sides[p][1], 127))
    at, n = params * (CORNER[0] + CORNER[1]), CORNER[2]
    gs_ref[...] = jnp.zeros_like(gs_ref)
    a, b = far_a_ref[at : at + n, :], far_b_ref[at : at + n, :]
    gs_ref[8 - n : 8, :] = jnp.where(odd, a, b)
    gs_ref[8:16, :] = cells
    gs_ref[16 : 16 + n, :] = jnp.where(odd, b, a)
    for r in (0, 8, 16):
        rows = slice(r, r + 8)
        spread_ends(ends_ref, [first_strip_ref[p, rows, :] for p in every], rows)

    def lookup(index, which):
        values = jnp.broadcast_to(table_ref[which // 2 : which // 2 + 1, :], tile)
        return jnp.take_along_axis(values, index + 64 * (which % 2), axis=1, mode="promise_in_bounds")

    for i in range(3):
        r = 8 * i
        for z in range(layers):
            index = map_ref[z] if i == 1 else g_ref[z, r : r + 8, :].astype(jnp.int32) & 63
            m_ref[z, r : r + 8, :] = lookup(index, 3 * i + 1)
        index = gs_ref[r : r + 8, :].astype(jnp.int32) & 63
        ms_ref[r : r + 8, :] = jnp.where(col < 5, lookup(index, 3 * i), lookup(index, 3 * i + 2))

    def step(t, windows, strip_windows, end_windows):
        old, old_strip = e_refs[t], strip_refs[t]
        last = t == ITERS - 1

        def core(z, i, r):
            rows = pl.ds(r, 8)
            base = base_of([old[p, z, rows, :] for p in every])
            m = m_ref[z, rows, :]
            stores = []
            for p in every:
                e = old[p, z, rows, :]
                rate = e * (base - 0.5 * (e * e)) - neighbours(old, ends_ref, e, p, z, r)
                new = e - m * rate
                stores.append(put(rate_refs[t], (p, z, rows, slice(None)), rate))
                if last:
                    stores.append(put(final_ref, (p, z), new))
                else:
                    stores.append(put(e_refs[t + 1], (p, z, rows, slice(None)), new))
            return stores

        each_tile(layers, windows, core)
        if last:
            return

        def strip(r):
            rows = pl.ds(r, 8)
            e = [old_strip[p, rows, :] for p in every]
            m = ms_ref[rows, :]
            base = base_of(e)
            near = strip_neighbours(old_strip, old, e, r, outer_ref if t == 0 else None)
            for p in every:
                rate = e[p] * (base - 0.5 * (e[p] * e[p])) - near[p]
                strip_refs[t + 1][p, rows, :] = e[p] - m * rate

        each_window(strip_windows, strip)

        def ends(r):
            rows = pl.ds(r, 8)
            spread_ends(ends_ref, [strip_refs[t + 1][p, rows, :] for p in every], rows)

        each_window(end_windows, ends)

    step(0, (3, 3, 13), (4, 2), (4, 2))
    step(1, (4, 2, 12), (4, 2), (4, 2))
    step(2, (4, 2, 12), (4, 2), (8, 1))
    step(3, (8, 1, 8), None, None)


def backward(
    cot_ref, map_ref, row_a_ref, row_b_ref, far_a_ref, far_b_ref, strip_a_ref, strip_b_ref,
    e_refs, rate_refs, se_refs, m_ref, ms_ref,
    adjoint_ref, sums_ref,
    lam_refs, slam_refs, u_refs, su_refs, ends_ref, work_ref, binned_ref,
):
    params, layers = cot_ref.shape[:2]
    cots = row_places(params, layers)[1]
    tile = (8, 128)
    every = range(params)

    odd = is_odd("wide")
    from_before = (jnp.where(odd, 1, 0), jnp.where(odd, 0, 1))

    def place(z, carry):
        for ref, base, before in zip((row_a_ref, row_b_ref), (cots, 0), from_before):
            rows = pl.ds(16 - 16 * before, 8)
            m = m_ref[z, rows, :]
            for p in every:
                k = base + LEAD + (p * layers + z) * ADJ_EDGE + before * (ADJ_EDGE - 8)
                value = ref[pl.ds(k, 8), :]
                lam_refs[0][p, z, rows, :] = value
                u_refs[0][p, z, rows, :] = m * value
        m = m_ref[z, 8:16, :]
        for p in every:
            lam_refs[0][p, z, 8:16, :] = cot_ref[p, z]
            u_refs[0][p, z, 8:16, :] = m * cot_ref[p, z]
        return carry

    for z in range(layers):
        place(z, 0)
    _, cot, _ = merged_strips(params, strip_a_ref, strip_b_ref)
    n = CORNER[1]
    for p in every:
        at = params * CORNER[0] + n * p
        ref = slam_refs[0].at[p]
        ref[0:8, :] = jnp.zeros(tile, jnp.float32)
        ref[16:24, :] = jnp.zeros(tile, jnp.float32)
        a, b = far_a_ref[at : at + n, :], far_b_ref[at : at + n, :]
        ref[8 - n : 8, :] = jnp.where(odd, a, b)
        ref[8:16, :] = cot[p]
        ref[16 : 16 + n, :] = jnp.where(odd, b, a)
        for r in (0, 8, 16):
            su_refs[0][p, r : r + 8, :] = ms_ref[r : r + 8, :] * ref[r : r + 8, :]

    def spread(slot, windows):
        def ends(r):
            rows = pl.ds(r, 8)
            spread_ends(ends_ref, [su_refs[slot][p, rows, :] for p in every], rows)

        each_window(windows, ends)

    def step(t, slot, windows, strip_windows, end_windows):
        old, old_strip = u_refs[slot], su_refs[slot]

        def core(z, i, r):
            rows = pl.ds(r, 8)
            e = [e_refs[t][p, z, rows, :] for p in every]
            u = [old[p, z, rows, :] for p in every]
            base, inner = base_of(e), inner_of(e, u)
            m = m_ref[z, rows, :]
            work = total_of([lam_refs[slot][p, z, rows, :] * rate_refs[t][p, z, rows, :] for p in every])
            stores = [put(work_ref, (t - 1, z, i), work)]
            for p in every:
                e, u = e_refs[t][p, z, rows, :], old[p, z, rows, :]
                change = u * (base - 1.5 * (e * e)) + e * inner - neighbours(old, ends_ref, u, p, z, r)
                new = lam_refs[slot][p, z, rows, :] - change
                stores.append(put(lam_refs[1 - slot], (p, z, rows, slice(None)), new))
                stores.append(put(u_refs[1 - slot], (p, z, rows, slice(None)), m * new))
            return stores

        each_tile(layers, windows, core)

        def strip(r):
            rows = pl.ds(r, 8)
            e = [se_refs[t - 1][p, rows, :] for p in every]
            u = [old_strip[p, rows, :] for p in every]
            m = ms_ref[rows, :]
            base, inner = base_of(e), inner_of(e, u)
            near = strip_neighbours(old_strip, old, u, r)
            for p in every:
                change = u[p] * (base - 1.5 * (e[p] * e[p])) + e[p] * inner - near[p]
                new = slam_refs[slot][p, rows, :] - change
                slam_refs[1 - slot][p, rows, :] = new
                su_refs[1 - slot][p, rows, :] = m * new

        each_window(strip_windows, strip)
        spread(1 - slot, end_windows)

    spread(0, (4, 2))
    step(3, 0, (4, 2, 12), (4, 2), (4, 2))
    step(2, 1, (4, 2, 12), (4, 2), (4, 2))
    step(1, 0, (4, 2, 12), (8, 1), (8, 1))

    def last(z, i, r):
        rows = pl.ds(r, 8)
        e = [e_refs[0][p, z, rows, :] for p in every]
        u = [u_refs[1][p, z, rows, :] for p in every]
        base, inner = base_of(e), inner_of(e, u)
        stores = []
        for p in every:
            e, u = e_refs[0][p, z, rows, :], u_refs[1][p, z, rows, :]
            change = u * (base - 1.5 * (e * e)) + e * inner - neighbours(u_refs[1], ends_ref, u, p, z, r)
            stores.append(put(adjoint_ref, (p, z), lam_refs[1][p, z, rows, :] - change))
        return stores

    each_tile(layers, (8, 1, 8), last)

    grains = [map_ref[z] for z in range(layers)]
    cells = []
    for z in range(layers):
        upper = work_ref[0, z, 0] + work_ref[1, z, 0] + work_ref[2, z, 0]
        lower = work_ref[0, z, 1] + work_ref[1, z, 1] + work_ref[2, z, 1]
        first = total_of([lam_refs[1][p, z, 8:16, :] * rate_refs[0][p, z, 8:16, :] for p in every])
        cells.append(jnp.concatenate([upper[4:8], lower[0:4]], axis=0) + first)

    def bin_one(g, carry):
        kept = [jnp.where(grains[z] == g, cells[z], 0.0) for z in range(layers)]
        total = sum(kept[1:4], kept[0]) + sum(kept[5:8], kept[4]) + sum(kept[9:], kept[8])
        binned_ref[pl.ds(g, 1), :] = jnp.sum(total, axis=0, keepdims=True)
        return carry

    lax.fori_loop(0, binned_ref.shape[0], bin_one, 0, unroll=16)
    ones = jnp.full((8, 128), -TIME_STEP, jnp.float32)
    sums = lax.dot_general(
        ones, binned_ref[...], (((1,), (1,)), ((), ())),
        precision=lax.Precision.HIGHEST, preferred_element_type=jnp.float32,
    )
    for k in range(0, sums_ref.shape[0], 8):
        sums_ref[k : k + 8, :] = sums


def pick_owned(owned, slots_ref, sums_ref, out_ref, total_ref, dense_ref):
    base = (lax.axis_index("wide") * lax.axis_size("narrow") + lax.axis_index("narrow")) * owned
    tile = (8, 128)
    for k in range(dense_ref.shape[0]):
        dense_ref[k : k + 1, 0:64] = sums_ref[2 * k : 2 * k + 1, :]
        dense_ref[k : k + 1, 64:128] = sums_ref[2 * k + 1 : 2 * k + 2, :]
    sub = lax.broadcasted_iota(jnp.int32, tile, 0)
    blocks = total_ref.shape[0] // 8
    step = 25
    for first in range(0, blocks, step):
        some = range(first, min(first + step, blocks))

        def body(k, acc, some=some):
            shifted = jnp.broadcast_to(slots_ref[pl.ds(k, 1), :], tile) - (sub + base)
            value = jnp.broadcast_to(dense_ref[pl.ds(k, 1), :], tile)
            return tuple(a + jnp.where(shifted == 8 * j, value, 0.0) for a, j in zip(acc, some))

        zero = tuple(jnp.zeros(tile, jnp.float32) for _ in some)
        acc = lax.fori_loop(0, slots_ref.shape[0], body, zero, unroll=8)
        for a, j in zip(acc, some):
            total_ref[8 * j : 8 * j + 8, :] = a
    whole = lax.dot_general(
        jnp.ones(tile, jnp.float32), total_ref[...], (((1,), (1,)), ((), ())),
        precision=lax.Precision.HIGHEST, preferred_element_type=jnp.float32,
    )
    out_ref[...] = whole[0:1, 0:owned]


def f32(*shape):
    return jax.ShapeDtypeStruct(shape, jnp.float32)


def kernel(body, out_shape, scratch=(), name=None, cost=0, **specs):
    if cost:
        specs["cost_estimate"] = pl.CostEstimate(flops=cost, bytes_accessed=cost // 1000, transcendentals=0)
    return pl.pallas_call(
        body, out_shape=out_shape, scratch_shapes=list(scratch), name=name, **specs,
        compiler_params=pltpu.CompilerParams(vmem_limit_bytes=VMEM_LIMIT),
    )


def opposite(value, axis):
    return lax.ppermute(value, axis, [(i, (i + 2) % 4) for i in range(4)])


def swapped(value, axis, count, partner):
    step = [1 if (i + partner) % 2 == 0 else -1 for i in range(count)]
    return lax.ppermute(value, axis, [(i, (i + by) % count) for i, by in enumerate(step)])


def per_device(counts, order_init, cotangent, grain_map, brick_grains, grain_slot, mobility):
    wide_count, narrow_count = counts
    params, layers = order_init.shape[:2]
    assert order_init.shape[2:] == (8, 128) and layers * COLS < 128
    owned = mobility.shape[0]
    listed = brick_grains.shape[1]
    bricks = brick_grains.shape[0]

    both = ("wide", "narrow")
    count = wide_count * narrow_count
    small = counts == (4, 4)
    assert listed == 64 and bricks == count and count % 16 == 0

    owned_rows = -(-owned // 128)
    block_rows = narrow_count * owned_rows
    strip_rows = 8 * (params + 1)
    edge_rows = row_places(params, layers)[1]
    cot_rows = params * layers * ADJ_EDGE + 2 * LEAD
    vmem = lambda *shape: pltpu.VMEM(shape, jnp.float32)

    arguments = (
        order_init, grain_map, cotangent, mobility.reshape(1, owned), brick_grains, grain_slot.reshape(-1, 128)
    )
    here, anywhere = pl.BlockSpec(memory_space=pltpu.VMEM), pl.BlockSpec(memory_space=pl.ANY)
    *fetched, near_a, row_b = kernel(
        pack_rows,
        tuple(jax.ShapeDtypeStruct(x.shape, x.dtype) for x in arguments)
        + (f32(edge_rows + cot_rows, 128), f32(edge_rows, 128)),
        (pltpu.SemaphoreType.DMA((len(arguments),)),), name="pack_rows",
        in_specs=[pl.BlockSpec(memory_space=pltpu.HBM)] * len(arguments),
    )(*(pltpu.with_memory_space_constraint(x, pltpu.HBM) for x in arguments))
    order_init, grain_map, cotangent, mobility_row, brick_grains, grain_slot = fetched
    strip_a, strip_b, block = kernel(
        pack_strips, (f32(strip_rows + block_rows, 128),) * 2 + (f32(block_rows, 128),),
        name="pack_strips", in_specs=[here] * 4 + [anywhere],
    )(order_init, grain_map, cotangent, mobility_row, row_b)
    row_b = swapped(row_b, "wide", wide_count, 1)
    near_a = swapped(near_a, "wide", wide_count, 0)
    strip_b = swapped(strip_b, "narrow", narrow_count, 1)
    strip_a = swapped(strip_a, "narrow", narrow_count, 0)
    others = [opposite(block, "narrow")] if small else []

    corners = corner_rows(params)
    far_a, far_b, block = kernel(
        functools.partial(pack_far, params),
        (f32(corners + block_rows, 128),) * 2 + (f32(block_rows, 128),), name="pack_far", cost=0,
    )(strip_a, strip_b, block, *others)
    far_b = swapped(far_b, "wide", wide_count, 1)
    far_a = swapped(far_a, "wide", wide_count, 0)
    slots = kernel(
        find_slots, jax.ShapeDtypeStruct((bricks // 2, 128), jnp.int32), name="find_slots",
        in_specs=[here, here, anywhere],
    )(brick_grains, grain_slot, block)
    cot_b = kernel(pack_cot, f32(cot_rows, 128), name="pack_cot", in_specs=[here, anywhere])(cotangent, far_a)
    cot_b = swapped(cot_b, "wide", wide_count, 1)

    if small:
        mobs = (block, far_a, far_b, opposite(block, "wide"))
    else:
        own = jnp.pad(mobility, (0, -owned % 128)).reshape(owned_rows, 128)
        mobs = (lax.all_gather(own, both, axis=0, tiled=True),)
    table = kernel(
        functools.partial(find_mobility, counts, owned), f32(8, 128),
        (pltpu.VMEM((8, 128), jnp.int32), vmem(wide_count * block_rows, 128)),
        name="find_mobility", cost=2_500_000_000,
    )(slots, *mobs)

    padded, strip = (params, layers, ROWS, 128), (params, ROWS, 128)
    final, states, rate, halos, m, ms = kernel(
        forward,
        (
            f32(*order_init.shape), [f32(*padded)] * ITERS, [f32(*padded)] * ITERS,
            [f32(*strip)] * (ITERS - 1), f32(layers, ROWS, 128), f32(ROWS, 128),
        ),
        (vmem(*strip), vmem(*strip), vmem(*padded), vmem(layers, ROWS, 128), vmem(ROWS, 128)),
        name="forward", cost=0,
    )(order_init, grain_map, near_a, row_b, far_a, far_b, strip_a, strip_b, table)
    adjoint, sums = kernel(
        backward,
        (f32(*order_init.shape), f32(bricks, listed)),
        (
            [vmem(*padded)] * 2, [vmem(*strip)] * 2, [vmem(*padded)] * 2, [vmem(*strip)] * 2, vmem(*padded),
            vmem(ITERS - 1, layers, 2, 8, 128), vmem(listed, 128),
        ),
        name="backward",
    )(
        cotangent, grain_map, near_a, cot_b, far_a, far_b, strip_a, strip_b,
        states, rate, halos, m, ms,
    )

    sums = lax.all_to_all(sums, both, 0, 0, tiled=True)
    grads = kernel(
        functools.partial(pick_owned, owned), f32(1, owned),
        (vmem(owned + -owned % 8, 128), vmem(bricks // 2, 128)), name="pick_owned",
    )(slots, sums)
    return final, adjoint, grads.reshape(owned)


def solution(mesh):
    counts = (mesh.shape["wide"], mesh.shape["narrow"])
    field = P("groups", None, "wide", "narrow")
    spread = P(("groups", "wide", "narrow"))
    return jax.shard_map(
        functools.partial(per_device, counts),
        mesh=mesh,
        in_specs=(field, field, P("groups", "wide", "narrow"), P("groups", None), P("groups"), spread),
        out_specs=(field, field, spread),
        check_vma=False,
    )
```

```python
import functools

import jax
import jax.numpy as jnp
from jax import lax
from jax.experimental import pallas as pl
from jax.experimental.pallas import tpu as pltpu
from jax.sharding import PartitionSpec as P

ITERS = 4
TIME_STEP = 0.05

EDGE = 6
MAP_EDGE = 5
ADJ_EDGE = 4
ROWS = 24
COLS = 10
LEAD = 8
CORNER = (5, 3, 4)

VMEM_LIMIT = 24 * 1024 * 1024


def lanes(shape):
    return lax.broadcasted_iota(jnp.int32, shape, len(shape) - 1)


def roll(value, shift):
    return pltpu.roll(value, shift, 1)


def is_odd(axis):
    return lax.rem(lax.axis_index(axis), 2) == 1


def pack_strips(order_ref, map_ref, cot_ref, mob_ref, after_ref, strip_a_ref, strip_b_ref, block_ref):
    params, layers = order_ref.shape[:2]
    odd = is_odd("narrow")
    lane = lanes((8, 128))
    zero = jnp.zeros((8, 128), jnp.float32)

    def span(first, size):
        return ((lane - first) & 127) < size

    for field in range(params + 1):
        right, left = zero, zero
        for z in range(layers):
            value = order_ref[field, z] if field < params else map_ref[z].astype(jnp.float32)
            moved = roll(value, 10 * z + 5)
            right = jnp.where(span(10 * z - 1, 6), moved, right)
            left = jnp.where(span(10 * z + 5, 6), moved, left)
            if field < params:
                right = jnp.where(span(10 * z + 5, 4), roll(cot_ref[field, z], 10 * z + 9), right)
                left = jnp.where(span(10 * z + 1, 4), roll(cot_ref[field, z], 10 * z + 1), left)
        rows = slice(8 * field, 8 * field + 8)
        strip_a_ref[rows, :] = jnp.where(odd, left, right)
        strip_b_ref[rows, :] = jnp.where(odd, right, left)
    owned = mob_ref.shape[1]
    owned_rows = -(-owned // 128)
    block_ref[...] = jnp.zeros_like(block_ref)
    first = lax.axis_index("narrow") * owned_rows
    for i in range(owned_rows):
        size = min(128, owned - 128 * i)
        row = mob_ref[0:1, 128 * i : 128 * i + size]
        if size < 128:
            row = jnp.concatenate([row, jnp.zeros((1, 128 - size), jnp.float32)], axis=1)
        block_ref[pl.ds(first + i, 1), :] = row
    for ref in (strip_a_ref, strip_b_ref):
        ref[8 * (params + 1) :, :] = block_ref[...]


def pack_rows(*refs):
    count = (len(refs) - 3) // 2
    sources, targets = refs[:count], refs[count : 2 * count]
    near_a_ref, row_b_ref, sems = refs[2 * count :]
    copies = [pltpu.make_async_copy(a, b, sems.at[i]) for i, (a, b) in enumerate(zip(sources, targets))]
    for copy in copies:
        copy.start()
    order_ref, map_ref, cot_ref = targets[:3]
    params, layers = order_ref.shape[:2]
    maps, cots = row_places(params, layers)
    gap = jnp.zeros((LEAD, 128), jnp.float32)
    odd = is_odd("wide")
    last = (jnp.where(odd, 0, 1), jnp.where(odd, 1, 0))
    row_refs = (near_a_ref, row_b_ref)
    for ref in row_refs:
        ref[0:LEAD, :] = gap
        ref[maps - LEAD : maps, :] = gap
        ref[cots - 2 * LEAD : cots - LEAD, :] = gap
        ref[cots - LEAD : cots, :] = gap
    near_a_ref[cots : cots + LEAD, :] = gap
    near_a_ref[near_a_ref.shape[0] - LEAD :, :] = gap
    copies[0].wait()
    for p in range(params):
        for z in range(layers):
            k = LEAD + (p * layers + z) * EDGE
            for ref, is_last in zip(row_refs, last):
                ref[k : k + EDGE, :] = order_ref[p, z, pl.ds((8 - EDGE) * is_last, EDGE), :]
    for copy in copies[1:]:
        copy.wait()
    for z in range(layers):
        k = maps + z * MAP_EDGE
        for ref, is_last in zip(row_refs, last):
            ref[k : k + MAP_EDGE, :] = map_ref[z, pl.ds((8 - MAP_EDGE) * is_last, MAP_EDGE), :].astype(jnp.float32)
    rows = pl.ds((8 - ADJ_EDGE) * last[0], ADJ_EDGE)
    for p in range(params):
        for z in range(layers):
            k = cots + LEAD + (p * layers + z) * ADJ_EDGE
            near_a_ref[k : k + ADJ_EDGE, :] = cot_ref[p, z, rows, :]


def pack_cot(cot_ref, after_ref, out_ref):
    params, layers = cot_ref.shape[:2]
    out_ref[0:LEAD, :] = jnp.zeros((LEAD, 128), jnp.float32)
    out_ref[out_ref.shape[0] - LEAD :, :] = jnp.zeros((LEAD, 128), jnp.float32)
    rows = pl.ds(jnp.where(is_odd("wide"), 8 - ADJ_EDGE, 0), ADJ_EDGE)
    for p in range(params):
        for z in range(layers):
            k = LEAD + (p * layers + z) * ADJ_EDGE
            out_ref[k : k + ADJ_EDGE, :] = cot_ref[p, z, rows, :]


def row_places(params, layers):
    maps = LEAD + params * layers * EDGE + LEAD
    length = maps + layers * MAP_EDGE
    return maps, length + -length % 8 + LEAD


def corner_rows(params):
    return -(-(params * (CORNER[0] + CORNER[1]) + CORNER[2]) // 8) * 8


def side_strips(params, strip_a_ref, strip_b_ref):
    odd = is_odd("narrow")
    fields = []
    for field in range(params + 1):
        rows = slice(8 * field, 8 * field + 8)
        a, b = strip_a_ref[rows, :], strip_b_ref[rows, :]
        fields.append((jnp.where(odd, a, b), jnp.where(odd, b, a)))
    return fields


def merged_strips(params, *strip_refs):
    first = lanes((8, 128)) % COLS < 5
    fields = side_strips(params, *strip_refs)
    order = [jnp.where(first, a, b) for a, b in fields[:params]]
    cot = [jnp.where(first, roll(a, 124), roll(b, 4)) for a, b in fields[:params]]
    return order, cot, jnp.where(first, *fields[params])


def pack_far(params, strip_a_ref, strip_b_ref, block_ref, *refs):
    *other_refs, far_a_ref, far_b_ref, out_block_ref = refs
    at = 8 * (params + 1)
    mobs = corner_rows(params)
    block = block_ref[...] + strip_a_ref[at:, :] + strip_b_ref[at:, :]
    for ref in other_refs:
        block = block + ref[...]
    out_block_ref[...] = block
    at = 0
    odd = is_odd("wide")
    order, cot, cells = merged_strips(params, strip_a_ref, strip_b_ref)
    for n, fields in zip(CORNER, (order, cot, [cells])):
        for both in fields:
            far_a_ref[at : at + n, :] = jnp.where(odd, both[0:n], both[8 - n : 8])
            far_b_ref[at : at + n, :] = jnp.where(odd, both[8 - n : 8], both[0:n])
            at += n
    for ref in (far_a_ref, far_b_ref):
        ref[at:mobs, :] = jnp.zeros((mobs - at, 128), jnp.float32)
        ref[mobs:, :] = block


def find_slots(bricks_ref, slot_ref, after_ref, out_ref):
    count, listed = bricks_ref.shape
    rows = slot_ref.shape[0]
    for k in range(0, out_ref.shape[0], 8):
        pairs = [
            jnp.concatenate([bricks_ref[2 * j : 2 * j + 1, :], bricks_ref[2 * j + 1 : 2 * j + 2, :]], axis=1)
            for j in range(k, k + 8)
        ]
        grain = jnp.concatenate(pairs, axis=0)
        row, col = grain >> 7, grain & 127

        def body(r, found, row=row, col=col):
            table = jnp.broadcast_to(slot_ref[pl.ds(r, 1), :], (8, 128))
            taken = jnp.take_along_axis(table, col, axis=1, mode="promise_in_bounds")
            return jnp.where(row == r, taken, found)

        out_ref[k : k + 8, :] = lax.fori_loop(0, rows, body, jnp.zeros((8, 128), jnp.int32), unroll=49)


def find_mobility(counts, owned, slots_ref, *refs):
    *mob_refs, table_ref, near_ref, all_ref = refs
    wide_count, narrow_count = counts
    tile = (8, 128)
    wide, narrow = lax.axis_index("wide"), lax.axis_index("narrow")
    if len(mob_refs) == 1:
        mob_ref = mob_refs[0]
    else:
        block_ref, far_a_ref, far_b_ref, other_ref = mob_refs
        mob_ref = all_ref
        size = block_ref.shape[0]
        odd = is_odd("wide")
        step = jnp.where(odd, 1, 3)
        for place, ref in (
            (wide, block_ref), (wide + 4 - step, far_a_ref), (wide + step, far_b_ref), (wide + 2, other_ref)
        ):
            at = pl.multiple_of(size * (place & 3), size)
            mob_ref[pl.ds(at, size), :] = ref[ref.shape[0] - size :, :]
    near_ref[...] = jnp.zeros_like(near_ref)
    for k in range(9):
        w = lax.rem(wide + k // 3 - 1 + wide_count, wide_count)
        n = lax.rem(narrow + k % 3 - 1 + narrow_count, narrow_count)
        brick = w * narrow_count + n
        row = slots_ref[pl.ds(brick >> 1, 1), :]
        half = jnp.where((brick & 1) == 0, row[:, 0:64], row[:, 64:128])
        near_ref[k // 2 : k // 2 + 1, 64 * (k % 2) : 64 * (k % 2) + 64] = half
    slot = near_ref[...]
    owned_rows = -(-owned // 128)
    owner = jnp.floor((slot.astype(jnp.float32) + 0.5) * (1.0 / owned)).astype(jnp.int32)
    inner = slot - owner * owned
    row = owner * owned_rows + (inner >> 7)
    place = inner & 127

    def body(r, found):
        values = jnp.broadcast_to(mob_ref[pl.ds(r, 1), :], tile)
        taken = jnp.take_along_axis(values, place, axis=1, mode="promise_in_bounds")
        return jnp.where(row == r, taken, found)

    found = lax.fori_loop(0, mob_ref.shape[0], body, jnp.zeros(tile, jnp.float32), unroll=32)
    table_ref[...] = TIME_STEP * found


def total_of(values):
    while len(values) > 1:
        values = [a + b for a, b in zip(values[::2], values[1::2])]
    return values[0]


def each_tile(layers, windows, body):
    start, count, most = windows
    nothing = lax.axis_index("wide") >> 20
    stores = []
    for z in range(layers):
        for i in range(count):
            stores += body(z, i, jnp.minimum(start + 8 * i, most) + nothing)
        if len(stores) >= 64 or z == layers - 1:
            for store in stores:
                store()
            stores = []


def each_window(windows, body):
    def one(i, carry):
        body(windows[0] + 8 * i)
        return carry

    lax.fori_loop(0, windows[1], one, 0)


def put(ref, index, value):
    def store():
        ref[index] = value

    return store


def neighbours(ref, ends_ref, value, p, z, r):
    layers = ref.shape[1]
    lane = lanes((8, 128))
    rows, before, after = pl.ds(r, 8), pl.ds(r - 1, 8), pl.ds(r + 1, 8)
    below, above = max(z - 1, 0), min(z + 1, layers - 1)
    ends = ends_ref[p, z, rows, :]
    left = roll(jnp.where(lane == 127, ends, value), 1)
    right = roll(jnp.where(lane == 0, ends, value), 127)
    total = (left + right) + (ref[p, z, before, :] + ref[p, z, after, :])
    return total + (ref[p, below, rows, :] + ref[p, above, rows, :])


def strip_neighbours(ref, core_ref, values, r, outer_ref=None):
    params, layers = core_ref.shape[:2]
    lane = lanes((8, 128))
    col = lane % COLS
    rows, before, after = pl.ds(r, 8), pl.ds(r - 1, 8), pl.ds(r + 1, 8)
    near = []
    for p in range(params):
        value = values[p]
        ends = jnp.zeros((8, 128), jnp.float32)
        for z in range(layers):
            here = (lane == 10 * z + 4) | (lane == 10 * z + 5)
            ends = jnp.where(here, roll(core_ref[p, z, rows, :], 10 * z + 5), ends)
        left = roll(jnp.where(col == 4, ends, value), 1)
        right = roll(jnp.where(col == 5, ends, value), 127)
        if outer_ref is not None:
            outer = outer_ref[p, rows, :]
            left = jnp.where(col == 0, outer, left)
            right = jnp.where(col == 9, outer, right)
        below = jnp.where(lane < COLS, value, roll(value, COLS))
        above = jnp.where(lane >= COLS * (layers - 1), value, roll(value, 128 - COLS))
        total = (left + right) + (below + above)
        near.append(total + (ref[p, before, :] + ref[p, after, :]))
    return near


def spread_ends(ends_ref, values, rows):
    params, layers = ends_ref.shape[:2]
    for p in range(params):
        for z in range(layers):
            ends_ref[p, z, rows, :] = roll(values[p], 123 - 10 * z)


def base_of(e):
    return 1.5 * total_of([x * x for x in e]) + 5.0


def inner_of(e, u):
    return 3.0 * total_of([x * y for x, y in zip(e, u)])


def forward(
    order_ref, map_ref, row_a_ref, row_b_ref, far_a_ref, far_b_ref, strip_a_ref, strip_b_ref, table_ref,
    final_ref, e_refs, rate_refs, se_refs, m_ref, ms_ref,
    first_strip_ref, outer_ref, ends_ref, g_ref, gs_ref,
):
    params, layers = order_ref.shape[:2]
    tile = (8, 128)
    col = lanes(tile) % COLS
    maps = row_places(params, layers)[0]
    strip_refs = [first_strip_ref, *se_refs]
    every = range(params)

    odd = is_odd("wide")
    from_before = (jnp.where(odd, 1, 0), jnp.where(odd, 0, 1))

    def place(z, carry):
        for ref, before in zip((row_a_ref, row_b_ref), from_before):
            k, target = maps + z * MAP_EDGE + before * (MAP_EDGE - 8), pl.ds(16 - 16 * before, 8)
            g_ref[z, target, :] = ref[pl.ds(k, 8), :]
            for p in every:
                k = LEAD + (p * layers + z) * EDGE + before * (EDGE - 8)
                e_refs[0][p, z, target, :] = ref[pl.ds(k, 8), :]
        for p in every:
            e_refs[0][p, z, 8:16, :] = order_ref[p, z]
        return carry

    lax.fori_loop(0, layers, place, 0)

    sides = side_strips(params, strip_a_ref, strip_b_ref)
    order, _, cells = merged_strips(params, strip_a_ref, strip_b_ref)
    n = CORNER[0]
    for p in every:
        ref = first_strip_ref.at[p]
        ref[0:8, :] = jnp.zeros(tile, jnp.float32)
        ref[16:24, :] = jnp.zeros(tile, jnp.float32)
        a, b = far_a_ref[n * p : n * p + n, :], far_b_ref[n * p : n * p + n, :]
        ref[8 - n : 8, :] = jnp.where(odd, a, b)
        ref[8:16, :] = order[p]
        ref[16 : 16 + n, :] = jnp.where(odd, b, a)
        outer_ref[p, 8:16, :] = jnp.where(col == 0, roll(sides[p][0], 1), roll(sides[p][1], 127))
    at, n = params * (CORNER[0] + CORNER[1]), CORNER[2]
    gs_ref[...] = jnp.zeros_like(gs_ref)
    a, b = far_a_ref[at : at + n, :], far_b_ref[at : at + n, :]
    gs_ref[8 - n : 8, :] = jnp.where(odd, a, b)
    gs_ref[8:16, :] = cells
    gs_ref[16 : 16 + n, :] = jnp.where(odd, b, a)
    for r in (0, 8, 16):
        rows = slice(r, r + 8)
        spread_ends(ends_ref, [first_strip_ref[p, rows, :] for p in every], rows)

    def lookup(index, which):
        values = jnp.broadcast_to(table_ref[which // 2 : which // 2 + 1, :], tile)
        return jnp.take_along_axis(values, index + 64 * (which % 2), axis=1, mode="promise_in_bounds")

    for i in range(3):
        r = 8 * i
        for z in range(layers):
            index = map_ref[z] if i == 1 else g_ref[z, r : r + 8, :].astype(jnp.int32) & 63
            m_ref[z, r : r + 8, :] = lookup(index, 3 * i + 1)
        index = gs_ref[r : r + 8, :].astype(jnp.int32) & 63
        ms_ref[r : r + 8, :] = jnp.where(col < 5, lookup(index, 3 * i), lookup(index, 3 * i + 2))

    def step(t, windows, strip_windows, end_windows):
        old, old_strip = e_refs[t], strip_refs[t]
        last = t == ITERS - 1

        def core(z, i, r):
            rows = pl.ds(r, 8)
            base = base_of([old[p, z, rows, :] for p in every])
            m = m_ref[z, rows, :]
            stores = []
            for p in every:
                e = old[p, z, rows, :]
                rate = e * (base - 0.5 * (e * e)) - neighbours(old, ends_ref, e, p, z, r)
                new = e - m * rate
                stores.append(put(rate_refs[t], (p, z, rows, slice(None)), rate))
                if last:
                    stores.append(put(final_ref, (p, z), new))
                else:
                    stores.append(put(e_refs[t + 1], (p, z, rows, slice(None)), new))
            return stores

        each_tile(layers, windows, core)
        if last:
            return

        def strip(r):
            rows = pl.ds(r, 8)
            e = [old_strip[p, rows, :] for p in every]
            m = ms_ref[rows, :]
            base = base_of(e)
            near = strip_neighbours(old_strip, old, e, r, outer_ref if t == 0 else None)
            for p in every:
                rate = e[p] * (base - 0.5 * (e[p] * e[p])) - near[p]
                strip_refs[t + 1][p, rows, :] = e[p] - m * rate

        each_window(strip_windows, strip)

        def ends(r):
            rows = pl.ds(r, 8)
            spread_ends(ends_ref, [strip_refs[t + 1][p, rows, :] for p in every], rows)

        each_window(end_windows, ends)

    step(0, (3, 3, 13), (4, 2), (4, 2))
    step(1, (4, 2, 12), (4, 2), (4, 2))
    step(2, (4, 2, 12), (4, 2), (8, 1))
    step(3, (8, 1, 8), None, None)


def backward(
    cot_ref, map_ref, row_a_ref, row_b_ref, far_a_ref, far_b_ref, strip_a_ref, strip_b_ref,
    e_refs, rate_refs, se_refs, m_ref, ms_ref,
    adjoint_ref, sums_ref,
    lam_refs, slam_refs, u_refs, su_refs, ends_ref, work_ref, binned_ref,
):
    params, layers = cot_ref.shape[:2]
    cots = row_places(params, layers)[1]
    tile = (8, 128)
    every = range(params)

    odd = is_odd("wide")
    from_before = (jnp.where(odd, 1, 0), jnp.where(odd, 0, 1))

    def place(z, carry):
        for ref, base, before in zip((row_a_ref, row_b_ref), (cots, 0), from_before):
            rows = pl.ds(16 - 16 * before, 8)
            m = m_ref[z, rows, :]
            for p in every:
                k = base + LEAD + (p * layers + z) * ADJ_EDGE + before * (ADJ_EDGE - 8)
                value = ref[pl.ds(k, 8), :]
                lam_refs[0][p, z, rows, :] = value
                u_refs[0][p, z, rows, :] = m * value
        m = m_ref[z, 8:16, :]
        for p in every:
            lam_refs[0][p, z, 8:16, :] = cot_ref[p, z]
            u_refs[0][p, z, 8:16, :] = m * cot_ref[p, z]
        return carry

    lax.fori_loop(0, layers, place, 0)
    _, cot, _ = merged_strips(params, strip_a_ref, strip_b_ref)
    n = CORNER[1]
    for p in every:
        at = params * CORNER[0] + n * p
        ref = slam_refs[0].at[p]
        ref[0:8, :] = jnp.zeros(tile, jnp.float32)
        ref[16:24, :] = jnp.zeros(tile, jnp.float32)
        a, b = far_a_ref[at : at + n, :], far_b_ref[at : at + n, :]
        ref[8 - n : 8, :] = jnp.where(odd, a, b)
        ref[8:16, :] = cot[p]
        ref[16 : 16 + n, :] = jnp.where(odd, b, a)
        for r in (0, 8, 16):
            su_refs[0][p, r : r + 8, :] = ms_ref[r : r + 8, :] * ref[r : r + 8, :]

    def spread(slot, windows):
        def ends(r):
            rows = pl.ds(r, 8)
            spread_ends(ends_ref, [su_refs[slot][p, rows, :] for p in every], rows)

        each_window(windows, ends)

    def step(t, slot, windows, strip_windows, end_windows):
        old, old_strip = u_refs[slot], su_refs[slot]

        def core(z, i, r):
            rows = pl.ds(r, 8)
            e = [e_refs[t][p, z, rows, :] for p in every]
            u = [old[p, z, rows, :] for p in every]
            base, inner = base_of(e), inner_of(e, u)
            m = m_ref[z, rows, :]
            work = total_of([lam_refs[slot][p, z, rows, :] * rate_refs[t][p, z, rows, :] for p in every])
            stores = [put(work_ref, (t - 1, z, i), work)]
            for p in every:
                e, u = e_refs[t][p, z, rows, :], old[p, z, rows, :]
                change = u * (base - 1.5 * (e * e)) + e * inner - neighbours(old, ends_ref, u, p, z, r)
                new = lam_refs[slot][p, z, rows, :] - change
                stores.append(put(lam_refs[1 - slot], (p, z, rows, slice(None)), new))
                stores.append(put(u_refs[1 - slot], (p, z, rows, slice(None)), m * new))
            return stores

        each_tile(layers, windows, core)

        def strip(r):
            rows = pl.ds(r, 8)
            e = [se_refs[t - 1][p, rows, :] for p in every]
            u = [old_strip[p, rows, :] for p in every]
            m = ms_ref[rows, :]
            base, inner = base_of(e), inner_of(e, u)
            near = strip_neighbours(old_strip, old, u, r)
            for p in every:
                change = u[p] * (base - 1.5 * (e[p] * e[p])) + e[p] * inner - near[p]
                new = slam_refs[slot][p, rows, :] - change
                slam_refs[1 - slot][p, rows, :] = new
                su_refs[1 - slot][p, rows, :] = m * new

        each_window(strip_windows, strip)
        spread(1 - slot, end_windows)

    spread(0, (4, 2))
    step(3, 0, (4, 2, 12), (4, 2), (4, 2))
    step(2, 1, (4, 2, 12), (4, 2), (4, 2))
    step(1, 0, (4, 2, 12), (8, 1), (8, 1))

    def last(z, i, r):
        rows = pl.ds(r, 8)
        e = [e_refs[0][p, z, rows, :] for p in every]
        u = [u_refs[1][p, z, rows, :] for p in every]
        base, inner = base_of(e), inner_of(e, u)
        stores = []
        for p in every:
            e, u = e_refs[0][p, z, rows, :], u_refs[1][p, z, rows, :]
            change = u * (base - 1.5 * (e * e)) + e * inner - neighbours(u_refs[1], ends_ref, u, p, z, r)
            stores.append(put(adjoint_ref, (p, z), lam_refs[1][p, z, rows, :] - change))
        return stores

    each_tile(layers, (8, 1, 8), last)

    grains = [map_ref[z] for z in range(layers)]
    cells = []
    for z in range(layers):
        upper = work_ref[0, z, 0] + work_ref[1, z, 0] + work_ref[2, z, 0]
        lower = work_ref[0, z, 1] + work_ref[1, z, 1] + work_ref[2, z, 1]
        first = total_of([lam_refs[1][p, z, 8:16, :] * rate_refs[0][p, z, 8:16, :] for p in every])
        cells.append(jnp.concatenate([upper[4:8], lower[0:4]], axis=0) + first)

    def bin_one(g, carry):
        kept = [jnp.where(grains[z] == g, cells[z], 0.0) for z in range(layers)]
        total = sum(kept[1:4], kept[0]) + sum(kept[5:8], kept[4]) + sum(kept[9:], kept[8])
        binned_ref[pl.ds(g, 1), :] = jnp.sum(total, axis=0, keepdims=True)
        return carry

    lax.fori_loop(0, binned_ref.shape[0], bin_one, 0, unroll=4)
    ones = jnp.full((8, 128), -TIME_STEP, jnp.float32)
    sums = lax.dot_general(
        ones, binned_ref[...], (((1,), (1,)), ((), ())),
        precision=lax.Precision.HIGHEST, preferred_element_type=jnp.float32,
    )
    for k in range(0, sums_ref.shape[0], 8):
        sums_ref[k : k + 8, :] = sums


def pick_owned(owned, slots_ref, sums_ref, out_ref, total_ref, dense_ref):
    base = (lax.axis_index("wide") * lax.axis_size("narrow") + lax.axis_index("narrow")) * owned
    tile = (8, 128)
    for k in range(dense_ref.shape[0]):
        dense_ref[k : k + 1, 0:64] = sums_ref[2 * k : 2 * k + 1, :]
        dense_ref[k : k + 1, 64:128] = sums_ref[2 * k + 1 : 2 * k + 2, :]
    sub = lax.broadcasted_iota(jnp.int32, tile, 0)
    blocks = total_ref.shape[0] // 8
    step = 25
    for first in range(0, blocks, step):
        some = range(first, min(first + step, blocks))

        def body(k, acc, some=some):
            shifted = jnp.broadcast_to(slots_ref[pl.ds(k, 1), :], tile) - (sub + base)
            value = jnp.broadcast_to(dense_ref[pl.ds(k, 1), :], tile)
            return tuple(a + jnp.where(shifted == 8 * j, value, 0.0) for a, j in zip(acc, some))

        zero = tuple(jnp.zeros(tile, jnp.float32) for _ in some)
        acc = lax.fori_loop(0, slots_ref.shape[0], body, zero, unroll=8)
        for a, j in zip(acc, some):
            total_ref[8 * j : 8 * j + 8, :] = a
    whole = lax.dot_general(
        jnp.ones(tile, jnp.float32), total_ref[...], (((1,), (1,)), ((), ())),
        precision=lax.Precision.HIGHEST, preferred_element_type=jnp.float32,
    )
    out_ref[...] = whole[0:1, 0:owned]


def f32(*shape):
    return jax.ShapeDtypeStruct(shape, jnp.float32)


def kernel(body, out_shape, scratch=(), name=None, cost=0, **specs):
    if cost:
        specs["cost_estimate"] = pl.CostEstimate(flops=cost, bytes_accessed=cost // 1000, transcendentals=0)
    return pl.pallas_call(
        body, out_shape=out_shape, scratch_shapes=list(scratch), name=name, **specs,
        compiler_params=pltpu.CompilerParams(vmem_limit_bytes=VMEM_LIMIT),
    )


def opposite(value, axis):
    return lax.ppermute(value, axis, [(i, (i + 2) % 4) for i in range(4)])


def swapped(value, axis, count, partner):
    step = [1 if (i + partner) % 2 == 0 else -1 for i in range(count)]
    return lax.ppermute(value, axis, [(i, (i + by) % count) for i, by in enumerate(step)])


def per_device(counts, order_init, cotangent, grain_map, brick_grains, grain_slot, mobility):
    wide_count, narrow_count = counts
    params, layers = order_init.shape[:2]
    assert order_init.shape[2:] == (8, 128) and layers * COLS < 128
    owned = mobility.shape[0]
    listed = brick_grains.shape[1]
    bricks = brick_grains.shape[0]

    both = ("wide", "narrow")
    count = wide_count * narrow_count
    small = counts == (4, 4)
    assert listed == 64 and bricks == count and count % 16 == 0

    owned_rows = -(-owned // 128)
    block_rows = narrow_count * owned_rows
    strip_rows = 8 * (params + 1)
    edge_rows = row_places(params, layers)[1]
    cot_rows = params * layers * ADJ_EDGE + 2 * LEAD
    vmem = lambda *shape: pltpu.VMEM(shape, jnp.float32)

    arguments = (
        order_init, grain_map, cotangent, mobility.reshape(1, owned), brick_grains, grain_slot.reshape(-1, 128)
    )
    here, anywhere = pl.BlockSpec(memory_space=pltpu.VMEM), pl.BlockSpec(memory_space=pl.ANY)
    *fetched, near_a, row_b = kernel(
        pack_rows,
        tuple(jax.ShapeDtypeStruct(x.shape, x.dtype) for x in arguments)
        + (f32(edge_rows + cot_rows, 128), f32(edge_rows, 128)),
        (pltpu.SemaphoreType.DMA((len(arguments),)),), name="pack_rows",
        in_specs=[pl.BlockSpec(memory_space=pltpu.HBM)] * len(arguments),
    )(*(pltpu.with_memory_space_constraint(x, pltpu.HBM) for x in arguments))
    order_init, grain_map, cotangent, mobility_row, brick_grains, grain_slot = fetched
    strip_a, strip_b, block = kernel(
        pack_strips, (f32(strip_rows + block_rows, 128),) * 2 + (f32(block_rows, 128),),
        name="pack_strips", in_specs=[here] * 4 + [anywhere],
    )(order_init, grain_map, cotangent, mobility_row, row_b)
    row_b = swapped(row_b, "wide", wide_count, 1)
    near_a = swapped(near_a, "wide", wide_count, 0)
    strip_b = swapped(strip_b, "narrow", narrow_count, 1)
    strip_a = swapped(strip_a, "narrow", narrow_count, 0)
    others = [opposite(block, "narrow")] if small else []

    corners = corner_rows(params)
    far_a, far_b, block = kernel(
        functools.partial(pack_far, params),
        (f32(corners + block_rows, 128),) * 2 + (f32(block_rows, 128),), name="pack_far", cost=0,
    )(strip_a, strip_b, block, *others)
    far_b = swapped(far_b, "wide", wide_count, 1)
    far_a = swapped(far_a, "wide", wide_count, 0)
    slots = kernel(
        find_slots, jax.ShapeDtypeStruct((bricks // 2, 128), jnp.int32), name="find_slots",
        in_specs=[here, here, anywhere],
    )(brick_grains, grain_slot, block)
    cot_b = kernel(pack_cot, f32(cot_rows, 128), name="pack_cot", in_specs=[here, anywhere])(cotangent, far_a)
    cot_b = swapped(cot_b, "wide", wide_count, 1)

    if small:
        mobs = (block, far_a, far_b, opposite(block, "wide"))
    else:
        own = jnp.pad(mobility, (0, -owned % 128)).reshape(owned_rows, 128)
        mobs = (lax.all_gather(own, both, axis=0, tiled=True),)
    table = kernel(
        functools.partial(find_mobility, counts, owned), f32(8, 128),
        (pltpu.VMEM((8, 128), jnp.int32), vmem(wide_count * block_rows, 128)),
        name="find_mobility", cost=2_500_000_000,
    )(slots, *mobs)

    padded, strip = (params, layers, ROWS, 128), (params, ROWS, 128)
    final, states, rate, halos, m, ms = kernel(
        forward,
        (
            f32(*order_init.shape), [f32(*padded)] * ITERS, [f32(*padded)] * ITERS,
            [f32(*strip)] * (ITERS - 1), f32(layers, ROWS, 128), f32(ROWS, 128),
        ),
        (vmem(*strip), vmem(*strip), vmem(*padded), vmem(layers, ROWS, 128), vmem(ROWS, 128)),
        name="forward", cost=0,
    )(order_init, grain_map, near_a, row_b, far_a, far_b, strip_a, strip_b, table)
    adjoint, sums = kernel(
        backward,
        (f32(*order_init.shape), f32(bricks, listed)),
        (
            [vmem(*padded)] * 2, [vmem(*strip)] * 2, [vmem(*padded)] * 2, [vmem(*strip)] * 2, vmem(*padded),
            vmem(ITERS - 1, layers, 2, 8, 128), vmem(listed, 128),
        ),
        name="backward",
    )(
        cotangent, grain_map, near_a, cot_b, far_a, far_b, strip_a, strip_b,
        states, rate, halos, m, ms,
    )

    sums = lax.all_to_all(sums, both, 0, 0, tiled=True)
    grads = kernel(
        functools.partial(pick_owned, owned), f32(1, owned),
        (vmem(owned + -owned % 8, 128), vmem(bricks // 2, 128)), name="pick_owned",
    )(slots, sums)
    return final, adjoint, grads.reshape(owned)


def solution(mesh):
    counts = (mesh.shape["wide"], mesh.shape["narrow"])
    field = P("groups", None, "wide", "narrow")
    spread = P(("groups", "wide", "narrow"))
    return jax.shard_map(
        functools.partial(per_device, counts),
        mesh=mesh,
        in_specs=(field, field, P("groups", "wide", "narrow"), P("groups", None), P("groups"), spread),
        out_specs=(field, field, spread),
        check_vma=False,
    )
```

```python
import functools

import jax
import jax.numpy as jnp
from jax import lax
from jax.experimental import pallas as pl
from jax.experimental.pallas import tpu as pltpu
from jax.sharding import PartitionSpec as P

ITERS = 4
TIME_STEP = 0.05

EDGE = 6
MAP_EDGE = 5
ADJ_EDGE = 4
ROWS = 24
COLS = 10
LEAD = 8
CORNER = (5, 3, 4)

VMEM_LIMIT = 24 * 1024 * 1024


def lanes(shape):
    return lax.broadcasted_iota(jnp.int32, shape, len(shape) - 1)


def roll(value, shift):
    return pltpu.roll(value, shift, 1)


def is_odd(axis):
    return lax.rem(lax.axis_index(axis), 2) == 1


def pack_strips(order_ref, map_ref, cot_ref, mob_ref, after_ref, strip_a_ref, strip_b_ref, block_ref):
    params, layers = order_ref.shape[:2]
    odd = is_odd("narrow")
    lane = lanes((8, 128))
    zero = jnp.zeros((8, 128), jnp.float32)

    def span(first, size):
        return ((lane - first) & 127) < size

    for field in range(params + 1):
        right, left = zero, zero
        for z in range(layers):
            value = order_ref[field, z] if field < params else map_ref[z].astype(jnp.float32)
            moved = roll(value, 10 * z + 5)
            right = jnp.where(span(10 * z - 1, 6), moved, right)
            left = jnp.where(span(10 * z + 5, 6), moved, left)
            if field < params:
                right = jnp.where(span(10 * z + 5, 4), roll(cot_ref[field, z], 10 * z + 9), right)
                left = jnp.where(span(10 * z + 1, 4), roll(cot_ref[field, z], 10 * z + 1), left)
        rows = slice(8 * field, 8 * field + 8)
        strip_a_ref[rows, :] = jnp.where(odd, left, right)
        strip_b_ref[rows, :] = jnp.where(odd, right, left)
    owned = mob_ref.shape[1]
    owned_rows = -(-owned // 128)
    block_ref[...] = jnp.zeros_like(block_ref)
    first = lax.axis_index("narrow") * owned_rows
    for i in range(owned_rows):
        size = min(128, owned - 128 * i)
        row = mob_ref[0:1, 128 * i : 128 * i + size]
        if size < 128:
            row = jnp.concatenate([row, jnp.zeros((1, 128 - size), jnp.float32)], axis=1)
        block_ref[pl.ds(first + i, 1), :] = row
    for ref in (strip_a_ref, strip_b_ref):
        ref[8 * (params + 1) :, :] = block_ref[...]


def pack_rows(*refs):
    count = (len(refs) - 3) // 2
    sources, targets = refs[:count], refs[count : 2 * count]
    near_a_ref, row_b_ref, sems = refs[2 * count :]
    copies = [pltpu.make_async_copy(a, b, sems.at[i]) for i, (a, b) in enumerate(zip(sources, targets))]
    for copy in copies:
        copy.start()
    order_ref, map_ref, cot_ref = targets[:3]
    params, layers = order_ref.shape[:2]
    maps, cots = row_places(params, layers)
    gap = jnp.zeros((LEAD, 128), jnp.float32)
    odd = is_odd("wide")
    last = (jnp.where(odd, 0, 1), jnp.where(odd, 1, 0))
    row_refs = (near_a_ref, row_b_ref)
    for ref in row_refs:
        ref[0:LEAD, :] = gap
        ref[maps - LEAD : maps, :] = gap
        ref[cots - 2 * LEAD : cots - LEAD, :] = gap
        ref[cots - LEAD : cots, :] = gap
    near_a_ref[cots : cots + LEAD, :] = gap
    near_a_ref[near_a_ref.shape[0] - LEAD :, :] = gap
    copies[0].wait()
    for p in range(params):
        for z in range(layers):
            k = LEAD + (p * layers + z) * EDGE
            for ref, is_last in zip(row_refs, last):
                ref[k : k + EDGE, :] = order_ref[p, z, pl.ds((8 - EDGE) * is_last, EDGE), :]
    for copy in copies[1:]:
        copy.wait()
    for z in range(layers):
        k = maps + z * MAP_EDGE
        for ref, is_last in zip(row_refs, last):
            ref[k : k + MAP_EDGE, :] = map_ref[z, pl.ds((8 - MAP_EDGE) * is_last, MAP_EDGE), :].astype(jnp.float32)
    rows = pl.ds((8 - ADJ_EDGE) * last[0], ADJ_EDGE)
    for p in range(params):
        for z in range(layers):
            k = cots + LEAD + (p * layers + z) * ADJ_EDGE
            near_a_ref[k : k + ADJ_EDGE, :] = cot_ref[p, z, rows, :]


def pack_cot(cot_ref, after_ref, out_ref):
    params, layers = cot_ref.shape[:2]
    out_ref[0:LEAD, :] = jnp.zeros((LEAD, 128), jnp.float32)
    out_ref[out_ref.shape[0] - LEAD :, :] = jnp.zeros((LEAD, 128), jnp.float32)
    rows = pl.ds(jnp.where(is_odd("wide"), 8 - ADJ_EDGE, 0), ADJ_EDGE)
    for p in range(params):
        for z in range(layers):
            k = LEAD + (p * layers + z) * ADJ_EDGE
            out_ref[k : k + ADJ_EDGE, :] = cot_ref[p, z, rows, :]


def row_places(params, layers):
    maps = LEAD + params * layers * EDGE + LEAD
    length = maps + layers * MAP_EDGE
    return maps, length + -length % 8 + LEAD


def corner_rows(params):
    return -(-(params * (CORNER[0] + CORNER[1]) + CORNER[2]) // 8) * 8


def side_strips(params, strip_a_ref, strip_b_ref):
    odd = is_odd("narrow")
    fields = []
    for field in range(params + 1):
        rows = slice(8 * field, 8 * field + 8)
        a, b = strip_a_ref[rows, :], strip_b_ref[rows, :]
        fields.append((jnp.where(odd, a, b), jnp.where(odd, b, a)))
    return fields


def merged_strips(params, *strip_refs):
    first = lanes((8, 128)) % COLS < 5
    fields = side_strips(params, *strip_refs)
    order = [jnp.where(first, a, b) for a, b in fields[:params]]
    cot = [jnp.where(first, roll(a, 124), roll(b, 4)) for a, b in fields[:params]]
    return order, cot, jnp.where(first, *fields[params])


def pack_far(params, strip_a_ref, strip_b_ref, block_ref, *refs):
    *other_refs, far_a_ref, far_b_ref, out_block_ref = refs
    at = 8 * (params + 1)
    mobs = corner_rows(params)
    block = block_ref[...] + strip_a_ref[at:, :] + strip_b_ref[at:, :]
    for ref in other_refs:
        block = block + ref[...]
    out_block_ref[...] = block
    at = 0
    odd = is_odd("wide")
    order, cot, cells = merged_strips(params, strip_a_ref, strip_b_ref)
    for n, fields in zip(CORNER, (order, cot, [cells])):
        for both in fields:
            far_a_ref[at : at + n, :] = jnp.where(odd, both[0:n], both[8 - n : 8])
            far_b_ref[at : at + n, :] = jnp.where(odd, both[8 - n : 8], both[0:n])
            at += n
    for ref in (far_a_ref, far_b_ref):
        ref[at:mobs, :] = jnp.zeros((mobs - at, 128), jnp.float32)
        ref[mobs:, :] = block


def find_slots(bricks_ref, slot_ref, after_ref, out_ref):
    count, listed = bricks_ref.shape
    rows = slot_ref.shape[0]
    for k in range(0, out_ref.shape[0], 8):
        pairs = [
            jnp.concatenate([bricks_ref[2 * j : 2 * j + 1, :], bricks_ref[2 * j + 1 : 2 * j + 2, :]], axis=1)
            for j in range(k, k + 8)
        ]
        grain = jnp.concatenate(pairs, axis=0)
        row, col = grain >> 7, grain & 127

        def body(r, found, row=row, col=col):
            table = jnp.broadcast_to(slot_ref[pl.ds(r, 1), :], (8, 128))
            taken = jnp.take_along_axis(table, col, axis=1, mode="promise_in_bounds")
            return jnp.where(row == r, taken, found)

        out_ref[k : k + 8, :] = lax.fori_loop(0, rows, body, jnp.zeros((8, 128), jnp.int32), unroll=49)


def find_mobility(counts, owned, slots_ref, *refs):
    *mob_refs, table_ref, near_ref, all_ref = refs
    wide_count, narrow_count = counts
    tile = (8, 128)
    wide, narrow = lax.axis_index("wide"), lax.axis_index("narrow")
    if len(mob_refs) == 1:
        mob_ref = mob_refs[0]
    else:
        block_ref, far_a_ref, far_b_ref, other_ref = mob_refs
        mob_ref = all_ref
        size = block_ref.shape[0]
        odd = is_odd("wide")
        step = jnp.where(odd, 1, 3)
        for place, ref in (
            (wide, block_ref), (wide + 4 - step, far_a_ref), (wide + step, far_b_ref), (wide + 2, other_ref)
        ):
            at = pl.multiple_of(size * (place & 3), size)
            mob_ref[pl.ds(at, size), :] = ref[ref.shape[0] - size :, :]
    near_ref[...] = jnp.zeros_like(near_ref)
    for k in range(9):
        w = lax.rem(wide + k // 3 - 1 + wide_count, wide_count)
        n = lax.rem(narrow + k % 3 - 1 + narrow_count, narrow_count)
        brick = w * narrow_count + n
        row = slots_ref[pl.ds(brick >> 1, 1), :]
        half = jnp.where((brick & 1) == 0, row[:, 0:64], row[:, 64:128])
        near_ref[k // 2 : k // 2 + 1, 64 * (k % 2) : 64 * (k % 2) + 64] = half
    slot = near_ref[...]
    owned_rows = -(-owned // 128)
    owner = jnp.floor((slot.astype(jnp.float32) + 0.5) * (1.0 / owned)).astype(jnp.int32)
    inner = slot - owner * owned
    row = owner * owned_rows + (inner >> 7)
    place = inner & 127

    def body(r, found):
        values = jnp.broadcast_to(mob_ref[pl.ds(r, 1), :], tile)
        taken = jnp.take_along_axis(values, place, axis=1, mode="promise_in_bounds")
        return jnp.where(row == r, taken, found)

    found = lax.fori_loop(0, mob_ref.shape[0], body, jnp.zeros(tile, jnp.float32), unroll=32)
    table_ref[...] = TIME_STEP * found


def total_of(values):
    while len(values) > 1:
        values = [a + b for a, b in zip(values[::2], values[1::2])]
    return values[0]


def each_tile(layers, windows, body):
    start, count, most = windows
    nothing = lax.axis_index("wide") >> 20
    stores = []
    for z in range(layers):
        for i in range(count):
            stores += body(z, i, jnp.minimum(start + 8 * i, most) + nothing)
        if len(stores) >= 16 or z == layers - 1:
            for store in stores:
                store()
            stores = []


def each_window(windows, body):
    def one(i, carry):
        body(windows[0] + 8 * i)
        return carry

    lax.fori_loop(0, windows[1], one, 0)


def put(ref, index, value):
    def store():
        ref[index] = value

    return store


def neighbours(ref, ends_ref, value, p, z, r):
    layers = ref.shape[1]
    lane = lanes((8, 128))
    rows, before, after = pl.ds(r, 8), pl.ds(r - 1, 8), pl.ds(r + 1, 8)
    below, above = max(z - 1, 0), min(z + 1, layers - 1)
    ends = ends_ref[p, z, rows, :]
    left = roll(jnp.where(lane == 127, ends, value), 1)
    right = roll(jnp.where(lane == 0, ends, value), 127)
    total = (left + right) + (ref[p, z, before, :] + ref[p, z, after, :])
    return total + (ref[p, below, rows, :] + ref[p, above, rows, :])


def strip_neighbours(ref, core_ref, values, r, outer_ref=None):
    params, layers = core_ref.shape[:2]
    lane = lanes((8, 128))
    col = lane % COLS
    rows, before, after = pl.ds(r, 8), pl.ds(r - 1, 8), pl.ds(r + 1, 8)
    near = []
    for p in range(params):
        value = values[p]
        ends = jnp.zeros((8, 128), jnp.float32)
        for z in range(layers):
            here = (lane == 10 * z + 4) | (lane == 10 * z + 5)
            ends = jnp.where(here, roll(core_ref[p, z, rows, :], 10 * z + 5), ends)
        left = roll(jnp.where(col == 4, ends, value), 1)
        right = roll(jnp.where(col == 5, ends, value), 127)
        if outer_ref is not None:
            outer = outer_ref[p, rows, :]
            left = jnp.where(col == 0, outer, left)
            right = jnp.where(col == 9, outer, right)
        below = jnp.where(lane < COLS, value, roll(value, COLS))
        above = jnp.where(lane >= COLS * (layers - 1), value, roll(value, 128 - COLS))
        total = (left + right) + (below + above)
        near.append(total + (ref[p, before, :] + ref[p, after, :]))
    return near


def spread_ends(ends_ref, values, rows):
    params, layers = ends_ref.shape[:2]
    for p in range(params):
        for z in range(layers):
            ends_ref[p, z, rows, :] = roll(values[p], 123 - 10 * z)


def base_of(e):
    return 1.5 * total_of([x * x for x in e]) + 5.0


def inner_of(e, u):
    return 3.0 * total_of([x * y for x, y in zip(e, u)])


def forward(
    order_ref, map_ref, row_a_ref, row_b_ref, far_a_ref, far_b_ref, strip_a_ref, strip_b_ref, table_ref,
    final_ref, e_refs, rate_refs, se_refs, m_ref, ms_ref,
    first_strip_ref, outer_ref, ends_ref, g_ref, gs_ref,
):
    params, layers = order_ref.shape[:2]
    tile = (8, 128)
    col = lanes(tile) % COLS
    maps = row_places(params, layers)[0]
    strip_refs = [first_strip_ref, *se_refs]
    every = range(params)

    odd = is_odd("wide")
    from_before = (jnp.where(odd, 1, 0), jnp.where(odd, 0, 1))

    def place(z, carry):
        for ref, before in zip((row_a_ref, row_b_ref), from_before):
            k, target = maps + z * MAP_EDGE + before * (MAP_EDGE - 8), pl.ds(16 - 16 * before, 8)
            g_ref[z, target, :] = ref[pl.ds(k, 8), :]
            for p in every:
                k = LEAD + (p * layers + z) * EDGE + before * (EDGE - 8)
                e_refs[0][p, z, target, :] = ref[pl.ds(k, 8), :]
        for p in every:
            e_refs[0][p, z, 8:16, :] = order_ref[p, z]
        return carry

    lax.fori_loop(0, layers, place, 0)

    sides = side_strips(params, strip_a_ref, strip_b_ref)
    order, _, cells = merged_strips(params, strip_a_ref, strip_b_ref)
    n = CORNER[0]
    for p in every:
        ref = first_strip_ref.at[p]
        ref[0:8, :] = jnp.zeros(tile, jnp.float32)
        ref[16:24, :] = jnp.zeros(tile, jnp.float32)
        a, b = far_a_ref[n * p : n * p + n, :], far_b_ref[n * p : n * p + n, :]
        ref[8 - n : 8, :] = jnp.where(odd, a, b)
        ref[8:16, :] = order[p]
        ref[16 : 16 + n, :] = jnp.where(odd, b, a)
        outer_ref[p, 8:16, :] = jnp.where(col == 0, roll(sides[p][0], 1), roll(sides[p][1], 127))
    at, n = params * (CORNER[0] + CORNER[1]), CORNER[2]
    gs_ref[...] = jnp.zeros_like(gs_ref)
    a, b = far_a_ref[at : at + n, :], far_b_ref[at : at + n, :]
    gs_ref[8 - n : 8, :] = jnp.where(odd, a, b)
    gs_ref[8:16, :] = cells
    gs_ref[16 : 16 + n, :] = jnp.where(odd, b, a)
    for r in (0, 8, 16):
        rows = slice(r, r + 8)
        spread_ends(ends_ref, [first_strip_ref[p, rows, :] for p in every], rows)

    def lookup(index, which):
        values = jnp.broadcast_to(table_ref[which // 2 : which // 2 + 1, :], tile)
        return jnp.take_along_axis(values, index + 64 * (which % 2), axis=1, mode="promise_in_bounds")

    for i in range(3):
        r = 8 * i
        for z in range(layers):
            index = map_ref[z] if i == 1 else g_ref[z, r : r + 8, :].astype(jnp.int32) & 63
            m_ref[z, r : r + 8, :] = lookup(index, 3 * i + 1)
        index = gs_ref[r : r + 8, :].astype(jnp.int32) & 63
        ms_ref[r : r + 8, :] = jnp.where(col < 5, lookup(index, 3 * i), lookup(index, 3 * i + 2))

    def step(t, windows, strip_windows, end_windows):
        old, old_strip = e_refs[t], strip_refs[t]
        last = t == ITERS - 1

        def core(z, i, r):
            rows = pl.ds(r, 8)
            base = base_of([old[p, z, rows, :] for p in every])
            m = m_ref[z, rows, :]
            stores = []
            for p in every:
                e = old[p, z, rows, :]
                rate = e * (base - 0.5 * (e * e)) - neighbours(old, ends_ref, e, p, z, r)
                new = e - m * rate
                stores.append(put(rate_refs[t], (p, z, rows, slice(None)), rate))
                if last:
                    stores.append(put(final_ref, (p, z), new))
                else:
                    stores.append(put(e_refs[t + 1], (p, z, rows, slice(None)), new))
            return stores

        each_tile(layers, windows, core)
        if last:
            return

        def strip(r):
            rows = pl.ds(r, 8)
            e = [old_strip[p, rows, :] for p in every]
            m = ms_ref[rows, :]
            base = base_of(e)
            near = strip_neighbours(old_strip, old, e, r, outer_ref if t == 0 else None)
            for p in every:
                rate = e[p] * (base - 0.5 * (e[p] * e[p])) - near[p]
                strip_refs[t + 1][p, rows, :] = e[p] - m * rate

        each_window(strip_windows, strip)

        def ends(r):
            rows = pl.ds(r, 8)
            spread_ends(ends_ref, [strip_refs[t + 1][p, rows, :] for p in every], rows)

        each_window(end_windows, ends)

    step(0, (3, 3, 13), (4, 2), (4, 2))
    step(1, (4, 2, 12), (4, 2), (4, 2))
    step(2, (4, 2, 12), (4, 2), (8, 1))
    step(3, (8, 1, 8), None, None)


def backward(
    cot_ref, map_ref, row_a_ref, row_b_ref, far_a_ref, far_b_ref, strip_a_ref, strip_b_ref,
    e_refs, rate_refs, se_refs, m_ref, ms_ref,
    adjoint_ref, sums_ref,
    lam_refs, slam_refs, u_refs, su_refs, ends_ref, work_ref, binned_ref,
):
    params, layers = cot_ref.shape[:2]
    cots = row_places(params, layers)[1]
    tile = (8, 128)
    every = range(params)

    odd = is_odd("wide")
    from_before = (jnp.where(odd, 1, 0), jnp.where(odd, 0, 1))

    def place(z, carry):
        for ref, base, before in zip((row_a_ref, row_b_ref), (cots, 0), from_before):
            rows = pl.ds(16 - 16 * before, 8)
            m = m_ref[z, rows, :]
            for p in every:
                k = base + LEAD + (p * layers + z) * ADJ_EDGE + before * (ADJ_EDGE - 8)
                value = ref[pl.ds(k, 8), :]
                lam_refs[0][p, z, rows, :] = value
                u_refs[0][p, z, rows, :] = m * value
        m = m_ref[z, 8:16, :]
        for p in every:
            lam_refs[0][p, z, 8:16, :] = cot_ref[p, z]
            u_refs[0][p, z, 8:16, :] = m * cot_ref[p, z]
        return carry

    lax.fori_loop(0, layers, place, 0)
    _, cot, _ = merged_strips(params, strip_a_ref, strip_b_ref)
    n = CORNER[1]
    for p in every:
        at = params * CORNER[0] + n * p
        ref = slam_refs[0].at[p]
        ref[0:8, :] = jnp.zeros(tile, jnp.float32)
        ref[16:24, :] = jnp.zeros(tile, jnp.float32)
        a, b = far_a_ref[at : at + n, :], far_b_ref[at : at + n, :]
        ref[8 - n : 8, :] = jnp.where(odd, a, b)
        ref[8:16, :] = cot[p]
        ref[16 : 16 + n, :] = jnp.where(odd, b, a)
        for r in (0, 8, 16):
            su_refs[0][p, r : r + 8, :] = ms_ref[r : r + 8, :] * ref[r : r + 8, :]

    def spread(slot, windows):
        def ends(r):
            rows = pl.ds(r, 8)
            spread_ends(ends_ref, [su_refs[slot][p, rows, :] for p in every], rows)

        each_window(windows, ends)

    def step(t, slot, windows, strip_windows, end_windows):
        old, old_strip = u_refs[slot], su_refs[slot]

        def core(z, i, r):
            rows = pl.ds(r, 8)
            e = [e_refs[t][p, z, rows, :] for p in every]
            u = [old[p, z, rows, :] for p in every]
            base, inner = base_of(e), inner_of(e, u)
            m = m_ref[z, rows, :]
            work = total_of([lam_refs[slot][p, z, rows, :] * rate_refs[t][p, z, rows, :] for p in every])
            stores = [put(work_ref, (t - 1, z, i), work)]
            for p in every:
                e, u = e_refs[t][p, z, rows, :], old[p, z, rows, :]
                change = u * (base - 1.5 * (e * e)) + e * inner - neighbours(old, ends_ref, u, p, z, r)
                new = lam_refs[slot][p, z, rows, :] - change
                stores.append(put(lam_refs[1 - slot], (p, z, rows, slice(None)), new))
                stores.append(put(u_refs[1 - slot], (p, z, rows, slice(None)), m * new))
            return stores

        each_tile(layers, windows, core)

        def strip(r):
            rows = pl.ds(r, 8)
            e = [se_refs[t - 1][p, rows, :] for p in every]
            u = [old_strip[p, rows, :] for p in every]
            m = ms_ref[rows, :]
            base, inner = base_of(e), inner_of(e, u)
            near = strip_neighbours(old_strip, old, u, r)
            for p in every:
                change = u[p] * (base - 1.5 * (e[p] * e[p])) + e[p] * inner - near[p]
                new = slam_refs[slot][p, rows, :] - change
                slam_refs[1 - slot][p, rows, :] = new
                su_refs[1 - slot][p, rows, :] = m * new

        each_window(strip_windows, strip)
        spread(1 - slot, end_windows)

    spread(0, (4, 2))
    step(3, 0, (4, 2, 12), (4, 2), (4, 2))
    step(2, 1, (4, 2, 12), (4, 2), (4, 2))
    step(1, 0, (4, 2, 12), (8, 1), (8, 1))

    def last(z, i, r):
        rows = pl.ds(r, 8)
        e = [e_refs[0][p, z, rows, :] for p in every]
        u = [u_refs[1][p, z, rows, :] for p in every]
        base, inner = base_of(e), inner_of(e, u)
        stores = []
        for p in every:
            e, u = e_refs[0][p, z, rows, :], u_refs[1][p, z, rows, :]
            change = u * (base - 1.5 * (e * e)) + e * inner - neighbours(u_refs[1], ends_ref, u, p, z, r)
            stores.append(put(adjoint_ref, (p, z), lam_refs[1][p, z, rows, :] - change))
        return stores

    each_tile(layers, (8, 1, 8), last)

    grains = [map_ref[z] for z in range(layers)]
    cells = []
    for z in range(layers):
        upper = work_ref[0, z, 0] + work_ref[1, z, 0] + work_ref[2, z, 0]
        lower = work_ref[0, z, 1] + work_ref[1, z, 1] + work_ref[2, z, 1]
        first = total_of([lam_refs[1][p, z, 8:16, :] * rate_refs[0][p, z, 8:16, :] for p in every])
        cells.append(jnp.concatenate([upper[4:8], lower[0:4]], axis=0) + first)

    def bin_one(g, carry):
        kept = [jnp.where(grains[z] == g, cells[z], 0.0) for z in range(layers)]
        total = sum(kept[1:4], kept[0]) + sum(kept[5:8], kept[4]) + sum(kept[9:], kept[8])
        binned_ref[pl.ds(g, 1), :] = jnp.sum(total, axis=0, keepdims=True)
        return carry

    lax.fori_loop(0, binned_ref.shape[0], bin_one, 0, unroll=4)
    ones = jnp.full((8, 128), -TIME_STEP, jnp.float32)
    sums = lax.dot_general(
        ones, binned_ref[...], (((1,), (1,)), ((), ())),
        precision=lax.Precision.HIGHEST, preferred_element_type=jnp.float32,
    )
    for k in range(0, sums_ref.shape[0], 8):
        sums_ref[k : k + 8, :] = sums


def pick_owned(owned, slots_ref, sums_ref, out_ref, total_ref, dense_ref):
    base = (lax.axis_index("wide") * lax.axis_size("narrow") + lax.axis_index("narrow")) * owned
    tile = (8, 128)
    for k in range(dense_ref.shape[0]):
        dense_ref[k : k + 1, 0:64] = sums_ref[2 * k : 2 * k + 1, :]
        dense_ref[k : k + 1, 64:128] = sums_ref[2 * k + 1 : 2 * k + 2, :]
    sub = lax.broadcasted_iota(jnp.int32, tile, 0)
    blocks = total_ref.shape[0] // 8
    step = 25
    for first in range(0, blocks, step):
        some = range(first, min(first + step, blocks))

        def body(k, acc, some=some):
            shifted = jnp.broadcast_to(slots_ref[pl.ds(k, 1), :], tile) - (sub + base)
            value = jnp.broadcast_to(dense_ref[pl.ds(k, 1), :], tile)
            return tuple(a + jnp.where(shifted == 8 * j, value, 0.0) for a, j in zip(acc, some))

        zero = tuple(jnp.zeros(tile, jnp.float32) for _ in some)
        acc = lax.fori_loop(0, slots_ref.shape[0], body, zero, unroll=8)
        for a, j in zip(acc, some):
            total_ref[8 * j : 8 * j + 8, :] = a
    whole = lax.dot_general(
        jnp.ones(tile, jnp.float32), total_ref[...], (((1,), (1,)), ((), ())),
        precision=lax.Precision.HIGHEST, preferred_element_type=jnp.float32,
    )
    out_ref[...] = whole[0:1, 0:owned]


def f32(*shape):
    return jax.ShapeDtypeStruct(shape, jnp.float32)


def kernel(body, out_shape, scratch=(), name=None, cost=0, **specs):
    if cost:
        specs["cost_estimate"] = pl.CostEstimate(flops=cost, bytes_accessed=cost // 1000, transcendentals=0)
    return pl.pallas_call(
        body, out_shape=out_shape, scratch_shapes=list(scratch), name=name, **specs,
        compiler_params=pltpu.CompilerParams(vmem_limit_bytes=VMEM_LIMIT),
    )


def opposite(value, axis):
    return lax.ppermute(value, axis, [(i, (i + 2) % 4) for i in range(4)])


def swapped(value, axis, count, partner):
    step = [1 if (i + partner) % 2 == 0 else -1 for i in range(count)]
    return lax.ppermute(value, axis, [(i, (i + by) % count) for i, by in enumerate(step)])


def per_device(counts, order_init, cotangent, grain_map, brick_grains, grain_slot, mobility):
    wide_count, narrow_count = counts
    params, layers = order_init.shape[:2]
    assert order_init.shape[2:] == (8, 128) and layers * COLS < 128
    owned = mobility.shape[0]
    listed = brick_grains.shape[1]
    bricks = brick_grains.shape[0]

    both = ("wide", "narrow")
    count = wide_count * narrow_count
    small = counts == (4, 4)
    assert listed == 64 and bricks == count and count % 16 == 0

    owned_rows = -(-owned // 128)
    block_rows = narrow_count * owned_rows
    strip_rows = 8 * (params + 1)
    edge_rows = row_places(params, layers)[1]
    cot_rows = params * layers * ADJ_EDGE + 2 * LEAD
    vmem = lambda *shape: pltpu.VMEM(shape, jnp.float32)

    arguments = (
        order_init, grain_map, cotangent, mobility.reshape(1, owned), brick_grains, grain_slot.reshape(-1, 128)
    )
    here, anywhere = pl.BlockSpec(memory_space=pltpu.VMEM), pl.BlockSpec(memory_space=pl.ANY)
    *fetched, near_a, row_b = kernel(
        pack_rows,
        tuple(jax.ShapeDtypeStruct(x.shape, x.dtype) for x in arguments)
        + (f32(edge_rows + cot_rows, 128), f32(edge_rows, 128)),
        (pltpu.SemaphoreType.DMA((len(arguments),)),), name="pack_rows",
        in_specs=[pl.BlockSpec(memory_space=pltpu.HBM)] * len(arguments),
    )(*(pltpu.with_memory_space_constraint(x, pltpu.HBM) for x in arguments))
    order_init, grain_map, cotangent, mobility_row, brick_grains, grain_slot = fetched
    strip_a, strip_b, block = kernel(
        pack_strips, (f32(strip_rows + block_rows, 128),) * 2 + (f32(block_rows, 128),),
        name="pack_strips", in_specs=[here] * 4 + [anywhere],
    )(order_init, grain_map, cotangent, mobility_row, row_b)
    row_b = swapped(row_b, "wide", wide_count, 1)
    near_a = swapped(near_a, "wide", wide_count, 0)
    strip_b = swapped(strip_b, "narrow", narrow_count, 1)
    strip_a = swapped(strip_a, "narrow", narrow_count, 0)
    others = [opposite(block, "narrow")] if small else []

    corners = corner_rows(params)
    far_a, far_b, block = kernel(
        functools.partial(pack_far, params),
        (f32(corners + block_rows, 128),) * 2 + (f32(block_rows, 128),), name="pack_far", cost=0,
    )(strip_a, strip_b, block, *others)
    far_b = swapped(far_b, "wide", wide_count, 1)
    far_a = swapped(far_a, "wide", wide_count, 0)
    slots = kernel(
        find_slots, jax.ShapeDtypeStruct((bricks // 2, 128), jnp.int32), name="find_slots",
        in_specs=[here, here, anywhere],
    )(brick_grains, grain_slot, block)
    cot_b = kernel(pack_cot, f32(cot_rows, 128), name="pack_cot", in_specs=[here, anywhere])(cotangent, far_a)
    cot_b = swapped(cot_b, "wide", wide_count, 1)

    if small:
        mobs = (block, far_a, far_b, opposite(block, "wide"))
    else:
        own = jnp.pad(mobility, (0, -owned % 128)).reshape(owned_rows, 128)
        mobs = (lax.all_gather(own, both, axis=0, tiled=True),)
    table = kernel(
        functools.partial(find_mobility, counts, owned), f32(8, 128),
        (pltpu.VMEM((8, 128), jnp.int32), vmem(wide_count * block_rows, 128)),
        name="find_mobility", cost=2_500_000_000,
    )(slots, *mobs)

    padded, strip = (params, layers, ROWS, 128), (params, ROWS, 128)
    final, states, rate, halos, m, ms = kernel(
        forward,
        (
            f32(*order_init.shape), [f32(*padded)] * ITERS, [f32(*padded)] * ITERS,
            [f32(*strip)] * (ITERS - 1), f32(layers, ROWS, 128), f32(ROWS, 128),
        ),
        (vmem(*strip), vmem(*strip), vmem(*padded), vmem(layers, ROWS, 128), vmem(ROWS, 128)),
        name="forward", cost=0,
    )(order_init, grain_map, near_a, row_b, far_a, far_b, strip_a, strip_b, table)
    adjoint, sums = kernel(
        backward,
        (f32(*order_init.shape), f32(bricks, listed)),
        (
            [vmem(*padded)] * 2, [vmem(*strip)] * 2, [vmem(*padded)] * 2, [vmem(*strip)] * 2, vmem(*padded),
            vmem(ITERS - 1, layers, 2, 8, 128), vmem(listed, 128),
        ),
        name="backward",
    )(
        cotangent, grain_map, near_a, cot_b, far_a, far_b, strip_a, strip_b,
        states, rate, halos, m, ms,
    )

    sums = lax.all_to_all(sums, both, 0, 0, tiled=True)
    grads = kernel(
        functools.partial(pick_owned, owned), f32(1, owned),
        (vmem(owned + -owned % 8, 128), vmem(bricks // 2, 128)), name="pick_owned",
    )(slots, sums)
    return final, adjoint, grads.reshape(owned)


def solution(mesh):
    counts = (mesh.shape["wide"], mesh.shape["narrow"])
    field = P("groups", None, "wide", "narrow")
    spread = P(("groups", "wide", "narrow"))
    return jax.shard_map(
        functools.partial(per_device, counts),
        mesh=mesh,
        in_specs=(field, field, P("groups", "wide", "narrow"), P("groups", None), P("groups"), spread),
        out_specs=(field, field, spread),
        check_vma=False,
    )
```
